32 devices in a mesh: resp: 2 (over x), fsdp: 4 (over y, core), head: 4 (over z).
Axes of the slice: x: 2, y: 2, z: 4, core: 2. Of those that a mesh axis runs over, the one named last changes fastest.
Arguments:
- queries: bfloat16 [2048, 4096], P(('resp', 'fsdp'), 'head'), may hold values from -12 to 12
- self_keys: bfloat16 [2048, 512], P(('resp', 'fsdp'), 'head'), may hold values from -12 to 12
- self_values: bfloat16 [2048, 512], P(('resp', 'fsdp'), 'head'), may hold values from -6 to 6
- d_out: bfloat16 [2048, 4096], P(('resp', 'fsdp'), 'head'), may hold values from -12 to 12
- prompt_keys: bfloat16 [4, 256, 512], P('resp', 'fsdp', 'head'), may hold values from -6 to 6
- prompt_values: bfloat16 [4, 256, 512], P('resp', 'fsdp', 'head'), may hold values from -6 to 6
- counts: int32 [4], replicated, may hold values from 1 to 4, 8 in all
- owner_slot: int32 [4], replicated, may hold values from 0 to 3, each once
- prompt_blocks: int32 [4], replicated, may hold values from 1 to 2
- resp_blocks: int32 [8], P(('resp', 'fsdp')), may hold values from 1 to 2
- grad_q: bfloat16 [8192, 4096], P('fsdp', ('resp', 'head')), may hold values from -4 to 4
- momentum: float32 [8192, 4096], P('fsdp', ('resp', 'head')), may hold values from -30 to 30
- basis: float32 [4096, 256], P(('resp', 'head')), may hold values from -0.09375 to 0.09375
Outputs:
- dq: bfloat16 [2048, 4096], P(('resp', 'fsdp'), 'head')
- resp_kv_grad: bfloat16 [2, 2048, 512], P(None, ('resp', 'fsdp'), 'head')
- prompt_kv_grad: float32 [2, 4, 256, 512], P(None, 'resp', 'fsdp', 'head')
- update: bfloat16 [8192, 4096], P('fsdp', ('resp', 'head'))
- momentum_out: float32 [8192, 4096], P('fsdp', ('resp', 'head'))
- basis_out: float32 [4096, 256], P(('resp', 'head'))
The draws below stay inside these ranges and needn't reach their ends.
Inputs may be any that keep to these rules, and one draw needn't show every extreme that they name: `counts`: responses are stored group by group in the order of the groups. `owner_slot`: each row of prompt_keys holds the prompt of exactly one group.
All inputs are finite; a program needn't handle non-finite values.
Results may differ from the reference program's by a relative error of at most 0.0087.
Values may be sent and summed in bfloat16 or wider, within the bound.
No kernel may reach another device: no remote copies, remote signals or barrier semaphores. Data moves between devices by JAX's collectives and lax.ppermute only.
A program may use at most 64 MiB of HBM per device.

```python
import math
import jax
import jax.numpy as jnp
import numpy as np
from jax import lax

D = 8192
QH = 32
KVH = 4
HD = 128
QCOLS = 4096
RANK = 256
RLEN = 256
PLEN = 256
RESPONSES = 8
PROMPTS = 4
TOKENS = 2048


def drawn_pair(key):
    rows = RESPONSES * RLEN
    q_base = jnp.clip(jax.random.normal(jax.random.fold_in(key, 11), (rows, QH * HD), jnp.float32), -6.0, 6.0)
    k_base = jnp.clip(jax.random.normal(jax.random.fold_in(key, 12), (rows, KVH * HD), jnp.float32), -6.0, 6.0)
    return (q_base, k_base)


def draw_queries(key, part):
    return drawn_pair(key)[0].astype(jnp.bfloat16)


def draw_self_keys(key, part):
    return drawn_pair(key)[1].astype(jnp.bfloat16)


def draw_momentum(key, part):
    base = jnp.clip(jax.random.normal(jax.random.fold_in(key, 21), (D, QCOLS), jnp.float32), -5.0, 5.0)
    row_scale = jnp.exp(jax.random.uniform(jax.random.fold_in(key, 22), (D,), jnp.float32, 0.0, math.log(10.0)))
    rising = jnp.exp(math.log(3.0) * jnp.arange(D, dtype=jnp.float32) / D)
    col_scale = jnp.exp(jax.random.uniform(jax.random.fold_in(key, 23), (QCOLS,), jnp.float32, 0.0, math.log(10.0)))
    return 0.02 * base * (row_scale * rising)[:, None] * col_scale[None, :]


def tagged_blocks(key, number, largest, salt):
    values = jax.random.randint(jax.random.fold_in(key, salt), (number,), 1, largest + 1)
    marked = jax.random.randint(jax.random.fold_in(key, salt + 1), (), 0, number)
    return jnp.where(jnp.arange(number) == marked, largest, values).astype(jnp.int32)


def draw_prompt_blocks(key, part):
    return tagged_blocks(key, PROMPTS, PLEN // 128, 41)


def draw_resp_blocks(key, part):
    return tagged_blocks(key, RESPONSES, RLEN // 128, 51)


def steps_of(stream_key, shape, pieces, least, top_value):
    loudness = 1.0
    for axis_at, parts in pieces:
        heights = jax.random.uniform(jax.random.fold_in(jax.random.fold_in(stream_key, 6), axis_at), (parts,), jnp.float32, least / len(pieces), top_value / len(pieces))
        loudness = loudness * jnp.repeat(jnp.exp(heights), shape[axis_at] // parts).reshape((-1,) + (1,) * (len(shape) - 1 - axis_at))
    return loudness


def split_up(count, total, bound, skew):
    weights = [(1 << 20) // math.isqrt(grade ** skew) + 1 for grade in range(2, count + 1)]
    surplus, holding = total - bound - (count - 1), [1] * (count - 1)
    while surplus > 0:
        movable = [i for i in range(count - 1) if holding[i] < bound]
        whole, remaining = sum([weights[i] for i in movable]), surplus
        for i in movable:
            extra = min(bound - holding[i], max(1, remaining * weights[i] // whole), surplus)
            holding[i] = holding[i] + extra
            surplus = surplus - extra
    return np.array([bound] + holding)


def uneven(key, number_of, total, limit, slope):
    if number_of == 2:
        one = jax.random.randint(key, (), max(1, total - limit), min(limit, total - 1) + 1)
        return jnp.stack([one, total - one])
    sizes = jnp.asarray(split_up(number_of, total, limit, slope), jnp.int32)
    twos = (number_of - 1) // 2
    source_of, sink = sizes[1:1 + 2 * twos:2], sizes[2:2 + 2 * twos:2]
    margin = jnp.minimum(source_of - 1, limit - sink)
    passed = jax.random.randint(jax.random.fold_in(key, 1), (twos,), 0, 1 << 20) % (margin + 1)
    sizes = sizes.at[1:1 + 2 * twos:2].set(source_of - passed).at[2:2 + 2 * twos:2].set(sink + passed)
    return sizes[jax.random.permutation(jax.random.fold_in(key, 2), number_of)]


def bell_draw(stream_key, shape, scale, bound, shards=(), held_as=jnp.bfloat16):
    result = scale * jax.random.normal(stream_key, shape, jnp.float32)
    if shards:
        result = result * steps_of(stream_key, shape, shards, -0.22, 0.18)
    return jnp.clip(result, -bound, bound).astype(held_as)


def setup_inputs(seed: int = 0) -> dict:
    seeds = jax.random.split(jax.random.key(seed), 14)
    queries = draw_queries(jax.random.fold_in(seeds[13], 71), 0)
    self_keys = draw_self_keys(jax.random.fold_in(seeds[13], 71), 0)
    self_values = bell_draw(seeds[2], (TOKENS, KVH * HD), 1.0, 6.0, ((0, 8), (1, 4)))
    d_out = bell_draw(seeds[3], (TOKENS, QH * HD), 2.0, 12.0, ((0, 8), (1, 4)))
    prompt_keys = bell_draw(seeds[4], (PROMPTS, PLEN, KVH * HD), 1.0, 6.0, ((0, 2), (1, 4), (2, 4)))
    prompt_values = bell_draw(seeds[5], (PROMPTS, PLEN, KVH * HD), 1.0, 6.0, ((0, 2), (1, 4), (2, 4)))
    counts = uneven(seeds[6], PROMPTS, RESPONSES, 2 * RESPONSES // PROMPTS, 2).astype(jnp.int32)
    owner_slot = jax.random.permutation(seeds[7], PROMPTS).astype(jnp.int32)
    prompt_blocks = draw_prompt_blocks(jax.random.fold_in(seeds[13], 71), 0)
    resp_blocks = draw_resp_blocks(jax.random.fold_in(seeds[13], 71), 0)
    grad_q = bell_draw(seeds[10], (D, QCOLS), 0.3, 4.0, ((0, 4), (1, 8)))
    momentum = draw_momentum(jax.random.fold_in(seeds[13], 71), 0)
    basis = bell_draw(seeds[12], (QCOLS, RANK), QCOLS ** -0.5, 0.09375, ((0, 8),), jnp.float32)
    return dict(queries=queries, self_keys=self_keys, self_values=self_values, d_out=d_out, prompt_keys=prompt_keys, prompt_values=prompt_values, counts=counts, owner_slot=owner_slot, prompt_blocks=prompt_blocks, resp_blocks=resp_blocks, grad_q=grad_q, momentum=momentum, basis=basis)


def reference(queries, self_keys, self_values, d_out, prompt_keys, prompt_values, counts, owner_slot, prompt_blocks, resp_blocks, grad_q, momentum, basis):
    scale = HD ** (-0.5)
    per_group = QH // KVH
    width = PLEN + RLEN
    ends = jnp.cumsum(counts)
    order = jnp.arange(RESPONSES, dtype=jnp.int32)
    groups = lax.optimization_barrier(jnp.sum((ends[None, :] <= order[:, None]).astype(jnp.int32), axis=1))

    def one_response(accum, index):
        group = groups[index]
        stored = owner_slot[group]
        prompt_len = prompt_blocks[group] * 128
        resp_len = resp_blocks[index] * 128
        start = (index * RLEN).astype(jnp.int32)
        query = lax.dynamic_slice_in_dim(queries, start, RLEN, 0).astype(jnp.float32).reshape(RLEN, KVH, per_group, HD)
        keys = jnp.concatenate([prompt_keys[stored], lax.dynamic_slice_in_dim(self_keys, start, RLEN, 0)], 0)
        keys = keys.astype(jnp.float32).reshape(width, KVH, HD)
        values = jnp.concatenate([prompt_values[stored], lax.dynamic_slice_in_dim(self_values, start, RLEN, 0)], 0)
        values = values.astype(jnp.float32).reshape(width, KVH, HD)
        place = jnp.arange(width, dtype=jnp.int32)[None, :]
        position = jnp.arange(RLEN, dtype=jnp.int32)[:, None]
        inner = place - PLEN
        visible = jnp.where(place < PLEN, place < prompt_len, (inner <= position) & (inner < resp_len))
        logits = jnp.einsum('tngd,knd->ngtk', query, keys) * scale
        logits = jnp.where(visible, logits, -jnp.inf)
        peak = lax.optimization_barrier(jnp.max(logits, axis=3, keepdims=True))
        lse = peak + jnp.log(lax.optimization_barrier(jnp.sum(jnp.exp(logits - peak), axis=3, keepdims=True)))
        weight = lax.optimization_barrier(jnp.exp(logits - lse).astype(jnp.bfloat16)).astype(jnp.float32)
        output = jnp.einsum('ngtk,knd->tngd', weight, values)
        live = jnp.arange(RLEN, dtype=jnp.int32) < resp_len
        o_grad = jnp.where(live[:, None], lax.dynamic_slice_in_dim(d_out, start, RLEN, 0), 0)
        o_grad = o_grad.astype(jnp.float32).reshape(RLEN, KVH, per_group, HD)
        diag = lax.optimization_barrier(jnp.sum(o_grad * output, axis=3))
        p_grad = jnp.einsum('tngd,knd->ngtk', o_grad, values)
        s_grad = weight * (p_grad - jnp.transpose(diag, (1, 2, 0))[..., None])
        s_grad = lax.optimization_barrier(s_grad.astype(jnp.bfloat16)).astype(jnp.float32)
        q_grad = (jnp.einsum('ngtk,knd->tngd', s_grad, keys) * scale).reshape(RLEN, QH * HD).astype(jnp.bfloat16)
        k_grad = (jnp.einsum('ngtk,tngd->knd', s_grad, query) * scale).reshape(width, KVH * HD)
        v_grad = jnp.einsum('ngtk,tngd->knd', weight, o_grad).reshape(width, KVH * HD)
        accum = accum.at[:, stored].add(jnp.stack([k_grad[:PLEN], v_grad[:PLEN]], 0))
        own = jnp.stack([k_grad[PLEN:], v_grad[PLEN:]], 0).astype(jnp.bfloat16)
        return (accum, (q_grad, own))
    start_accum = jnp.zeros((2, PROMPTS, PLEN, KVH * HD), jnp.float32)
    prompt_grad, (q_grads, own_grads) = lax.scan(one_response, start_accum, order)
    dq = q_grads.reshape(TOKENS, QH * HD)
    resp_grad = jnp.transpose(own_grads, (1, 0, 2, 3)).reshape(2, TOKENS, KVH * HD)
    highest = lax.Precision.HIGHEST
    total = momentum + grad_q.astype(jnp.float32)
    projected = jnp.dot(total, basis, precision=highest)
    gram = jnp.dot(projected.T, projected, precision=highest)
    lower = jnp.linalg.cholesky(gram)
    ortho = jax.scipy.linalg.solve_triangular(lower, projected.T, lower=True).T
    back = jnp.dot(total.T, ortho, precision=highest)
    momentum_out = total - 0.05 * jnp.dot(ortho, back.T, precision=highest)
    basis_out = back * lax.rsqrt(lax.optimization_barrier(jnp.sum(back * back, axis=0)) + 1e-06)
    update = (math.sqrt(D * QCOLS / RANK) * jnp.dot(ortho, basis_out.T, precision=highest)).astype(jnp.bfloat16)
    return (dq, resp_grad, prompt_grad, update, momentum_out, basis_out)
```

```python
import functools
import math

import jax
import jax.numpy as jnp
from jax import lax
from jax.experimental import pallas as pl
from jax.experimental.pallas import tpu as pltpu
from jax.sharding import PartitionSpec as P

HD = 128
PANEL = 8
OUTER = 32
MIB = 1 << 20

momentum_keep = 0.95
norm_eps = 1e-06

F32 = jnp.float32
BF16 = jnp.bfloat16
HIGHEST = lax.Precision.HIGHEST

SMEM = pl.BlockSpec(memory_space=pltpu.SMEM)
VMEM = pl.BlockSpec(memory_space=pltpu.VMEM)


def swap(value, axes, k):
    axes = (axes,) if isinstance(axes, str) else axes
    n = math.prod(lax.axis_size(a) for a in axes)
    return lax.ppermute(value, axes, [(i, i ^ k) for i in range(n)])


def params(mib=24):
    return pltpu.CompilerParams(vmem_limit_bytes=mib * MIB)


def cost(flops, nbytes):
    return pl.CostEstimate(flops=int(flops), bytes_accessed=int(nbytes), transcendentals=0)


def halves(x):
    hi = x.astype(BF16)
    return hi, (x - hi.astype(F32)).astype(BF16)


def mm(a, b):
    return jnp.dot(a, b, preferred_element_type=F32)


def mm_full(a, b):
    return jnp.dot(a, b, precision=HIGHEST, preferred_element_type=F32)


def project_kernel(ranks, mom, grad, basis, out, b_hi, b_lo):
    @pl.when(pl.program_id(0) == 0)
    def _():
        hi, lo = halves(basis[...])
        b_hi[...] = hi
        b_lo[...] = lo

    t_hi, t_lo = halves(mom[...] + grad[...].astype(F32))
    acc = mm(t_hi, b_hi[...]) + (mm(t_hi, b_lo[...]) + mm(t_lo, b_hi[...]))
    out[...] = acc.astype(out.dtype)


def project(ranks, momentum, grad_q, basis, k, segments, dtype):
    rows, cols = momentum.shape
    rank = basis.shape[1]
    seg = rows // segments
    tile = min(seg, 256)
    nb = seg // tile

    def rows_at(i, ranks):
        return ((ranks[0] ^ k) * nb + i, 0)

    return pl.pallas_call(
        project_kernel,
        grid_spec=pltpu.PrefetchScalarGridSpec(
            num_scalar_prefetch=1,
            grid=(nb,),
            in_specs=[
                pl.BlockSpec((tile, cols), rows_at),
                pl.BlockSpec((tile, cols), rows_at),
                pl.BlockSpec((cols, rank), lambda i, ranks: (0, 0)),
            ],
            out_specs=pl.BlockSpec((tile, rank), lambda i, ranks: (i, 0)),
            scratch_shapes=[pltpu.VMEM((cols, rank), BF16)] * 2,
        ),
        out_shape=jax.ShapeDtypeStruct((seg, rank), dtype),
        compiler_params=params(),
        cost_estimate=cost(6 * seg * cols * rank, seg * cols * 6),
    )(ranks, momentum, grad_q, basis)


def split_kernel(n_recv, n_head, ranks, *refs):
    own, recvs, outs = refs[0], refs[1 : 1 + n_recv], refs[1 + n_recv :]
    chunk = outs[0].shape[0]
    for k in range(n_head):
        rows = pl.ds(pl.multiple_of((ranks[2] ^ k) * chunk, chunk), chunk)
        acc = own[rows, :]
        for r in recvs:
            acc = acc + r[rows, :].astype(F32)
        outs[k][...] = acc.astype(outs[k].dtype)


def split_sum(ranks, own, recvs, n_head):
    rows, rank = own.shape
    chunk = rows // n_head
    return pl.pallas_call(
        functools.partial(split_kernel, len(recvs), n_head),
        in_specs=[SMEM] + [VMEM] * (1 + len(recvs)),
        out_specs=[VMEM] * n_head,
        out_shape=[
            jax.ShapeDtypeStruct((chunk, rank), BF16 if k else F32) for k in range(n_head)
        ],
        compiler_params=params(),
        cost_estimate=cost(rows * rank, rows * rank * 8),
    )(ranks, own, *recvs)


def gram_kernel(n_resp, n_head, ranks, *refs):
    chunks, (pcat, gram) = refs[: n_resp * n_head], refs[n_resp * n_head :]
    size = chunks[0].shape[0]
    for j in range(n_resp):
        for k in range(n_head):
            at = (ranks[0] ^ j) * n_head + (ranks[2] ^ k)
            pcat[pl.ds(pl.multiple_of(at * size, size), size), :] = chunks[j * n_head + k][...]
    p = pcat[...]
    gram[...] = mm(p.T, p)


def gather_gram(ranks, chunks, n_resp, n_head):
    size, rank = chunks[0].shape
    rows = size * n_resp * n_head
    return pl.pallas_call(
        functools.partial(gram_kernel, n_resp, n_head),
        in_specs=[SMEM] + [VMEM] * len(chunks),
        out_specs=[VMEM] * 2,
        out_shape=[
            jax.ShapeDtypeStruct((rows, rank), BF16),
            jax.ShapeDtypeStruct((rank, rank), F32),
        ],
        compiler_params=params(),
        cost_estimate=cost(2 * rows * rank * rank, rows * rank * 4),
    )(ranks, *chunks)


def back_part_kernel(pcat, mom, grad, out, acc):
    i = pl.program_id(0)
    t_hi, t_lo = halves(mom[...] + grad[...].astype(F32))
    pt = pcat[...].T
    part = mm(pt, t_hi) + mm(pt, t_lo)

    @pl.when(i == 0)
    def _():
        acc[...] = part

    @pl.when(i > 0)
    def _():
        acc[...] += part

    @pl.when(i == pl.num_programs(0) - 1)
    def _():
        out[...] = acc[...].astype(BF16)


def back_part(pcat, momentum, grad_q):
    rows, cols = momentum.shape
    rank = pcat.shape[1]
    tile = min(rows, 512)
    return pl.pallas_call(
        back_part_kernel,
        grid=(rows // tile,),
        in_specs=[
            pl.BlockSpec((tile, rank), lambda i: (i, 0)),
            pl.BlockSpec((tile, cols), lambda i: (i, 0)),
            pl.BlockSpec((tile, cols), lambda i: (i, 0)),
        ],
        out_specs=pl.BlockSpec((rank, cols), lambda i: (0, 0)),
        scratch_shapes=[pltpu.VMEM((rank, cols), F32)],
        out_shape=jax.ShapeDtypeStruct((rank, cols), BF16),
        compiler_params=params(),
        cost_estimate=cost(4 * rows * cols * rank, rows * cols * 6),
    )(pcat, momentum, grad_q)


def factor_panel(panel, off):
    shape = (PANEL, 128)
    d = {}
    for j in range(PANEL):
        col = jnp.broadcast_to(panel[:, off + j : off + j + 1], shape)
        for i in range(j, PANEL):
            d[i, j] = jnp.broadcast_to(col[i : i + 1, :], shape)
    low, inv = {}, {}
    for j in range(PANEL):
        r = lax.rsqrt(d[j, j])
        inv[j, j] = r
        for i in range(j + 1, PANEL):
            low[i, j] = d[i, j] * r
        for k in range(j + 1, PANEL):
            for i in range(k, PANEL):
                d[i, k] = d[i, k] - low[i, j] * low[k, j]
    for j in range(PANEL):
        for i in range(j + 1, PANEL):
            acc = low[i, j] * inv[j, j]
            for k in range(j + 1, i):
                acc = acc + low[i, k] * inv[k, j]
            inv[i, j] = -(acc * inv[i, i])
    return inv


def three_parts(x):
    a = x.astype(BF16)
    rest = x - a.astype(F32)
    b = rest.astype(BF16)
    return a, b, (rest - b.astype(F32)).astype(BF16)


def cholesky_kernel(n_parts, *refs):
    parts, out, work = refs[:n_parts], refs[n_parts], refs[n_parts + 1]
    n = out.shape[0]
    wide = 2 * n
    tiles = wide // 128
    total = parts[0][...]
    for part in parts[1:]:
        total = total + part[...]
    work[:, :n] = total
    rows = lax.broadcasted_iota(jnp.int32, (n, n), 0)
    cols = lax.broadcasted_iota(jnp.int32, (n, n), 1)
    work[:, n:] = jnp.where(rows == cols, 1.0, 0.0).astype(F32)
    sub = lax.broadcasted_iota(jnp.int32, (PANEL, 128), 0)
    n_panels = OUTER // PANEL

    def step(o, carry):
        blk = [
            [work[p * PANEL : (p + 1) * PANEL, t * 128 : (t + 1) * 128] for t in range(tiles)]
            for p in range(n_panels)
        ]
        for p in range(n_panels):
            off = p * PANEL
            inv = factor_panel(blk[p][0], off)
            rows_of = [
                [jnp.broadcast_to(blk[p][t][j : j + 1, :], (PANEL, 128)) for t in range(tiles)]
                for j in range(PANEL)
            ]
            new = [None] * tiles
            for j in range(PANEL):
                col = inv[PANEL - 1, j]
                for i in range(PANEL - 2, j - 1, -1):
                    col = jnp.where(sub == i, inv[i, j], col)
                if j:
                    col = jnp.where(sub < j, 0.0, col)
                for t in range(tiles):
                    term = col * rows_of[j][t]
                    new[t] = term if new[t] is None else new[t] + term
            blk[p] = new
            if p + 1 < n_panels:
                u_rows = [
                    [jnp.broadcast_to(new[t][j : j + 1, :], (PANEL, 128)) for t in range(tiles)]
                    for j in range(PANEL)
                ]
                for b in range(p + 1, n_panels):
                    lanes = [
                        jnp.broadcast_to(blk[b][0][:, off + m : off + m + 1], (PANEL, 128))
                        for m in range(PANEL)
                    ]
                    upd = list(blk[b])
                    for k in range(PANEL):
                        v = lanes[0] * inv[k, 0]
                        for m in range(1, k + 1):
                            v = v + lanes[m] * inv[k, m]
                        for t in range(tiles):
                            upd[t] = upd[t] - v * u_rows[k][t]
                    blk[b] = upd
        u = jnp.concatenate([jnp.concatenate(row, axis=1) for row in blk], axis=0)
        lane = lax.broadcasted_iota(jnp.int32, (OUTER, n), 1)
        left = jnp.where(lane < n - OUTER * o, u[:, :n], 0.0)
        la, lb, lc = three_parts(left)
        ua, ub, uc = three_parts(u)
        lhs = jnp.concatenate([la, la, lb, la, lc, lb], axis=0)
        rhs = jnp.concatenate([ua, ub, ua, uc, ua, ub], axis=0)
        upd = mm(lhs.T, rhs)
        rest = work[OUTER:, :] - upd[OUTER:, :]
        work[: n - OUTER, :] = pltpu.roll(rest, wide - OUTER, 1)
        work[n - OUTER :, :] = pltpu.roll(u, wide - OUTER, 1)
        return carry

    lax.fori_loop(0, n // OUTER, step, 0)
    out[...] = work[:, :n]


def inverse_factor(*parts):
    n = parts[0].shape[0]
    return pl.pallas_call(
        functools.partial(cholesky_kernel, len(parts)),
        in_specs=[VMEM] * len(parts),
        out_specs=VMEM,
        scratch_shapes=[pltpu.VMEM((n, 2 * n), F32)],
        out_shape=jax.ShapeDtypeStruct((n, n), F32),
        compiler_params=params(),
        cost_estimate=cost(10_000_000_000, 4 * n * n * 4),
    )(*parts)


def back_kernel(x, wa, wb, bt_out, y_out, s_out):
    w = wa[...].astype(F32) + wb[...].astype(F32)
    bt = mm_full(x[...], w)
    bt_out[...] = bt
    y_out[...] = ((1.0 - momentum_keep) * mm_full(x[...].T, bt)).astype(BF16)
    ones = jnp.ones((8, bt.shape[1]), F32)
    s_out[...] = lax.dot_general(
        ones, bt * bt, (((1,), (1,)), ((), ())), precision=HIGHEST, preferred_element_type=F32
    )


def back_full(x, wa, wb):
    rank, cols = wa.shape
    return pl.pallas_call(
        back_kernel,
        in_specs=[VMEM] * 3,
        out_specs=[VMEM] * 3,
        out_shape=[
            jax.ShapeDtypeStruct((rank, cols), F32),
            jax.ShapeDtypeStruct((rank, cols), BF16),
            jax.ShapeDtypeStruct((8, rank), F32),
        ],
        compiler_params=params(),
        cost_estimate=cost(24 * rank * rank * cols, rank * cols * 12),
    )(x, wa, wb)


def momentum_kernel(pcat, mom, grad, y, out):
    out[...] = mom[...] + grad[...].astype(F32) - mm(pcat[...], y[...])


def new_momentum(pcat, momentum, grad_q, y):
    rows, cols = momentum.shape
    rank = pcat.shape[1]
    tile = min(rows, 256)
    return pl.pallas_call(
        momentum_kernel,
        grid=(rows // tile,),
        in_specs=[
            pl.BlockSpec((tile, rank), lambda i: (i, 0)),
            pl.BlockSpec((tile, cols), lambda i: (i, 0)),
            pl.BlockSpec((tile, cols), lambda i: (i, 0)),
            pl.BlockSpec((rank, cols), lambda i: (0, 0)),
        ],
        out_specs=pl.BlockSpec((tile, cols), lambda i: (i, 0)),
        out_shape=jax.ShapeDtypeStruct((rows, cols), F32),
        compiler_params=params(),
        cost_estimate=cost(2 * rows * cols * rank, rows * cols * 10),
    )(pcat, momentum, grad_q, y)


def update_kernel(n_sums, gain, pcat, x, bt, *refs):
    sums, (upd, basis_out, z_hi, z_lo) = refs[:n_sums], refs[n_sums:]

    @pl.when(pl.program_id(0) == 0)
    def _():
        total = sums[0][...]
        for s in sums[1:]:
            total = total + s[...]
        scale = lax.rsqrt(total + norm_eps).T[:, :1]
        scaled = bt[...] * scale
        basis_out[...] = scaled.T
        hi, lo = halves(gain * mm_full(x[...].T, scaled))
        z_hi[...] = hi
        z_lo[...] = lo

    p = pcat[...]
    upd[...] = (mm(p, z_hi[...]) + mm(p, z_lo[...])).astype(BF16)


def final_update(pcat, x, bt, sums, gain):
    rows, rank = pcat.shape
    cols = bt.shape[1]
    tile = min(rows, 512)
    whole = lambda i: (0, 0)
    return pl.pallas_call(
        functools.partial(update_kernel, len(sums), gain),
        grid=(rows // tile,),
        in_specs=[
            pl.BlockSpec((tile, rank), lambda i: (i, 0)),
            pl.BlockSpec((rank, rank), whole),
            pl.BlockSpec((rank, cols), whole),
        ]
        + [pl.BlockSpec((8, rank), whole)] * len(sums),
        out_specs=[
            pl.BlockSpec((tile, cols), lambda i: (i, 0)),
            pl.BlockSpec((cols, rank), whole),
        ],
        scratch_shapes=[pltpu.VMEM((rank, cols), BF16)] * 2,
        out_shape=[
            jax.ShapeDtypeStruct((rows, cols), BF16),
            jax.ShapeDtypeStruct((cols, rank), F32),
        ],
        compiler_params=params(),
        cost_estimate=cost(4 * rows * cols * rank, rows * cols * 3),
    )(pcat, x, bt, *sums)


def group_of(counts, response):
    group = jnp.int32(0)
    end = jnp.int32(0)
    for g in range(counts.shape[0]):
        end = end + counts[g]
        group = group + (end <= response).astype(jnp.int32)
    return group


def select_kernel(n_resp, n_fsdp, ranks, counts, slots, *refs):
    keys, values, outs = refs[:n_resp], refs[n_resp : 2 * n_resp], refs[2 * n_resp :]
    held = keys[0].shape[0]
    for k in range(n_fsdp):
        slot = slots[group_of(counts, ranks[0] * n_fsdp + (ranks[1] ^ k))]
        owner, local = slot // held, slot % held
        for a, arrays in enumerate((keys, values)):
            for j in range(n_resp):

                @pl.when(owner == (ranks[0] ^ j))
                def _():
                    outs[k][a] = arrays[j][local]


def select_prompts(ranks, counts, slots, keys, values, n_fsdp):
    _, piece, width = keys[0].shape
    return pl.pallas_call(
        functools.partial(select_kernel, len(keys), n_fsdp),
        in_specs=[SMEM] * 3 + [VMEM] * (2 * len(keys)),
        out_specs=[VMEM] * n_fsdp,
        out_shape=[jax.ShapeDtypeStruct((2, piece, width), BF16)] * n_fsdp,
        compiler_params=params(),
        cost_estimate=cost(1000, 8 * n_fsdp * piece * width),
    )(ranks, counts, slots, *keys, *values)


def attention_kernel(n_fsdp, ranks, counts, prompt_blocks, resp_blocks, q, sk, sv, go, *refs):
    pieces, refs = refs[:n_fsdp], refs[n_fsdp:]
    dq, own, refs = refs[0], refs[1], refs[2:]
    sends, (keys, values, dk, dv) = refs[:n_fsdp], refs[n_fsdp:]
    piece = pieces[0].shape[1]
    cap = piece * n_fsdp
    length = q.shape[0]
    scale = HD ** (-0.5)
    for k in range(n_fsdp):
        rows = pl.ds(pl.multiple_of((ranks[1] ^ k) * piece, piece), piece)
        keys[rows, :] = pieces[k][0]
        values[rows, :] = pieces[k][1]
    keys[cap:, :] = sk[...]
    values[cap:, :] = sv[...]
    prompt_len = prompt_blocks[group_of(counts, ranks[0] * n_fsdp + ranks[1])] * 128
    resp_len = resp_blocks[0] * 128
    width = keys.shape[0]
    place = lax.broadcasted_iota(jnp.int32, (width, length), 0)
    pos = lax.broadcasted_iota(jnp.int32, (width, length), 1)
    inner = place - cap
    seen = ((place < cap) & (place < prompt_len)) | (
        (place >= cap) & (inner <= pos) & (inner < resp_len)
    )
    bias = jnp.where(seen, 0.0, -jnp.inf).astype(F32)
    live = lax.broadcasted_iota(jnp.int32, (length, HD), 0) < resp_len
    nt = (((1,), (1,)), ((), ()))
    kall = keys[...]
    vall = values[...]
    kt = kall.T
    dk[...] = jnp.zeros_like(dk)
    dv[...] = jnp.zeros_like(dv)
    for h in range(q.shape[1] // HD):
        cols = slice(h * HD, (h + 1) * HD)
        qh = q[:, cols]
        gh = jnp.where(live, go[:, cols], jnp.zeros((), BF16))
        logits = lax.dot_general(kall, qh, nt, preferred_element_type=F32) * scale + bias
        peak = jnp.max(logits, axis=0, keepdims=True)
        e = jnp.exp(logits - peak)
        w = (e * (1.0 / jnp.sum(e, axis=0, keepdims=True))).astype(BF16)
        dp = lax.dot_general(vall, gh, nt, preferred_element_type=F32)
        wf = w.astype(F32)
        diag = jnp.sum(wf * dp, axis=0, keepdims=True)
        ds = (wf * (dp - diag)).astype(BF16)
        dk[...] += mm(ds, qh)
        dv[...] += mm(w, gh)
        dq[:, cols] = (mm(kt, ds) * scale).T.astype(BF16)
    own[0] = (dk[cap:, :] * scale).astype(BF16)
    own[1] = dv[cap:, :].astype(BF16)
    for k in range(n_fsdp):
        rows = pl.ds(pl.multiple_of((ranks[1] ^ k) * piece, piece), piece)
        sends[k][0] = dk[rows, :] * scale
        sends[k][1] = dv[rows, :]


def attention(ranks, counts, prompt_blocks, resp_blocks, q, sk, sv, go, pieces):
    n_fsdp = len(pieces)
    piece = pieces[0].shape[1]
    length, width = q.shape
    total = piece * n_fsdp + length
    return pl.pallas_call(
        functools.partial(attention_kernel, n_fsdp),
        in_specs=[SMEM] * 4 + [VMEM] * (4 + n_fsdp),
        out_specs=[VMEM] * (2 + n_fsdp),
        out_shape=[
            jax.ShapeDtypeStruct((length, width), BF16),
            jax.ShapeDtypeStruct((2, length, HD), BF16),
        ]
        + [jax.ShapeDtypeStruct((2, piece, HD), F32)] * n_fsdp,
        scratch_shapes=[pltpu.VMEM((total, HD), BF16)] * 2 + [pltpu.VMEM((total, HD), F32)] * 2,
        compiler_params=params(32),
        cost_estimate=cost(6_000_000_000, length * width * 8),
    )(ranks, counts, prompt_blocks, resp_blocks, q, sk, sv, go, *pieces)


def by_slot_kernel(n_resp, n_fsdp, ranks, counts, slots, *refs):
    parts, outs = refs[:n_fsdp], refs[n_fsdp:]
    held = outs[0].shape[1]
    slot_of = [
        slots[group_of(counts, ranks[0] * n_fsdp + (ranks[1] ^ k))] for k in range(n_fsdp)
    ]
    for j in range(n_resp):
        for local in range(held):
            slot = (ranks[0] ^ j) * held + local
            acc = jnp.zeros(parts[0].shape, F32)
            for k in range(n_fsdp):
                acc = acc + jnp.where(slot_of[k] == slot, parts[k][...], 0.0)
            outs[j][:, local] = acc


def sum_by_slot(ranks, counts, slots, parts, n_resp):
    held = counts.shape[0] // n_resp
    _, piece, width = parts[0].shape
    return pl.pallas_call(
        functools.partial(by_slot_kernel, n_resp, len(parts)),
        in_specs=[SMEM] * 3 + [VMEM] * len(parts),
        out_specs=[VMEM] * n_resp,
        out_shape=[jax.ShapeDtypeStruct((2, held, piece, width), F32)] * n_resp,
        compiler_params=params(),
        cost_estimate=cost(1000, 8 * len(parts) * piece * width * 4),
    )(ranks, counts, slots, *parts)


def on_device(
    queries,
    self_keys,
    self_values,
    d_out,
    prompt_keys,
    prompt_values,
    counts,
    owner_slot,
    prompt_blocks,
    resp_blocks,
    grad_q,
    momentum,
    basis,
):
    n_resp, n_fsdp, n_head = (lax.axis_size(a) for a in ("resp", "fsdp", "head"))
    ranks = jnp.stack([lax.axis_index(a) for a in ("resp", "fsdp", "head")]).astype(jnp.int32)
    gain = math.sqrt(
        momentum.shape[0] * n_fsdp * momentum.shape[1] * n_resp * n_head / basis.shape[1]
    )

    keys = [prompt_keys] + [swap(prompt_keys, "resp", j) for j in range(1, n_resp)]
    values = [prompt_values] + [swap(prompt_values, "resp", j) for j in range(1, n_resp)]

    sent = [project(ranks, momentum, grad_q, basis, j, n_resp, BF16) for j in range(1, n_resp)]
    recvs = [swap(s, "resp", j + 1) for j, s in enumerate(sent)]
    mine = project(ranks, momentum, grad_q, basis, 0, n_resp, F32)

    chosen = select_prompts(ranks, counts, owner_slot, keys, values, n_fsdp)
    pieces = [chosen[0]] + [swap(chosen[k], "fsdp", k) for k in range(1, n_fsdp)]

    split = split_sum(ranks, mine, recvs, n_head)
    acc = split[0]
    for part in [swap(split[k], "head", k) for k in range(1, n_head)]:
        acc = acc + part.astype(F32)
    piece0 = acc.astype(BF16)

    attended = attention(
        ranks, counts, prompt_blocks, resp_blocks, queries, self_keys, self_values, d_out, pieces
    )
    dq, resp_grad, parts = attended[0], attended[1], attended[2:]

    along = [piece0] + [swap(piece0, "head", k) for k in range(1, n_head)]
    chunks = list(along)
    for j in range(1, n_resp):
        chunks += [swap(c, "resp", j) for c in along]
    pcat, gram = gather_gram(ranks, chunks, n_resp, n_head)

    returned = [parts[0]] + [swap(parts[k], "fsdp", k) for k in range(1, n_fsdp)]
    slots = sum_by_slot(ranks, counts, owner_slot, returned, n_resp)
    prompt_grad = slots[0]
    for j in range(1, n_resp):
        prompt_grad = prompt_grad + swap(slots[j], "resp", j)

    bits = [1 << b for b in range(n_fsdp.bit_length() - 1)]
    for bit in bits[:-1]:
        gram = gram + swap(gram, "fsdp", bit)
    gram_parts = (gram, swap(gram, "fsdp", bits[-1]))
    w = back_part(pcat, momentum, grad_q)
    for bit in bits[:-1]:
        w = (w.astype(F32) + swap(w, "fsdp", bit).astype(F32)).astype(BF16)
    w_other = swap(w, "fsdp", bits[-1])

    x = inverse_factor(*gram_parts)
    bt, y, squares = back_full(x, w, w_other)
    sums = [squares] + [
        swap(squares, ("resp", "head"), k) for k in range(1, n_resp * n_head)
    ]
    momentum_out = new_momentum(pcat, momentum, grad_q, y)
    update, basis_out = final_update(pcat, x, bt, sums, gain)
    return (dq, resp_grad, prompt_grad, update, momentum_out, basis_out)


def solution(mesh):
    placed = (
        P(("resp", "fsdp"), "head"),
        P(("resp", "fsdp"), "head"),
        P(("resp", "fsdp"), "head"),
        P(("resp", "fsdp"), "head"),
        P("resp", "fsdp", "head"),
        P("resp", "fsdp", "head"),
        P(),
        P(),
        P(),
        P(("resp", "fsdp")),
        P("fsdp", ("resp", "head")),
        P("fsdp", ("resp", "head")),
        P(("resp", "head"), None),
    )
    return jax.shard_map(
        on_device,
        mesh=mesh,
        in_specs=placed,
        out_specs=(
            P(("resp", "fsdp"), "head"),
            P(None, ("resp", "fsdp"), "head"),
            P(None, "resp", "fsdp", "head"),
            P("fsdp", ("resp", "head")),
            P("fsdp", ("resp", "head")),
            P(("resp", "head"), None),
        ),
        check_vma=False,
    )
```

```python
import functools
import math

import jax
import jax.numpy as jnp
from jax import lax
from jax.experimental import pallas as pl
from jax.experimental.pallas import tpu as pltpu
from jax.sharding import PartitionSpec as P

HD = 128
PANEL = 8
OUTER = 32
MIB = 1 << 20

momentum_keep = 0.95
norm_eps = 1e-06

F32 = jnp.float32
BF16 = jnp.bfloat16
HIGHEST = lax.Precision.HIGHEST

SMEM = pl.BlockSpec(memory_space=pltpu.SMEM)
VMEM = pl.BlockSpec(memory_space=pltpu.VMEM)
ANY = pl.BlockSpec(memory_space=pl.ANY)


def swap(value, axes, k):
    axes = (axes,) if isinstance(axes, str) else axes
    n = math.prod(lax.axis_size(a) for a in axes)
    return lax.ppermute(value, axes, [(i, i ^ k) for i in range(n)])


def params(mib=24):
    return pltpu.CompilerParams(vmem_limit_bytes=mib * MIB)


def cost(flops, nbytes):
    return pl.CostEstimate(flops=int(flops), bytes_accessed=int(nbytes), transcendentals=0)


def halves(x):
    hi = x.astype(BF16)
    return hi, (x - hi.astype(F32)).astype(BF16)


def mm(a, b):
    return jnp.dot(a, b, preferred_element_type=F32)


def mm_full(a, b):
    return jnp.dot(a, b, precision=HIGHEST, preferred_element_type=F32)


def project_kernel(ranks, mom, grad, basis, *refs):
    out, b_hi, b_lo = refs[-3:]

    @pl.when(pl.program_id(0) == 0)
    def _():
        hi, lo = halves(basis[...])
        b_hi[...] = hi
        b_lo[...] = lo

    t_hi, t_lo = halves(mom[...] + grad[...].astype(F32))
    acc = mm(t_hi, b_hi[...]) + (mm(t_hi, b_lo[...]) + mm(t_lo, b_hi[...]))
    out[...] = acc.astype(out.dtype)


def project(ranks, momentum, grad_q, basis, j, first, number, n_resp, n_head, dtype, after):
    rows, cols = momentum.shape
    rank = basis.shape[1]
    chunk = rows // (n_resp * n_head)

    def rows_at(i, ranks):
        return ((ranks[0] ^ j) * n_head + (ranks[2] ^ (first + i)), 0)

    return pl.pallas_call(
        project_kernel,
        grid_spec=pltpu.PrefetchScalarGridSpec(
            num_scalar_prefetch=1,
            grid=(number,),
            in_specs=[
                pl.BlockSpec((chunk, cols), rows_at),
                pl.BlockSpec((chunk, cols), rows_at),
                pl.BlockSpec((cols, rank), lambda i, ranks: (0, 0)),
            ]
            + [ANY] * len(after),
            out_specs=pl.BlockSpec((chunk, rank), lambda i, ranks: (i, 0)),
            scratch_shapes=[pltpu.VMEM((cols, rank), BF16)] * 2,
        ),
        out_shape=jax.ShapeDtypeStruct((number * chunk, rank), dtype),
        compiler_params=params(60),
        cost_estimate=cost(6 * number * chunk * cols * rank, number * chunk * cols * 6),
    )(ranks, momentum, grad_q, basis, *after)


def split_kernel(n_recv, first, number, own, *refs):
    recvs, outs = refs[:n_recv], refs[-number:]
    chunk = outs[0].shape[0]
    for i in range(number):
        acc = own[(first + i) * chunk : (first + i + 1) * chunk, :]
        for r in recvs:
            acc = acc + r[i * chunk : (i + 1) * chunk, :].astype(F32)
        outs[i][...] = acc.astype(outs[i].dtype)


def split_sum(own, recvs, first, number, n_head, after):
    rows, rank = own.shape
    chunk = rows // n_head
    return pl.pallas_call(
        functools.partial(split_kernel, len(recvs), first, number),
        in_specs=[VMEM] * (1 + len(recvs)) + [ANY] * len(after),
        out_specs=[VMEM] * number,
        out_shape=[
            jax.ShapeDtypeStruct((chunk, rank), BF16 if first + i else F32)
            for i in range(number)
        ],
        compiler_params=params(),
        cost_estimate=cost(rows * rank, rows * rank * 8),
    )(own, *recvs, *after)


def sum_kernel(n_parts, *refs):
    acc = refs[0][...].astype(F32)
    for r in refs[1:n_parts]:
        acc = acc + r[...].astype(F32)
    refs[-1][...] = acc.astype(refs[-1].dtype)


def sum_parts(parts, dtype, after=()):
    shape = parts[0].shape
    return pl.pallas_call(
        functools.partial(sum_kernel, len(parts)),
        in_specs=[VMEM] * len(parts) + [ANY] * len(after),
        out_specs=VMEM,
        out_shape=jax.ShapeDtypeStruct(shape, dtype),
        compiler_params=params(),
        cost_estimate=cost(1000, 12 * math.prod(shape)),
    )(*parts, *after)


def gram_kernel(n_resp, n_head, ranks, *refs):
    chunks, (pcat, gram) = refs[: n_resp * n_head], refs[-2:]
    size = chunks[0].shape[0]
    for j in range(n_resp):
        for k in range(n_head):
            at = (ranks[0] ^ j) * n_head + (ranks[2] ^ k)
            pcat[pl.ds(pl.multiple_of(at * size, size), size), :] = chunks[j * n_head + k][...]
    p = pcat[...]
    gram[...] = mm(p.T, p)


def gather_gram(ranks, chunks, n_resp, n_head, after):
    size, rank = chunks[0].shape
    rows = size * n_resp * n_head
    return pl.pallas_call(
        functools.partial(gram_kernel, n_resp, n_head),
        in_specs=[SMEM] + [VMEM] * len(chunks) + [ANY] * len(after),
        out_specs=[VMEM] * 2,
        out_shape=[
            jax.ShapeDtypeStruct((rows, rank), BF16),
            jax.ShapeDtypeStruct((rank, rank), F32),
        ],
        compiler_params=params(),
        cost_estimate=cost(2 * rows * rank * rank, rows * rank * 4),
    )(ranks, *chunks, *after)


def back_part_kernel(pcat, mom, grad, out, acc):
    i = pl.program_id(0)
    t_hi, t_lo = halves(mom[...] + grad[...].astype(F32))
    pt = pcat[...].T
    part = mm(pt, t_hi) + mm(pt, t_lo)

    @pl.when(i == 0)
    def _():
        acc[...] = part

    @pl.when(i > 0)
    def _():
        acc[...] += part

    @pl.when(i == pl.num_programs(0) - 1)
    def _():
        out[...] = acc[...].astype(BF16)


def back_part(pcat, momentum, grad_q):
    rows, cols = momentum.shape
    rank = pcat.shape[1]
    tile = min(rows, 512)
    return pl.pallas_call(
        back_part_kernel,
        grid=(rows // tile,),
        in_specs=[
            pl.BlockSpec((tile, rank), lambda i: (i, 0)),
            pl.BlockSpec((tile, cols), lambda i: (i, 0)),
            pl.BlockSpec((tile, cols), lambda i: (i, 0)),
        ],
        out_specs=pl.BlockSpec((rank, cols), lambda i: (0, 0)),
        scratch_shapes=[pltpu.VMEM((rank, cols), F32)],
        out_shape=jax.ShapeDtypeStruct((rank, cols), BF16),
        compiler_params=params(),
        cost_estimate=cost(4 * rows * cols * rank, rows * cols * 6),
    )(pcat, momentum, grad_q)


def factor_panel(panel, off):
    shape = (PANEL, 128)
    d = {}
    for j in range(PANEL):
        col = jnp.broadcast_to(panel[:, off + j : off + j + 1], shape)
        for i in range(j, PANEL):
            d[i, j] = jnp.broadcast_to(col[i : i + 1, :], shape)
    low, inv = {}, {}
    for j in range(PANEL):
        r = lax.rsqrt(d[j, j])
        inv[j, j] = r
        for i in range(j + 1, PANEL):
            low[i, j] = d[i, j] * r
        for k in range(j + 1, PANEL):
            for i in range(k, PANEL):
                d[i, k] = d[i, k] - low[i, j] * low[k, j]
    for j in range(PANEL):
        for i in range(j + 1, PANEL):
            acc = low[i, j] * inv[j, j]
            for k in range(j + 1, i):
                acc = acc + low[i, k] * inv[k, j]
            inv[i, j] = -(acc * inv[i, i])
    return inv


def three_parts(x):
    a = x.astype(BF16)
    rest = x - a.astype(F32)
    b = rest.astype(BF16)
    return a, b, (rest - b.astype(F32)).astype(BF16)


def cholesky_kernel(n_parts, *refs):
    parts, out, work = refs[:n_parts], refs[n_parts], refs[n_parts + 1]
    n = out.shape[0]
    wide = 2 * n
    tiles = wide // 128
    total = parts[0][...]
    for part in parts[1:]:
        total = total + part[...]
    work[:, :n] = total
    rows = lax.broadcasted_iota(jnp.int32, (n, n), 0)
    cols = lax.broadcasted_iota(jnp.int32, (n, n), 1)
    work[:, n:] = jnp.where(rows == cols, 1.0, 0.0).astype(F32)
    sub = lax.broadcasted_iota(jnp.int32, (PANEL, 128), 0)
    n_panels = OUTER // PANEL

    def step(o, carry):
        blk = [
            [work[p * PANEL : (p + 1) * PANEL, t * 128 : (t + 1) * 128] for t in range(tiles)]
            for p in range(n_panels)
        ]
        for p in range(n_panels):
            off = p * PANEL
            inv = factor_panel(blk[p][0], off)
            rows_of = [
                [jnp.broadcast_to(blk[p][t][j : j + 1, :], (PANEL, 128)) for t in range(tiles)]
                for j in range(PANEL)
            ]
            new = [None] * tiles
            for j in range(PANEL):
                col = inv[PANEL - 1, j]
                for i in range(PANEL - 2, j - 1, -1):
                    col = jnp.where(sub == i, inv[i, j], col)
                if j:
                    col = jnp.where(sub < j, 0.0, col)
                for t in range(tiles):
                    term = col * rows_of[j][t]
                    new[t] = term if new[t] is None else new[t] + term
            blk[p] = new
            if p + 1 < n_panels:
                u_rows = [
                    [jnp.broadcast_to(new[t][j : j + 1, :], (PANEL, 128)) for t in range(tiles)]
                    for j in range(PANEL)
                ]
                for b in range(p + 1, n_panels):
                    lanes = [
                        jnp.broadcast_to(blk[b][0][:, off + m : off + m + 1], (PANEL, 128))
                        for m in range(PANEL)
                    ]
                    upd = list(blk[b])
                    for k in range(PANEL):
                        v = lanes[0] * inv[k, 0]
                        for m in range(1, k + 1):
                            v = v + lanes[m] * inv[k, m]
                        for t in range(tiles):
                            upd[t] = upd[t] - v * u_rows[k][t]
                    blk[b] = upd
        u = jnp.concatenate([jnp.concatenate(row, axis=1) for row in blk], axis=0)
        lane = lax.broadcasted_iota(jnp.int32, (OUTER, n), 1)
        left = jnp.where(lane < n - OUTER * o, u[:, :n], 0.0)
        la, lb, lc = three_parts(left)
        ua, ub, uc = three_parts(u)
        lhs = jnp.concatenate([la, la, lb, la, lc, lb], axis=0)
        rhs = jnp.concatenate([ua, ub, ua, uc, ua, ub], axis=0)
        upd = mm(lhs.T, rhs)
        rest = work[OUTER:, :] - upd[OUTER:, :]
        work[: n - OUTER, :] = pltpu.roll(rest, wide - OUTER, 1)
        work[n - OUTER :, :] = pltpu.roll(u, wide - OUTER, 1)
        return carry

    lax.fori_loop(0, n // OUTER, step, 0)
    out[...] = work[:, :n]


def inverse_factor(*parts):
    n = parts[0].shape[0]
    return pl.pallas_call(
        functools.partial(cholesky_kernel, len(parts)),
        in_specs=[VMEM] * len(parts),
        out_specs=VMEM,
        scratch_shapes=[pltpu.VMEM((n, 2 * n), F32)],
        out_shape=jax.ShapeDtypeStruct((n, n), F32),
        compiler_params=params(),
        cost_estimate=cost(10_000_000_000, 4 * n * n * 4),
    )(*parts)


def back_kernel(x, wa, wb, bt_out, y_out, s_out):
    w = wa[...].astype(F32) + wb[...].astype(F32)
    bt = mm_full(x[...], w)
    bt_out[...] = bt
    y_out[...] = ((1.0 - momentum_keep) * mm_full(x[...].T, bt)).astype(BF16)
    ones = jnp.ones((8, bt.shape[1]), F32)
    squares = lax.dot_general(
        ones, bt * bt, (((1,), (1,)), ((), ())), precision=HIGHEST, preferred_element_type=F32
    )
    for i in range(s_out.shape[0]):
        s_out[i] = squares


def back_full(x, wa, wb, copies):
    rank, cols = wa.shape
    return pl.pallas_call(
        back_kernel,
        in_specs=[VMEM] * 3,
        out_specs=[VMEM] * 3,
        out_shape=[
            jax.ShapeDtypeStruct((rank, cols), F32),
            jax.ShapeDtypeStruct((rank, cols), BF16),
            jax.ShapeDtypeStruct((copies, 8, rank), F32),
        ],
        compiler_params=params(),
        cost_estimate=cost(24 * rank * rank * cols, rank * cols * 12),
    )(x, wa, wb)


def momentum_kernel(pcat, mom, grad, y, out):
    out[...] = mom[...] + grad[...].astype(F32) - mm(pcat[...], y[...])


def new_momentum(pcat, momentum, grad_q, y):
    rows, cols = momentum.shape
    rank = pcat.shape[1]
    tile = min(rows, 256)
    return pl.pallas_call(
        momentum_kernel,
        grid=(rows // tile,),
        in_specs=[
            pl.BlockSpec((tile, rank), lambda i: (i, 0)),
            pl.BlockSpec((tile, cols), lambda i: (i, 0)),
            pl.BlockSpec((tile, cols), lambda i: (i, 0)),
            pl.BlockSpec((rank, cols), lambda i: (0, 0)),
        ],
        out_specs=pl.BlockSpec((tile, cols), lambda i: (i, 0)),
        out_shape=jax.ShapeDtypeStruct((rows, cols), F32),
        compiler_params=params(),
        cost_estimate=cost(2 * rows * cols * rank, rows * cols * 10),
    )(pcat, momentum, grad_q, y)


def update_kernel(gain, pcat, x, bt, sums, upd, basis_out, z_hi, z_lo):
    @pl.when(pl.program_id(0) == 0)
    def _():
        total = sums[0]
        for i in range(1, sums.shape[0]):
            total = total + sums[i]
        scale = lax.rsqrt(total + norm_eps).T[:, :1]
        scaled = bt[...] * scale
        basis_out[...] = scaled.T
        hi, lo = halves(gain * mm_full(x[...].T, scaled))
        z_hi[...] = hi
        z_lo[...] = lo

    p = pcat[...]
    upd[...] = (mm(p, z_hi[...]) + mm(p, z_lo[...])).astype(BF16)


def final_update(pcat, x, bt, sums, gain):
    rows, rank = pcat.shape
    cols = bt.shape[1]
    tile = min(rows, 512)
    whole = lambda i: (0, 0)
    return pl.pallas_call(
        functools.partial(update_kernel, gain),
        grid=(rows // tile,),
        in_specs=[
            pl.BlockSpec((tile, rank), lambda i: (i, 0)),
            pl.BlockSpec((rank, rank), whole),
            pl.BlockSpec((rank, cols), whole),
            pl.BlockSpec(sums.shape, lambda i: (0, 0, 0)),
        ],
        out_specs=[
            pl.BlockSpec((tile, cols), lambda i: (i, 0)),
            pl.BlockSpec((cols, rank), whole),
        ],
        scratch_shapes=[pltpu.VMEM((rank, cols), BF16)] * 2,
        out_shape=[
            jax.ShapeDtypeStruct((rows, cols), BF16),
            jax.ShapeDtypeStruct((cols, rank), F32),
        ],
        compiler_params=params(),
        cost_estimate=cost(4 * rows * cols * rank, rows * cols * 3),
    )(pcat, x, bt, sums)


def group_of(counts, response):
    group = jnp.int32(0)
    end = jnp.int32(0)
    for g in range(counts.shape[0]):
        end = end + counts[g]
        group = group + (end <= response).astype(jnp.int32)
    return group


def pack_kernel(*refs):
    keys, values, out = refs[0], refs[1], refs[-1]
    out[0] = keys[...]
    out[1] = values[...]


def pack_prompts(keys, values, after):
    return pl.pallas_call(
        pack_kernel,
        in_specs=[VMEM] * 2 + [ANY] * len(after),
        out_specs=VMEM,
        out_shape=jax.ShapeDtypeStruct((2,) + keys.shape, BF16),
        compiler_params=params(),
        cost_estimate=cost(1000, 8 * math.prod(keys.shape)),
    )(keys, values, *after)


def select_kernel(n_resp, n_fsdp, ranks, counts, slots, *refs):
    stored, out = refs[:n_resp], refs[-1]
    held = stored[0].shape[1]
    for f in range(n_fsdp):
        slot = slots[group_of(counts, ranks[0] * n_fsdp + f)]
        owner, local = slot // held, slot % held
        for j in range(n_resp):

            @pl.when(owner == (ranks[0] ^ j))
            def _():
                out[f, 0] = stored[j][0, local]
                out[f, 1] = stored[j][1, local]


def select_prompts(ranks, counts, slots, stored, n_fsdp, after):
    _, _, piece, width = stored[0].shape
    return pl.pallas_call(
        functools.partial(select_kernel, len(stored), n_fsdp),
        in_specs=[SMEM] * 3 + [VMEM] * len(stored) + [ANY] * len(after),
        out_specs=VMEM,
        out_shape=jax.ShapeDtypeStruct((n_fsdp, 2, piece, width), BF16),
        compiler_params=params(),
        cost_estimate=cost(1000, 8 * n_fsdp * piece * width),
    )(ranks, counts, slots, *stored, *after)


def attention_kernel(ranks, counts, prompt_blocks, resp_blocks, q, sk, sv, go, pieces, *refs):
    dq, own, part, keys, values, dk, dv = refs[-7:]
    n_fsdp, _, piece, _ = pieces.shape
    cap = piece * n_fsdp
    length = q.shape[0]
    scale = HD ** (-0.5)
    for f in range(n_fsdp):
        keys[f * piece : (f + 1) * piece, :] = pieces[f, 0]
        values[f * piece : (f + 1) * piece, :] = pieces[f, 1]
    keys[cap:, :] = sk[...]
    values[cap:, :] = sv[...]
    prompt_len = prompt_blocks[group_of(counts, ranks[0] * n_fsdp + ranks[1])] * 128
    resp_len = resp_blocks[0] * 128
    width = keys.shape[0]
    place = lax.broadcasted_iota(jnp.int32, (width, length), 0)
    pos = lax.broadcasted_iota(jnp.int32, (width, length), 1)
    inner = place - cap
    seen = ((place < cap) & (place < prompt_len)) | (
        (place >= cap) & (inner <= pos) & (inner < resp_len)
    )
    bias = jnp.where(seen, 0.0, -jnp.inf).astype(F32)
    live = lax.broadcasted_iota(jnp.int32, (length, HD), 0) < resp_len
    nt = (((1,), (1,)), ((), ()))
    kall = keys[...]
    vall = values[...]
    kt = kall.T
    dk[...] = jnp.zeros_like(dk)
    dv[...] = jnp.zeros_like(dv)
    for h in range(q.shape[1] // HD):
        cols = slice(h * HD, (h + 1) * HD)
        qh = q[:, cols]
        gh = jnp.where(live, go[:, cols], jnp.zeros((), BF16))
        logits = lax.dot_general(kall, qh, nt, preferred_element_type=F32) * scale + bias
        peak = jnp.max(logits, axis=0, keepdims=True)
        e = jnp.exp(logits - peak)
        w = (e * (1.0 / jnp.sum(e, axis=0, keepdims=True))).astype(BF16)
        dp = lax.dot_general(vall, gh, nt, preferred_element_type=F32)
        wf = w.astype(F32)
        diag = jnp.sum(wf * dp, axis=0, keepdims=True)
        ds = (wf * (dp - diag)).astype(BF16)
        dk[...] += mm(ds, qh)
        dv[...] += mm(w, gh)
        dq[:, cols] = (mm(kt, ds) * scale).T.astype(BF16)
    own[0] = (dk[cap:, :] * scale).astype(BF16)
    own[1] = dv[cap:, :].astype(BF16)
    part[0] = dk[:cap, :] * scale
    part[1] = dv[:cap, :]


def attention(ranks, counts, prompt_blocks, resp_blocks, q, sk, sv, go, pieces, after):
    n_fsdp, _, piece, _ = pieces.shape
    length, width = q.shape
    cap = piece * n_fsdp
    total = cap + length
    return pl.pallas_call(
        attention_kernel,
        in_specs=[SMEM] * 4 + [VMEM] * 5 + [ANY] * len(after),
        out_specs=[VMEM] * 3,
        out_shape=[
            jax.ShapeDtypeStruct((length, width), BF16),
            jax.ShapeDtypeStruct((2, length, HD), BF16),
            jax.ShapeDtypeStruct((2, cap, HD), F32),
        ],
        scratch_shapes=[pltpu.VMEM((total, HD), BF16)] * 2 + [pltpu.VMEM((total, HD), F32)] * 2,
        compiler_params=params(32),
        cost_estimate=cost(6_000_000_000, length * width * 8),
    )(ranks, counts, prompt_blocks, resp_blocks, q, sk, sv, go, pieces, *after)


def address_kernel(n_resp, n_fsdp, ranks, counts, slots, part, *refs):
    out = refs[-1]
    piece = out.shape[2]
    held = counts.shape[0] // n_resp
    owner = slots[group_of(counts, ranks[0] * n_fsdp + ranks[1])] // held
    for r in range(n_resp):
        for f in range(n_fsdp):
            out[r * n_fsdp + f] = jnp.where(
                owner == r, part[:, f * piece : (f + 1) * piece, :], 0.0
            )


def address_parts(ranks, counts, slots, part, n_resp, n_fsdp, after):
    piece = part.shape[1] // n_fsdp
    shape = (n_resp * n_fsdp, 2, piece, part.shape[2])
    return pl.pallas_call(
        functools.partial(address_kernel, n_resp, n_fsdp),
        in_specs=[SMEM] * 3 + [VMEM] + [ANY] * len(after),
        out_specs=VMEM,
        out_shape=jax.ShapeDtypeStruct(shape, F32),
        compiler_params=params(),
        cost_estimate=cost(1000, 8 * math.prod(shape)),
    )(ranks, counts, slots, part, *after)


def collect_kernel(ranks, counts, slots, arrived, out):
    held = out.shape[1]
    sources = arrived.shape[0]
    slot_of = [slots[group_of(counts, jnp.int32(i))] for i in range(sources)]
    for local in range(held):
        slot = ranks[0] * held + local
        acc = jnp.where(slot_of[0] == slot, arrived[0], 0.0)
        for i in range(1, sources):
            acc = acc + jnp.where(slot_of[i] == slot, arrived[i], 0.0)
        out[:, local] = acc


def collect(ranks, counts, slots, arrived, held):
    _, two, piece, width = arrived.shape
    return pl.pallas_call(
        collect_kernel,
        in_specs=[SMEM] * 3 + [VMEM],
        out_specs=VMEM,
        out_shape=jax.ShapeDtypeStruct((two, held, piece, width), F32),
        compiler_params=params(),
        cost_estimate=cost(1000, 4 * math.prod(arrived.shape)),
    )(ranks, counts, slots, arrived)


def on_device(
    queries,
    self_keys,
    self_values,
    d_out,
    prompt_keys,
    prompt_values,
    counts,
    owner_slot,
    prompt_blocks,
    resp_blocks,
    grad_q,
    momentum,
    basis,
):
    n_resp, n_fsdp, n_head = (lax.axis_size(a) for a in ("resp", "fsdp", "head"))
    ranks = jnp.stack([lax.axis_index(a) for a in ("resp", "fsdp", "head")]).astype(jnp.int32)
    gain = math.sqrt(
        momentum.shape[0] * n_fsdp * momentum.shape[1] * n_resp * n_head / basis.shape[1]
    )

    half = n_head // 2
    groups = [(half, half), (0, half)] if half else [(0, n_head)]

    sent, after = [], ()
    for first, number in groups:
        row = []
        for j in range(1, n_resp):
            row.append(
                project(
                    ranks, momentum, grad_q, basis, j, first, number, n_resp, n_head, BF16, after
                )
            )
            after = (row[-1],)
        sent.append(row)
    arrived = [[swap(s, "resp", j + 1) for j, s in enumerate(row)] for row in sent]
    mine = project(
        ranks, momentum, grad_q, basis, 0, 0, n_head, n_resp, n_head, F32, after
    )
    packed = pack_prompts(prompt_keys, prompt_values, after)
    stored = [packed] + [swap(packed, "resp", j) for j in range(1, n_resp)]

    split, after = {}, ()
    for (first, number), recvs in zip(groups, arrived):
        outs = split_sum(mine, recvs, first, number, n_head, after)
        after = (outs[0],)
        for i in range(number):
            split[first + i] = outs[i]
    chosen = select_prompts(ranks, counts, owner_slot, stored, n_fsdp, after)
    pieces = lax.all_to_all(chosen, "fsdp", 0, 0, tiled=True)
    far_first = [k for first, number in groups for k in range(first, first + number) if k]
    summands = {k: swap(split[k], "head", k) for k in far_first}
    piece0 = sum_parts([split[0]] + [summands[k] for k in range(1, n_head)], BF16, (chosen,))

    along = {0: piece0}
    for k in far_first:
        along[k] = swap(piece0, "head", k)
    chunks = [along[k] for k in range(n_head)]
    for j in range(1, n_resp):
        chunks += [swap(along[k], "resp", j) for k in range(n_head)]

    dq, resp_grad, part = attention(
        ranks, counts, prompt_blocks, resp_blocks, queries, self_keys, self_values, d_out, pieces,
        (along[n_head - 1],),
    )
    pcat, gram = gather_gram(ranks, chunks, n_resp, n_head, (part,))

    bits = [1 << b for b in range(n_fsdp.bit_length() - 1)]
    w = back_part(pcat, momentum, grad_q)
    addressed = address_parts(ranks, counts, owner_slot, part, n_resp, n_fsdp, (w,))
    for bit in bits[:-1]:
        gram = sum_parts([gram, swap(gram, "fsdp", bit)], F32)
        w = sum_parts([w, swap(w, "fsdp", bit)], BF16, (gram,))
    gram_parts = (gram, swap(gram, "fsdp", bits[-1]))
    w_other = swap(w, "fsdp", bits[-1])
    returned = lax.all_to_all(addressed, ("resp", "fsdp"), 0, 0, tiled=True)

    x = inverse_factor(*gram_parts)
    bt, y, squares = back_full(x, w, w_other, n_resp * n_head)
    sums = lax.all_to_all(squares, ("resp", "head"), 0, 0, tiled=True)
    momentum_out = new_momentum(pcat, momentum, grad_q, y)
    prompt_grad = collect(ranks, counts, owner_slot, returned, prompt_keys.shape[0])
    update, basis_out = final_update(pcat, x, bt, sums, gain)
    return (dq, resp_grad, prompt_grad, update, momentum_out, basis_out)


def solution(mesh):
    placed = (
        P(("resp", "fsdp"), "head"),
        P(("resp", "fsdp"), "head"),
        P(("resp", "fsdp"), "head"),
        P(("resp", "fsdp"), "head"),
        P("resp", "fsdp", "head"),
        P("resp", "fsdp", "head"),
        P(),
        P(),
        P(),
        P(("resp", "fsdp")),
        P("fsdp", ("resp", "head")),
        P("fsdp", ("resp", "head")),
        P(("resp", "head"), None),
    )
    return jax.shard_map(
        on_device,
        mesh=mesh,
        in_specs=placed,
        out_specs=(
            P(("resp", "fsdp"), "head"),
            P(None, ("resp", "fsdp"), "head"),
            P(None, "resp", "fsdp", "head"),
            P("fsdp", ("resp", "head")),
            P("fsdp", ("resp", "head")),
            P(("resp", "head"), None),
        ),
        check_vma=False,
    )
```

```python
import functools
import math

import jax
import jax.numpy as jnp
from jax import lax
from jax.experimental import pallas as pl
from jax.experimental.pallas import tpu as pltpu
from jax.sharding import PartitionSpec as P

HD = 128
PANEL = 8
OUTER = 32
MIB = 1 << 20

momentum_keep = 0.95
norm_eps = 1e-06

F32 = jnp.float32
BF16 = jnp.bfloat16
HIGHEST = lax.Precision.HIGHEST

SMEM = pl.BlockSpec(memory_space=pltpu.SMEM)
VMEM = pl.BlockSpec(memory_space=pltpu.VMEM)
ANY = pl.BlockSpec(memory_space=pl.ANY)
HBM = pl.BlockSpec(memory_space=pltpu.HBM)


def swap(value, axes, k):
    axes = (axes,) if isinstance(axes, str) else axes
    n = math.prod(lax.axis_size(a) for a in axes)
    return lax.ppermute(value, axes, [(i, i ^ k) for i in range(n)])


def params(mib=6):
    return pltpu.CompilerParams(vmem_limit_bytes=mib * MIB)


def cost(flops, nbytes):
    return pl.CostEstimate(flops=int(flops), bytes_accessed=int(nbytes), transcendentals=0)


def halves(x):
    hi = x.astype(BF16)
    return hi, (x - hi.astype(F32)).astype(BF16)


def mm(a, b):
    return jnp.dot(a, b, preferred_element_type=F32)


def mm_full(a, b):
    return jnp.dot(a, b, precision=HIGHEST, preferred_element_type=F32)


def project_kernel(j, n_head, groups, ranks, mom, grad, basis, *refs):
    n_out = len(groups)
    total, outs = refs[-5], refs[-5 - n_out : -5]
    grads, right, sems, right_sem = refs[-4:]
    chunk = total.shape[0] // n_head
    pieces = 2 if chunk % 32 == 0 else 1
    size = chunk // pieces
    copies = {}
    order = [k for first, number in groups for k in range(first, first + number)]
    fetch = pltpu.make_async_copy(basis, right, right_sem)
    fetch.start()
    for k in order:
        at = ((ranks[0] ^ j) * n_head + (ranks[2] ^ k)) * chunk
        copies[k] = []
        for i in range(pieces):
            src = pl.ds(pl.multiple_of(at + i * size, size), size)
            dst = pl.ds(k * chunk + i * size, size)
            n = k * pieces + i
            copies[k].append(
                pltpu.make_async_copy(mom.at[src, :], total.at[dst, :], sems.at[0, n])
            )
            copies[k].append(
                pltpu.make_async_copy(grad.at[src, :], grads.at[dst, :], sems.at[1, n])
            )
        for c in copies[k]:
            c.start()
    fetch.wait()
    b_hi, b_lo = halves(right[...])
    for (first, number), out in zip(groups, outs):
        for k in range(first, first + number):
            for c in copies[k]:
                c.wait()
            rows = slice(k * chunk, (k + 1) * chunk)
            t = total[rows, :] + grads[rows, :].astype(F32)
            total[rows, :] = t
            t_hi, t_lo = halves(t)
            acc = mm(t_hi, b_hi) + (mm(t_hi, b_lo) + mm(t_lo, b_hi))
            out[(k - first) * chunk : (k - first + 1) * chunk, :] = acc.astype(out.dtype)


def project(ranks, momentum, grad_q, basis, j, groups, n_resp, n_head, dtype, after):
    rows, cols = momentum.shape
    rank = basis.shape[1]
    chunk = rows // (n_resp * n_head)
    seg = chunk * n_head
    return pl.pallas_call(
        functools.partial(project_kernel, j, n_head, groups),
        in_specs=[SMEM] + [HBM] * 3 + [ANY] * len(after),
        out_specs=[VMEM] * (len(groups) + 1),
        scratch_shapes=[
            pltpu.VMEM((seg, cols), BF16),
            pltpu.VMEM((cols, rank), F32),
            pltpu.SemaphoreType.DMA((2, 2 * n_head)),
            pltpu.SemaphoreType.DMA,
        ],
        out_shape=[jax.ShapeDtypeStruct((n * chunk, rank), dtype) for _, n in groups]
        + [jax.ShapeDtypeStruct((seg, cols), F32)],
        compiler_params=params(14),
        cost_estimate=cost(6 * seg * cols * rank, seg * cols * 6),
    )(ranks, momentum, grad_q, basis, *after)


def split_kernel(n_recv, first, number, own, *refs):
    recvs, outs = refs[:n_recv], refs[-number:]
    chunk = outs[0].shape[0]
    for i in range(number):
        acc = own[(first + i) * chunk : (first + i + 1) * chunk, :]
        for r in recvs:
            acc = acc + r[i * chunk : (i + 1) * chunk, :].astype(F32)
        outs[i][...] = acc.astype(outs[i].dtype)


def split_sum(own, recvs, first, number, n_head, after):
    rows, rank = own.shape
    chunk = rows // n_head
    return pl.pallas_call(
        functools.partial(split_kernel, len(recvs), first, number),
        in_specs=[VMEM] * (1 + len(recvs)) + [ANY] * len(after),
        out_specs=[VMEM] * number,
        out_shape=[
            jax.ShapeDtypeStruct((chunk, rank), BF16 if first + i else F32)
            for i in range(number)
        ],
        compiler_params=params(),
        cost_estimate=cost(rows * rank, rows * rank * 8),
    )(own, *recvs, *after)


def sum_kernel(n_parts, *refs):
    acc = refs[0][...].astype(F32)
    for r in refs[1:n_parts]:
        acc = acc + r[...].astype(F32)
    refs[-1][...] = acc.astype(refs[-1].dtype)


def sum_parts(parts, dtype, after=()):
    shape = parts[0].shape
    return pl.pallas_call(
        functools.partial(sum_kernel, len(parts)),
        in_specs=[VMEM] * len(parts) + [ANY] * len(after),
        out_specs=VMEM,
        out_shape=jax.ShapeDtypeStruct(shape, dtype),
        compiler_params=params(),
        cost_estimate=cost(1000, 12 * math.prod(shape)),
    )(*parts, *after)


def gram_kernel(n_chunks, *refs):
    chunks, (pcat, pcat_t, gram) = refs[:n_chunks], refs[-3:]
    size = chunks[0].shape[0]
    for i in range(n_chunks):
        pcat[i * size : (i + 1) * size, :] = chunks[i][...]
    p = pcat[...]
    pt = p.T
    pcat_t[...] = pt
    gram[...] = mm(pt, p)


def gather_gram(chunks, after):
    size, rank = chunks[0].shape
    rows = size * len(chunks)
    return pl.pallas_call(
        functools.partial(gram_kernel, len(chunks)),
        in_specs=[VMEM] * len(chunks) + [ANY] * len(after),
        out_specs=[VMEM] * 3,
        out_shape=[
            jax.ShapeDtypeStruct((rows, rank), BF16),
            jax.ShapeDtypeStruct((rank, rows), BF16),
            jax.ShapeDtypeStruct((rank, rank), F32),
        ],
        compiler_params=params(8),
        cost_estimate=cost(2 * rows * rank * rank, rows * rank * 6),
    )(*chunks, *after)


def back_part_kernel(pcat_t, *refs):
    totals, out = refs[:-1], refs[-1]
    seg = totals[0].shape[0]
    step = min(seg, 512)
    acc = None
    for j, total in enumerate(totals):
        for i in range(0, seg, step):
            t_hi, t_lo = halves(total[i : i + step, :])
            pt = pcat_t[:, j * seg + i : j * seg + i + step]
            part = mm(pt, t_hi) + mm(pt, t_lo)
            acc = part if acc is None else acc + part
    out[...] = acc.astype(BF16)


def back_part(pcat_t, totals):
    rank = pcat_t.shape[0]
    seg, cols = totals[0].shape
    rows = seg * len(totals)
    return pl.pallas_call(
        back_part_kernel,
        in_specs=[VMEM] * (1 + len(totals)),
        out_specs=VMEM,
        out_shape=jax.ShapeDtypeStruct((rank, cols), BF16),
        compiler_params=params(14),
        cost_estimate=cost(4 * rows * cols * rank, rows * cols * 4),
    )(pcat_t, *totals)


def factor_panel(panel, off):
    shape = (PANEL, 128)
    d = {}
    for j in range(PANEL):
        col = jnp.broadcast_to(panel[:, off + j : off + j + 1], shape)
        for i in range(j, PANEL):
            d[i, j] = jnp.broadcast_to(col[i : i + 1, :], shape)
    low, inv = {}, {}
    for j in range(PANEL):
        r = lax.rsqrt(d[j, j])
        inv[j, j] = r
        for i in range(j + 1, PANEL):
            low[i, j] = d[i, j] * r
        for k in range(j + 1, PANEL):
            for i in range(k, PANEL):
                d[i, k] = d[i, k] - low[i, j] * low[k, j]
    for j in range(PANEL):
        for i in range(j + 1, PANEL):
            acc = low[i, j] * inv[j, j]
            for k in range(j + 1, i):
                acc = acc + low[i, k] * inv[k, j]
            inv[i, j] = -(acc * inv[i, i])
    return inv


def three_parts(x):
    a = x.astype(BF16)
    rest = x - a.astype(F32)
    b = rest.astype(BF16)
    return a, b, (rest - b.astype(F32)).astype(BF16)


def cholesky_kernel(n_parts, *refs):
    parts, out, work = refs[:n_parts], refs[n_parts], refs[n_parts + 1]
    n = out.shape[0]
    wide = 2 * n
    tiles = wide // 128
    total = parts[0][...]
    for part in parts[1:]:
        total = total + part[...]
    work[:, :n] = total
    rows = lax.broadcasted_iota(jnp.int32, (n, n), 0)
    cols = lax.broadcasted_iota(jnp.int32, (n, n), 1)
    work[:, n:] = jnp.where(rows == cols, 1.0, 0.0).astype(F32)
    sub = lax.broadcasted_iota(jnp.int32, (PANEL, 128), 0)
    n_panels = OUTER // PANEL

    def step(o, carry):
        blk = [
            [work[p * PANEL : (p + 1) * PANEL, t * 128 : (t + 1) * 128] for t in range(tiles)]
            for p in range(n_panels)
        ]
        for p in range(n_panels):
            off = p * PANEL
            inv = factor_panel(blk[p][0], off)
            rows_of = [
                [jnp.broadcast_to(blk[p][t][j : j + 1, :], (PANEL, 128)) for t in range(tiles)]
                for j in range(PANEL)
            ]
            new = [None] * tiles
            for j in range(PANEL):
                col = inv[PANEL - 1, j]
                for i in range(PANEL - 2, j - 1, -1):
                    col = jnp.where(sub == i, inv[i, j], col)
                if j:
                    col = jnp.where(sub < j, 0.0, col)
                for t in range(tiles):
                    term = col * rows_of[j][t]
                    new[t] = term if new[t] is None else new[t] + term
            blk[p] = new
            if p + 1 < n_panels:
                u_rows = [
                    [jnp.broadcast_to(new[t][j : j + 1, :], (PANEL, 128)) for t in range(tiles)]
                    for j in range(PANEL)
                ]
                for b in range(p + 1, n_panels):
                    lanes = [
                        jnp.broadcast_to(blk[b][0][:, off + m : off + m + 1], (PANEL, 128))
                        for m in range(PANEL)
                    ]
                    upd = list(blk[b])
                    for k in range(PANEL):
                        v = lanes[0] * inv[k, 0]
                        for m in range(1, k + 1):
                            v = v + lanes[m] * inv[k, m]
                        for t in range(tiles):
                            upd[t] = upd[t] - v * u_rows[k][t]
                    blk[b] = upd
        u = jnp.concatenate([jnp.concatenate(row, axis=1) for row in blk], axis=0)
        lane = lax.broadcasted_iota(jnp.int32, (OUTER, n), 1)
        left = jnp.where(lane < n - OUTER * o, u[:, :n], 0.0)
        la, lb, lc = three_parts(left)
        ua, ub, uc = three_parts(u)
        lhs = jnp.concatenate([la, la, lb, la, lc, lb], axis=0)
        rhs = jnp.concatenate([ua, ub, ua, uc, ua, ub], axis=0)
        upd = mm(lhs.T, rhs)
        rest = work[OUTER:, :] - upd[OUTER:, :]
        work[: n - OUTER, :] = pltpu.roll(rest, wide - OUTER, 1)
        work[n - OUTER :, :] = pltpu.roll(u, wide - OUTER, 1)
        return carry

    lax.fori_loop(0, n // OUTER, step, 0)
    out[...] = work[:, :n]


def inverse_factor(*parts):
    n = parts[0].shape[0]
    return pl.pallas_call(
        functools.partial(cholesky_kernel, len(parts)),
        in_specs=[VMEM] * len(parts),
        out_specs=VMEM,
        scratch_shapes=[pltpu.VMEM((n, 2 * n), F32)],
        out_shape=jax.ShapeDtypeStruct((n, n), F32),
        compiler_params=params(),
        cost_estimate=cost(10_000_000_000, 4 * n * n * 4),
    )(*parts)


def back_kernel(x, wa, wb, bt_out, y_out, s_out):
    w = wa[...].astype(F32) + wb[...].astype(F32)
    bt = mm_full(x[...], w)
    bt_out[...] = bt
    y_out[...] = ((1.0 - momentum_keep) * mm_full(x[...].T, bt)).astype(BF16)
    ones = jnp.ones((8, bt.shape[1]), F32)
    squares = lax.dot_general(
        ones, bt * bt, (((1,), (1,)), ((), ())), precision=HIGHEST, preferred_element_type=F32
    )
    for i in range(s_out.shape[0]):
        s_out[i] = squares


def back_full(x, wa, wb, copies):
    rank, cols = wa.shape
    return pl.pallas_call(
        back_kernel,
        in_specs=[VMEM] * 3,
        out_specs=[VMEM] * 3,
        out_shape=[
            jax.ShapeDtypeStruct((rank, cols), F32),
            jax.ShapeDtypeStruct((rank, cols), BF16),
            jax.ShapeDtypeStruct((copies, 8, rank), F32),
        ],
        compiler_params=params(),
        cost_estimate=cost(24 * rank * rank * cols, rank * cols * 12),
    )(x, wa, wb)


def row_blocks(ranks, n_resp, n_head, chunk):
    return [
        pl.multiple_of(((ranks[0] ^ j) * n_head + (ranks[2] ^ k)) * chunk, chunk)
        for j in range(n_resp)
        for k in range(n_head)
    ]


def momentum_kernel(n_resp, n_head, ranks, pcat, y, *refs):
    totals, (out, held, sems) = refs[:-3], refs[-3:]
    seg = totals[0].shape[0]
    chunk = seg // n_head
    copies = []
    for i, at in enumerate(row_blocks(ranks, n_resp, n_head, chunk)):
        rows = slice(i * chunk, (i + 1) * chunk)
        off = i % n_head * chunk
        total = totals[i // n_head][off : off + chunk, :]
        held[rows, :] = total - mm(pcat[rows, :], y[...])
        copies.append(
            pltpu.make_async_copy(held.at[rows, :], out.at[pl.ds(at, chunk), :], sems.at[i])
        )
        copies[-1].start()
    for c in copies:
        c.wait()


def new_momentum(ranks, pcat, totals, y, n_resp, n_head):
    rows, rank = pcat.shape
    cols = totals[0].shape[1]
    return pl.pallas_call(
        functools.partial(momentum_kernel, n_resp, n_head),
        in_specs=[SMEM] + [VMEM] * (2 + len(totals)),
        out_specs=HBM,
        scratch_shapes=[
            pltpu.VMEM((rows, cols), F32),
            pltpu.SemaphoreType.DMA((n_resp * n_head,)),
        ],
        out_shape=jax.ShapeDtypeStruct((rows, cols), F32),
        compiler_params=params(14),
        cost_estimate=cost(2 * rows * cols * rank, rows * cols * 8),
    )(ranks, pcat, y, *totals)


def update_kernel(gain, n_resp, n_head, ranks, pcat, x, bt, sums, upd, basis_out, held, sems):
    total = sums[0]
    for i in range(1, sums.shape[0]):
        total = total + sums[i]
    scale = lax.rsqrt(total + norm_eps).T[:, :1]
    scaled = bt[...] * scale
    z_hi, z_lo = halves(gain * mm_full(x[...].T, scaled))
    basis_out[...] = scaled.T
    chunk = pcat.shape[0] // (n_resp * n_head)
    copies = []
    for i, at in enumerate(row_blocks(ranks, n_resp, n_head, chunk)):
        rows = slice(i * chunk, (i + 1) * chunk)
        p = pcat[rows, :]
        held[rows, :] = (mm(p, z_hi) + mm(p, z_lo)).astype(BF16)
        copies.append(
            pltpu.make_async_copy(held.at[rows, :], upd.at[pl.ds(at, chunk), :], sems.at[i])
        )
        copies[-1].start()
    for c in copies:
        c.wait()


def final_update(ranks, pcat, x, bt, sums, gain, n_resp, n_head):
    rows, rank = pcat.shape
    cols = bt.shape[1]
    return pl.pallas_call(
        functools.partial(update_kernel, gain, n_resp, n_head),
        in_specs=[SMEM] + [VMEM] * 4,
        out_specs=[HBM, VMEM],
        scratch_shapes=[
            pltpu.VMEM((rows, cols), BF16),
            pltpu.SemaphoreType.DMA((n_resp * n_head,)),
        ],
        out_shape=[
            jax.ShapeDtypeStruct((rows, cols), BF16),
            jax.ShapeDtypeStruct((cols, rank), F32),
        ],
        compiler_params=params(10),
        cost_estimate=cost(4 * rows * cols * rank, rows * cols * 3),
    )(ranks, pcat, x, bt, sums)


def group_of(counts, response):
    group = jnp.int32(0)
    end = jnp.int32(0)
    for g in range(counts.shape[0]):
        end = end + counts[g]
        group = group + (end <= response).astype(jnp.int32)
    return group


def pack_kernel(*refs):
    keys, values, out = refs[0], refs[1], refs[-1]
    out[0] = keys[...]
    out[1] = values[...]


def pack_prompts(keys, values, after):
    return pl.pallas_call(
        pack_kernel,
        in_specs=[VMEM] * 2 + [ANY] * len(after),
        out_specs=VMEM,
        out_shape=jax.ShapeDtypeStruct((2,) + keys.shape, BF16),
        compiler_params=params(),
        cost_estimate=cost(1000, 8 * math.prod(keys.shape)),
    )(keys, values, *after)


def select_kernel(n_resp, n_fsdp, ranks, counts, slots, *refs):
    stored, out = refs[:n_resp], refs[-1]
    held = stored[0].shape[1]
    for f in range(n_fsdp):
        slot = slots[group_of(counts, ranks[0] * n_fsdp + f)]
        owner, local = slot // held, slot % held
        for j in range(n_resp):

            @pl.when(owner == (ranks[0] ^ j))
            def _():
                out[f, 0] = stored[j][0, local]
                out[f, 1] = stored[j][1, local]


def select_prompts(ranks, counts, slots, stored, n_fsdp, after):
    _, _, piece, width = stored[0].shape
    return pl.pallas_call(
        functools.partial(select_kernel, len(stored), n_fsdp),
        in_specs=[SMEM] * 3 + [VMEM] * len(stored) + [ANY] * len(after),
        out_specs=VMEM,
        out_shape=jax.ShapeDtypeStruct((n_fsdp, 2, piece, width), BF16),
        compiler_params=params(),
        cost_estimate=cost(1000, 8 * n_fsdp * piece * width),
    )(ranks, counts, slots, *stored, *after)


def attention_kernel(ranks, counts, prompt_blocks, resp_blocks, q, sk, sv, go, pieces, *refs):
    dq, own, part, keys, values, dk, dv = refs[-7:]
    n_fsdp, _, piece, _ = pieces.shape
    cap = piece * n_fsdp
    length = q.shape[0]
    scale = HD ** (-0.5)
    for f in range(n_fsdp):
        keys[f * piece : (f + 1) * piece, :] = pieces[f, 0]
        values[f * piece : (f + 1) * piece, :] = pieces[f, 1]
    keys[cap:, :] = sk[...]
    values[cap:, :] = sv[...]
    prompt_len = prompt_blocks[group_of(counts, ranks[0] * n_fsdp + ranks[1])] * 128
    resp_len = resp_blocks[0] * 128
    width = keys.shape[0]
    place = lax.broadcasted_iota(jnp.int32, (width, length), 0)
    pos = lax.broadcasted_iota(jnp.int32, (width, length), 1)
    inner = place - cap
    seen = ((place < cap) & (place < prompt_len)) | (
        (place >= cap) & (inner <= pos) & (inner < resp_len)
    )
    bias = jnp.where(seen, 0.0, -jnp.inf).astype(F32)
    live = lax.broadcasted_iota(jnp.int32, (length, HD), 0) < resp_len
    nt = (((1,), (1,)), ((), ()))
    kall = keys[...]
    vall = values[...]
    kt = kall.T
    dk[...] = jnp.zeros_like(dk)
    dv[...] = jnp.zeros_like(dv)
    for h in range(q.shape[1] // HD):
        cols = slice(h * HD, (h + 1) * HD)
        qh = q[:, cols]
        gh = jnp.where(live, go[:, cols], jnp.zeros((), BF16))
        logits = lax.dot_general(kall, qh, nt, preferred_element_type=F32) * scale + bias
        peak = jnp.max(logits, axis=0, keepdims=True)
        e = jnp.exp(logits - peak)
        w = (e * (1.0 / jnp.sum(e, axis=0, keepdims=True))).astype(BF16)
        dp = lax.dot_general(vall, gh, nt, preferred_element_type=F32)
        wf = w.astype(F32)
        diag = jnp.sum(wf * dp, axis=0, keepdims=True)
        ds = (wf * (dp - diag)).astype(BF16)
        dk[...] += mm(ds, qh)
        dv[...] += mm(w, gh)
        dq[:, cols] = (mm(kt, ds) * scale).T.astype(BF16)
    own[0] = (dk[cap:, :] * scale).astype(BF16)
    own[1] = dv[cap:, :].astype(BF16)
    part[0] = dk[:cap, :] * scale
    part[1] = dv[:cap, :]


def attention(ranks, counts, prompt_blocks, resp_blocks, q, sk, sv, go, pieces, after):
    n_fsdp, _, piece, _ = pieces.shape
    length, width = q.shape
    cap = piece * n_fsdp
    total = cap + length
    return pl.pallas_call(
        attention_kernel,
        in_specs=[SMEM] * 4 + [VMEM] * 5 + [ANY] * len(after),
        out_specs=[VMEM] * 3,
        out_shape=[
            jax.ShapeDtypeStruct((length, width), BF16),
            jax.ShapeDtypeStruct((2, length, HD), BF16),
            jax.ShapeDtypeStruct((2, cap, HD), F32),
        ],
        scratch_shapes=[pltpu.VMEM((total, HD), BF16)] * 2 + [pltpu.VMEM((total, HD), F32)] * 2,
        compiler_params=params(12),
        cost_estimate=cost(6_000_000_000, length * width * 8),
    )(ranks, counts, prompt_blocks, resp_blocks, q, sk, sv, go, pieces, *after)


def address_kernel(n_resp, n_fsdp, ranks, counts, slots, part, *refs):
    out = refs[-1]
    piece = out.shape[2]
    held = counts.shape[0] // n_resp
    owner = slots[group_of(counts, ranks[0] * n_fsdp + ranks[1])] // held
    for r in range(n_resp):
        for f in range(n_fsdp):
            out[r * n_fsdp + f] = jnp.where(
                owner == r, part[:, f * piece : (f + 1) * piece, :], 0.0
            )


def address_parts(ranks, counts, slots, part, n_resp, n_fsdp, after):
    piece = part.shape[1] // n_fsdp
    shape = (n_resp * n_fsdp, 2, piece, part.shape[2])
    return pl.pallas_call(
        functools.partial(address_kernel, n_resp, n_fsdp),
        in_specs=[SMEM] * 3 + [VMEM] + [ANY] * len(after),
        out_specs=VMEM,
        out_shape=jax.ShapeDtypeStruct(shape, F32),
        compiler_params=params(),
        cost_estimate=cost(1000, 8 * math.prod(shape)),
    )(ranks, counts, slots, part, *after)


def collect_kernel(ranks, counts, slots, arrived, out):
    held = out.shape[1]
    sources = arrived.shape[0]
    slot_of = [slots[group_of(counts, jnp.int32(i))] for i in range(sources)]
    for local in range(held):
        slot = ranks[0] * held + local
        acc = jnp.where(slot_of[0] == slot, arrived[0], 0.0)
        for i in range(1, sources):
            acc = acc + jnp.where(slot_of[i] == slot, arrived[i], 0.0)
        out[:, local] = acc


def collect(ranks, counts, slots, arrived, held):
    _, two, piece, width = arrived.shape
    return pl.pallas_call(
        collect_kernel,
        in_specs=[SMEM] * 3 + [VMEM],
        out_specs=VMEM,
        out_shape=jax.ShapeDtypeStruct((two, held, piece, width), F32),
        compiler_params=params(),
        cost_estimate=cost(1000, 4 * math.prod(arrived.shape)),
    )(ranks, counts, slots, arrived)


def on_device(
    queries,
    self_keys,
    self_values,
    d_out,
    prompt_keys,
    prompt_values,
    counts,
    owner_slot,
    prompt_blocks,
    resp_blocks,
    grad_q,
    momentum,
    basis,
):
    n_resp, n_fsdp, n_head = (lax.axis_size(a) for a in ("resp", "fsdp", "head"))
    ranks = jnp.stack([lax.axis_index(a) for a in ("resp", "fsdp", "head")]).astype(jnp.int32)
    gain = math.sqrt(
        momentum.shape[0] * n_fsdp * momentum.shape[1] * n_resp * n_head / basis.shape[1]
    )

    in_hbm = [pltpu.with_memory_space_constraint(a, pltpu.HBM) for a in (momentum, grad_q, basis)]
    half = n_head // 2
    groups = [(half, half), (0, half)] if half else [(0, n_head)]

    sent, totals, after = [], {}, ()
    for j in range(1, n_resp):
        *outs, totals[j] = project(
            ranks, *in_hbm, j, groups, n_resp, n_head, BF16, after
        )
        after = (outs[0],)
        sent.append(outs)
    arrived = [
        [swap(outs[g], "resp", j + 1) for j, outs in enumerate(sent)] for g in range(len(groups))
    ]
    mine, totals[0] = project(
        ranks, *in_hbm, 0, [(0, n_head)], n_resp, n_head, F32, after
    )
    totals = [totals[j] for j in range(n_resp)]
    packed = pack_prompts(prompt_keys, prompt_values, (mine,))
    stored = [packed] + [swap(packed, "resp", j) for j in range(1, n_resp)]

    split, after = {}, ()
    for (first, number), recvs in zip(groups, arrived):
        outs = split_sum(mine, recvs, first, number, n_head, after)
        after = (outs[0],)
        for i in range(number):
            split[first + i] = outs[i]
    chosen = select_prompts(ranks, counts, owner_slot, stored, n_fsdp, after)
    pieces = lax.all_to_all(chosen, "fsdp", 0, 0, tiled=True)
    far_first = [k for first, number in groups for k in range(first, first + number) if k]
    summands = {k: swap(split[k], "head", k) for k in far_first}
    piece0 = sum_parts([split[0]] + [summands[k] for k in range(1, n_head)], BF16, (pieces,))

    along = {0: piece0}
    for k in far_first:
        along[k] = swap(piece0, "head", k)
    chunks = [along[k] for k in range(n_head)]
    for j in range(1, n_resp):
        chunks += [swap(along[k], "resp", j) for k in range(n_head)]

    dq, resp_grad, part = attention(
        ranks, counts, prompt_blocks, resp_blocks, queries, self_keys, self_values, d_out, pieces,
        (along[n_head - 1],),
    )
    pcat, pcat_t, gram = gather_gram(chunks, (part,))

    bits = [1 << b for b in range(n_fsdp.bit_length() - 1)]
    w = back_part(pcat_t, totals)
    addressed = address_parts(ranks, counts, owner_slot, part, n_resp, n_fsdp, (w,))
    for bit in bits[:-1]:
        gram = sum_parts([gram, swap(gram, "fsdp", bit)], F32)
        w = sum_parts([w, swap(w, "fsdp", bit)], BF16, (gram,))
    gram_parts = (gram, swap(gram, "fsdp", bits[-1]))
    w_other = swap(w, "fsdp", bits[-1])
    returned = lax.all_to_all(addressed, ("resp", "fsdp"), 0, 0, tiled=True)

    x = inverse_factor(*gram_parts)
    bt, y, squares = back_full(x, w, w_other, n_resp * n_head)
    sums = lax.all_to_all(squares, ("resp", "head"), 0, 0, tiled=True)
    momentum_out = new_momentum(ranks, pcat, totals, y, n_resp, n_head)
    prompt_grad = collect(ranks, counts, owner_slot, returned, prompt_keys.shape[0])
    update, basis_out = final_update(ranks, pcat, x, bt, sums, gain, n_resp, n_head)
    return (dq, resp_grad, prompt_grad, update, momentum_out, basis_out)


def solution(mesh):
    placed = (
        P(("resp", "fsdp"), "head"),
        P(("resp", "fsdp"), "head"),
        P(("resp", "fsdp"), "head"),
        P(("resp", "fsdp"), "head"),
        P("resp", "fsdp", "head"),
        P("resp", "fsdp", "head"),
        P(),
        P(),
        P(),
        P(("resp", "fsdp")),
        P("fsdp", ("resp", "head")),
        P("fsdp", ("resp", "head")),
        P(("resp", "head"), None),
    )
    return jax.shard_map(
        on_device,
        mesh=mesh,
        in_specs=placed,
        out_specs=(
            P(("resp", "fsdp"), "head"),
            P(None, ("resp", "fsdp"), "head"),
            P(None, "resp", "fsdp", "head"),
            P("fsdp", ("resp", "head")),
            P("fsdp", ("resp", "head")),
            P(("resp", "head"), None),
        ),
        check_vma=False,
    )
```

```python
import functools
import math

import jax
import jax.numpy as jnp
from jax import lax
from jax.experimental import pallas as pl
from jax.experimental.pallas import tpu as pltpu
from jax.sharding import PartitionSpec as P

HD = 128
PANEL = 8
OUTER = 32
MIB = 1 << 20

momentum_keep = 0.95
norm_eps = 1e-06

F32 = jnp.float32
BF16 = jnp.bfloat16
HIGHEST = lax.Precision.HIGHEST

SMEM = pl.BlockSpec(memory_space=pltpu.SMEM)
VMEM = pl.BlockSpec(memory_space=pltpu.VMEM)
ANY = pl.BlockSpec(memory_space=pl.ANY)
HBM = pl.BlockSpec(memory_space=pltpu.HBM)


def swap(value, axes, k):
    axes = (axes,) if isinstance(axes, str) else axes
    n = math.prod(lax.axis_size(a) for a in axes)
    return lax.ppermute(value, axes, [(i, i ^ k) for i in range(n)])


def params(mib=6):
    return pltpu.CompilerParams(vmem_limit_bytes=mib * MIB)


def cost(flops, nbytes):
    return pl.CostEstimate(flops=int(flops), bytes_accessed=int(nbytes), transcendentals=0)


def halves(x):
    hi = x.astype(BF16)
    return hi, (x - hi.astype(F32)).astype(BF16)


def mm(a, b):
    return jnp.dot(a, b, preferred_element_type=F32)


def mm_full(a, b):
    return jnp.dot(a, b, precision=HIGHEST, preferred_element_type=F32)


def project_kernel(j, n_head, first, number, ranks, mom, grad, basis, *refs):
    out, total, grads, right, sems, right_sem = refs[-6:]
    chunk = total.shape[0] // number
    pieces = 2 if chunk % 32 == 0 else 1
    size = chunk // pieces
    fetch = pltpu.make_async_copy(basis, right, right_sem)
    copies = []
    for i in range(number):
        at = ((ranks[0] ^ j) * n_head + (ranks[2] ^ (first + i))) * chunk
        copies.append([])
        for p in range(pieces):
            src = pl.ds(pl.multiple_of(at + p * size, size), size)
            dst = pl.ds(i * chunk + p * size, size)
            n = i * pieces + p
            copies[i].append(
                pltpu.make_async_copy(mom.at[src, :], total.at[dst, :], sems.at[0, n])
            )
            copies[i].append(
                pltpu.make_async_copy(grad.at[src, :], grads.at[dst, :], sems.at[1, n])
            )
        for c in copies[i]:
            c.start()
        if i == 0:
            fetch.start()
    fetch.wait()
    b_hi, b_lo = halves(right[...])
    for i in range(number):
        for c in copies[i]:
            c.wait()
        rows = slice(i * chunk, (i + 1) * chunk)
        t = total[rows, :] + grads[rows, :].astype(F32)
        total[rows, :] = t
        t_hi, t_lo = halves(t)
        acc = mm(t_hi, b_hi) + (mm(t_hi, b_lo) + mm(t_lo, b_hi))
        out[rows, :] = acc.astype(out.dtype)


def project(ranks, momentum, grad_q, basis, j, first, number, n_resp, n_head, dtype, after):
    rows, cols = momentum.shape
    rank = basis.shape[1]
    size = rows // (n_resp * n_head) * number
    return pl.pallas_call(
        functools.partial(project_kernel, j, n_head, first, number),
        in_specs=[SMEM] + [HBM] * 3 + [ANY] * len(after),
        out_specs=[VMEM] * 2,
        scratch_shapes=[
            pltpu.VMEM((size, cols), BF16),
            pltpu.VMEM((cols, rank), F32),
            pltpu.SemaphoreType.DMA((2, 2 * number)),
            pltpu.SemaphoreType.DMA,
        ],
        out_shape=[
            jax.ShapeDtypeStruct((size, rank), dtype),
            jax.ShapeDtypeStruct((size, cols), F32),
        ],
        compiler_params=params(10),
        cost_estimate=cost(6 * size * cols * rank, size * cols * 6),
    )(ranks, momentum, grad_q, basis, *after)


def split_kernel(n_recv, number, own, *refs):
    recvs, outs = refs[:n_recv], refs[-number:]
    chunk = outs[0].shape[0]
    for i in range(number):
        rows = slice(i * chunk, (i + 1) * chunk)
        acc = own[rows, :]
        for r in recvs:
            acc = acc + r[rows, :].astype(F32)
        outs[i][...] = acc.astype(outs[i].dtype)


def split_sum(own, recvs, first, number):
    rows, rank = own.shape
    chunk = rows // number
    return pl.pallas_call(
        functools.partial(split_kernel, len(recvs), number),
        in_specs=[VMEM] * (1 + len(recvs)),
        out_specs=[VMEM] * number,
        out_shape=[
            jax.ShapeDtypeStruct((chunk, rank), BF16 if first + i else F32)
            for i in range(number)
        ],
        compiler_params=params(),
        cost_estimate=cost(rows * rank, rows * rank * 8),
    )(own, *recvs)


def sum_kernel(n_parts, *refs):
    acc = refs[0][...].astype(F32)
    for r in refs[1:n_parts]:
        acc = acc + r[...].astype(F32)
    refs[-1][...] = acc.astype(refs[-1].dtype)


def sum_parts(parts, dtype, after=()):
    shape = parts[0].shape
    return pl.pallas_call(
        functools.partial(sum_kernel, len(parts)),
        in_specs=[VMEM] * len(parts) + [ANY] * len(after),
        out_specs=VMEM,
        out_shape=jax.ShapeDtypeStruct(shape, dtype),
        compiler_params=params(),
        cost_estimate=cost(1000, 12 * math.prod(shape)),
    )(*parts, *after)


def gram_kernel(n_chunks, *refs):
    chunks, (pcat, pcat_t, gram) = refs[:n_chunks], refs[-3:]
    size = chunks[0].shape[0]
    for i in range(n_chunks):
        pcat[i * size : (i + 1) * size, :] = chunks[i][...]
    p = pcat[...]
    pt = p.T
    pcat_t[...] = pt
    half = p.shape[1] // 2
    gram[:half, :] = mm(pt[:half, :], p[:, :half])
    low = mm(pt[half:, :], p)
    gram[half : 2 * half, :] = low[:, :half]
    gram[2 * half :, :] = low[:, half:]


def gather_gram(chunks, after):
    size, rank = chunks[0].shape
    rows = size * len(chunks)
    return pl.pallas_call(
        functools.partial(gram_kernel, len(chunks)),
        in_specs=[VMEM] * len(chunks) + [ANY] * len(after),
        out_specs=[VMEM] * 3,
        out_shape=[
            jax.ShapeDtypeStruct((rows, rank), BF16),
            jax.ShapeDtypeStruct((rank, rows), BF16),
            jax.ShapeDtypeStruct((3 * rank // 2, rank // 2), F32),
        ],
        compiler_params=params(8),
        cost_estimate=cost(2 * rows * rank * rank, rows * rank * 6),
    )(*chunks, *after)


def back_part_kernel(pcat_t, *refs):
    totals, out = refs[:-1], refs[-1]
    seg = totals[0].shape[0]
    step = min(seg, 512)
    acc = None
    for j, total in enumerate(totals):
        for i in range(0, seg, step):
            t_hi, t_lo = halves(total[i : i + step, :])
            pt = pcat_t[:, j * seg + i : j * seg + i + step]
            part = mm(pt, t_hi) + mm(pt, t_lo)
            acc = part if acc is None else acc + part
    out[...] = acc.astype(BF16)


def back_part(pcat_t, totals):
    rank = pcat_t.shape[0]
    seg, cols = totals[0].shape
    rows = seg * len(totals)
    return pl.pallas_call(
        back_part_kernel,
        in_specs=[VMEM] * (1 + len(totals)),
        out_specs=VMEM,
        out_shape=jax.ShapeDtypeStruct((rank, cols), BF16),
        compiler_params=params(14),
        cost_estimate=cost(4 * rows * cols * rank, rows * cols * 4),
    )(pcat_t, *totals)


def factor_panel(panel, off):
    shape = (PANEL, 128)
    d = {}
    for j in range(PANEL):
        col = jnp.broadcast_to(panel[:, off + j : off + j + 1], shape)
        for i in range(j, PANEL):
            d[i, j] = jnp.broadcast_to(col[i : i + 1, :], shape)
    low, inv = {}, {}
    for j in range(PANEL):
        r = lax.rsqrt(d[j, j])
        inv[j, j] = r
        for i in range(j + 1, PANEL):
            low[i, j] = d[i, j] * r
        for k in range(j + 1, PANEL):
            for i in range(k, PANEL):
                d[i, k] = d[i, k] - low[i, j] * low[k, j]
    for j in range(PANEL):
        for i in range(j + 1, PANEL):
            acc = low[i, j] * inv[j, j]
            for k in range(j + 1, i):
                acc = acc + low[i, k] * inv[k, j]
            inv[i, j] = -(acc * inv[i, i])
    return inv


def three_parts(x):
    a = x.astype(BF16)
    rest = x - a.astype(F32)
    b = rest.astype(BF16)
    return a, b, (rest - b.astype(F32)).astype(BF16)


def cholesky_kernel(n_parts, *refs):
    parts, out, work = refs[:n_parts], refs[n_parts], refs[n_parts + 1]
    n = out.shape[0]
    half = n // 2
    tiles = n // 128 + 1
    total = parts[0][...]
    for part in parts[1:]:
        total = total + part[...]
    low = total[half : 2 * half, :]
    work[:half, :half] = total[:half, :]
    work[half:, :half] = low
    work[:half, half:] = low.T
    work[half:, half:] = total[2 * half :, :]
    sub = lax.broadcasted_iota(jnp.int32, (PANEL, 128), 0)
    lane = lax.broadcasted_iota(jnp.int32, (PANEL, 128), 1)
    n_panels = OUTER // PANEL

    def step(o, carry):
        blk = [
            [work[p * PANEL : (p + 1) * PANEL, t * 128 : (t + 1) * 128] for t in range(tiles - 1)]
            + [jnp.where(lane == sub + p * PANEL, 1.0, 0.0).astype(F32)]
            for p in range(n_panels)
        ]
        for p in range(n_panels):
            off = p * PANEL
            inv = factor_panel(blk[p][0], off)
            rows_of = [
                [jnp.broadcast_to(blk[p][t][j : j + 1, :], (PANEL, 128)) for t in range(tiles)]
                for j in range(PANEL)
            ]
            new = [None] * tiles
            for j in range(PANEL):
                col = inv[PANEL - 1, j]
                for i in range(PANEL - 2, j - 1, -1):
                    col = jnp.where(sub == i, inv[i, j], col)
                if j:
                    col = jnp.where(sub < j, 0.0, col)
                for t in range(tiles):
                    term = col * rows_of[j][t]
                    new[t] = term if new[t] is None else new[t] + term
            blk[p] = new
            if p + 1 < n_panels:
                u_rows = [
                    [jnp.broadcast_to(new[t][j : j + 1, :], (PANEL, 128)) for t in range(tiles)]
                    for j in range(PANEL)
                ]
                for b in range(p + 1, n_panels):
                    lanes = [
                        jnp.broadcast_to(blk[b][0][:, off + m : off + m + 1], (PANEL, 128))
                        for m in range(PANEL)
                    ]
                    upd = list(blk[b])
                    for k in range(PANEL):
                        v = lanes[0] * inv[k, 0]
                        for m in range(1, k + 1):
                            v = v + lanes[m] * inv[k, m]
                        for t in range(tiles):
                            upd[t] = upd[t] - v * u_rows[k][t]
                    blk[b] = upd
        u = jnp.concatenate([jnp.concatenate(row, axis=1) for row in blk], axis=0)
        u = pltpu.roll(u, tiles * 128 - OUTER, 1)[:, :n]
        at = lax.broadcasted_iota(jnp.int32, (OUTER, n), 1)
        left = jnp.where(at < n - OUTER * (o + 1), u, 0.0)
        la, lb, lc = three_parts(left)
        ua, ub, uc = three_parts(u)
        lhs = jnp.concatenate([la, la, lb, la, lc, lb], axis=0)
        rhs = jnp.concatenate([ua, ub, ua, uc, ua, ub], axis=0)
        upd = mm(lhs.T, rhs)
        rest = work[OUTER:, :]
        lanes_at = lax.broadcasted_iota(jnp.int32, rest.shape, 1)
        rest = pltpu.roll(jnp.where(lanes_at < OUTER, 0.0, rest), n - OUTER, 1)
        work[: n - OUTER, :] = rest - upd[: n - OUTER, :]
        work[n - OUTER :, :] = u
        return carry

    lax.fori_loop(0, n // OUTER, step, 0)
    out[...] = work[...]


def inverse_factor(*parts):
    n = 2 * parts[0].shape[1]
    return pl.pallas_call(
        functools.partial(cholesky_kernel, len(parts)),
        in_specs=[VMEM] * len(parts),
        out_specs=VMEM,
        scratch_shapes=[pltpu.VMEM((n, n), F32)],
        out_shape=jax.ShapeDtypeStruct((n, n), F32),
        compiler_params=params(),
        cost_estimate=cost(10_000_000_000, 4 * n * n * 4),
    )(*parts)


def mm_three(a, b):
    a_hi, a_lo = halves(a)
    b_hi, b_lo = halves(b)
    return mm(a_hi, b_hi) + (mm(a_hi, b_lo) + mm(a_lo, b_hi))


def back_kernel(x, wa, wb, bt_out, y_out, s_out):
    w = wa[...].astype(F32) + wb[...].astype(F32)
    bt = mm_three(x[...], w)
    bt_out[...] = bt
    s = jnp.sum(bt * bt, axis=1, keepdims=True)
    s_out[...] = jnp.broadcast_to(s, (s.shape[0], 128)).T[:8, :]
    y_out[...] = ((1.0 - momentum_keep) * mm(x[...].T.astype(BF16), bt.astype(BF16))).astype(BF16)


def back_full(x, wa, wb):
    rank, cols = wa.shape
    return pl.pallas_call(
        back_kernel,
        in_specs=[VMEM] * 3,
        out_specs=[VMEM] * 3,
        out_shape=[
            jax.ShapeDtypeStruct((rank, cols), F32),
            jax.ShapeDtypeStruct((rank, cols), BF16),
            jax.ShapeDtypeStruct((8, rank), F32),
        ],
        compiler_params=params(),
        cost_estimate=cost(8 * rank * rank * cols, rank * cols * 12),
    )(x, wa, wb)


def row_blocks(ranks, n_resp, n_head, chunk):
    return [
        pl.multiple_of(((ranks[0] ^ j) * n_head + (ranks[2] ^ k)) * chunk, chunk)
        for j in range(n_resp)
        for k in range(n_head)
    ]


def momentum_kernel(n_resp, n_head, ranks, pcat, y, *refs):
    totals, (out, held, sems) = refs[:-3], refs[-3:]
    seg = totals[0].shape[0]
    chunk = pcat.shape[0] // (n_resp * n_head)
    copies = []
    for i, at in enumerate(row_blocks(ranks, n_resp, n_head, chunk)):
        rows = slice(i * chunk, (i + 1) * chunk)
        off = i * chunk % seg
        total = totals[i * chunk // seg][off : off + chunk, :]
        held[rows, :] = total - mm(pcat[rows, :], y[...])
        copies.append(
            pltpu.make_async_copy(held.at[rows, :], out.at[pl.ds(at, chunk), :], sems.at[i])
        )
        copies[-1].start()
    for c in copies:
        c.wait()


def new_momentum(ranks, pcat, totals, y, n_resp, n_head):
    rows, rank = pcat.shape
    cols = totals[0].shape[1]
    return pl.pallas_call(
        functools.partial(momentum_kernel, n_resp, n_head),
        in_specs=[SMEM] + [VMEM] * (2 + len(totals)),
        out_specs=HBM,
        scratch_shapes=[
            pltpu.VMEM((rows, cols), F32),
            pltpu.SemaphoreType.DMA((n_resp * n_head,)),
        ],
        out_shape=jax.ShapeDtypeStruct((rows, cols), F32),
        compiler_params=params(14),
        cost_estimate=cost(2 * rows * cols * rank, rows * cols * 8),
    )(ranks, pcat, y, *totals)


def update_kernel(gain, n_resp, n_head, n_sums, ranks, pcat, x, bt, *refs):
    sums, (upd, basis_out, held, held_basis, sems, basis_sem) = refs[:n_sums], refs[n_sums:]
    total = sums[0][...]
    for s in sums[1:]:
        total = total + s[...]
    scale = lax.rsqrt(total + norm_eps).T[:, :1]
    scaled = bt[...] * scale
    held_basis[...] = scaled.T
    basis_copy = pltpu.make_async_copy(held_basis, basis_out, basis_sem)
    basis_copy.start()
    z_hi, z_lo = halves(gain * mm_three(x[...].T, scaled))
    chunk = pcat.shape[0] // (n_resp * n_head)
    copies = []
    for i, at in enumerate(row_blocks(ranks, n_resp, n_head, chunk)):
        rows = slice(i * chunk, (i + 1) * chunk)
        p = pcat[rows, :]
        held[rows, :] = (mm(p, z_hi) + mm(p, z_lo)).astype(BF16)
        copies.append(
            pltpu.make_async_copy(held.at[rows, :], upd.at[pl.ds(at, chunk), :], sems.at[i])
        )
        copies[-1].start()
    for c in copies:
        c.wait()
    basis_copy.wait()


def final_update(ranks, pcat, x, bt, sums, gain, n_resp, n_head):
    rows, rank = pcat.shape
    cols = bt.shape[1]
    return pl.pallas_call(
        functools.partial(update_kernel, gain, n_resp, n_head, len(sums)),
        in_specs=[SMEM] + [VMEM] * (3 + len(sums)),
        out_specs=[HBM, HBM],
        scratch_shapes=[
            pltpu.VMEM((rows, cols), BF16),
            pltpu.VMEM((cols, rank), F32),
            pltpu.SemaphoreType.DMA((n_resp * n_head,)),
            pltpu.SemaphoreType.DMA,
        ],
        out_shape=[
            jax.ShapeDtypeStruct((rows, cols), BF16),
            jax.ShapeDtypeStruct((cols, rank), F32),
        ],
        compiler_params=params(10),
        cost_estimate=cost(4 * rows * cols * rank, rows * cols * 3),
    )(ranks, pcat, x, bt, *sums)


def group_of(counts, response):
    group = jnp.int32(0)
    end = jnp.int32(0)
    for g in range(counts.shape[0]):
        end = end + counts[g]
        group = group + (end <= response).astype(jnp.int32)
    return group


def pack_kernel(*refs):
    keys, values, out = refs[0], refs[1], refs[-1]
    out[0] = keys[...]
    out[1] = values[...]


def pack_prompts(keys, values, after):
    return pl.pallas_call(
        pack_kernel,
        in_specs=[VMEM] * 2 + [ANY] * len(after),
        out_specs=VMEM,
        out_shape=jax.ShapeDtypeStruct((2,) + keys.shape, BF16),
        compiler_params=params(),
        cost_estimate=cost(1000, 8 * math.prod(keys.shape)),
    )(keys, values, *after)


def select_kernel(n_resp, n_fsdp, ranks, counts, slots, *refs):
    stored, outs = refs[:n_resp], refs[-n_fsdp:]
    held = stored[0].shape[1]
    for k in range(n_fsdp):
        slot = slots[group_of(counts, ranks[0] * n_fsdp + (ranks[1] ^ k))]
        owner, local = slot // held, slot % held
        for j in range(n_resp):

            @pl.when(owner == (ranks[0] ^ j))
            def _():
                outs[k][0] = stored[j][0, local]
                outs[k][1] = stored[j][1, local]


def select_prompts(ranks, counts, slots, stored, n_fsdp, after):
    _, _, piece, width = stored[0].shape
    return pl.pallas_call(
        functools.partial(select_kernel, len(stored), n_fsdp),
        in_specs=[SMEM] * 3 + [VMEM] * len(stored) + [ANY] * len(after),
        out_specs=[VMEM] * n_fsdp,
        out_shape=[jax.ShapeDtypeStruct((2, piece, width), BF16)] * n_fsdp,
        compiler_params=params(),
        cost_estimate=cost(1000, 8 * n_fsdp * piece * width),
    )(ranks, counts, slots, *stored, *after)


def attention_kernel(
    n_fsdp, heads, last, ranks, counts, prompt_blocks, resp_blocks, q, sk, sv, go, *refs
):
    pieces, refs = refs[:n_fsdp], refs[n_fsdp:]
    dq_held, keys, values, dk, dv, sem = refs[-6:]
    n_out = 2 + n_fsdp if last else 3
    outs = refs[-6 - n_out : -6]
    dq = outs[0]
    piece = pieces[0].shape[1]
    cap = piece * n_fsdp
    length = q.shape[0]
    scale = HD ** (-0.5)
    for k in range(n_fsdp):
        rows = pl.ds(pl.multiple_of((ranks[1] ^ k) * piece, piece), piece)
        keys[rows, :] = pieces[k][0]
        values[rows, :] = pieces[k][1]
    keys[cap:, :] = sk[...]
    values[cap:, :] = sv[...]
    prompt_len = prompt_blocks[group_of(counts, ranks[0] * n_fsdp + ranks[1])] * 128
    resp_len = resp_blocks[0] * 128
    width = keys.shape[0]
    place = lax.broadcasted_iota(jnp.int32, (width, length), 0)
    pos = lax.broadcasted_iota(jnp.int32, (width, length), 1)
    inner = place - cap
    seen = ((place < cap) & (place < prompt_len)) | (
        (place >= cap) & (inner <= pos) & (inner < resp_len)
    )
    bias = jnp.where(seen, 0.0, -jnp.inf).astype(F32)
    live = lax.broadcasted_iota(jnp.int32, (length, HD), 0) < resp_len
    nt = (((1,), (1,)), ((), ()))
    kall = keys[...]
    vall = values[...]
    kt = kall.T
    if last:
        dk[...] = refs[0][...]
        dv[...] = refs[1][...]
    else:
        dk[...] = jnp.zeros_like(dk)
        dv[...] = jnp.zeros_like(dv)
    for i, h in enumerate(heads):
        cols = slice(h * HD, (h + 1) * HD)
        qh = q[:, cols]
        gh = jnp.where(live, go[:, cols], jnp.zeros((), BF16))
        logits = lax.dot_general(kall, qh, nt, preferred_element_type=F32) * scale + bias
        peak = jnp.max(logits, axis=0, keepdims=True)
        e = jnp.exp(logits - peak)
        w = (e * (1.0 / jnp.sum(e, axis=0, keepdims=True))).astype(BF16)
        dp = lax.dot_general(vall, gh, nt, preferred_element_type=F32)
        wf = w.astype(F32)
        diag = jnp.sum(wf * dp, axis=0, keepdims=True)
        ds = (wf * (dp - diag)).astype(BF16)
        dk[...] += mm(ds, qh)
        dv[...] += mm(w, gh)
        dq_held[:, i * HD : (i + 1) * HD] = (mm(kt, ds) * scale).T.astype(BF16)
    to = dq.at[:, pl.ds(heads[0] * HD, len(heads) * HD)]
    copy = pltpu.make_async_copy(dq_held, to, sem)
    copy.start()
    if last:
        own, sends = outs[1], outs[2:]
        own[0] = (dk[cap:, :] * scale).astype(BF16)
        own[1] = dv[cap:, :].astype(BF16)
        for k in range(n_fsdp):
            rows = pl.ds(pl.multiple_of((ranks[1] ^ k) * piece, piece), piece)
            sends[k][0] = (dk[rows, :] * scale).astype(sends[k].dtype)
            sends[k][1] = dv[rows, :].astype(sends[k].dtype)
    else:
        outs[1][...] = dk[...]
        outs[2][...] = dv[...]
    copy.wait()


def attention(heads, earlier, ranks, counts, prompt_blocks, resp_blocks, q, sk, sv, go, pieces, after):
    n_fsdp = len(pieces)
    piece = pieces[0].shape[1]
    length, width = q.shape
    cap = piece * n_fsdp
    total = cap + length
    last = earlier is not None
    dq_shape = jax.ShapeDtypeStruct((length, width), BF16)
    if last:
        extra, specs = (earlier[1], earlier[2], earlier[0]), [VMEM, VMEM, HBM]
        out_shape = [dq_shape, jax.ShapeDtypeStruct((2, length, HD), BF16)] + [
            jax.ShapeDtypeStruct((2, piece, HD), BF16 if k else F32) for k in range(n_fsdp)
        ]
        aliases = {8 + n_fsdp + 2: 0}
    else:
        extra, specs = (), []
        out_shape = [dq_shape] + [jax.ShapeDtypeStruct((total, HD), F32)] * 2
        aliases = {}
    return pl.pallas_call(
        functools.partial(attention_kernel, n_fsdp, heads, last),
        in_specs=[SMEM] * 4 + [VMEM] * (4 + n_fsdp) + specs + [ANY] * len(after),
        out_specs=[HBM] + [VMEM] * (len(out_shape) - 1),
        scratch_shapes=[pltpu.VMEM((length, len(heads) * HD), BF16)]
        + [pltpu.VMEM((total, HD), BF16)] * 2
        + [pltpu.VMEM((total, HD), F32)] * 2
        + [pltpu.SemaphoreType.DMA],
        out_shape=out_shape,
        input_output_aliases=aliases,
        compiler_params=params(12),
        cost_estimate=cost(3_000_000_000, length * width * 8),
    )(ranks, counts, prompt_blocks, resp_blocks, q, sk, sv, go, *pieces, *extra, *after)


def by_slot_kernel(n_resp, n_fsdp, ranks, counts, slots, *refs):
    parts, outs = refs[:n_fsdp], refs[-n_resp:]
    held = outs[0].shape[1]
    slot_of = [
        slots[group_of(counts, ranks[0] * n_fsdp + (ranks[1] ^ k))] for k in range(n_fsdp)
    ]
    for j in range(n_resp):
        for local in range(held):
            slot = (ranks[0] ^ j) * held + local
            acc = jnp.zeros(parts[0].shape, F32)
            for k in range(n_fsdp):
                acc = acc + jnp.where(slot_of[k] == slot, parts[k][...].astype(F32), 0.0)
            outs[j][:, local] = acc.astype(outs[j].dtype)


def sum_by_slot(ranks, counts, slots, parts, n_resp, after):
    held = counts.shape[0] // n_resp
    _, piece, width = parts[0].shape
    return pl.pallas_call(
        functools.partial(by_slot_kernel, n_resp, len(parts)),
        in_specs=[SMEM] * 3 + [VMEM] * len(parts) + [ANY] * len(after),
        out_specs=[VMEM] * n_resp,
        out_shape=[
            jax.ShapeDtypeStruct((2, held, piece, width), BF16 if j else F32)
            for j in range(n_resp)
        ],
        compiler_params=params(),
        cost_estimate=cost(1000, 8 * len(parts) * piece * width * 4),
    )(ranks, counts, slots, *parts, *after)


def on_device(
    queries,
    self_keys,
    self_values,
    d_out,
    prompt_keys,
    prompt_values,
    counts,
    owner_slot,
    prompt_blocks,
    resp_blocks,
    grad_q,
    momentum,
    basis,
):
    n_resp, n_fsdp, n_head = (lax.axis_size(a) for a in ("resp", "fsdp", "head"))
    ranks = jnp.stack([lax.axis_index(a) for a in ("resp", "fsdp", "head")]).astype(jnp.int32)
    gain = math.sqrt(
        momentum.shape[0] * n_fsdp * momentum.shape[1] * n_resp * n_head / basis.shape[1]
    )

    in_hbm = [pltpu.with_memory_space_constraint(a, pltpu.HBM) for a in (momentum, grad_q, basis)]
    half = n_head // 2
    groups = [(half, half), (0, half)] if half else [(0, n_head)]

    totals, after = {}, ()
    arrived = []
    for first, number in groups:
        row = []
        for j in range(1, n_resp):
            sent, totals[j, first] = project(
                ranks, *in_hbm, j, first, number, n_resp, n_head, BF16, after
            )
            after = (sent,)
            row.append(swap(sent, "resp", j))
        arrived.append(row)
    packed = pack_prompts(prompt_keys, prompt_values, after)
    stored = [packed] + [swap(packed, "resp", j) for j in range(1, n_resp)]
    after = (packed,)
    split = {}
    for (first, number), recvs in zip(groups, arrived):
        mine, totals[0, first] = project(
            ranks, *in_hbm, 0, first, number, n_resp, n_head, F32, after
        )
        outs = split_sum(mine, recvs, first, number)
        after = (outs[0],)
        for i in range(number):
            split[first + i] = outs[i]
    totals = [totals[at] for at in sorted(totals)]
    chosen = select_prompts(ranks, counts, owner_slot, stored, n_fsdp, after)
    far_first = [k for first, number in groups for k in range(first, first + number) if k]
    summands = {k: swap(split[k], "head", k) for k in far_first}
    pieces = [chosen[0]] + [swap(chosen[k], "fsdp", k) for k in range(1, n_fsdp)]
    piece0 = sum_parts(
        [split[0]] + [summands[k] for k in range(1, n_head)], BF16, (pieces[-1],)
    )

    along = {0: piece0}
    for k in far_first:
        along[k] = swap(piece0, "head", k)
    chunks = [along[k] for k in range(n_head)]
    for j in range(1, n_resp):
        chunks += [swap(along[k], "resp", j) for k in range(n_head)]

    n_q = queries.shape[1] // HD
    heads = [list(range(n_q // 2)), list(range(n_q // 2, n_q))]
    held = (
        ranks, counts, prompt_blocks, resp_blocks, queries, self_keys, self_values, d_out, pieces
    )
    earlier = attention(heads[0], None, *held, (piece0,))
    dq, resp_grad, *parts = attention(heads[1], earlier, *held, (along[n_head - 1],))
    pcat, pcat_t, gram = gather_gram(chunks, (resp_grad,))

    bits = [1 << b for b in range(n_fsdp.bit_length() - 1)]
    w = back_part(pcat_t, totals)
    for bit in bits[:-1]:
        gram = sum_parts([gram, swap(gram, "fsdp", bit)], F32)
        w = sum_parts([w, swap(w, "fsdp", bit)], BF16, (gram,))
    gram_parts = (gram, swap(gram, "fsdp", bits[-1]))
    w_other = swap(w, "fsdp", bits[-1])
    returned = [parts[0]] + [swap(parts[k], "fsdp", k) for k in range(1, n_fsdp)]
    slots = sum_by_slot(ranks, counts, owner_slot, returned, n_resp, (w,))
    x = inverse_factor(*gram_parts)
    prompt_grad = sum_parts(
        [slots[0]] + [swap(slots[j], "resp", j) for j in range(1, n_resp)], F32
    )

    bt, y, squares = back_full(x, w, w_other)
    squares = sum_parts([squares] + [swap(squares, "head", k) for k in range(1, n_head)], F32)
    momentum_out = new_momentum(ranks, pcat, totals, y, n_resp, n_head)
    sums = [squares] + [swap(squares, "resp", j) for j in range(1, n_resp)]
    update, basis_out = final_update(ranks, pcat, x, bt, sums, gain, n_resp, n_head)
    return (dq, resp_grad, prompt_grad, update, momentum_out, basis_out)


def solution(mesh):
    placed = (
        P(("resp", "fsdp"), "head"),
        P(("resp", "fsdp"), "head"),
        P(("resp", "fsdp"), "head"),
        P(("resp", "fsdp"), "head"),
        P("resp", "fsdp", "head"),
        P("resp", "fsdp", "head"),
        P(),
        P(),
        P(),
        P(("resp", "fsdp")),
        P("fsdp", ("resp", "head")),
        P("fsdp", ("resp", "head")),
        P(("resp", "head"), None),
    )
    return jax.shard_map(
        on_device,
        mesh=mesh,
        in_specs=placed,
        out_specs=(
            P(("resp", "fsdp"), "head"),
            P(None, ("resp", "fsdp"), "head"),
            P(None, "resp", "fsdp", "head"),
            P("fsdp", ("resp", "head")),
            P("fsdp", ("resp", "head")),
            P(("resp", "head"), None),
        ),
        check_vma=False,
    )
```

```python
import functools
import math

import jax
import jax.numpy as jnp
from jax import lax
from jax.experimental import pallas as pl
from jax.experimental.pallas import tpu as pltpu
from jax.sharding import PartitionSpec as P

HD = 128
PANEL = 8
OUTER = 32
MIB = 1 << 20

momentum_keep = 0.95
norm_eps = 1e-06

F32 = jnp.float32
BF16 = jnp.bfloat16
HIGHEST = lax.Precision.HIGHEST

SMEM = pl.BlockSpec(memory_space=pltpu.SMEM)
VMEM = pl.BlockSpec(memory_space=pltpu.VMEM)
ANY = pl.BlockSpec(memory_space=pl.ANY)
HBM = pl.BlockSpec(memory_space=pltpu.HBM)


def swap(value, axes, k):
    axes = (axes,) if isinstance(axes, str) else axes
    n = math.prod(lax.axis_size(a) for a in axes)
    return lax.ppermute(value, axes, [(i, i ^ k) for i in range(n)])


def params(mib=6):
    return pltpu.CompilerParams(vmem_limit_bytes=mib * MIB)


def cost(flops, nbytes):
    return pl.CostEstimate(flops=int(flops), bytes_accessed=int(nbytes), transcendentals=0)


def halves(x):
    hi = x.astype(BF16)
    return hi, (x - hi.astype(F32)).astype(BF16)


def mm(a, b):
    return jnp.dot(a, b, preferred_element_type=F32)


def mm_full(a, b):
    return jnp.dot(a, b, precision=HIGHEST, preferred_element_type=F32)


def row_copies(ranks, n_head, part, mom, grad, mom_to, grad_to, sems):
    j, first, number = part
    chunk = mom_to.shape[0] // number
    pieces = 2 if chunk % 32 == 0 else 1
    size = chunk // pieces
    copies = []
    for i in range(number):
        at = ((ranks[0] ^ j) * n_head + (ranks[2] ^ (first + i))) * chunk
        copies.append([])
        for p in range(pieces):
            src = pl.ds(pl.multiple_of(at + p * size, size), size)
            dst = pl.ds(i * chunk + p * size, size)
            n = i * pieces + p
            copies[i].append(pltpu.make_async_copy(mom.at[src, :], mom_to.at[dst, :], sems.at[0, n]))
            copies[i].append(
                pltpu.make_async_copy(grad.at[src, :], grad_to.at[dst, :], sems.at[1, n])
            )
    return copies


def start_all(copies):
    for row in copies:
        for c in row:
            c.start()


def project_kernel(n_head, part, following, is_first, n_in, ranks, mom, grad, *refs):
    ins, refs = refs[:n_in], list(refs)
    number = part[2]
    sems = refs.pop()
    ahead = []
    if is_first:
        right_sem, right, grad_in = refs.pop(), refs.pop(), refs.pop()
    if following:
        next_grad, next_mom = refs.pop(), refs.pop()
        ahead = row_copies(ranks, n_head, following, mom, grad, next_mom, next_grad, sems.at[1])
    if is_first:
        b_lo, b_hi = refs.pop(), refs.pop()
        total, out = refs.pop(), refs.pop()
        mom_in = total
        copies = row_copies(ranks, n_head, part, mom, grad, mom_in, grad_in, sems.at[0])
        fetch = pltpu.make_async_copy(ins[0], right, right_sem)
        start_all(copies[:1])
        fetch.start()
        start_all(copies[1:])
        fetch.wait()
        hi, lo = halves(right[...])
        b_hi[...] = hi
        b_lo[...] = lo
    else:
        total, out = refs.pop(), refs.pop()
        b_hi, b_lo, mom_in, grad_in = ins
        copies = [[]] * number
        start_all(ahead)
    chunk = total.shape[0] // number
    for i in range(number):
        for c in copies[i]:
            c.wait()
        if is_first and i == 0:
            start_all(ahead)
        rows = slice(i * chunk, (i + 1) * chunk)
        t = mom_in[rows, :] + grad_in[rows, :].astype(F32)
        total[rows, :] = t
        t_hi, t_lo = halves(t)
        acc = mm(t_hi, b_hi[...]) + (mm(t_hi, b_lo[...]) + mm(t_lo, b_hi[...]))
        out[rows, :] = acc.astype(out.dtype)
    for row in ahead:
        for c in row:
            c.wait()


def project(ranks, momentum, grad_q, ins, part, following, n_resp, n_head, dtype, after):
    is_first = len(ins) == 1
    rows, cols = momentum.shape
    chunk = rows // (n_resp * n_head)
    size = part[2] * chunk
    if is_first:
        right = ins[0]
        rank = right.shape[1]
        specs = [HBM]
    else:
        rank = ins[0].shape[1]
        specs = [VMEM] * 4
    out_shape = [jax.ShapeDtypeStruct((size, rank), dtype), jax.ShapeDtypeStruct((size, cols), F32)]
    if is_first:
        out_shape += [jax.ShapeDtypeStruct((cols, rank), BF16)] * 2
    if following:
        ahead = following[2] * chunk
        out_shape += [
            jax.ShapeDtypeStruct((ahead, cols), F32), jax.ShapeDtypeStruct((ahead, cols), BF16)
        ]
    scratch = [pltpu.SemaphoreType.DMA((2, 2, 2 * n_head))]
    if is_first:
        scratch = [
            pltpu.VMEM((size, cols), BF16), pltpu.VMEM((cols, rank), F32), pltpu.SemaphoreType.DMA
        ] + scratch
    outs = pl.pallas_call(
        functools.partial(project_kernel, n_head, part, following, is_first, len(ins)),
        in_specs=[SMEM, HBM, HBM] + specs + [ANY] * len(after),
        out_specs=[VMEM] * len(out_shape),
        scratch_shapes=scratch,
        out_shape=out_shape,
        compiler_params=params(14),
        cost_estimate=cost(6 * size * cols * rank, size * cols * 6),
    )(ranks, momentum, grad_q, *ins, *after)
    right = tuple(outs[2:4]) if is_first else tuple(ins[:2])
    return outs[0], outs[1], right + tuple(outs[-2:] if following else ())


def split_kernel(n_recv, number, own, *refs):
    recvs, outs = refs[:n_recv], refs[-number:]
    chunk = outs[0].shape[0]
    for i in range(number):
        rows = slice(i * chunk, (i + 1) * chunk)
        acc = own[rows, :]
        for r in recvs:
            acc = acc + r[rows, :].astype(F32)
        outs[i][...] = acc.astype(outs[i].dtype)


def split_sum(own, recvs, first, number):
    rows, rank = own.shape
    chunk = rows // number
    return pl.pallas_call(
        functools.partial(split_kernel, len(recvs), number),
        in_specs=[VMEM] * (1 + len(recvs)),
        out_specs=[VMEM] * number,
        out_shape=[
            jax.ShapeDtypeStruct((chunk, rank), BF16 if first + i else F32)
            for i in range(number)
        ],
        compiler_params=params(),
        cost_estimate=cost(rows * rank, rows * rank * 8),
    )(own, *recvs)


def sum_kernel(n_parts, *refs):
    acc = refs[0][...].astype(F32)
    for r in refs[1:n_parts]:
        acc = acc + r[...].astype(F32)
    refs[-1][...] = acc.astype(refs[-1].dtype)


def sum_parts(parts, dtype, after=()):
    shape = parts[0].shape
    return pl.pallas_call(
        functools.partial(sum_kernel, len(parts)),
        in_specs=[VMEM] * len(parts) + [ANY] * len(after),
        out_specs=VMEM,
        out_shape=jax.ShapeDtypeStruct(shape, dtype),
        compiler_params=params(),
        cost_estimate=cost(1000, 12 * math.prod(shape)),
    )(*parts, *after)


def gram_kernel(n_chunks, *refs):
    chunks, (pcat, pcat_t, gram) = refs[:n_chunks], refs[-3:]
    size = chunks[0].shape[0]
    for i in range(n_chunks):
        pcat[i * size : (i + 1) * size, :] = chunks[i][...]
    p = pcat[...]
    pt = p.T
    pcat_t[...] = pt
    half = p.shape[1] // 2
    gram[:half, :] = mm(pt[:half, :], p[:, :half])
    low = mm(pt[half:, :], p)
    gram[half : 2 * half, :] = low[:, :half]
    gram[2 * half :, :] = low[:, half:]


def gather_gram(chunks, after):
    size, rank = chunks[0].shape
    rows = size * len(chunks)
    return pl.pallas_call(
        functools.partial(gram_kernel, len(chunks)),
        in_specs=[VMEM] * len(chunks) + [ANY] * len(after),
        out_specs=[VMEM] * 3,
        out_shape=[
            jax.ShapeDtypeStruct((rows, rank), BF16),
            jax.ShapeDtypeStruct((rank, rows), BF16),
            jax.ShapeDtypeStruct((3 * rank // 2, rank // 2), F32),
        ],
        compiler_params=params(8),
        cost_estimate=cost(2 * rows * rank * rank, rows * rank * 6),
    )(*chunks, *after)


def back_part_kernel(pcat_t, *refs):
    totals, out = refs[:-1], refs[-1]
    seg = totals[0].shape[0]
    step = min(seg, 512)
    acc = None
    for j, total in enumerate(totals):
        for i in range(0, seg, step):
            t_hi, t_lo = halves(total[i : i + step, :])
            pt = pcat_t[:, j * seg + i : j * seg + i + step]
            part = mm(pt, t_hi) + mm(pt, t_lo)
            acc = part if acc is None else acc + part
    out[...] = acc.astype(BF16)


def back_part(pcat_t, totals):
    rank = pcat_t.shape[0]
    seg, cols = totals[0].shape
    rows = seg * len(totals)
    return pl.pallas_call(
        back_part_kernel,
        in_specs=[VMEM] * (1 + len(totals)),
        out_specs=VMEM,
        out_shape=jax.ShapeDtypeStruct((rank, cols), BF16),
        compiler_params=params(14),
        cost_estimate=cost(4 * rows * cols * rank, rows * cols * 4),
    )(pcat_t, *totals)


def factor_panel(panel, off):
    shape = (PANEL, 128)
    d = {}
    for j in range(PANEL):
        col = jnp.broadcast_to(panel[:, off + j : off + j + 1], shape)
        for i in range(j, PANEL):
            d[i, j] = jnp.broadcast_to(col[i : i + 1, :], shape)
    low, inv = {}, {}
    for j in range(0, PANEL, 2):
        a, b, c = d[j, j], d[j + 1, j], d[j + 1, j + 1]
        first = lax.rsqrt(a)
        second = lax.rsqrt(a * c - b * b) * (a * first)
        inv[j, j], inv[j + 1, j + 1] = first, second
        low[j + 1, j] = b * first
        for i in range(j + 2, PANEL):
            low[i, j] = d[i, j] * first
            low[i, j + 1] = (d[i, j + 1] - low[i, j] * low[j + 1, j]) * second
        for k in range(j + 2, PANEL):
            for i in range(k, PANEL):
                d[i, k] = d[i, k] - (low[i, j] * low[k, j] + low[i, j + 1] * low[k, j + 1])
    for j in range(PANEL):
        for i in range(j + 1, PANEL):
            acc = low[i, j] * inv[j, j]
            for k in range(j + 1, i):
                acc = acc + low[i, k] * inv[k, j]
            inv[i, j] = -(acc * inv[i, i])
    return inv


def three_parts(x):
    a = x.astype(BF16)
    rest = x - a.astype(F32)
    b = rest.astype(BF16)
    return a, b, (rest - b.astype(F32)).astype(BF16)


def cholesky_kernel(n_parts, *refs):
    parts, out, work = refs[:n_parts], refs[n_parts], refs[n_parts + 1]
    n = out.shape[0]
    half = n // 2
    tiles = n // 128 + 1
    total = parts[0][...]
    for part in parts[1:]:
        total = total + part[...]
    low = total[half : 2 * half, :]
    work[:half, :half] = total[:half, :]
    work[half:, :half] = low
    work[:half, half:] = low.T
    work[half:, half:] = total[2 * half :, :]
    eye = lax.broadcasted_iota(jnp.int32, (n, n), 0) == lax.broadcasted_iota(jnp.int32, (n, n), 1)
    whole = work[...]
    diag = jnp.where(eye, whole, 0.0)
    across = lax.rsqrt(jnp.sum(diag, axis=0, keepdims=True))
    work[...] = whole * lax.rsqrt(jnp.sum(diag, axis=1, keepdims=True)) * across
    sub = lax.broadcasted_iota(jnp.int32, (PANEL, 128), 0)
    lane = lax.broadcasted_iota(jnp.int32, (PANEL, 128), 1)
    n_panels = OUTER // PANEL

    def step(o, carry):
        blk = [
            [work[p * PANEL : (p + 1) * PANEL, t * 128 : (t + 1) * 128] for t in range(tiles - 1)]
            + [jnp.where(lane == sub + p * PANEL, 1.0, 0.0).astype(F32)]
            for p in range(n_panels)
        ]
        for p in range(n_panels):
            off = p * PANEL
            inv = factor_panel(blk[p][0], off)
            rows_of = [
                [jnp.broadcast_to(blk[p][t][j : j + 1, :], (PANEL, 128)) for t in range(tiles)]
                for j in range(PANEL)
            ]
            new = [None] * tiles
            for j in range(PANEL):
                col = inv[PANEL - 1, j]
                for i in range(PANEL - 2, j - 1, -1):
                    col = jnp.where(sub == i, inv[i, j], col)
                if j:
                    col = jnp.where(sub < j, 0.0, col)
                for t in range(tiles):
                    term = col * rows_of[j][t]
                    new[t] = term if new[t] is None else new[t] + term
            blk[p] = new
            if p + 1 < n_panels:
                u_rows = [
                    [jnp.broadcast_to(new[t][j : j + 1, :], (PANEL, 128)) for t in range(tiles)]
                    for j in range(PANEL)
                ]
                for b in range(p + 1, n_panels):
                    lanes = [
                        jnp.broadcast_to(blk[b][0][:, off + m : off + m + 1], (PANEL, 128))
                        for m in range(PANEL)
                    ]
                    upd = list(blk[b])
                    for k in range(PANEL):
                        v = lanes[0] * inv[k, 0]
                        for m in range(1, k + 1):
                            v = v + lanes[m] * inv[k, m]
                        for t in range(tiles):
                            upd[t] = upd[t] - v * u_rows[k][t]
                    blk[b] = upd
        u = jnp.concatenate([jnp.concatenate(row, axis=1) for row in blk], axis=0)
        u = pltpu.roll(u, tiles * 128 - OUTER, 1)[:, :n]
        at = lax.broadcasted_iota(jnp.int32, (OUTER, n), 1)
        left = jnp.where(at < n - OUTER * (o + 1), u, 0.0)
        la, lb, lc = three_parts(left)
        ua, ub, uc = three_parts(u)
        lhs = jnp.concatenate([la, la, lb, la, lc, lb], axis=0)
        rhs = jnp.concatenate([ua, ub, ua, uc, ua, ub], axis=0)
        upd = mm(lhs.T, rhs)
        rest = work[OUTER:, :]
        lanes_at = lax.broadcasted_iota(jnp.int32, rest.shape, 1)
        rest = pltpu.roll(jnp.where(lanes_at < OUTER, 0.0, rest), n - OUTER, 1)
        work[: n - OUTER, :] = rest - upd[: n - OUTER, :]
        work[n - OUTER :, :] = u
        return carry

    lax.fori_loop(0, n // OUTER, step, 0)
    out[...] = work[...] * across


def inverse_factor(*parts):
    n = 2 * parts[0].shape[1]
    return pl.pallas_call(
        functools.partial(cholesky_kernel, len(parts)),
        in_specs=[VMEM] * len(parts),
        out_specs=VMEM,
        scratch_shapes=[pltpu.VMEM((n, n), F32)],
        out_shape=jax.ShapeDtypeStruct((n, n), F32),
        compiler_params=params(),
        cost_estimate=cost(10_000_000_000, 4 * n * n * 4),
    )(*parts)


def mm_three(a, b):
    a_hi, a_lo = halves(a)
    b_hi, b_lo = halves(b)
    return mm(a_hi, b_hi) + (mm(a_hi, b_lo) + mm(a_lo, b_hi))


def back_kernel(x, wa, wb, bt_out, y_out, s_out):
    w = wa[...].astype(F32) + wb[...].astype(F32)
    bt = mm_three(x[...], w)
    bt_out[...] = bt
    s = jnp.sum(bt * bt, axis=1, keepdims=True)
    s_out[...] = jnp.broadcast_to(s, (s.shape[0], 128)).T[:8, :]
    y_out[...] = ((1.0 - momentum_keep) * mm(x[...].T.astype(BF16), bt.astype(BF16))).astype(BF16)


def back_full(x, wa, wb):
    rank, cols = wa.shape
    return pl.pallas_call(
        back_kernel,
        in_specs=[VMEM] * 3,
        out_specs=[VMEM] * 3,
        out_shape=[
            jax.ShapeDtypeStruct((rank, cols), F32),
            jax.ShapeDtypeStruct((rank, cols), BF16),
            jax.ShapeDtypeStruct((8, rank), F32),
        ],
        compiler_params=params(),
        cost_estimate=cost(8 * rank * rank * cols, rank * cols * 12),
    )(x, wa, wb)


def row_blocks(ranks, n_resp, n_head, chunk):
    return [
        pl.multiple_of(((ranks[0] ^ j) * n_head + (ranks[2] ^ k)) * chunk, chunk)
        for j in range(n_resp)
        for k in range(n_head)
    ]


def momentum_kernel(n_resp, n_head, begin, end, n_totals, ranks, pcat, y, *refs):
    totals, (out, held, sems) = refs[:n_totals], refs[-3:]
    seg = totals[0].shape[0]
    chunk = pcat.shape[0] // (n_resp * n_head)
    blocks = row_blocks(ranks, n_resp, n_head, chunk)
    copies = []
    for i in range(begin, end):
        rows = slice(i * chunk, (i + 1) * chunk)
        kept = slice((i - begin) * chunk, (i - begin + 1) * chunk)
        off = i * chunk % seg
        total = totals[(i - begin) * chunk // seg][off : off + chunk, :]
        held[kept, :] = total - mm(pcat[rows, :], y[...])
        copies.append(
            pltpu.make_async_copy(
                held.at[kept, :], out.at[pl.ds(blocks[i], chunk), :], sems.at[i - begin]
            )
        )
        copies[-1].start()
    for c in copies:
        c.wait()


def new_momentum(ranks, pcat, totals, y, n_resp, n_head, half, earlier):
    rows, rank = pcat.shape
    cols = totals[0].shape[1]
    n_chunks = n_resp * n_head // 2
    part = len(totals) // 2
    totals = totals[half * part : (half + 1) * part]
    aliases = {3 + part: 0} if earlier else {}
    return pl.pallas_call(
        functools.partial(
            momentum_kernel, n_resp, n_head, half * n_chunks, (half + 1) * n_chunks, part
        ),
        in_specs=[SMEM] + [VMEM] * (2 + part) + [HBM] * len(earlier),
        out_specs=HBM,
        scratch_shapes=[pltpu.VMEM((rows // 2, cols), F32), pltpu.SemaphoreType.DMA((n_chunks,))],
        out_shape=jax.ShapeDtypeStruct((rows, cols), F32),
        input_output_aliases=aliases,
        compiler_params=params(10),
        cost_estimate=cost(rows * cols * rank, rows * cols * 4),
    )(ranks, pcat, y, *totals, *earlier)


def update_kernel(gain, n_resp, n_head, n_sums, ranks, pcat, x, bt, *refs):
    sums, (upd, basis_out, held, held_basis, sems, basis_sem) = refs[:n_sums], refs[n_sums:]
    total = sums[0][...]
    for s in sums[1:]:
        total = total + s[...]
    scale = lax.rsqrt(total + norm_eps).T[:, :1]
    scaled = bt[...] * scale
    held_basis[...] = scaled.T
    basis_copy = pltpu.make_async_copy(held_basis, basis_out, basis_sem)
    basis_copy.start()
    z_hi, z_lo = halves(gain * mm_three(x[...].T, scaled))
    chunk = pcat.shape[0] // (n_resp * n_head)
    copies = []
    for i, at in enumerate(row_blocks(ranks, n_resp, n_head, chunk)):
        rows = slice(i * chunk, (i + 1) * chunk)
        p = pcat[rows, :]
        held[rows, :] = (mm(p, z_hi) + mm(p, z_lo)).astype(BF16)
        copies.append(
            pltpu.make_async_copy(held.at[rows, :], upd.at[pl.ds(at, chunk), :], sems.at[i])
        )
        copies[-1].start()
    for c in copies:
        c.wait()
    basis_copy.wait()


def final_update(ranks, pcat, x, bt, sums, gain, n_resp, n_head):
    rows, rank = pcat.shape
    cols = bt.shape[1]
    return pl.pallas_call(
        functools.partial(update_kernel, gain, n_resp, n_head, len(sums)),
        in_specs=[SMEM] + [VMEM] * (3 + len(sums)),
        out_specs=[HBM, HBM],
        scratch_shapes=[
            pltpu.VMEM((rows, cols), BF16),
            pltpu.VMEM((cols, rank), F32),
            pltpu.SemaphoreType.DMA((n_resp * n_head,)),
            pltpu.SemaphoreType.DMA,
        ],
        out_shape=[
            jax.ShapeDtypeStruct((rows, cols), BF16),
            jax.ShapeDtypeStruct((cols, rank), F32),
        ],
        compiler_params=params(10),
        cost_estimate=cost(4 * rows * cols * rank, rows * cols * 3),
    )(ranks, pcat, x, bt, *sums)


def group_of(counts, response):
    group = jnp.int32(0)
    end = jnp.int32(0)
    for g in range(counts.shape[0]):
        end = end + counts[g]
        group = group + (end <= response).astype(jnp.int32)
    return group


def pack_kernel(*refs):
    keys, values, out = refs[0], refs[1], refs[-1]
    out[0] = keys[...]
    out[1] = values[...]


def pack_prompts(keys, values, after):
    return pl.pallas_call(
        pack_kernel,
        in_specs=[VMEM] * 2 + [ANY] * len(after),
        out_specs=VMEM,
        out_shape=jax.ShapeDtypeStruct((2,) + keys.shape, BF16),
        compiler_params=params(),
        cost_estimate=cost(1000, 8 * math.prod(keys.shape)),
    )(keys, values, *after)


def select_kernel(n_resp, n_fsdp, ranks, counts, slots, *refs):
    stored, outs = refs[:n_resp], refs[-n_fsdp:]
    held = stored[0].shape[1]
    for k in range(n_fsdp):
        slot = slots[group_of(counts, ranks[0] * n_fsdp + (ranks[1] ^ k))]
        owner, local = slot // held, slot % held
        for j in range(n_resp):

            @pl.when(owner == (ranks[0] ^ j))
            def _():
                outs[k][0] = stored[j][0, local]
                outs[k][1] = stored[j][1, local]


def select_prompts(ranks, counts, slots, stored, n_fsdp, after):
    _, _, piece, width = stored[0].shape
    return pl.pallas_call(
        functools.partial(select_kernel, len(stored), n_fsdp),
        in_specs=[SMEM] * 3 + [VMEM] * len(stored) + [ANY] * len(after),
        out_specs=[VMEM] * n_fsdp,
        out_shape=[jax.ShapeDtypeStruct((2, piece, width), BF16)] * n_fsdp,
        compiler_params=params(),
        cost_estimate=cost(1000, 8 * n_fsdp * piece * width),
    )(ranks, counts, slots, *stored, *after)


def attention_kernel(
    n_fsdp, heads, last, ranks, counts, prompt_blocks, resp_blocks, q, sk, sv, go, *refs
):
    pieces, refs = refs[:n_fsdp], refs[n_fsdp:]
    keys, values, dk, dv = refs[-4:]
    n_out = 2 + n_fsdp if last else 3
    outs = refs[-4 - n_out : -4]
    dq = outs[0]
    piece = pieces[0].shape[1]
    cap = piece * n_fsdp
    length = q.shape[0]
    scale = HD ** (-0.5)
    for k in range(n_fsdp):
        rows = pl.ds(pl.multiple_of((ranks[1] ^ k) * piece, piece), piece)
        keys[rows, :] = pieces[k][0]
        values[rows, :] = pieces[k][1]
    keys[cap:, :] = sk[...]
    values[cap:, :] = sv[...]
    prompt_len = prompt_blocks[group_of(counts, ranks[0] * n_fsdp + ranks[1])] * 128
    resp_len = resp_blocks[0] * 128
    width = keys.shape[0]
    place = lax.broadcasted_iota(jnp.int32, (width, length), 0)
    pos = lax.broadcasted_iota(jnp.int32, (width, length), 1)
    inner = place - cap
    seen = ((place < cap) & (place < prompt_len)) | (
        (place >= cap) & (inner <= pos) & (inner < resp_len)
    )
    bias = jnp.where(seen, 0.0, -jnp.inf).astype(F32)
    live = lax.broadcasted_iota(jnp.int32, (length, HD), 0) < resp_len
    nt = (((1,), (1,)), ((), ()))
    kall = keys[...]
    vall = values[...]
    kt = kall.T
    if last:
        dk[...] = refs[0][...]
        dv[...] = refs[1][...]
    else:
        dk[...] = jnp.zeros_like(dk)
        dv[...] = jnp.zeros_like(dv)
    for h in heads:
        cols = slice(h * HD, (h + 1) * HD)
        qh = q[:, cols]
        gh = jnp.where(live, go[:, cols], jnp.zeros((), BF16))
        logits = lax.dot_general(kall, qh, nt, preferred_element_type=F32) * scale + bias
        peak = jnp.max(logits, axis=0, keepdims=True)
        e = jnp.exp(logits - peak)
        w = (e * (1.0 / jnp.sum(e, axis=0, keepdims=True))).astype(BF16)
        dp = lax.dot_general(vall, gh, nt, preferred_element_type=F32)
        wf = w.astype(F32)
        diag = jnp.sum(wf * dp, axis=0, keepdims=True)
        ds = (wf * (dp - diag)).astype(BF16)
        dk[...] += mm(ds, qh)
        dv[...] += mm(w, gh)
        dq[:, cols] = (mm(kt, ds) * scale).T.astype(BF16)
    if last:
        done = heads[0] * HD
        dq[:, :done] = refs[2][...]
        own, sends = outs[1], outs[2:]
        own[0] = (dk[cap:, :] * scale).astype(BF16)
        own[1] = dv[cap:, :].astype(BF16)
        for k in range(n_fsdp):
            rows = pl.ds(pl.multiple_of((ranks[1] ^ k) * piece, piece), piece)
            sends[k][0] = (dk[rows, :] * scale).astype(sends[k].dtype)
            sends[k][1] = dv[rows, :].astype(sends[k].dtype)
    else:
        outs[1][...] = dk[...]
        outs[2][...] = dv[...]


def attention(heads, earlier, ranks, counts, prompt_blocks, resp_blocks, q, sk, sv, go, pieces, after):
    n_fsdp = len(pieces)
    piece = pieces[0].shape[1]
    length, width = q.shape
    cap = piece * n_fsdp
    total = cap + length
    last = earlier is not None
    if last:
        extra, specs = (earlier[1], earlier[2], earlier[0]), [VMEM] * 3
        out_shape = [pltpu.VMEM((length, width), BF16), jax.ShapeDtypeStruct((2, length, HD), BF16)] + [
            jax.ShapeDtypeStruct((2, piece, HD), BF16 if k else F32) for k in range(n_fsdp)
        ]
    else:
        extra, specs = (), []
        out_shape = [jax.ShapeDtypeStruct((length, len(heads) * HD), BF16)]
        out_shape += [jax.ShapeDtypeStruct((total, HD), F32)] * 2
    return pl.pallas_call(
        functools.partial(attention_kernel, n_fsdp, heads, last),
        in_specs=[SMEM] * 4 + [VMEM] * (4 + n_fsdp) + specs + [ANY] * len(after),
        out_specs=[VMEM] * len(out_shape),
        scratch_shapes=[pltpu.VMEM((total, HD), BF16)] * 2 + [pltpu.VMEM((total, HD), F32)] * 2,
        out_shape=out_shape,
        compiler_params=params(12),
        cost_estimate=cost(3_000_000_000, length * width * 8),
    )(ranks, counts, prompt_blocks, resp_blocks, q, sk, sv, go, *pieces, *extra, *after)


def by_slot_kernel(n_resp, n_fsdp, ranks, counts, slots, *refs):
    parts, outs = refs[:n_fsdp], refs[-n_resp:]
    held = outs[0].shape[1]
    slot_of = [
        slots[group_of(counts, ranks[0] * n_fsdp + (ranks[1] ^ k))] for k in range(n_fsdp)
    ]
    for j in range(n_resp):
        for local in range(held):
            slot = (ranks[0] ^ j) * held + local
            acc = jnp.zeros(parts[0].shape, F32)
            for k in range(n_fsdp):
                acc = acc + jnp.where(slot_of[k] == slot, parts[k][...].astype(F32), 0.0)
            outs[j][:, local] = acc.astype(outs[j].dtype)


def sum_by_slot(ranks, counts, slots, parts, n_resp, after):
    held = counts.shape[0] // n_resp
    _, piece, width = parts[0].shape
    return pl.pallas_call(
        functools.partial(by_slot_kernel, n_resp, len(parts)),
        in_specs=[SMEM] * 3 + [VMEM] * len(parts) + [ANY] * len(after),
        out_specs=[VMEM] * n_resp,
        out_shape=[
            jax.ShapeDtypeStruct((2, held, piece, width), BF16 if j else F32)
            for j in range(n_resp)
        ],
        compiler_params=params(),
        cost_estimate=cost(1000, 8 * len(parts) * piece * width * 4),
    )(ranks, counts, slots, *parts, *after)


def on_device(
    queries,
    self_keys,
    self_values,
    d_out,
    prompt_keys,
    prompt_values,
    counts,
    owner_slot,
    prompt_blocks,
    resp_blocks,
    grad_q,
    momentum,
    basis,
):
    n_resp, n_fsdp, n_head = (lax.axis_size(a) for a in ("resp", "fsdp", "head"))
    ranks = jnp.stack([lax.axis_index(a) for a in ("resp", "fsdp", "head")]).astype(jnp.int32)
    gain = math.sqrt(
        momentum.shape[0] * n_fsdp * momentum.shape[1] * n_resp * n_head / basis.shape[1]
    )

    in_hbm = [pltpu.with_memory_space_constraint(a, pltpu.HBM) for a in (momentum, grad_q, basis)]
    half = n_head // 2
    groups = [(half, half), (0, half)] if half else [(0, n_head)]

    mom_hbm, grad_hbm, basis_hbm = in_hbm
    order = [(j, *group) for group in groups for j in range(1, n_resp)]
    order += [(0, *group) for group in groups]
    nexts = dict(zip(order, order[1:] + [None]))
    totals, arrived, ins = {}, [], (basis_hbm,)

    def project_next(part, dtype, after):
        return project(
            ranks, mom_hbm, grad_hbm, ins, part, nexts[part], n_resp, n_head, dtype, after
        )

    for group in groups:
        row = []
        for j in range(1, n_resp):
            sent, totals[j, group[0]], ins = project_next((j, *group), BF16, ())
            row.append(swap(sent, "resp", j))
        arrived.append(row)
    packed = pack_prompts(prompt_keys, prompt_values, (sent,))
    stored = [packed] + [swap(packed, "resp", j) for j in range(1, n_resp)]
    after = (packed,)
    split = {}
    for group, recvs in zip(groups, arrived):
        mine, totals[0, group[0]], ins = project_next((0, *group), F32, after)
        outs = split_sum(mine, recvs, *group)
        after = (outs[0],)
        for i in range(group[1]):
            split[group[0] + i] = outs[i]
    totals = [totals[at] for at in sorted(totals)]
    chosen = select_prompts(ranks, counts, owner_slot, stored, n_fsdp, after)
    far_first = [k for first, number in groups for k in range(first, first + number) if k]
    summands = {k: swap(split[k], "head", k) for k in far_first}
    pieces = [chosen[0]] + [swap(chosen[k], "fsdp", k) for k in range(1, n_fsdp)]
    piece0 = sum_parts(
        [split[0]] + [summands[k] for k in range(1, n_head)], BF16, (pieces[-1],)
    )

    along = {0: piece0}
    for k in far_first:
        along[k] = swap(piece0, "head", k)
    chunks = [along[k] for k in range(n_head)]
    for j in range(1, n_resp):
        chunks += [swap(along[k], "resp", j) for k in range(n_head)]

    n_q = queries.shape[1] // HD
    heads = [list(range(n_q // 2)), list(range(n_q // 2, n_q))]
    held = (
        ranks, counts, prompt_blocks, resp_blocks, queries, self_keys, self_values, d_out, pieces
    )
    earlier = attention(heads[0], None, *held, (piece0,))
    dq, resp_grad, *parts = attention(heads[1], earlier, *held, (along[n_head - 1],))
    pcat, pcat_t, gram = gather_gram(chunks, (resp_grad,))

    bits = [1 << b for b in range(n_fsdp.bit_length() - 1)]
    w = back_part(pcat_t, totals)
    for bit in bits[:-1]:
        gram = sum_parts([gram, swap(gram, "fsdp", bit)], F32)
        w = sum_parts([w, swap(w, "fsdp", bit)], BF16, (gram,))
    gram_parts = (gram, swap(gram, "fsdp", bits[-1]))
    w_other = swap(w, "fsdp", bits[-1])
    returned = [parts[0]] + [swap(parts[k], "fsdp", k) for k in range(1, n_fsdp)]
    x = inverse_factor(*gram_parts)
    slots = sum_by_slot(ranks, counts, owner_slot, returned, n_resp, (x,))
    prompt_grad = sum_parts(
        [slots[0]] + [swap(slots[j], "resp", j) for j in range(1, n_resp)], F32
    )

    bt, y, squares = back_full(x, w, w_other)
    from_head = [swap(squares, "head", k) for k in range(1, n_head)]
    momentum_out = new_momentum(ranks, pcat, totals, y, n_resp, n_head, 0, ())
    squares = sum_parts([squares] + from_head, F32, (momentum_out,))
    sums = [squares] + [swap(squares, "resp", j) for j in range(1, n_resp)]
    momentum_out = new_momentum(ranks, pcat, totals, y, n_resp, n_head, 1, (momentum_out,))
    update, basis_out = final_update(ranks, pcat, x, bt, sums, gain, n_resp, n_head)
    return (dq, resp_grad, prompt_grad, update, momentum_out, basis_out)


def solution(mesh):
    placed = (
        P(("resp", "fsdp"), "head"),
        P(("resp", "fsdp"), "head"),
        P(("resp", "fsdp"), "head"),
        P(("resp", "fsdp"), "head"),
        P("resp", "fsdp", "head"),
        P("resp", "fsdp", "head"),
        P(),
        P(),
        P(),
        P(("resp", "fsdp")),
        P("fsdp", ("resp", "head")),
        P("fsdp", ("resp", "head")),
        P(("resp", "head"), None),
    )
    return jax.shard_map(
        on_device,
        mesh=mesh,
        in_specs=placed,
        out_specs=(
            P(("resp", "fsdp"), "head"),
            P(None, ("resp", "fsdp"), "head"),
            P(None, "resp", "fsdp", "head"),
            P("fsdp", ("resp", "head")),
            P("fsdp", ("resp", "head")),
            P(("resp", "head"), None),
        ),
        check_vma=False,
    )
```

```python
import functools
import math

import jax
import jax.numpy as jnp
from jax import lax
from jax.experimental import pallas as pl
from jax.experimental.pallas import tpu as pltpu
from jax.sharding import PartitionSpec as P

HD = 128
PANEL = 8
OUTER = 32
MIB = 1 << 20

momentum_keep = 0.95
norm_eps = 1e-06

F32 = jnp.float32
BF16 = jnp.bfloat16
HIGHEST = lax.Precision.HIGHEST

SMEM = pl.BlockSpec(memory_space=pltpu.SMEM)
VMEM = pl.BlockSpec(memory_space=pltpu.VMEM)
ANY = pl.BlockSpec(memory_space=pl.ANY)
HBM = pl.BlockSpec(memory_space=pltpu.HBM)


def swap(value, axes, k):
    axes = (axes,) if isinstance(axes, str) else axes
    n = math.prod(lax.axis_size(a) for a in axes)
    return lax.ppermute(value, axes, [(i, i ^ k) for i in range(n)])


def params(mib=6):
    return pltpu.CompilerParams(vmem_limit_bytes=mib * MIB)


def cost(weight=0):
    return pl.CostEstimate(flops=1 + weight * 10**9, bytes_accessed=1, transcendentals=0)


def halves(x):
    hi = x.astype(BF16)
    return hi, (x - hi.astype(F32)).astype(BF16)


def mm(a, b):
    return jnp.dot(a, b, preferred_element_type=F32)


def mm_full(a, b):
    return jnp.dot(a, b, precision=HIGHEST, preferred_element_type=F32)


def row_copies(ranks, n_head, part, mom, grad, mom_to, grad_to, sems):
    j, first, number = part
    chunk = mom_to.shape[0] // number
    pieces = 2 if chunk % 32 == 0 else 1
    size = chunk // pieces
    copies = []
    for i in range(number):
        at = ((ranks[0] ^ j) * n_head + (ranks[2] ^ (first + i))) * chunk
        copies.append([])
        for p in range(pieces):
            src = pl.ds(pl.multiple_of(at + p * size, size), size)
            dst = pl.ds(i * chunk + p * size, size)
            n = i * pieces + p
            copies[i].append(pltpu.make_async_copy(mom.at[src, :], mom_to.at[dst, :], sems.at[0, n]))
            copies[i].append(
                pltpu.make_async_copy(grad.at[src, :], grad_to.at[dst, :], sems.at[1, n])
            )
    return copies


def start_all(copies):
    for row in copies:
        for c in row:
            c.start()


def project_kernel(n_head, part, following, is_first, n_in, ranks, mom, grad, *refs):
    ins, refs = refs[:n_in], list(refs)
    number = part[2]
    sems = refs.pop()
    ahead = []
    if is_first:
        right_sem, right, grad_in = refs.pop(), refs.pop(), refs.pop()
    if following:
        next_grad, next_mom = refs.pop(), refs.pop()
        ahead = row_copies(ranks, n_head, following, mom, grad, next_mom, next_grad, sems.at[1])
    if is_first:
        b_lo, b_hi = refs.pop(), refs.pop()
        total, out = refs.pop(), refs.pop()
        mom_in = total
        copies = row_copies(ranks, n_head, part, mom, grad, mom_in, grad_in, sems.at[0])
        fetch = pltpu.make_async_copy(ins[0], right, right_sem)
        start_all(copies[:1])
        fetch.start()
        start_all(copies[1:])
        fetch.wait()
        hi, lo = halves(right[...])
        b_hi[...] = hi
        b_lo[...] = lo
    else:
        total, out = refs.pop(), refs.pop()
        b_hi, b_lo, mom_in, grad_in = ins
        copies = [[]] * number
        start_all(ahead)
    chunk = total.shape[0] // number
    for i in range(number):
        for c in copies[i]:
            c.wait()
        if is_first and i == 0:
            start_all(ahead)
        rows = slice(i * chunk, (i + 1) * chunk)
        t = mom_in[rows, :] + grad_in[rows, :].astype(F32)
        total[rows, :] = t
        t_hi, t_lo = halves(t)
        acc = mm(t_hi, b_hi[...]) + (mm(t_hi, b_lo[...]) + mm(t_lo, b_hi[...]))
        out[rows, :] = acc.astype(out.dtype)
    for row in ahead:
        for c in row:
            c.wait()


def project(ranks, momentum, grad_q, ins, part, following, n_resp, n_head, dtype, after):
    is_first = len(ins) == 1
    rows, cols = momentum.shape
    chunk = rows // (n_resp * n_head)
    size = part[2] * chunk
    if is_first:
        right = ins[0]
        rank = right.shape[1]
        specs = [HBM]
    else:
        rank = ins[0].shape[1]
        specs = [VMEM] * 4
    out_shape = [jax.ShapeDtypeStruct((size, rank), dtype), jax.ShapeDtypeStruct((size, cols), F32)]
    if is_first:
        out_shape += [jax.ShapeDtypeStruct((cols, rank), BF16)] * 2
    if following:
        ahead = following[2] * chunk
        out_shape += [
            jax.ShapeDtypeStruct((ahead, cols), F32), jax.ShapeDtypeStruct((ahead, cols), BF16)
        ]
    scratch = [pltpu.SemaphoreType.DMA((2, 2, 2 * n_head))]
    if is_first:
        scratch = [
            pltpu.VMEM((size, cols), BF16), pltpu.VMEM((cols, rank), F32), pltpu.SemaphoreType.DMA
        ] + scratch
    outs = pl.pallas_call(
        functools.partial(project_kernel, n_head, part, following, is_first, len(ins)),
        in_specs=[SMEM, HBM, HBM] + specs + [ANY] * len(after),
        out_specs=[VMEM] * len(out_shape),
        scratch_shapes=scratch,
        out_shape=out_shape,
        compiler_params=params(14),
        name="project",
        cost_estimate=cost(),
    )(ranks, momentum, grad_q, *ins, *after)
    right = tuple(outs[2:4]) if is_first else tuple(ins[:2])
    return outs[0], outs[1], right + tuple(outs[-2:] if following else ())


def split_kernel(n_recv, number, own, *refs):
    recvs, outs = refs[:n_recv], refs[-number:]
    chunk = outs[0].shape[0]
    for i in range(number):
        rows = slice(i * chunk, (i + 1) * chunk)
        acc = own[rows, :]
        for r in recvs:
            acc = acc + r[rows, :].astype(F32)
        outs[i][...] = acc.astype(outs[i].dtype)


def split_sum(own, recvs, first, number):
    rows, rank = own.shape
    chunk = rows // number
    return pl.pallas_call(
        functools.partial(split_kernel, len(recvs), number),
        in_specs=[VMEM] * (1 + len(recvs)),
        out_specs=[VMEM] * number,
        out_shape=[
            jax.ShapeDtypeStruct((chunk, rank), BF16 if first + i else F32)
            for i in range(number)
        ],
        compiler_params=params(),
        name="split_sum",
        cost_estimate=cost(),
    )(own, *recvs)


def sum_kernel(n_parts, *refs):
    acc = refs[0][...].astype(F32)
    for r in refs[1:n_parts]:
        acc = acc + r[...].astype(F32)
    refs[-1][...] = acc.astype(refs[-1].dtype)


def sum_parts(parts, dtype, after=(), weight=0):
    shape = parts[0].shape
    return pl.pallas_call(
        functools.partial(sum_kernel, len(parts)),
        in_specs=[VMEM] * len(parts) + [ANY] * len(after),
        out_specs=VMEM,
        out_shape=jax.ShapeDtypeStruct(shape, dtype),
        compiler_params=params(),
        name="sum_parts",
        cost_estimate=cost(weight),
    )(*parts, *after)


def gram_kernel(n_chunks, *refs):
    chunks, (pcat, pcat_t, gram) = refs[:n_chunks], refs[-3:]
    size = chunks[0].shape[0]
    for i in range(n_chunks):
        pcat[i * size : (i + 1) * size, :] = chunks[i][...]
    p = pcat[...]
    pt = p.T
    pcat_t[...] = pt
    half = p.shape[1] // 2
    gram[:half, :] = mm(pt[:half, :], p[:, :half])
    low = mm(pt[half:, :], p)
    gram[half : 2 * half, :] = low[:, :half]
    gram[2 * half :, :] = low[:, half:]


def gather_gram(chunks, after):
    size, rank = chunks[0].shape
    rows = size * len(chunks)
    return pl.pallas_call(
        functools.partial(gram_kernel, len(chunks)),
        in_specs=[VMEM] * len(chunks) + [ANY] * len(after),
        out_specs=[VMEM] * 3,
        out_shape=[
            jax.ShapeDtypeStruct((rows, rank), BF16),
            jax.ShapeDtypeStruct((rank, rows), BF16),
            jax.ShapeDtypeStruct((3 * rank // 2, rank // 2), F32),
        ],
        compiler_params=params(8),
        name="gather_gram",
        cost_estimate=cost(),
    )(*chunks, *after)


def back_part_kernel(n_totals, pcat_t, *refs):
    totals, out = refs[:n_totals], refs[-1]
    seg = totals[0].shape[0]
    step = min(seg, 512)
    acc = None
    for j, total in enumerate(totals):
        for i in range(0, seg, step):
            t_hi, t_lo = halves(total[i : i + step, :])
            pt = pcat_t[:, j * seg + i : j * seg + i + step]
            part = mm(pt, t_hi) + mm(pt, t_lo)
            acc = part if acc is None else acc + part
    out[...] = acc.astype(BF16)


def back_part(pcat_t, totals, after):
    rank = pcat_t.shape[0]
    seg, cols = totals[0].shape
    rows = seg * len(totals)
    return pl.pallas_call(
        functools.partial(back_part_kernel, len(totals)),
        in_specs=[VMEM] * (1 + len(totals)) + [ANY] * len(after),
        out_specs=VMEM,
        out_shape=jax.ShapeDtypeStruct((rank, cols), BF16),
        compiler_params=params(14),
        name="back_part",
        cost_estimate=cost(5),
    )(pcat_t, *totals, *after)


def factor_panel(panel, off):
    shape = (PANEL, 128)
    d = {}
    for j in range(PANEL):
        col = jnp.broadcast_to(panel[:, off + j : off + j + 1], shape)
        for i in range(j, PANEL):
            d[i, j] = jnp.broadcast_to(col[i : i + 1, :], shape)
    low, inv = {}, {}
    for j in range(0, PANEL, 2):
        a, b, c = d[j, j], d[j + 1, j], d[j + 1, j + 1]
        first = lax.rsqrt(a)
        second = lax.rsqrt(a * c - b * b) * (a * first)
        inv[j, j], inv[j + 1, j + 1] = first, second
        low[j + 1, j] = b * first
        for i in range(j + 2, PANEL):
            low[i, j] = d[i, j] * first
            low[i, j + 1] = (d[i, j + 1] - low[i, j] * low[j + 1, j]) * second
        for k in range(j + 2, PANEL):
            for i in range(k, PANEL):
                d[i, k] = d[i, k] - (low[i, j] * low[k, j] + low[i, j + 1] * low[k, j + 1])
    for j in range(PANEL):
        for i in range(j + 1, PANEL):
            acc = low[i, j] * inv[j, j]
            for k in range(j + 1, i):
                acc = acc + low[i, k] * inv[k, j]
            inv[i, j] = -(acc * inv[i, i])
    return inv


def three_parts(x):
    a = x.astype(BF16)
    rest = x - a.astype(F32)
    b = rest.astype(BF16)
    return a, b, (rest - b.astype(F32)).astype(BF16)


def cholesky_kernel(n_parts, *refs):
    parts, out, work = refs[:n_parts], refs[n_parts], refs[n_parts + 1]
    n = out.shape[0]
    half = n // 2
    tiles = n // 128 + 1
    total = parts[0][...]
    for part in parts[1:]:
        total = total + part[...]
    low = total[half : 2 * half, :]
    work[:half, :half] = total[:half, :]
    work[half:, :half] = low
    work[:half, half:] = low.T
    work[half:, half:] = total[2 * half :, :]
    eye = lax.broadcasted_iota(jnp.int32, (n, n), 0) == lax.broadcasted_iota(jnp.int32, (n, n), 1)
    whole = work[...]
    diag = jnp.where(eye, whole, 0.0)
    across = lax.rsqrt(jnp.sum(diag, axis=0, keepdims=True))
    work[...] = whole * lax.rsqrt(jnp.sum(diag, axis=1, keepdims=True)) * across
    sub = lax.broadcasted_iota(jnp.int32, (PANEL, 128), 0)
    lane = lax.broadcasted_iota(jnp.int32, (PANEL, 128), 1)
    n_panels = OUTER // PANEL

    def step(o, carry):
        blk = [
            [work[p * PANEL : (p + 1) * PANEL, t * 128 : (t + 1) * 128] for t in range(tiles - 1)]
            + [jnp.where(lane == sub + p * PANEL, 1.0, 0.0).astype(F32)]
            for p in range(n_panels)
        ]
        for p in range(n_panels):
            off = p * PANEL
            inv = factor_panel(blk[p][0], off)
            rows_of = [
                [jnp.broadcast_to(blk[p][t][j : j + 1, :], (PANEL, 128)) for t in range(tiles)]
                for j in range(PANEL)
            ]
            new = [None] * tiles
            for j in range(PANEL):
                col = inv[PANEL - 1, j]
                for i in range(PANEL - 2, j - 1, -1):
                    col = jnp.where(sub == i, inv[i, j], col)
                if j:
                    col = jnp.where(sub < j, 0.0, col)
                for t in range(tiles):
                    term = col * rows_of[j][t]
                    new[t] = term if new[t] is None else new[t] + term
            blk[p] = new
            if p + 1 < n_panels:
                u_rows = [
                    [jnp.broadcast_to(new[t][j : j + 1, :], (PANEL, 128)) for t in range(tiles)]
                    for j in range(PANEL)
                ]
                for b in range(p + 1, n_panels):
                    lanes = [
                        jnp.broadcast_to(blk[b][0][:, off + m : off + m + 1], (PANEL, 128))
                        for m in range(PANEL)
                    ]
                    upd = list(blk[b])
                    for k in range(PANEL):
                        v = lanes[0] * inv[k, 0]
                        for m in range(1, k + 1):
                            v = v + lanes[m] * inv[k, m]
                        for t in range(tiles):
                            upd[t] = upd[t] - v * u_rows[k][t]
                    blk[b] = upd
        u = jnp.concatenate([jnp.concatenate(row, axis=1) for row in blk], axis=0)
        u = pltpu.roll(u, tiles * 128 - OUTER, 1)[:, :n]
        at = lax.broadcasted_iota(jnp.int32, (OUTER, n), 1)
        left = jnp.where(at < n - OUTER * (o + 1), u, 0.0)
        la, lb, lc = three_parts(left)
        ua, ub, uc = three_parts(u)
        lhs = jnp.concatenate([la, la, lb, la, lc, lb], axis=0)
        rhs = jnp.concatenate([ua, ub, ua, uc, ua, ub], axis=0)
        upd = mm(lhs.T, rhs)
        rest = work[OUTER:, :]
        lanes_at = lax.broadcasted_iota(jnp.int32, rest.shape, 1)
        rest = pltpu.roll(jnp.where(lanes_at < OUTER, 0.0, rest), n - OUTER, 1)
        work[: n - OUTER, :] = rest - upd[: n - OUTER, :]
        work[n - OUTER :, :] = u
        return carry

    lax.fori_loop(0, n // OUTER, step, 0)
    out[...] = work[...] * across


def inverse_factor(*parts):
    n = 2 * parts[0].shape[1]
    return pl.pallas_call(
        functools.partial(cholesky_kernel, len(parts)),
        in_specs=[VMEM] * len(parts),
        out_specs=VMEM,
        scratch_shapes=[pltpu.VMEM((n, n), F32)],
        out_shape=jax.ShapeDtypeStruct((n, n), F32),
        compiler_params=params(),
        name="inverse_factor",
        cost_estimate=cost(2),
    )(*parts)


def mm_three(a, b):
    a_hi, a_lo = halves(a)
    b_hi, b_lo = halves(b)
    return mm(a_hi, b_hi) + (mm(a_hi, b_lo) + mm(a_lo, b_hi))


def back_kernel(x, wa, wb, bt_out, y_out, s_out):
    w = wa[...].astype(F32) + wb[...].astype(F32)
    bt = mm_three(x[...], w)
    bt_out[...] = bt
    s = jnp.sum(bt * bt, axis=1, keepdims=True)
    s_out[...] = jnp.broadcast_to(s, (s.shape[0], 128)).T[:8, :]
    y_out[...] = ((1.0 - momentum_keep) * mm(x[...].T.astype(BF16), bt.astype(BF16))).astype(BF16)


def back_full(x, wa, wb):
    rank, cols = wa.shape
    return pl.pallas_call(
        back_kernel,
        in_specs=[VMEM] * 3,
        out_specs=[VMEM] * 3,
        out_shape=[
            jax.ShapeDtypeStruct((rank, cols), F32),
            jax.ShapeDtypeStruct((rank, cols), BF16),
            jax.ShapeDtypeStruct((8, rank), F32),
        ],
        compiler_params=params(),
        name="back_full",
        cost_estimate=cost(),
    )(x, wa, wb)


def row_blocks(ranks, n_resp, n_head, chunk):
    return [
        pl.multiple_of(((ranks[0] ^ j) * n_head + (ranks[2] ^ k)) * chunk, chunk)
        for j in range(n_resp)
        for k in range(n_head)
    ]


def momentum_kernel(n_resp, n_head, begin, end, n_totals, ranks, pcat, y, *refs):
    totals, (out, token, held, sems) = refs[:n_totals], refs[-4:]
    token[...] = jnp.zeros_like(token)
    seg = totals[0].shape[0]
    chunk = pcat.shape[0] // (n_resp * n_head)
    blocks = row_blocks(ranks, n_resp, n_head, chunk)
    copies = []
    for i in range(begin, end):
        rows = slice(i * chunk, (i + 1) * chunk)
        kept = slice((i - begin) * chunk, (i - begin + 1) * chunk)
        off = i * chunk % seg
        total = totals[(i - begin) * chunk // seg][off : off + chunk, :]
        held[kept, :] = total - mm(pcat[rows, :], y[...])
        copies.append(
            pltpu.make_async_copy(
                held.at[kept, :], out.at[pl.ds(blocks[i], chunk), :], sems.at[i - begin]
            )
        )
        copies[-1].start()
    for c in copies:
        c.wait()


def new_momentum(ranks, pcat, totals, y, n_resp, n_head, half, earlier, after):
    rows, rank = pcat.shape
    cols = totals[0].shape[1]
    n_chunks = n_resp * n_head // 2
    part = len(totals) // 2
    totals = totals[half * part : (half + 1) * part]
    aliases = {3 + part: 0} if earlier else {}
    return pl.pallas_call(
        functools.partial(
            momentum_kernel, n_resp, n_head, half * n_chunks, (half + 1) * n_chunks, part
        ),
        in_specs=[SMEM] + [VMEM] * (2 + part) + [HBM] * len(earlier) + [ANY] * len(after),
        out_specs=[HBM, VMEM],
        scratch_shapes=[pltpu.VMEM((rows // 2, cols), F32), pltpu.SemaphoreType.DMA((n_chunks,))],
        out_shape=[
            jax.ShapeDtypeStruct((rows, cols), F32), jax.ShapeDtypeStruct((8, 128), F32)
        ],
        input_output_aliases=aliases,
        compiler_params=params(10),
        name="new_momentum",
        cost_estimate=cost(5),
    )(ranks, pcat, y, *totals, *earlier, *after)


def update_kernel(gain, n_resp, n_head, n_sums, ranks, pcat, x, bt, *refs):
    sums, (upd, basis_out, held, held_basis, sems, basis_sem) = refs[:n_sums], refs[n_sums:]
    total = sums[0][...]
    for s in sums[1:]:
        total = total + s[...]
    scale = lax.rsqrt(total + norm_eps).T[:, :1]
    scaled = bt[...] * scale
    held_basis[...] = scaled.T
    basis_copy = pltpu.make_async_copy(held_basis, basis_out, basis_sem)
    basis_copy.start()
    z_hi, z_lo = halves(gain * mm_three(x[...].T, scaled))
    chunk = pcat.shape[0] // (n_resp * n_head)
    copies = []
    for i, at in enumerate(row_blocks(ranks, n_resp, n_head, chunk)):
        rows = slice(i * chunk, (i + 1) * chunk)
        p = pcat[rows, :]
        held[rows, :] = (mm(p, z_hi) + mm(p, z_lo)).astype(BF16)
        copies.append(
            pltpu.make_async_copy(held.at[rows, :], upd.at[pl.ds(at, chunk), :], sems.at[i])
        )
        copies[-1].start()
    for c in copies:
        c.wait()
    basis_copy.wait()


def final_update(ranks, pcat, x, bt, sums, gain, n_resp, n_head):
    rows, rank = pcat.shape
    cols = bt.shape[1]
    return pl.pallas_call(
        functools.partial(update_kernel, gain, n_resp, n_head, len(sums)),
        in_specs=[SMEM] + [VMEM] * (3 + len(sums)),
        out_specs=[HBM, HBM],
        scratch_shapes=[
            pltpu.VMEM((rows, cols), BF16),
            pltpu.VMEM((cols, rank), F32),
            pltpu.SemaphoreType.DMA((n_resp * n_head,)),
            pltpu.SemaphoreType.DMA,
        ],
        out_shape=[
            jax.ShapeDtypeStruct((rows, cols), BF16),
            jax.ShapeDtypeStruct((cols, rank), F32),
        ],
        compiler_params=params(10),
        name="final_update",
        cost_estimate=cost(),
    )(ranks, pcat, x, bt, *sums)


def group_of(counts, response):
    group = jnp.int32(0)
    end = jnp.int32(0)
    for g in range(counts.shape[0]):
        end = end + counts[g]
        group = group + (end <= response).astype(jnp.int32)
    return group


def pack_kernel(*refs):
    keys, values, out = refs[0], refs[1], refs[-1]
    out[0] = keys[...]
    out[1] = values[...]


def pack_prompts(keys, values, after):
    return pl.pallas_call(
        pack_kernel,
        in_specs=[VMEM] * 2 + [ANY] * len(after),
        out_specs=VMEM,
        out_shape=jax.ShapeDtypeStruct((2,) + keys.shape, BF16),
        compiler_params=params(),
        name="pack_prompts",
        cost_estimate=cost(),
    )(keys, values, *after)


def select_kernel(n_resp, n_fsdp, ranks, counts, slots, *refs):
    stored, outs = refs[:n_resp], refs[-n_fsdp:]
    held = stored[0].shape[1]
    for k in range(n_fsdp):
        slot = slots[group_of(counts, ranks[0] * n_fsdp + (ranks[1] ^ k))]
        owner, local = slot // held, slot % held
        for j in range(n_resp):

            @pl.when(owner == (ranks[0] ^ j))
            def _():
                outs[k][0] = stored[j][0, local]
                outs[k][1] = stored[j][1, local]


def select_prompts(ranks, counts, slots, stored, n_fsdp, after):
    _, _, piece, width = stored[0].shape
    return pl.pallas_call(
        functools.partial(select_kernel, len(stored), n_fsdp),
        in_specs=[SMEM] * 3 + [VMEM] * len(stored) + [ANY] * len(after),
        out_specs=[VMEM] * n_fsdp,
        out_shape=[jax.ShapeDtypeStruct((2, piece, width), BF16)] * n_fsdp,
        compiler_params=params(),
        name="select_prompts",
        cost_estimate=cost(),
    )(ranks, counts, slots, *stored, *after)


def attention_kernel(
    n_fsdp, heads, last, ranks, counts, prompt_blocks, resp_blocks, q, sk, sv, go, *refs
):
    pieces, refs = refs[:n_fsdp], refs[n_fsdp:]
    dq_held, keys, values, dk, dv, sems = refs[-6:]
    n_out = 2 + n_fsdp if last else 3
    outs = refs[-6 - n_out : -6]
    dq, copies = outs[0], []
    piece = pieces[0].shape[1]
    cap = piece * n_fsdp
    length = q.shape[0]
    scale = HD ** (-0.5)
    for k in range(n_fsdp):
        rows = pl.ds(pl.multiple_of((ranks[1] ^ k) * piece, piece), piece)
        keys[rows, :] = pieces[k][0]
        values[rows, :] = pieces[k][1]
    keys[cap:, :] = sk[...]
    values[cap:, :] = sv[...]
    prompt_len = prompt_blocks[group_of(counts, ranks[0] * n_fsdp + ranks[1])] * 128
    resp_len = resp_blocks[0] * 128
    width = keys.shape[0]
    place = lax.broadcasted_iota(jnp.int32, (width, length), 0)
    pos = lax.broadcasted_iota(jnp.int32, (width, length), 1)
    inner = place - cap
    seen = ((place < cap) & (place < prompt_len)) | (
        (place >= cap) & (inner <= pos) & (inner < resp_len)
    )
    bias = jnp.where(seen, 0.0, -jnp.inf).astype(F32)
    live = lax.broadcasted_iota(jnp.int32, (length, HD), 0) < resp_len
    nt = (((1,), (1,)), ((), ()))
    kall = keys[...]
    vall = values[...]
    kt = kall.T
    if last:
        dk[...] = refs[0][...]
        dv[...] = refs[1][...]
    else:
        dk[...] = jnp.zeros_like(dk)
        dv[...] = jnp.zeros_like(dv)
    for i, h in enumerate(heads):
        cols = pl.ds(h * HD, HD)
        qh = q[:, cols]
        gh = jnp.where(live, go[:, cols], jnp.zeros((), BF16))
        logits = lax.dot_general(kall, qh, nt, preferred_element_type=F32) * scale + bias
        peak = jnp.max(logits, axis=0, keepdims=True)
        e = jnp.exp(logits - peak)
        w = (e * (1.0 / jnp.sum(e, axis=0, keepdims=True))).astype(BF16)
        dp = lax.dot_general(vall, gh, nt, preferred_element_type=F32)
        wf = w.astype(F32)
        diag = jnp.sum(wf * dp, axis=0, keepdims=True)
        ds = (wf * (dp - diag)).astype(BF16)
        dk[...] += mm(ds, qh)
        dv[...] += mm(w, gh)
        dq_held[i] = (mm(kt, ds) * scale).T.astype(BF16)
        copies.append(pltpu.make_async_copy(dq_held.at[i], dq.at[:, cols], sems.at[i]))
        copies[-1].start()
    if last:
        own, sends = outs[1], outs[2:]
        own[0] = (dk[cap:, :] * scale).astype(BF16)
        own[1] = dv[cap:, :].astype(BF16)
        for k in range(n_fsdp):
            rows = pl.ds(pl.multiple_of((ranks[1] ^ k) * piece, piece), piece)
            sends[k][0] = (dk[rows, :] * scale).astype(sends[k].dtype)
            sends[k][1] = dv[rows, :].astype(sends[k].dtype)
    else:
        outs[1][...] = dk[...]
        outs[2][...] = dv[...]
    for c in copies:
        c.wait()


def attention(heads, earlier, ranks, counts, prompt_blocks, resp_blocks, q, sk, sv, go, pieces, after):
    n_fsdp = len(pieces)
    piece = pieces[0].shape[1]
    length, width = q.shape
    cap = piece * n_fsdp
    total = cap + length
    last = earlier is not None
    dq_shape = jax.ShapeDtypeStruct((length, width), BF16)
    aliases = {8 + n_fsdp + 2: 0} if last else {}
    if last:
        extra, specs = (earlier[1], earlier[2], earlier[0]), [VMEM, VMEM, HBM]
        out_shape = [dq_shape, jax.ShapeDtypeStruct((2, length, HD), BF16)] + [
            jax.ShapeDtypeStruct((2, piece, HD), BF16 if k else F32) for k in range(n_fsdp)
        ]
    else:
        extra, specs = (), []
        out_shape = [dq_shape] + [jax.ShapeDtypeStruct((total, HD), F32)] * 2
    return pl.pallas_call(
        functools.partial(attention_kernel, n_fsdp, heads, last),
        in_specs=[SMEM] * 4 + [VMEM] * (4 + n_fsdp) + specs + [ANY] * len(after),
        out_specs=[HBM] + [VMEM] * (len(out_shape) - 1),
        scratch_shapes=[pltpu.VMEM((len(heads), length, HD), BF16)]
        + [pltpu.VMEM((total, HD), BF16)] * 2
        + [pltpu.VMEM((total, HD), F32)] * 2
        + [pltpu.SemaphoreType.DMA((len(heads),))],
        out_shape=out_shape,
        input_output_aliases=aliases,
        compiler_params=params(12),
        name="attention",
        cost_estimate=cost(),
    )(ranks, counts, prompt_blocks, resp_blocks, q, sk, sv, go, *pieces, *extra, *after)


def by_slot_kernel(n_resp, n_fsdp, ranks, counts, slots, *refs):
    parts, outs = refs[:n_fsdp], refs[-n_resp:]
    held = outs[0].shape[1]
    slot_of = [
        slots[group_of(counts, ranks[0] * n_fsdp + (ranks[1] ^ k))] for k in range(n_fsdp)
    ]
    for j in range(n_resp):
        for local in range(held):
            slot = (ranks[0] ^ j) * held + local
            acc = jnp.zeros(parts[0].shape, F32)
            for k in range(n_fsdp):
                acc = acc + jnp.where(slot_of[k] == slot, parts[k][...].astype(F32), 0.0)
            outs[j][:, local] = acc.astype(outs[j].dtype)


def sum_by_slot(ranks, counts, slots, parts, n_resp, after):
    held = counts.shape[0] // n_resp
    _, piece, width = parts[0].shape
    return pl.pallas_call(
        functools.partial(by_slot_kernel, n_resp, len(parts)),
        in_specs=[SMEM] * 3 + [VMEM] * len(parts) + [ANY] * len(after),
        out_specs=[VMEM] * n_resp,
        out_shape=[
            jax.ShapeDtypeStruct((2, held, piece, width), BF16 if j else F32)
            for j in range(n_resp)
        ],
        compiler_params=params(),
        name="sum_by_slot",
        cost_estimate=cost(),
    )(ranks, counts, slots, *parts, *after)


def on_device(
    queries,
    self_keys,
    self_values,
    d_out,
    prompt_keys,
    prompt_values,
    counts,
    owner_slot,
    prompt_blocks,
    resp_blocks,
    grad_q,
    momentum,
    basis,
):
    n_resp, n_fsdp, n_head = (lax.axis_size(a) for a in ("resp", "fsdp", "head"))
    ranks = jnp.stack([lax.axis_index(a) for a in ("resp", "fsdp", "head")]).astype(jnp.int32)
    gain = math.sqrt(
        momentum.shape[0] * n_fsdp * momentum.shape[1] * n_resp * n_head / basis.shape[1]
    )

    in_hbm = [pltpu.with_memory_space_constraint(a, pltpu.HBM) for a in (momentum, grad_q, basis)]
    half = n_head // 2
    groups = [(half, half), (0, half)] if half else [(0, n_head)]

    mom_hbm, grad_hbm, basis_hbm = in_hbm
    order = [(j, *group) for group in groups for j in range(1, n_resp)]
    order += [(0, *group) for group in groups]
    nexts = dict(zip(order, order[1:] + [None]))
    totals, arrived, split, ins, after = {}, {}, {}, (basis_hbm,), ()
    for part in order:
        j, first, number = part
        value, totals[part[:2]], ins = project(
            ranks, mom_hbm, grad_hbm, ins, part, nexts[part], n_resp, n_head, BF16 if j else F32,
            after,
        )
        if j:
            arrived.setdefault(first, []).append(swap(value, "resp", j))
            if part[1:] == groups[-1] and j == n_resp - 1:
                packed = pack_prompts(prompt_keys, prompt_values, (value,))
                stored = [packed] + [swap(packed, "resp", k) for k in range(1, n_resp)]
                after = (packed,)
        else:
            outs = split_sum(value, arrived[first], first, number)
            after = (outs[0],)
            for i in range(number):
                split[first + i] = outs[i]
    totals = [totals[at] for at in sorted(totals)]
    chosen = select_prompts(ranks, counts, owner_slot, stored, n_fsdp, (outs[0],))
    far_first = [k for first, number in groups for k in range(first, first + number) if k]
    summands = {k: swap(split[k], "head", k) for k in far_first}
    pieces = [chosen[0]] + [swap(chosen[k], "fsdp", k) for k in range(1, n_fsdp)]
    later = groups[-1][1] if len(groups) > 1 else 1
    far = sum_parts(
        [split[0]] + [summands[k] for k in range(later, n_head)], F32, (), 10
    )
    piece0 = sum_parts(
        [far] + [summands[k] for k in range(1, later)], BF16, (pieces[-1],)
    )

    along = {0: piece0}
    for k in far_first:
        along[k] = swap(piece0, "head", k)
    n_q = queries.shape[1] // HD
    heads = [list(range(n_q // 2)), list(range(n_q // 2, n_q))]
    held = (
        ranks, counts, prompt_blocks, resp_blocks, queries, self_keys, self_values, d_out, pieces
    )
    earlier = attention(heads[0], None, *held, (along[1 % n_head],))
    last = n_head - 1
    passed = dict(along)
    passed[last] = sum_parts([along[last]], BF16, (earlier[1],))
    chunks = [along[k] for k in range(n_head)]
    for j in range(1, n_resp):
        chunks += [swap(passed[k], "resp", j) for k in range(n_head)]
    dq, resp_grad, *parts = attention(heads[1], earlier, *held, (passed[last],))
    pcat, pcat_t, gram = gather_gram(chunks, (parts[0],))

    bits = [1 << b for b in range(n_fsdp.bit_length() - 1)]
    w = back_part(pcat_t, totals, (gram,))
    for bit in bits[:-1]:
        gram = sum_parts([gram, swap(gram, "fsdp", bit)], F32, (), 3)
        w = sum_parts([w, swap(w, "fsdp", bit)], BF16, (gram,), 5)
    gram_parts = (gram, swap(gram, "fsdp", bits[-1]))
    w_other = swap(w, "fsdp", bits[-1])
    returned = [parts[0]] + [swap(parts[k], "fsdp", k) for k in range(1, n_fsdp)]
    x = inverse_factor(*gram_parts)
    bt, y, squares = back_full(x, w, w_other)
    from_head = [swap(squares, "head", k) for k in range(1, n_head)]
    momentum_out, token = new_momentum(
        ranks, pcat, totals, y, n_resp, n_head, 0, (), (squares,)
    )
    slots = sum_by_slot(ranks, counts, owner_slot, returned, n_resp, (token,))
    squares = sum_parts([squares] + from_head, F32, (token,))
    sums = [squares] + [swap(squares, "resp", j) for j in range(1, n_resp)]
    momentum_out, token = new_momentum(
        ranks, pcat, totals, y, n_resp, n_head, 1, (momentum_out,), (squares,)
    )
    prompt_grad = sum_parts(
        [slots[0]] + [swap(slots[j], "resp", j) for j in range(1, n_resp)], F32, (token,)
    )
    update, basis_out = final_update(ranks, pcat, x, bt, sums, gain, n_resp, n_head)
    return (dq, resp_grad, prompt_grad, update, momentum_out, basis_out)


def solution(mesh):
    placed = (
        P(("resp", "fsdp"), "head"),
        P(("resp", "fsdp"), "head"),
        P(("resp", "fsdp"), "head"),
        P(("resp", "fsdp"), "head"),
        P("resp", "fsdp", "head"),
        P("resp", "fsdp", "head"),
        P(),
        P(),
        P(),
        P(("resp", "fsdp")),
        P("fsdp", ("resp", "head")),
        P("fsdp", ("resp", "head")),
        P(("resp", "head"), None),
    )
    return jax.shard_map(
        on_device,
        mesh=mesh,
        in_specs=placed,
        out_specs=(
            P(("resp", "fsdp"), "head"),
            P(None, ("resp", "fsdp"), "head"),
            P(None, "resp", "fsdp", "head"),
            P("fsdp", ("resp", "head")),
            P("fsdp", ("resp", "head")),
            P(("resp", "head"), None),
        ),
        check_vma=False,
    )
```

```python
import functools
import math

import jax
import jax.numpy as jnp
from jax import lax
from jax.experimental import pallas as pl
from jax.experimental.pallas import tpu as pltpu
from jax.sharding import PartitionSpec as P

HD = 128
PANEL = 8
OUTER = 32
MIB = 1 << 20

momentum_keep = 0.95
norm_eps = 1e-06

F32 = jnp.float32
BF16 = jnp.bfloat16
HIGHEST = lax.Precision.HIGHEST

SMEM = pl.BlockSpec(memory_space=pltpu.SMEM)
VMEM = pl.BlockSpec(memory_space=pltpu.VMEM)
ANY = pl.BlockSpec(memory_space=pl.ANY)
HBM = pl.BlockSpec(memory_space=pltpu.HBM)


def swap(value, axes, k):
    axes = (axes,) if isinstance(axes, str) else axes
    n = math.prod(lax.axis_size(a) for a in axes)
    return lax.ppermute(value, axes, [(i, i ^ k) for i in range(n)])


def params(mib=6):
    return pltpu.CompilerParams(vmem_limit_bytes=mib * MIB)


def cost(weight=0):
    return pl.CostEstimate(flops=1 + weight * 10**9, bytes_accessed=1, transcendentals=0)


def halves(x):
    hi = x.astype(BF16)
    return hi, (x - hi.astype(F32)).astype(BF16)


def mm(a, b):
    return jnp.dot(a, b, preferred_element_type=F32)


def mm_full(a, b):
    return jnp.dot(a, b, precision=HIGHEST, preferred_element_type=F32)


def row_copies(ranks, n_head, part, mom, grad, mom_to, grad_to, sems):
    j, first, number = part
    chunk = mom_to.shape[0] // number
    pieces = 2 if chunk % 32 == 0 else 1
    size = chunk // pieces
    copies = []
    for i in range(number):
        at = ((ranks[0] ^ j) * n_head + (ranks[2] ^ (first + i))) * chunk
        copies.append([])
        for p in range(pieces):
            src = pl.ds(pl.multiple_of(at + p * size, size), size)
            dst = pl.ds(i * chunk + p * size, size)
            n = i * pieces + p
            copies[i].append(pltpu.make_async_copy(mom.at[src, :], mom_to.at[dst, :], sems.at[0, n]))
            copies[i].append(
                pltpu.make_async_copy(grad.at[src, :], grad_to.at[dst, :], sems.at[1, n])
            )
    return copies


def start_all(copies):
    for row in copies:
        for c in row:
            c.start()


def project_kernel(n_head, part, following, is_first, n_in, ranks, mom, grad, *refs):
    ins, refs = refs[:n_in], list(refs)
    number = part[2]
    sems = refs.pop()
    ahead = []
    if is_first:
        right_sem, right, grad_in = refs.pop(), refs.pop(), refs.pop()
    if following:
        next_grad, next_mom = refs.pop(), refs.pop()
        ahead = row_copies(ranks, n_head, following, mom, grad, next_mom, next_grad, sems.at[1])
    if is_first:
        b_lo, b_hi = refs.pop(), refs.pop()
        total, out = refs.pop(), refs.pop()
        mom_in = total
        copies = row_copies(ranks, n_head, part, mom, grad, mom_in, grad_in, sems.at[0])
        fetch = pltpu.make_async_copy(ins[0], right, right_sem)
        start_all(copies[:1])
        fetch.start()
        start_all(copies[1:])
        fetch.wait()
        hi, lo = halves(right[...])
        b_hi[...] = hi
        b_lo[...] = lo
    else:
        total, out = refs.pop(), refs.pop()
        b_hi, b_lo, mom_in, grad_in = ins
        copies = [[]] * number
        start_all(ahead)
    chunk = total.shape[0] // number
    for i in range(number):
        for c in copies[i]:
            c.wait()
        if is_first and i == 0:
            start_all(ahead)
        rows = slice(i * chunk, (i + 1) * chunk)
        t = mom_in[rows, :] + grad_in[rows, :].astype(F32)
        total[rows, :] = t
        t_hi, t_lo = halves(t)
        acc = mm(t_hi, b_hi[...]) + (mm(t_hi, b_lo[...]) + mm(t_lo, b_hi[...]))
        out[rows, :] = acc.astype(out.dtype)
    for row in ahead:
        for c in row:
            c.wait()


def project(
    ranks, momentum, grad_q, ins, part, following, n_resp, n_head, dtype, after, weight=0
):
    is_first = len(ins) == 1
    rows, cols = momentum.shape
    chunk = rows // (n_resp * n_head)
    size = part[2] * chunk
    if is_first:
        right = ins[0]
        rank = right.shape[1]
        specs = [HBM]
    else:
        rank = ins[0].shape[1]
        specs = [VMEM] * 4
    out_shape = [jax.ShapeDtypeStruct((size, rank), dtype), jax.ShapeDtypeStruct((size, cols), F32)]
    if is_first:
        out_shape += [jax.ShapeDtypeStruct((cols, rank), BF16)] * 2
    if following:
        ahead = following[2] * chunk
        out_shape += [
            jax.ShapeDtypeStruct((ahead, cols), F32), jax.ShapeDtypeStruct((ahead, cols), BF16)
        ]
    scratch = [pltpu.SemaphoreType.DMA((2, 2, 2 * n_head))]
    if is_first:
        scratch = [
            pltpu.VMEM((size, cols), BF16), pltpu.VMEM((cols, rank), F32), pltpu.SemaphoreType.DMA
        ] + scratch
    outs = pl.pallas_call(
        functools.partial(project_kernel, n_head, part, following, is_first, len(ins)),
        in_specs=[SMEM, HBM, HBM] + specs + [ANY] * len(after),
        out_specs=[VMEM] * len(out_shape),
        scratch_shapes=scratch,
        out_shape=out_shape,
        compiler_params=params(14),
        name="project",
        cost_estimate=cost(weight),
    )(ranks, momentum, grad_q, *ins, *after)
    right = tuple(outs[2:4]) if is_first else tuple(ins[:2])
    return outs[0], outs[1], right + tuple(outs[-2:] if following else ())


def split_kernel(n_recv, number, own, *refs):
    recvs, outs = refs[:n_recv], refs[-number:]
    chunk = outs[0].shape[0]
    for i in range(number):
        rows = slice(i * chunk, (i + 1) * chunk)
        acc = own[rows, :]
        for r in recvs:
            acc = acc + r[rows, :].astype(F32)
        outs[i][...] = acc.astype(outs[i].dtype)


def split_sum(own, recvs, first, number):
    rows, rank = own.shape
    chunk = rows // number
    return pl.pallas_call(
        functools.partial(split_kernel, len(recvs), number),
        in_specs=[VMEM] * (1 + len(recvs)),
        out_specs=[VMEM] * number,
        out_shape=[
            jax.ShapeDtypeStruct((chunk, rank), BF16 if first + i else F32)
            for i in range(number)
        ],
        compiler_params=params(),
        name="split_sum",
        cost_estimate=cost(),
    )(own, *recvs)


def sum_kernel(n_parts, *refs):
    acc = refs[0][...].astype(F32)
    for r in refs[1:n_parts]:
        acc = acc + r[...].astype(F32)
    refs[-1][...] = acc.astype(refs[-1].dtype)


def sum_parts(parts, dtype, after=(), weight=0):
    shape = parts[0].shape
    return pl.pallas_call(
        functools.partial(sum_kernel, len(parts)),
        in_specs=[VMEM] * len(parts) + [ANY] * len(after),
        out_specs=VMEM,
        out_shape=jax.ShapeDtypeStruct(shape, dtype),
        compiler_params=params(),
        name="sum_parts",
        cost_estimate=cost(weight),
    )(*parts, *after)


def relay_kernel(n_parts, *refs):
    out = refs[-1]
    size = out.shape[0] // n_parts
    for i in range(n_parts):
        out[i * size : (i + 1) * size, :] = refs[i][...]


def relay(parts, after):
    rows, rank = parts[0].shape
    return pl.pallas_call(
        functools.partial(relay_kernel, len(parts)),
        in_specs=[VMEM] * len(parts) + [ANY] * len(after),
        out_specs=VMEM,
        out_shape=jax.ShapeDtypeStruct((len(parts) * rows, rank), parts[0].dtype),
        compiler_params=params(),
        name="relay",
        cost_estimate=cost(),
    )(*parts, *after)


def gram_kernel(n_chunks, *refs):
    chunks, (pcat, pcat_t, gram) = refs[:n_chunks], refs[-3:]
    at = 0
    for c in chunks:
        pcat[at : at + c.shape[0], :] = c[...]
        at += c.shape[0]
    p = pcat[...]
    pt = p.T
    pcat_t[...] = pt
    half = p.shape[1] // 2
    gram[:half, :] = mm(pt[:half, :], p[:, :half])
    low = mm(pt[half:, :], p)
    gram[half : 2 * half, :] = low[:, :half]
    gram[2 * half :, :] = low[:, half:]


def gather_gram(chunks, after):
    rank = chunks[0].shape[1]
    rows = sum(c.shape[0] for c in chunks)
    return pl.pallas_call(
        functools.partial(gram_kernel, len(chunks)),
        in_specs=[VMEM] * len(chunks) + [ANY] * len(after),
        out_specs=[VMEM] * 3,
        out_shape=[
            jax.ShapeDtypeStruct((rows, rank), BF16),
            jax.ShapeDtypeStruct((rank, rows), BF16),
            jax.ShapeDtypeStruct((3 * rank // 2, rank // 2), F32),
        ],
        compiler_params=params(8),
        name="gather_gram",
        cost_estimate=cost(),
    )(*chunks, *after)


def back_part_kernel(n_totals, pcat_t, *refs):
    totals, out = refs[:n_totals], refs[-1]
    seg = totals[0].shape[0]
    step = min(seg, 512)
    acc = None
    for j, total in enumerate(totals):
        for i in range(0, seg, step):
            t_hi, t_lo = halves(total[i : i + step, :])
            pt = pcat_t[:, j * seg + i : j * seg + i + step]
            part = mm(pt, t_hi) + mm(pt, t_lo)
            acc = part if acc is None else acc + part
    out[...] = acc.astype(BF16)


def back_part(pcat_t, totals, after):
    rank = pcat_t.shape[0]
    seg, cols = totals[0].shape
    rows = seg * len(totals)
    return pl.pallas_call(
        functools.partial(back_part_kernel, len(totals)),
        in_specs=[VMEM] * (1 + len(totals)) + [ANY] * len(after),
        out_specs=VMEM,
        out_shape=jax.ShapeDtypeStruct((rank, cols), BF16),
        compiler_params=params(14),
        name="back_part",
        cost_estimate=cost(5),
    )(pcat_t, *totals, *after)


def factor_panel(panel, off):
    shape = (PANEL, 128)
    d = {}
    for j in range(PANEL):
        col = jnp.broadcast_to(panel[:, off + j : off + j + 1], shape)
        for i in range(j, PANEL):
            d[i, j] = jnp.broadcast_to(col[i : i + 1, :], shape)
    low, inv = {}, {}
    for j in range(0, PANEL, 2):
        a, b, c = d[j, j], d[j + 1, j], d[j + 1, j + 1]
        first = lax.rsqrt(a)
        second = lax.rsqrt(a * c - b * b) * (a * first)
        inv[j, j], inv[j + 1, j + 1] = first, second
        low[j + 1, j] = b * first
        for i in range(j + 2, PANEL):
            low[i, j] = d[i, j] * first
            low[i, j + 1] = (d[i, j + 1] - low[i, j] * low[j + 1, j]) * second
        for k in range(j + 2, PANEL):
            for i in range(k, PANEL):
                d[i, k] = d[i, k] - (low[i, j] * low[k, j] + low[i, j + 1] * low[k, j + 1])
    for j in range(PANEL):
        for i in range(j + 1, PANEL):
            acc = low[i, j] * inv[j, j]
            for k in range(j + 1, i):
                acc = acc + low[i, k] * inv[k, j]
            inv[i, j] = -(acc * inv[i, i])
    return inv


def three_parts(x):
    a = x.astype(BF16)
    rest = x - a.astype(F32)
    b = rest.astype(BF16)
    return a, b, (rest - b.astype(F32)).astype(BF16)


def cholesky_kernel(n_parts, *refs):
    parts, out, work = refs[:n_parts], refs[n_parts], refs[n_parts + 1]
    n = out.shape[0]
    half = n // 2
    tiles = n // 128 + 1
    total = parts[0][...]
    for part in parts[1:]:
        total = total + part[...]
    low = total[half : 2 * half, :]
    work[:half, :half] = total[:half, :]
    work[half:, :half] = low
    work[:half, half:] = low.T
    work[half:, half:] = total[2 * half :, :]
    eye = lax.broadcasted_iota(jnp.int32, (n, n), 0) == lax.broadcasted_iota(jnp.int32, (n, n), 1)
    whole = work[...]
    diag = jnp.where(eye, whole, 0.0)
    across = lax.rsqrt(jnp.sum(diag, axis=0, keepdims=True))
    work[...] = whole * lax.rsqrt(jnp.sum(diag, axis=1, keepdims=True)) * across
    sub = lax.broadcasted_iota(jnp.int32, (PANEL, 128), 0)
    lane = lax.broadcasted_iota(jnp.int32, (PANEL, 128), 1)
    n_panels = OUTER // PANEL

    def step(o, carry):
        blk = [
            [work[p * PANEL : (p + 1) * PANEL, t * 128 : (t + 1) * 128] for t in range(tiles - 1)]
            + [jnp.where(lane == sub + p * PANEL, 1.0, 0.0).astype(F32)]
            for p in range(n_panels)
        ]
        for p in range(n_panels):
            off = p * PANEL
            inv = factor_panel(blk[p][0], off)
            rows_of = [
                [jnp.broadcast_to(blk[p][t][j : j + 1, :], (PANEL, 128)) for t in range(tiles)]
                for j in range(PANEL)
            ]
            new = [None] * tiles
            for j in range(PANEL):
                col = inv[PANEL - 1, j]
                for i in range(PANEL - 2, j - 1, -1):
                    col = jnp.where(sub == i, inv[i, j], col)
                if j:
                    col = jnp.where(sub < j, 0.0, col)
                for t in range(tiles):
                    term = col * rows_of[j][t]
                    new[t] = term if new[t] is None else new[t] + term
            blk[p] = new
            if p + 1 < n_panels:
                u_rows = [
                    [jnp.broadcast_to(new[t][j : j + 1, :], (PANEL, 128)) for t in range(tiles)]
                    for j in range(PANEL)
                ]
                for b in range(p + 1, n_panels):
                    lanes = [
                        jnp.broadcast_to(blk[b][0][:, off + m : off + m + 1], (PANEL, 128))
                        for m in range(PANEL)
                    ]
                    upd = list(blk[b])
                    for k in range(PANEL):
                        v = lanes[0] * inv[k, 0]
                        for m in range(1, k + 1):
                            v = v + lanes[m] * inv[k, m]
                        for t in range(tiles):
                            upd[t] = upd[t] - v * u_rows[k][t]
                    blk[b] = upd
        u = jnp.concatenate([jnp.concatenate(row, axis=1) for row in blk], axis=0)
        u = pltpu.roll(u, tiles * 128 - OUTER, 1)[:, :n]
        at = lax.broadcasted_iota(jnp.int32, (OUTER, n), 1)
        left = jnp.where(at < n - OUTER * (o + 1), u, 0.0)
        la, lb, lc = three_parts(left)
        ua, ub, uc = three_parts(u)
        lhs = jnp.concatenate([la, la, lb, la, lc, lb], axis=0)
        rhs = jnp.concatenate([ua, ub, ua, uc, ua, ub], axis=0)
        upd = mm(lhs.T, rhs)
        rest = work[OUTER:, :]
        lanes_at = lax.broadcasted_iota(jnp.int32, rest.shape, 1)
        rest = pltpu.roll(jnp.where(lanes_at < OUTER, 0.0, rest), n - OUTER, 1)
        work[: n - OUTER, :] = rest - upd[: n - OUTER, :]
        work[n - OUTER :, :] = u
        return carry

    lax.fori_loop(0, n // OUTER, step, 0)
    out[...] = work[...] * across


def inverse_factor(*parts):
    n = 2 * parts[0].shape[1]
    return pl.pallas_call(
        functools.partial(cholesky_kernel, len(parts)),
        in_specs=[VMEM] * len(parts),
        out_specs=VMEM,
        scratch_shapes=[pltpu.VMEM((n, n), F32)],
        out_shape=jax.ShapeDtypeStruct((n, n), F32),
        compiler_params=params(),
        name="inverse_factor",
        cost_estimate=cost(2),
    )(*parts)


def mm_three(a, b):
    a_hi, a_lo = halves(a)
    b_hi, b_lo = halves(b)
    return mm(a_hi, b_hi) + (mm(a_hi, b_lo) + mm(a_lo, b_hi))


def back_kernel(x, wa, wb, *refs):
    bt_out, y_out, s_out = refs[-3:]
    w = wa[...].astype(F32) + wb[...].astype(F32)
    bt = mm_three(x[...], w)
    bt_out[...] = bt
    s = jnp.sum(bt * bt, axis=1, keepdims=True)
    s_out[...] = jnp.broadcast_to(s, (s.shape[0], 128)).T[:8, :]
    y_out[...] = ((1.0 - momentum_keep) * mm(x[...].T.astype(BF16), bt.astype(BF16))).astype(BF16)


def back_full(x, wa, wb, after):
    rank, cols = wa.shape
    return pl.pallas_call(
        back_kernel,
        in_specs=[VMEM] * 3 + [ANY] * len(after),
        out_specs=[VMEM] * 3,
        out_shape=[
            jax.ShapeDtypeStruct((rank, cols), F32),
            jax.ShapeDtypeStruct((rank, cols), BF16),
            jax.ShapeDtypeStruct((8, rank), F32),
        ],
        compiler_params=params(),
        name="back_full",
        cost_estimate=cost(),
    )(x, wa, wb, *after)


def row_blocks(ranks, n_resp, n_head, chunk):
    return [
        pl.multiple_of(((ranks[0] ^ j) * n_head + (ranks[2] ^ k)) * chunk, chunk)
        for j in range(n_resp)
        for k in range(n_head)
    ]


def momentum_rows(blocks, pcat, y, totals, held, out, sems, begin, end):
    chunk = held.shape[0] // (end - begin)
    seg = totals[0].shape[0]
    copies = []
    for i in range(begin, end):
        rows = slice(i * chunk, (i + 1) * chunk)
        kept = slice((i - begin) * chunk, (i - begin + 1) * chunk)
        off = i * chunk % seg
        total = totals[(i - begin) * chunk // seg][off : off + chunk, :]
        held[kept, :] = total - mm(pcat[rows, :], y[...])
        copies.append(
            pltpu.make_async_copy(
                held.at[kept, :], out.at[pl.ds(blocks[i], chunk), :], sems.at[i - begin]
            )
        )
        copies[-1].start()
    return copies


def momentum_kernel(n_resp, n_head, n_totals, ranks, pcat, y, *refs):
    totals, refs = refs[:n_totals], refs[n_totals:]
    dq_parts, rg, refs = refs[:2], refs[2], refs[-7:]
    out, dq, resp_grad, token, held, sems, more = refs
    token[...] = jnp.zeros_like(token)
    width = dq_parts[0].shape[1]
    copies = [
        pltpu.make_async_copy(part, dq.at[:, pl.ds(i * width, width)], more.at[i])
        for i, part in enumerate(dq_parts)
    ]
    copies.append(pltpu.make_async_copy(rg, resp_grad, more.at[2]))
    n = n_resp * n_head
    blocks = row_blocks(ranks, n_resp, n_head, pcat.shape[0] // n)
    copies[2].start()
    moved = momentum_rows(blocks, pcat, y, totals, held, out, sems, 0, n // 2)
    for c in copies[:2]:
        c.start()
    for c in copies + moved:
        c.wait()


def new_momentum(ranks, pcat, totals, y, n_resp, n_head, dq_parts, rg, after):
    rows, rank = pcat.shape
    cols = totals[0].shape[1]
    length, width = dq_parts[0].shape
    return pl.pallas_call(
        functools.partial(momentum_kernel, n_resp, n_head, len(totals)),
        in_specs=[SMEM] + [VMEM] * (5 + len(totals)) + [ANY] * len(after),
        out_specs=[HBM, HBM, HBM, VMEM],
        scratch_shapes=[
            pltpu.VMEM((rows // 2, cols), F32),
            pltpu.SemaphoreType.DMA((n_resp * n_head // 2,)),
            pltpu.SemaphoreType.DMA((3,)),
        ],
        out_shape=[
            jax.ShapeDtypeStruct((rows, cols), F32),
            jax.ShapeDtypeStruct((length, 2 * width), BF16),
            jax.ShapeDtypeStruct(rg.shape, BF16),
            jax.ShapeDtypeStruct((8, 128), F32),
        ],
        compiler_params=params(12),
        name="new_momentum",
        cost_estimate=cost(5),
    )(ranks, pcat, y, *totals, *dq_parts, rg, *after)


def update_kernel(gain, n_resp, n_head, n_sums, n_totals, n_prompt, ranks, pcat, x, bt, y, *refs):
    sums, refs = refs[:n_sums], refs[n_sums:]
    totals, refs = refs[:n_totals], refs[n_totals:]
    prompts, refs = refs[:n_prompt], refs[n_prompt + 1 :]
    upd, basis_out, mom_out, prompt_out, held, held_mom, held_basis, held_prompt, sems, more = refs
    n = n_resp * n_head
    chunk = pcat.shape[0] // n
    blocks = row_blocks(ranks, n_resp, n_head, chunk)
    total = sums[0][...]
    for s in sums[1:]:
        total = total + s[...]
    scale = lax.rsqrt(total + norm_eps).T[:, :1]
    scaled = bt[...] * scale
    held_basis[...] = scaled.T
    acc = prompts[0][...]
    for p in prompts[1:]:
        acc = acc + p[...].astype(F32)
    held_prompt[...] = acc
    copies = [
        pltpu.make_async_copy(held_basis, basis_out, more.at[0]),
        pltpu.make_async_copy(held_prompt, prompt_out, more.at[1]),
    ]
    for c in copies:
        c.start()
    copies += momentum_rows(blocks, pcat, y, totals, held_mom, mom_out, sems.at[1], n // 2, n)
    z_hi, z_lo = halves(gain * mm_three(x[...].T, scaled))
    for i, at in enumerate(blocks):
        rows = slice(i * chunk, (i + 1) * chunk)
        p = pcat[rows, :]
        held[rows, :] = (mm(p, z_hi) + mm(p, z_lo)).astype(BF16)
        copies.append(
            pltpu.make_async_copy(held.at[rows, :], upd.at[pl.ds(at, chunk), :], sems.at[0, i])
        )
        copies[-1].start()
    for c in copies:
        c.wait()


def final_update(ranks, pcat, x, bt, y, sums, totals, prompts, momentum, gain, n_resp, n_head):
    rows, rank = pcat.shape
    cols = bt.shape[1]
    n_vmem = 4 + len(sums) + len(totals) + len(prompts)
    return pl.pallas_call(
        functools.partial(
            update_kernel, gain, n_resp, n_head, len(sums), len(totals), len(prompts)
        ),
        in_specs=[SMEM] + [VMEM] * n_vmem + [HBM],
        out_specs=[HBM] * 4,
        scratch_shapes=[
            pltpu.VMEM((rows, cols), BF16),
            pltpu.VMEM((rows // 2, cols), F32),
            pltpu.VMEM((cols, rank), F32),
            pltpu.VMEM(prompts[0].shape, F32),
            pltpu.SemaphoreType.DMA((2, n_resp * n_head)),
            pltpu.SemaphoreType.DMA((2,)),
        ],
        out_shape=[
            jax.ShapeDtypeStruct((rows, cols), BF16),
            jax.ShapeDtypeStruct((cols, rank), F32),
            jax.ShapeDtypeStruct((rows, cols), F32),
            jax.ShapeDtypeStruct(prompts[0].shape, F32),
        ],
        input_output_aliases={1 + n_vmem: 2},
        compiler_params=params(14),
        name="final_update",
        cost_estimate=cost(5),
    )(ranks, pcat, x, bt, y, *sums, *totals, *prompts, momentum)


def group_of(counts, response):
    group = jnp.int32(0)
    end = jnp.int32(0)
    for g in range(counts.shape[0]):
        end = end + counts[g]
        group = group + (end <= response).astype(jnp.int32)
    return group


def pack_kernel(*refs):
    keys, values, out = refs[0], refs[1], refs[-1]
    out[0] = keys[...]
    out[1] = values[...]


def pack_prompts(keys, values, after):
    return pl.pallas_call(
        pack_kernel,
        in_specs=[VMEM] * 2 + [ANY] * len(after),
        out_specs=VMEM,
        out_shape=jax.ShapeDtypeStruct((2,) + keys.shape, BF16),
        compiler_params=params(),
        name="pack_prompts",
        cost_estimate=cost(),
    )(keys, values, *after)


def select_kernel(n_resp, n_fsdp, ranks, counts, slots, *refs):
    stored, outs = refs[:n_resp], refs[-n_fsdp:]
    held = stored[0].shape[1]
    for k in range(n_fsdp):
        slot = slots[group_of(counts, ranks[0] * n_fsdp + (ranks[1] ^ k))]
        owner, local = slot // held, slot % held
        for j in range(n_resp):

            @pl.when(owner == (ranks[0] ^ j))
            def _():
                outs[k][0] = stored[j][0, local]
                outs[k][1] = stored[j][1, local]


def select_prompts(ranks, counts, slots, stored, n_fsdp, after):
    _, _, piece, width = stored[0].shape
    return pl.pallas_call(
        functools.partial(select_kernel, len(stored), n_fsdp),
        in_specs=[SMEM] * 3 + [VMEM] * len(stored) + [ANY] * len(after),
        out_specs=[VMEM] * n_fsdp,
        out_shape=[jax.ShapeDtypeStruct((2, piece, width), BF16)] * n_fsdp,
        compiler_params=params(),
        name="select_prompts",
        cost_estimate=cost(),
    )(ranks, counts, slots, *stored, *after)


def attention_kernel(
    n_fsdp, heads, last, ranks, counts, prompt_blocks, resp_blocks, q, sk, sv, go, *refs
):
    pieces, refs = refs[:n_fsdp], refs[n_fsdp:]
    keys, values, dk, dv = refs[-4:]
    n_out = 2 + n_fsdp if last else 3
    outs = refs[-4 - n_out : -4]
    dq = outs[0]
    piece = pieces[0].shape[1]
    cap = piece * n_fsdp
    length = q.shape[0]
    scale = HD ** (-0.5)
    for k in range(n_fsdp):
        rows = pl.ds(pl.multiple_of((ranks[1] ^ k) * piece, piece), piece)
        keys[rows, :] = pieces[k][0]
        values[rows, :] = pieces[k][1]
    keys[cap:, :] = sk[...]
    values[cap:, :] = sv[...]
    prompt_len = prompt_blocks[group_of(counts, ranks[0] * n_fsdp + ranks[1])] * 128
    resp_len = resp_blocks[0] * 128
    width = keys.shape[0]
    place = lax.broadcasted_iota(jnp.int32, (width, length), 0)
    pos = lax.broadcasted_iota(jnp.int32, (width, length), 1)
    inner = place - cap
    seen = ((place < cap) & (place < prompt_len)) | (
        (place >= cap) & (inner <= pos) & (inner < resp_len)
    )
    bias = jnp.where(seen, 0.0, -jnp.inf).astype(F32)
    live = lax.broadcasted_iota(jnp.int32, (length, HD), 0) < resp_len
    nt = (((1,), (1,)), ((), ()))
    kall = keys[...]
    vall = values[...]
    kt = kall.T
    if last:
        dk[...] = refs[0][...]
        dv[...] = refs[1][...]
    else:
        dk[...] = jnp.zeros_like(dk)
        dv[...] = jnp.zeros_like(dv)
    for i, h in enumerate(heads):
        cols = slice(h * HD, (h + 1) * HD)
        qh = q[:, cols]
        gh = jnp.where(live, go[:, cols], jnp.zeros((), BF16))
        logits = lax.dot_general(kall, qh, nt, preferred_element_type=F32) * scale + bias
        peak = jnp.max(logits, axis=0, keepdims=True)
        e = jnp.exp(logits - peak)
        w = (e * (1.0 / jnp.sum(e, axis=0, keepdims=True))).astype(BF16)
        dp = lax.dot_general(vall, gh, nt, preferred_element_type=F32)
        wf = w.astype(F32)
        diag = jnp.sum(wf * dp, axis=0, keepdims=True)
        ds = (wf * (dp - diag)).astype(BF16)
        dk[...] += mm(ds, qh)
        dv[...] += mm(w, gh)
        dq[:, i * HD : (i + 1) * HD] = (mm(kt, ds) * scale).T.astype(BF16)
    if last:
        own, sends = outs[1], outs[2:]
        own[0] = (dk[cap:, :] * scale).astype(BF16)
        own[1] = dv[cap:, :].astype(BF16)
        for k in range(n_fsdp):
            rows = pl.ds(pl.multiple_of((ranks[1] ^ k) * piece, piece), piece)
            sends[k][0] = (dk[rows, :] * scale).astype(sends[k].dtype)
            sends[k][1] = dv[rows, :].astype(sends[k].dtype)
    else:
        outs[1][...] = dk[...]
        outs[2][...] = dv[...]


def attention(heads, earlier, ranks, counts, prompt_blocks, resp_blocks, q, sk, sv, go, pieces, after):
    n_fsdp = len(pieces)
    piece = pieces[0].shape[1]
    length, width = q.shape
    cap = piece * n_fsdp
    total = cap + length
    last = earlier is not None
    dq_shape = jax.ShapeDtypeStruct((length, len(heads) * HD), BF16)
    if last:
        extra, specs = (earlier[1], earlier[2]), [VMEM] * 2
        out_shape = [dq_shape, jax.ShapeDtypeStruct((2, length, HD), BF16)] + [
            jax.ShapeDtypeStruct((2, piece, HD), BF16 if k else F32) for k in range(n_fsdp)
        ]
    else:
        extra, specs = (), []
        out_shape = [dq_shape] + [jax.ShapeDtypeStruct((total, HD), F32)] * 2
    return pl.pallas_call(
        functools.partial(attention_kernel, n_fsdp, heads, last),
        in_specs=[SMEM] * 4 + [VMEM] * (4 + n_fsdp) + specs + [ANY] * len(after),
        out_specs=[VMEM] * len(out_shape),
        scratch_shapes=[pltpu.VMEM((total, HD), BF16)] * 2 + [pltpu.VMEM((total, HD), F32)] * 2,
        out_shape=out_shape,
        compiler_params=params(12),
        name="attention",
        cost_estimate=cost(),
    )(ranks, counts, prompt_blocks, resp_blocks, q, sk, sv, go, *pieces, *extra, *after)


def by_slot_kernel(n_resp, n_fsdp, ranks, counts, slots, *refs):
    parts, outs = refs[:n_fsdp], refs[-n_resp:]
    held = outs[0].shape[1]
    slot_of = [
        slots[group_of(counts, ranks[0] * n_fsdp + (ranks[1] ^ k))] for k in range(n_fsdp)
    ]
    for j in range(n_resp):
        for local in range(held):
            slot = (ranks[0] ^ j) * held + local
            acc = jnp.zeros(parts[0].shape, F32)
            for k in range(n_fsdp):
                acc = acc + jnp.where(slot_of[k] == slot, parts[k][...].astype(F32), 0.0)
            outs[j][:, local] = acc.astype(outs[j].dtype)


def sum_by_slot(ranks, counts, slots, parts, n_resp, after):
    held = counts.shape[0] // n_resp
    _, piece, width = parts[0].shape
    return pl.pallas_call(
        functools.partial(by_slot_kernel, n_resp, len(parts)),
        in_specs=[SMEM] * 3 + [VMEM] * len(parts) + [ANY] * len(after),
        out_specs=[VMEM] * n_resp,
        out_shape=[
            jax.ShapeDtypeStruct((2, held, piece, width), BF16 if j else F32)
            for j in range(n_resp)
        ],
        compiler_params=params(),
        name="sum_by_slot",
        cost_estimate=cost(),
    )(ranks, counts, slots, *parts, *after)


def on_device(
    queries,
    self_keys,
    self_values,
    d_out,
    prompt_keys,
    prompt_values,
    counts,
    owner_slot,
    prompt_blocks,
    resp_blocks,
    grad_q,
    momentum,
    basis,
):
    n_resp, n_fsdp, n_head = (lax.axis_size(a) for a in ("resp", "fsdp", "head"))
    ranks = jnp.stack([lax.axis_index(a) for a in ("resp", "fsdp", "head")]).astype(jnp.int32)
    gain = math.sqrt(
        momentum.shape[0] * n_fsdp * momentum.shape[1] * n_resp * n_head / basis.shape[1]
    )

    in_hbm = [pltpu.with_memory_space_constraint(a, pltpu.HBM) for a in (momentum, grad_q, basis)]
    half = n_head // 2
    groups = [(half, half), (0, half)] if half else [(0, n_head)]

    mom_hbm, grad_hbm, basis_hbm = in_hbm
    order = [(j, *group) for group in groups for j in [*range(1, n_resp), 0]]
    nexts = dict(zip(order, order[1:] + [None]))
    totals, arrived, split, ins, after = {}, {}, {}, (basis_hbm,), ()
    for part in order:
        j, first, number = part
        value, totals[part[:2]], ins = project(
            ranks, mom_hbm, grad_hbm, ins, part, nexts[part], n_resp, n_head, BF16 if j else F32,
            after, 0 if j or first == 0 else 10,
        )
        after = ()
        if j:
            arrived.setdefault(first, []).append(swap(value, "resp", j))
            if part[1:] == groups[-1] and j == n_resp - 1:
                packed = pack_prompts(prompt_keys, prompt_values, (value,))
                stored = [packed] + [swap(packed, "resp", k) for k in range(1, n_resp)]
                outs = split_sum(owned, arrived[groups[0][0]], *groups[0])
                for i in range(groups[0][1]):
                    split[groups[0][0] + i] = outs[i]
                after = (outs[0],)
        elif part[1:] == groups[0] and len(groups) > 1:
            owned = value
        else:
            outs = split_sum(value, arrived[first], first, number)
            for i in range(number):
                split[first + i] = outs[i]
    totals = [totals[at] for at in sorted(totals)]
    chosen = select_prompts(
        ranks, counts, owner_slot, stored, n_fsdp, (split[1 % n_head],)
    )
    far_first = [k for first, number in groups for k in range(first, first + number) if k]
    summands = {k: swap(split[k], "head", k) for k in far_first}
    pieces = [chosen[0]] + [swap(chosen[k], "fsdp", k) for k in range(1, n_fsdp)]
    later = groups[-1][1] if len(groups) > 1 else 1
    far = sum_parts(
        [split[0]] + [summands[k] for k in range(later, n_head)], F32, (), 10
    )
    piece0 = sum_parts(
        [far] + [summands[k] for k in range(1, later)], BF16, tuple(pieces[1:])
    )

    along = {0: piece0}
    for k in far_first:
        along[k] = swap(piece0, "head", k)
    n_q = queries.shape[1] // HD
    heads = [list(range(n_q // 2)), list(range(n_q // 2, n_q))]
    held = (
        ranks, counts, prompt_blocks, resp_blocks, queries, self_keys, self_values, d_out, pieces
    )
    earlier = attention(heads[0], None, *held, (along[1 % n_head],))
    near = [along[k] for k in range(later)]
    passed = [[swap(c, "resp", j) for c in near] for j in range(1, n_resp)]
    far = relay(
        [along[k] for k in range(later, n_head)], (earlier[1], *[c for row in passed for c in row])
    )
    chunks = near + [along[k] for k in range(later, n_head)]
    for j in range(1, n_resp):
        chunks += passed[j - 1] + [swap(far, "resp", j)]
    dq_parts, resp_grad, *parts = attention(heads[1], earlier, *held, (far,))
    dq_parts = (earlier[0], dq_parts)
    pcat, pcat_t, gram = gather_gram(chunks, (parts[0],))

    bits = [1 << b for b in range(n_fsdp.bit_length() - 1)]
    w = back_part(pcat_t, totals, (gram,))
    for bit in bits[:-1]:
        gram = sum_parts([gram, swap(gram, "fsdp", bit)], F32, (), 3)
        w = sum_parts([w, swap(w, "fsdp", bit)], BF16, (gram,), 5)
    gram_parts = (gram, swap(gram, "fsdp", bits[-1]))
    w_other = swap(w, "fsdp", bits[-1])
    returned = [parts[0]] + [swap(parts[k], "fsdp", k) for k in range(1, n_fsdp)]
    x = inverse_factor(*gram_parts)
    bt, y, squares = back_full(x, w, w_other, tuple(returned[1:]))
    from_head = [swap(squares, "head", k) for k in range(1, n_head)]
    half = len(totals) // 2
    momentum_out, dq, resp_grad, token = new_momentum(
        ranks, pcat, totals[:half], y, n_resp, n_head, dq_parts, resp_grad, (squares,)
    )
    squares = sum_parts([squares] + from_head, F32, (token,))
    sums = sum_parts(
        [squares] + [swap(squares, "resp", j) for j in range(1, n_resp)], F32, (), 5
    )
    slots = sum_by_slot(ranks, counts, owner_slot, returned, n_resp, (squares,))
    prompts = [slots[0]] + [swap(slots[j], "resp", j) for j in range(1, n_resp)]
    update, basis_out, momentum_out, prompt_grad = final_update(
        ranks, pcat, x, bt, y, [sums], totals[half:], prompts, momentum_out, gain, n_resp, n_head
    )
    return (dq, resp_grad, prompt_grad, update, momentum_out, basis_out)


def solution(mesh):
    placed = (
        P(("resp", "fsdp"), "head"),
        P(("resp", "fsdp"), "head"),
        P(("resp", "fsdp"), "head"),
        P(("resp", "fsdp"), "head"),
        P("resp", "fsdp", "head"),
        P("resp", "fsdp", "head"),
        P(),
        P(),
        P(),
        P(("resp", "fsdp")),
        P("fsdp", ("resp", "head")),
        P("fsdp", ("resp", "head")),
        P(("resp", "head"), None),
    )
    return jax.shard_map(
        on_device,
        mesh=mesh,
        in_specs=placed,
        out_specs=(
            P(("resp", "fsdp"), "head"),
            P(None, ("resp", "fsdp"), "head"),
            P(None, "resp", "fsdp", "head"),
            P("fsdp", ("resp", "head")),
            P("fsdp", ("resp", "head")),
            P(("resp", "head"), None),
        ),
        check_vma=False,
    )
```

```python
import functools
import math

import jax
import jax.numpy as jnp
from jax import lax
from jax.experimental import pallas as pl
from jax.experimental.pallas import tpu as pltpu
from jax.sharding import PartitionSpec as P

HD = 128
PANEL = 8
OUTER = 32
MIB = 1 << 20

momentum_keep = 0.95
norm_eps = 1e-06

F32 = jnp.float32
BF16 = jnp.bfloat16
HIGHEST = lax.Precision.HIGHEST

SMEM = pl.BlockSpec(memory_space=pltpu.SMEM)
VMEM = pl.BlockSpec(memory_space=pltpu.VMEM)
ANY = pl.BlockSpec(memory_space=pl.ANY)
HBM = pl.BlockSpec(memory_space=pltpu.HBM)


def swap(value, axes, k):
    axes = (axes,) if isinstance(axes, str) else axes
    n = math.prod(lax.axis_size(a) for a in axes)
    return lax.ppermute(value, axes, [(i, i ^ k) for i in range(n)])


def params(mib=6):
    return pltpu.CompilerParams(vmem_limit_bytes=mib * MIB)


def cost(weight=0):
    return pl.CostEstimate(flops=1 + weight * 10**9, bytes_accessed=1, transcendentals=0)


def halves(x):
    hi = x.astype(BF16)
    return hi, (x - hi.astype(F32)).astype(BF16)


def mm(a, b):
    return jnp.dot(a, b, preferred_element_type=F32)


def mm_full(a, b):
    return jnp.dot(a, b, precision=HIGHEST, preferred_element_type=F32)


def row_copies(ranks, n_head, part, mom, grad, mom_to, grad_to, sems):
    j, first, number = part
    chunk = mom_to.shape[0] // number
    pieces = 2 if chunk % 32 == 0 else 1
    size = chunk // pieces
    copies = []
    for i in range(number):
        at = ((ranks[0] ^ j) * n_head + (ranks[2] ^ (first + i))) * chunk
        copies.append([])
        for p in range(pieces):
            src = pl.ds(pl.multiple_of(at + p * size, size), size)
            dst = pl.ds(i * chunk + p * size, size)
            n = i * pieces + p
            copies[i].append(pltpu.make_async_copy(mom.at[src, :], mom_to.at[dst, :], sems.at[0, n]))
            copies[i].append(
                pltpu.make_async_copy(grad.at[src, :], grad_to.at[dst, :], sems.at[1, n])
            )
    return copies


def start_all(copies):
    for row in copies:
        for c in row:
            c.start()


def project_kernel(n_head, part, following, is_first, n_in, ranks, mom, grad, *refs):
    ins, refs = refs[:n_in], list(refs)
    number = part[2]
    sems = refs.pop()
    ahead = []
    if is_first:
        right_sem, right, grad_in = refs.pop(), refs.pop(), refs.pop()
    if following:
        next_grad, next_mom = refs.pop(), refs.pop()
        ahead = row_copies(ranks, n_head, following, mom, grad, next_mom, next_grad, sems.at[1])
    if is_first:
        b_lo, b_hi = refs.pop(), refs.pop()
        total, out = refs.pop(), refs.pop()
        mom_in = total
        copies = row_copies(ranks, n_head, part, mom, grad, mom_in, grad_in, sems.at[0])
        fetch = pltpu.make_async_copy(ins[0], right, right_sem)
        start_all(copies[:1])
        fetch.start()
        start_all(copies[1:])
        fetch.wait()
        hi, lo = halves(right[...])
        b_hi[...] = hi
        b_lo[...] = lo
    else:
        total, out = refs.pop(), refs.pop()
        b_hi, b_lo, mom_in, grad_in = ins
        copies = [[]] * number
        start_all(ahead)
    chunk = total.shape[0] // number
    for i in range(number):
        for c in copies[i]:
            c.wait()
        if is_first and i == 0:
            start_all(ahead)
        rows = slice(i * chunk, (i + 1) * chunk)
        t = mom_in[rows, :] + grad_in[rows, :].astype(F32)
        total[rows, :] = t
        t_hi, t_lo = halves(t)
        acc = mm(t_hi, b_hi[...]) + (mm(t_hi, b_lo[...]) + mm(t_lo, b_hi[...]))
        out[rows, :] = acc.astype(out.dtype)
    for row in ahead:
        for c in row:
            c.wait()


def project(
    ranks, momentum, grad_q, ins, part, following, n_resp, n_head, dtype, after, weight=0
):
    is_first = len(ins) == 1
    rows, cols = momentum.shape
    chunk = rows // (n_resp * n_head)
    size = part[2] * chunk
    if is_first:
        right = ins[0]
        rank = right.shape[1]
        specs = [HBM]
    else:
        rank = ins[0].shape[1]
        specs = [VMEM] * 4
    out_shape = [jax.ShapeDtypeStruct((size, rank), dtype), jax.ShapeDtypeStruct((size, cols), F32)]
    if is_first:
        out_shape += [jax.ShapeDtypeStruct((cols, rank), BF16)] * 2
    if following:
        ahead = following[2] * chunk
        out_shape += [
            jax.ShapeDtypeStruct((ahead, cols), F32), jax.ShapeDtypeStruct((ahead, cols), BF16)
        ]
    scratch = [pltpu.SemaphoreType.DMA((2, 2, 2 * n_head))]
    if is_first:
        scratch = [
            pltpu.VMEM((size, cols), BF16), pltpu.VMEM((cols, rank), F32), pltpu.SemaphoreType.DMA
        ] + scratch
    outs = pl.pallas_call(
        functools.partial(project_kernel, n_head, part, following, is_first, len(ins)),
        in_specs=[SMEM, HBM, HBM] + specs + [ANY] * len(after),
        out_specs=[VMEM] * len(out_shape),
        scratch_shapes=scratch,
        out_shape=out_shape,
        compiler_params=params(14),
        name="project",
        cost_estimate=cost(weight),
    )(ranks, momentum, grad_q, *ins, *after)
    right = tuple(outs[2:4]) if is_first else tuple(ins[:2])
    return outs[0], outs[1], right + tuple(outs[-2:] if following else ())


def split_kernel(n_recv, number, own, *refs):
    recvs, outs = refs[:n_recv], refs[-number:]
    chunk = outs[0].shape[0]
    for i in range(number):
        rows = slice(i * chunk, (i + 1) * chunk)
        acc = own[rows, :]
        for r in recvs:
            acc = acc + r[rows, :].astype(F32)
        outs[i][...] = acc.astype(outs[i].dtype)


def split_sum(own, recvs, first, number):
    rows, rank = own.shape
    chunk = rows // number
    return pl.pallas_call(
        functools.partial(split_kernel, len(recvs), number),
        in_specs=[VMEM] * (1 + len(recvs)),
        out_specs=[VMEM] * number,
        out_shape=[
            jax.ShapeDtypeStruct((chunk, rank), BF16 if first + i else F32)
            for i in range(number)
        ],
        compiler_params=params(),
        name="split_sum",
        cost_estimate=cost(),
    )(own, *recvs)


def sum_kernel(n_parts, *refs):
    acc = refs[0][...].astype(F32)
    for r in refs[1:n_parts]:
        acc = acc + r[...].astype(F32)
    refs[-1][...] = acc.astype(refs[-1].dtype)


def sum_parts(parts, dtype, after=(), weight=0):
    shape = parts[0].shape
    return pl.pallas_call(
        functools.partial(sum_kernel, len(parts)),
        in_specs=[VMEM] * len(parts) + [ANY] * len(after),
        out_specs=VMEM,
        out_shape=jax.ShapeDtypeStruct(shape, dtype),
        compiler_params=params(),
        name="sum_parts",
        cost_estimate=cost(weight),
    )(*parts, *after)


def relay_kernel(n_parts, *refs):
    out = refs[-1]
    size = out.shape[0] // n_parts
    for i in range(n_parts):
        out[i * size : (i + 1) * size, :] = refs[i][...]


def relay(parts, after):
    rows, rank = parts[0].shape
    return pl.pallas_call(
        functools.partial(relay_kernel, len(parts)),
        in_specs=[VMEM] * len(parts) + [ANY] * len(after),
        out_specs=VMEM,
        out_shape=jax.ShapeDtypeStruct((len(parts) * rows, rank), parts[0].dtype),
        compiler_params=params(),
        name="relay",
        cost_estimate=cost(),
    )(*parts, *after)


def gram_kernel(n_chunks, *refs):
    chunks, (pcat, pcat_t, gram) = refs[:n_chunks], refs[-3:]
    at = 0
    for c in chunks:
        pcat[at : at + c.shape[0], :] = c[...]
        at += c.shape[0]
    p = pcat[...]
    pt = p.T
    pcat_t[...] = pt
    half = p.shape[1] // 2
    gram[:half, :] = mm(pt[:half, :], p[:, :half])
    low = mm(pt[half:, :], p)
    gram[half : 2 * half, :] = low[:, :half]
    gram[2 * half :, :] = low[:, half:]


def gather_gram(chunks, after):
    rank = chunks[0].shape[1]
    rows = sum(c.shape[0] for c in chunks)
    return pl.pallas_call(
        functools.partial(gram_kernel, len(chunks)),
        in_specs=[VMEM] * len(chunks) + [ANY] * len(after),
        out_specs=[VMEM] * 3,
        out_shape=[
            jax.ShapeDtypeStruct((rows, rank), BF16),
            jax.ShapeDtypeStruct((rank, rows), BF16),
            jax.ShapeDtypeStruct((3 * rank // 2, rank // 2), F32),
        ],
        compiler_params=params(8),
        name="gather_gram",
        cost_estimate=cost(),
    )(*chunks, *after)


def back_part_kernel(n_totals, pcat_t, *refs):
    totals, out = refs[:n_totals], refs[-1]
    seg = totals[0].shape[0]
    step = min(seg, 512)
    acc = None
    for j, total in enumerate(totals):
        for i in range(0, seg, step):
            t_hi, t_lo = halves(total[i : i + step, :])
            pt = pcat_t[:, j * seg + i : j * seg + i + step]
            part = mm(pt, t_hi) + mm(pt, t_lo)
            acc = part if acc is None else acc + part
    out[...] = acc.astype(BF16)


def back_part(pcat_t, totals, after):
    rank = pcat_t.shape[0]
    seg, cols = totals[0].shape
    rows = seg * len(totals)
    return pl.pallas_call(
        functools.partial(back_part_kernel, len(totals)),
        in_specs=[VMEM] * (1 + len(totals)) + [ANY] * len(after),
        out_specs=VMEM,
        out_shape=jax.ShapeDtypeStruct((rank, cols), BF16),
        compiler_params=params(14),
        name="back_part",
        cost_estimate=cost(5),
    )(pcat_t, *totals, *after)


def factor_panel(panel, off):
    shape = (PANEL, 128)
    d = {}
    for j in range(PANEL):
        col = jnp.broadcast_to(panel[:, off + j : off + j + 1], shape)
        for i in range(j, PANEL):
            d[i, j] = jnp.broadcast_to(col[i : i + 1, :], shape)
    low, inv = {}, {}
    for j in range(0, PANEL, 2):
        a, b, c = d[j, j], d[j + 1, j], d[j + 1, j + 1]
        first = lax.rsqrt(a)
        second = lax.rsqrt(a * c - b * b) * (a * first)
        inv[j, j], inv[j + 1, j + 1] = first, second
        low[j + 1, j] = b * first
        for i in range(j + 2, PANEL):
            low[i, j] = d[i, j] * first
            low[i, j + 1] = (d[i, j + 1] - low[i, j] * low[j + 1, j]) * second
        for k in range(j + 2, PANEL):
            for i in range(k, PANEL):
                d[i, k] = d[i, k] - (low[i, j] * low[k, j] + low[i, j + 1] * low[k, j + 1])
    for j in range(PANEL):
        for i in range(j + 1, PANEL):
            acc = low[i, j] * inv[j, j]
            for k in range(j + 1, i):
                acc = acc + low[i, k] * inv[k, j]
            inv[i, j] = -(acc * inv[i, i])
    return inv


def three_parts(x):
    a = x.astype(BF16)
    rest = x - a.astype(F32)
    b = rest.astype(BF16)
    return a, b, (rest - b.astype(F32)).astype(BF16)


def cholesky_kernel(n_parts, *refs):
    parts, out, work = refs[:n_parts], refs[n_parts], refs[n_parts + 1]
    n = out.shape[0]
    half = n // 2
    tiles = n // 128 + 1
    total = parts[0][...]
    for part in parts[1:]:
        total = total + part[...]
    low = total[half : 2 * half, :]
    work[:half, :half] = total[:half, :]
    work[half:, :half] = low
    work[:half, half:] = low.T
    work[half:, half:] = total[2 * half :, :]
    eye = lax.broadcasted_iota(jnp.int32, (n, n), 0) == lax.broadcasted_iota(jnp.int32, (n, n), 1)
    whole = work[...]
    diag = jnp.where(eye, whole, 0.0)
    across = lax.rsqrt(jnp.sum(diag, axis=0, keepdims=True))
    work[...] = whole * lax.rsqrt(jnp.sum(diag, axis=1, keepdims=True)) * across
    sub = lax.broadcasted_iota(jnp.int32, (PANEL, 128), 0)
    lane = lax.broadcasted_iota(jnp.int32, (PANEL, 128), 1)
    n_panels = OUTER // PANEL

    def step(o, carry):
        blk = [
            [work[p * PANEL : (p + 1) * PANEL, t * 128 : (t + 1) * 128] for t in range(tiles - 1)]
            + [jnp.where(lane == sub + p * PANEL, 1.0, 0.0).astype(F32)]
            for p in range(n_panels)
        ]
        for p in range(n_panels):
            off = p * PANEL
            inv = factor_panel(blk[p][0], off)
            rows_of = [
                [jnp.broadcast_to(blk[p][t][j : j + 1, :], (PANEL, 128)) for t in range(tiles)]
                for j in range(PANEL)
            ]
            new = [None] * tiles
            for j in range(PANEL):
                col = inv[PANEL - 1, j]
                for i in range(PANEL - 2, j - 1, -1):
                    col = jnp.where(sub == i, inv[i, j], col)
                if j:
                    col = jnp.where(sub < j, 0.0, col)
                for t in range(tiles):
                    term = col * rows_of[j][t]
                    new[t] = term if new[t] is None else new[t] + term
            blk[p] = new
            if p + 1 < n_panels:
                u_rows = [
                    [jnp.broadcast_to(new[t][j : j + 1, :], (PANEL, 128)) for t in range(tiles)]
                    for j in range(PANEL)
                ]
                for b in range(p + 1, n_panels):
                    lanes = [
                        jnp.broadcast_to(blk[b][0][:, off + m : off + m + 1], (PANEL, 128))
                        for m in range(PANEL)
                    ]
                    upd = list(blk[b])
                    for k in range(PANEL):
                        v = lanes[0] * inv[k, 0]
                        for m in range(1, k + 1):
                            v = v + lanes[m] * inv[k, m]
                        for t in range(tiles):
                            upd[t] = upd[t] - v * u_rows[k][t]
                    blk[b] = upd
        u = jnp.concatenate([jnp.concatenate(row, axis=1) for row in blk], axis=0)
        u = pltpu.roll(u, tiles * 128 - OUTER, 1)[:, :n]
        at = lax.broadcasted_iota(jnp.int32, (OUTER, n), 1)
        left = jnp.where(at < n - OUTER * (o + 1), u, 0.0)
        la, lb, lc = three_parts(left)
        ua, ub, uc = three_parts(u)
        lhs = jnp.concatenate([la, la, lb, la, lc, lb], axis=0)
        rhs = jnp.concatenate([ua, ub, ua, uc, ua, ub], axis=0)
        upd = mm(lhs.T, rhs)
        rest = work[OUTER:, :]
        lanes_at = lax.broadcasted_iota(jnp.int32, rest.shape, 1)
        rest = pltpu.roll(jnp.where(lanes_at < OUTER, 0.0, rest), n - OUTER, 1)
        work[: n - OUTER, :] = rest - upd[: n - OUTER, :]
        work[n - OUTER :, :] = u
        return carry

    lax.fori_loop(0, n // OUTER, step, 0)
    out[...] = work[...] * across


def inverse_factor(*parts):
    n = 2 * parts[0].shape[1]
    return pl.pallas_call(
        functools.partial(cholesky_kernel, len(parts)),
        in_specs=[VMEM] * len(parts),
        out_specs=VMEM,
        scratch_shapes=[pltpu.VMEM((n, n), F32)],
        out_shape=jax.ShapeDtypeStruct((n, n), F32),
        compiler_params=params(),
        name="inverse_factor",
        cost_estimate=cost(2),
    )(*parts)


def mm_three(a, b):
    a_hi, a_lo = halves(a)
    b_hi, b_lo = halves(b)
    return mm(a_hi, b_hi) + (mm(a_hi, b_lo) + mm(a_lo, b_hi))


def back_kernel(x, wa, wb, *refs):
    bt_out, y_out, s_out = refs[-3:]
    w = wa[...].astype(F32) + wb[...].astype(F32)
    bt = mm_three(x[...], w)
    bt_out[...] = bt
    s = jnp.sum(bt * bt, axis=1, keepdims=True)
    s_out[...] = jnp.broadcast_to(s, (s.shape[0], 128)).T[:8, :]
    y_out[...] = ((1.0 - momentum_keep) * mm(x[...].T.astype(BF16), bt.astype(BF16))).astype(BF16)


def back_full(x, wa, wb, after):
    rank, cols = wa.shape
    return pl.pallas_call(
        back_kernel,
        in_specs=[VMEM] * 3 + [ANY] * len(after),
        out_specs=[VMEM] * 3,
        out_shape=[
            jax.ShapeDtypeStruct((rank, cols), F32),
            jax.ShapeDtypeStruct((rank, cols), BF16),
            jax.ShapeDtypeStruct((8, rank), F32),
        ],
        compiler_params=params(),
        name="back_full",
        cost_estimate=cost(),
    )(x, wa, wb, *after)


def row_blocks(ranks, n_resp, n_head, chunk):
    return [
        pl.multiple_of(((ranks[0] ^ j) * n_head + (ranks[2] ^ k)) * chunk, chunk)
        for j in range(n_resp)
        for k in range(n_head)
    ]


def momentum_rows(blocks, pcat, y, totals, held, out, sems, begin, end):
    chunk = held.shape[0] // (end - begin)
    seg = totals[0].shape[0]
    copies = []
    for i in range(begin, end):
        rows = slice(i * chunk, (i + 1) * chunk)
        kept = slice((i - begin) * chunk, (i - begin + 1) * chunk)
        off = i * chunk % seg
        total = totals[(i - begin) * chunk // seg][off : off + chunk, :]
        held[kept, :] = total - mm(pcat[rows, :], y[...])
        copies.append(
            pltpu.make_async_copy(
                held.at[kept, :], out.at[pl.ds(blocks[i], chunk), :], sems.at[i - begin]
            )
        )
        copies[-1].start()
    return copies


def momentum_kernel(n_resp, n_head, n_totals, ranks, pcat, y, *refs):
    totals, refs = refs[:n_totals], refs[n_totals:]
    dq_parts, rg, refs = refs[:2], refs[2], refs[-7:]
    out, dq, resp_grad, token, held, sems, more = refs
    token[...] = jnp.zeros_like(token)
    width = dq_parts[0].shape[1]
    copies = [
        pltpu.make_async_copy(part, dq.at[:, pl.ds(i * width, width)], more.at[i])
        for i, part in enumerate(dq_parts)
    ]
    copies.append(pltpu.make_async_copy(rg, resp_grad, more.at[2]))
    n = n_resp * n_head
    blocks = row_blocks(ranks, n_resp, n_head, pcat.shape[0] // n)
    copies[2].start()
    moved = momentum_rows(blocks, pcat, y, totals, held, out, sems, 0, n // 2)
    for c in copies[:2]:
        c.start()
    for c in copies + moved:
        c.wait()


def new_momentum(ranks, pcat, totals, y, n_resp, n_head, dq_parts, rg, after):
    rows, rank = pcat.shape
    cols = totals[0].shape[1]
    length, width = dq_parts[0].shape
    return pl.pallas_call(
        functools.partial(momentum_kernel, n_resp, n_head, len(totals)),
        in_specs=[SMEM] + [VMEM] * (5 + len(totals)) + [ANY] * len(after),
        out_specs=[HBM, HBM, HBM, VMEM],
        scratch_shapes=[
            pltpu.VMEM((rows // 2, cols), F32),
            pltpu.SemaphoreType.DMA((n_resp * n_head // 2,)),
            pltpu.SemaphoreType.DMA((3,)),
        ],
        out_shape=[
            jax.ShapeDtypeStruct((rows, cols), F32),
            jax.ShapeDtypeStruct((length, 2 * width), BF16),
            jax.ShapeDtypeStruct(rg.shape, BF16),
            jax.ShapeDtypeStruct((8, 128), F32),
        ],
        compiler_params=params(12),
        name="new_momentum",
        cost_estimate=cost(5),
    )(ranks, pcat, y, *totals, *dq_parts, rg, *after)


def update_kernel(gain, n_resp, n_head, n_sums, n_totals, n_prompt, ranks, pcat, x, bt, y, *refs):
    sums, refs = refs[:n_sums], refs[n_sums:]
    totals, refs = refs[:n_totals], refs[n_totals:]
    prompts, refs = refs[:n_prompt], refs[n_prompt + 1 :]
    upd, basis_out, mom_out, prompt_out, held, held_mom, held_basis, held_prompt, sems, more = refs
    n = n_resp * n_head
    chunk = pcat.shape[0] // n
    blocks = row_blocks(ranks, n_resp, n_head, chunk)
    total = sums[0][...]
    for s in sums[1:]:
        total = total + s[...]
    scale = lax.rsqrt(total + norm_eps).T[:, :1]
    scaled = bt[...] * scale
    held_basis[...] = scaled.T
    acc = prompts[0][...]
    for p in prompts[1:]:
        acc = acc + p[...].astype(F32)
    held_prompt[...] = acc
    copies = [
        pltpu.make_async_copy(held_basis, basis_out, more.at[0]),
        pltpu.make_async_copy(held_prompt, prompt_out, more.at[1]),
    ]
    for c in copies:
        c.start()
    copies += momentum_rows(blocks, pcat, y, totals, held_mom, mom_out, sems.at[1], n // 2, n)
    z_hi, z_lo = halves(gain * mm_three(x[...].T, scaled))
    for i, at in enumerate(blocks):
        rows = slice(i * chunk, (i + 1) * chunk)
        p = pcat[rows, :]
        held[rows, :] = (mm(p, z_hi) + mm(p, z_lo)).astype(BF16)
        copies.append(
            pltpu.make_async_copy(held.at[rows, :], upd.at[pl.ds(at, chunk), :], sems.at[0, i])
        )
        copies[-1].start()
    for c in copies:
        c.wait()


def final_update(ranks, pcat, x, bt, y, sums, totals, prompts, momentum, gain, n_resp, n_head):
    rows, rank = pcat.shape
    cols = bt.shape[1]
    n_vmem = 4 + len(sums) + len(totals) + len(prompts)
    return pl.pallas_call(
        functools.partial(
            update_kernel, gain, n_resp, n_head, len(sums), len(totals), len(prompts)
        ),
        in_specs=[SMEM] + [VMEM] * n_vmem + [HBM],
        out_specs=[HBM] * 4,
        scratch_shapes=[
            pltpu.VMEM((rows, cols), BF16),
            pltpu.VMEM((rows // 2, cols), F32),
            pltpu.VMEM((cols, rank), F32),
            pltpu.VMEM(prompts[0].shape, F32),
            pltpu.SemaphoreType.DMA((2, n_resp * n_head)),
            pltpu.SemaphoreType.DMA((2,)),
        ],
        out_shape=[
            jax.ShapeDtypeStruct((rows, cols), BF16),
            jax.ShapeDtypeStruct((cols, rank), F32),
            jax.ShapeDtypeStruct((rows, cols), F32),
            jax.ShapeDtypeStruct(prompts[0].shape, F32),
        ],
        input_output_aliases={1 + n_vmem: 2},
        compiler_params=params(14),
        name="final_update",
        cost_estimate=cost(5),
    )(ranks, pcat, x, bt, y, *sums, *totals, *prompts, momentum)


def group_of(counts, response):
    group = jnp.int32(0)
    end = jnp.int32(0)
    for g in range(counts.shape[0]):
        end = end + counts[g]
        group = group + (end <= response).astype(jnp.int32)
    return group


def pack_kernel(*refs):
    keys, values, out = refs[0], refs[1], refs[-1]
    out[0] = keys[...]
    out[1] = values[...]


def pack_prompts(keys, values, after):
    return pl.pallas_call(
        pack_kernel,
        in_specs=[VMEM] * 2 + [ANY] * len(after),
        out_specs=VMEM,
        out_shape=jax.ShapeDtypeStruct((2,) + keys.shape, BF16),
        compiler_params=params(),
        name="pack_prompts",
        cost_estimate=cost(),
    )(keys, values, *after)


def select_kernel(n_resp, n_fsdp, ranks, counts, slots, *refs):
    stored, outs = refs[:n_resp], refs[-n_fsdp:]
    held = stored[0].shape[1]
    for k in range(n_fsdp):
        slot = slots[group_of(counts, ranks[0] * n_fsdp + (ranks[1] ^ k))]
        owner, local = slot // held, slot % held
        for j in range(n_resp):

            @pl.when(owner == (ranks[0] ^ j))
            def _():
                outs[k][0] = stored[j][0, local]
                outs[k][1] = stored[j][1, local]


def select_prompts(ranks, counts, slots, stored, n_fsdp, after):
    _, _, piece, width = stored[0].shape
    return pl.pallas_call(
        functools.partial(select_kernel, len(stored), n_fsdp),
        in_specs=[SMEM] * 3 + [VMEM] * len(stored) + [ANY] * len(after),
        out_specs=[VMEM] * n_fsdp,
        out_shape=[jax.ShapeDtypeStruct((2, piece, width), BF16)] * n_fsdp,
        compiler_params=params(),
        name="select_prompts",
        cost_estimate=cost(),
    )(ranks, counts, slots, *stored, *after)


def attention_kernel(
    n_fsdp, heads, last, ranks, counts, prompt_blocks, resp_blocks, q, sk, sv, go, *refs
):
    pieces, refs = refs[:n_fsdp], refs[n_fsdp:]
    keys, values, dk, dv = refs[-4:]
    n_out = 2 + n_fsdp if last else 3
    outs = refs[-4 - n_out : -4]
    dq = outs[0]
    piece = pieces[0].shape[1]
    cap = piece * n_fsdp
    length = q.shape[0]
    scale = HD ** (-0.5)
    for k in range(n_fsdp):
        rows = pl.ds(pl.multiple_of((ranks[1] ^ k) * piece, piece), piece)
        keys[rows, :] = pieces[k][0]
        values[rows, :] = pieces[k][1]
    keys[cap:, :] = sk[...]
    values[cap:, :] = sv[...]
    prompt_len = prompt_blocks[group_of(counts, ranks[0] * n_fsdp + ranks[1])] * 128
    resp_len = resp_blocks[0] * 128
    width = keys.shape[0]
    place = lax.broadcasted_iota(jnp.int32, (width, length), 0)
    pos = lax.broadcasted_iota(jnp.int32, (width, length), 1)
    inner = place - cap
    seen = ((place < cap) & (place < prompt_len)) | (
        (place >= cap) & (inner <= pos) & (inner < resp_len)
    )
    bias = jnp.where(seen, 0.0, -jnp.inf).astype(F32)
    live = lax.broadcasted_iota(jnp.int32, (length, HD), 0) < resp_len
    nt = (((1,), (1,)), ((), ()))
    kall = keys[...]
    vall = values[...]
    kt = kall.T
    if last:
        dk[...] = refs[0][...]
        dv[...] = refs[1][...]
    else:
        dk[...] = jnp.zeros_like(dk)
        dv[...] = jnp.zeros_like(dv)
    for i, h in enumerate(heads):
        cols = slice(h * HD, (h + 1) * HD)
        qh = q[:, cols]
        gh = jnp.where(live, go[:, cols], jnp.zeros((), BF16))
        logits = lax.dot_general(kall, qh, nt, preferred_element_type=F32) * scale + bias
        peak = jnp.max(logits, axis=0, keepdims=True)
        e = jnp.exp(logits - peak)
        w = (e * (1.0 / jnp.sum(e, axis=0, keepdims=True))).astype(BF16)
        dp = lax.dot_general(vall, gh, nt, preferred_element_type=F32)
        wf = w.astype(F32)
        diag = jnp.sum(wf * dp, axis=0, keepdims=True)
        ds = (wf * (dp - diag)).astype(BF16)
        dk[...] += mm(ds, qh)
        dv[...] += mm(w, gh)
        dq[:, i * HD : (i + 1) * HD] = (mm(kt, ds) * scale).T.astype(BF16)
    if last:
        own, sends = outs[1], outs[2:]
        own[0] = (dk[cap:, :] * scale).astype(BF16)
        own[1] = dv[cap:, :].astype(BF16)
        for k in range(n_fsdp):
            rows = pl.ds(pl.multiple_of((ranks[1] ^ k) * piece, piece), piece)
            sends[k][0] = (dk[rows, :] * scale).astype(sends[k].dtype)
            sends[k][1] = dv[rows, :].astype(sends[k].dtype)
    else:
        outs[1][...] = dk[...]
        outs[2][...] = dv[...]


def attention(heads, earlier, ranks, counts, prompt_blocks, resp_blocks, q, sk, sv, go, pieces, after):
    n_fsdp = len(pieces)
    piece = pieces[0].shape[1]
    length, width = q.shape
    cap = piece * n_fsdp
    total = cap + length
    last = earlier is not None
    dq_shape = jax.ShapeDtypeStruct((length, len(heads) * HD), BF16)
    if last:
        extra, specs = (earlier[1], earlier[2]), [VMEM] * 2
        out_shape = [dq_shape, jax.ShapeDtypeStruct((2, length, HD), BF16)] + [
            jax.ShapeDtypeStruct((2, piece, HD), BF16 if k else F32) for k in range(n_fsdp)
        ]
    else:
        extra, specs = (), []
        out_shape = [dq_shape] + [jax.ShapeDtypeStruct((total, HD), F32)] * 2
    return pl.pallas_call(
        functools.partial(attention_kernel, n_fsdp, heads, last),
        in_specs=[SMEM] * 4 + [VMEM] * (4 + n_fsdp) + specs + [ANY] * len(after),
        out_specs=[VMEM] * len(out_shape),
        scratch_shapes=[pltpu.VMEM((total, HD), BF16)] * 2 + [pltpu.VMEM((total, HD), F32)] * 2,
        out_shape=out_shape,
        compiler_params=params(12),
        name="attention",
        cost_estimate=cost(),
    )(ranks, counts, prompt_blocks, resp_blocks, q, sk, sv, go, *pieces, *extra, *after)


def by_slot_kernel(n_resp, n_fsdp, ranks, counts, slots, *refs):
    parts, outs = refs[:n_fsdp], refs[-n_resp:]
    held = outs[0].shape[1]
    slot_of = [
        slots[group_of(counts, ranks[0] * n_fsdp + (ranks[1] ^ k))] for k in range(n_fsdp)
    ]
    for j in range(n_resp):
        for local in range(held):
            slot = (ranks[0] ^ j) * held + local
            acc = jnp.zeros(parts[0].shape, F32)
            for k in range(n_fsdp):
                acc = acc + jnp.where(slot_of[k] == slot, parts[k][...].astype(F32), 0.0)
            outs[j][:, local] = acc.astype(outs[j].dtype)


def sum_by_slot(ranks, counts, slots, parts, n_resp, after):
    held = counts.shape[0] // n_resp
    _, piece, width = parts[0].shape
    return pl.pallas_call(
        functools.partial(by_slot_kernel, n_resp, len(parts)),
        in_specs=[SMEM] * 3 + [VMEM] * len(parts) + [ANY] * len(after),
        out_specs=[VMEM] * n_resp,
        out_shape=[
            jax.ShapeDtypeStruct((2, held, piece, width), BF16 if j else F32)
            for j in range(n_resp)
        ],
        compiler_params=params(),
        name="sum_by_slot",
        cost_estimate=cost(),
    )(ranks, counts, slots, *parts, *after)


def on_device(
    queries,
    self_keys,
    self_values,
    d_out,
    prompt_keys,
    prompt_values,
    counts,
    owner_slot,
    prompt_blocks,
    resp_blocks,
    grad_q,
    momentum,
    basis,
):
    n_resp, n_fsdp, n_head = (lax.axis_size(a) for a in ("resp", "fsdp", "head"))
    ranks = jnp.stack([lax.axis_index(a) for a in ("resp", "fsdp", "head")]).astype(jnp.int32)
    gain = math.sqrt(
        momentum.shape[0] * n_fsdp * momentum.shape[1] * n_resp * n_head / basis.shape[1]
    )

    in_hbm = [pltpu.with_memory_space_constraint(a, pltpu.HBM) for a in (momentum, grad_q, basis)]
    half = n_head // 2
    groups = [(half, half), (0, half)] if half else [(0, n_head)]

    mom_hbm, grad_hbm, basis_hbm = in_hbm
    order = [(j, *group) for group in groups for j in [*range(1, n_resp), 0]]
    nexts = dict(zip(order, order[1:] + [None]))
    totals, arrived, split, ins, after = {}, {}, {}, (basis_hbm,), ()
    for part in order:
        j, first, number = part
        value, totals[part[:2]], ins = project(
            ranks, mom_hbm, grad_hbm, ins, part, nexts[part], n_resp, n_head, BF16 if j else F32,
            after, 0 if j or first == 0 else 10,
        )
        after = ()
        if j:
            arrived.setdefault(first, []).append(swap(value, "resp", j))
            if part[1:] == groups[-1] and j == n_resp - 1:
                packed = pack_prompts(prompt_keys, prompt_values, (value,))
                stored = [packed] + [swap(packed, "resp", k) for k in range(1, n_resp)]
                outs = split_sum(owned, arrived[groups[0][0]], *groups[0])
                for i in range(groups[0][1]):
                    split[groups[0][0] + i] = outs[i]
                after = (outs[0],)
        elif part[1:] == groups[0] and len(groups) > 1:
            owned = value
        else:
            outs = split_sum(value, arrived[first], first, number)
            for i in range(number):
                split[first + i] = outs[i]
    totals = [totals[at] for at in sorted(totals)]
    chosen = select_prompts(
        ranks, counts, owner_slot, stored, n_fsdp, (split[1 % n_head],)
    )
    far_first = [k for first, number in groups for k in range(first, first + number) if k]
    summands = {k: swap(split[k], "head", k) for k in far_first}
    pieces = [chosen[0]] + [swap(chosen[k], "fsdp", k) for k in range(1, n_fsdp)]
    later = groups[-1][1] if len(groups) > 1 else 1
    far = sum_parts(
        [split[0]] + [summands[k] for k in range(later, n_head)], F32, (), 10
    )
    piece0 = sum_parts(
        [far] + [summands[k] for k in range(1, later)], BF16, tuple(pieces[1:])
    )

    along = {0: piece0}
    for k in range(1, later):
        along[k] = swap(piece0, "head", k)
    held_back = relay([piece0], (along[max(1, later) - 1],))
    for k in range(later, n_head):
        along[k] = swap(held_back if k > later else piece0, "head", k)

    n_q = queries.shape[1] // HD
    heads = [list(range(n_q // 2)), list(range(n_q // 2, n_q))]
    held = (
        ranks, counts, prompt_blocks, resp_blocks, queries, self_keys, self_values, d_out, pieces
    )
    early = [along[k] for k in range(n_head - 1)]
    last = along[n_head - 1]
    earlier = attention(heads[0], None, *held, (early[-1],))
    passed = [[swap(c, "resp", j) for c in early] for j in range(1, n_resp)]
    sent_last = relay([last], (earlier[1], *[c for row in passed for c in row]))
    chunks = early + [last]
    for j in range(1, n_resp):
        chunks += passed[j - 1] + [swap(sent_last, "resp", j)]
    dq_parts, resp_grad, *parts = attention(heads[1], earlier, *held, (sent_last,))
    dq_parts = (earlier[0], dq_parts)
    pcat, pcat_t, gram = gather_gram(chunks, (parts[0],))

    bits = [1 << b for b in range(n_fsdp.bit_length() - 1)]
    w = back_part(pcat_t, totals, (gram,))
    for bit in bits[:-1]:
        gram = sum_parts([gram, swap(gram, "fsdp", bit)], F32, (), 3)
        w = sum_parts([w, swap(w, "fsdp", bit)], BF16, (gram,), 5)
    gram_parts = (gram, swap(gram, "fsdp", bits[-1]))
    w_other = swap(w, "fsdp", bits[-1])
    returned = [parts[0]] + [swap(parts[k], "fsdp", k) for k in range(1, n_fsdp)]
    x = inverse_factor(*gram_parts)
    bt, y, squares = back_full(x, w, w_other, tuple(returned[1:]))
    from_head = [swap(squares, "head", k) for k in range(1, n_head)]
    half = len(totals) // 2
    slots = sum_by_slot(ranks, counts, owner_slot, returned, n_resp, (squares,))
    prompts = [slots[0]] + [swap(slots[j], "resp", j) for j in range(1, n_resp)]
    momentum_out, dq, resp_grad, token = new_momentum(
        ranks, pcat, totals[:half], y, n_resp, n_head, dq_parts, resp_grad, (squares, slots[-1])
    )
    squares = sum_parts([squares] + from_head, F32, (token,))
    sums = sum_parts(
        [squares] + [swap(squares, "resp", j) for j in range(1, n_resp)], F32
    )
    update, basis_out, momentum_out, prompt_grad = final_update(
        ranks, pcat, x, bt, y, [sums], totals[half:], prompts, momentum_out, gain, n_resp, n_head
    )
    return (dq, resp_grad, prompt_grad, update, momentum_out, basis_out)


def solution(mesh):
    placed = (
        P(("resp", "fsdp"), "head"),
        P(("resp", "fsdp"), "head"),
        P(("resp", "fsdp"), "head"),
        P(("resp", "fsdp"), "head"),
        P("resp", "fsdp", "head"),
        P("resp", "fsdp", "head"),
        P(),
        P(),
        P(),
        P(("resp", "fsdp")),
        P("fsdp", ("resp", "head")),
        P("fsdp", ("resp", "head")),
        P(("resp", "head"), None),
    )
    return jax.shard_map(
        on_device,
        mesh=mesh,
        in_specs=placed,
        out_specs=(
            P(("resp", "fsdp"), "head"),
            P(None, ("resp", "fsdp"), "head"),
            P(None, "resp", "fsdp", "head"),
            P("fsdp", ("resp", "head")),
            P("fsdp", ("resp", "head")),
            P(("resp", "head"), None),
        ),
        check_vma=False,
    )
```

```python
import functools
import math

import jax
import jax.numpy as jnp
from jax import lax
from jax.experimental import pallas as pl
from jax.experimental.pallas import tpu as pltpu
from jax.sharding import PartitionSpec as P

HD = 128
PANEL = 8
OUTER = 32
MIB = 1 << 20

momentum_keep = 0.95
norm_eps = 1e-06

F32 = jnp.float32
BF16 = jnp.bfloat16
HIGHEST = lax.Precision.HIGHEST

SMEM = pl.BlockSpec(memory_space=pltpu.SMEM)
VMEM = pl.BlockSpec(memory_space=pltpu.VMEM)
ANY = pl.BlockSpec(memory_space=pl.ANY)
HBM = pl.BlockSpec(memory_space=pltpu.HBM)


def swap(value, axes, k):
    axes = (axes,) if isinstance(axes, str) else axes
    n = math.prod(lax.axis_size(a) for a in axes)
    return lax.ppermute(value, axes, [(i, i ^ k) for i in range(n)])


def params(mib=6):
    return pltpu.CompilerParams(vmem_limit_bytes=mib * MIB)


def cost(weight=0):
    return pl.CostEstimate(flops=1 + weight * 10**9, bytes_accessed=1, transcendentals=0)


def halves(x):
    hi = x.astype(BF16)
    return hi, (x - hi.astype(F32)).astype(BF16)


def mm(a, b):
    return jnp.dot(a, b, preferred_element_type=F32)


def mm_full(a, b):
    return jnp.dot(a, b, precision=HIGHEST, preferred_element_type=F32)


def row_copies(ranks, n_head, part, mom, grad, mom_to, grad_to, sems):
    j, first, number = part
    chunk = mom_to.shape[0] // number
    pieces = 2 if chunk % 32 == 0 else 1
    size = chunk // pieces
    copies = []
    for i in range(number):
        at = ((ranks[0] ^ j) * n_head + (ranks[2] ^ (first + i))) * chunk
        copies.append([])
        for p in range(pieces):
            src = pl.ds(pl.multiple_of(at + p * size, size), size)
            dst = pl.ds(i * chunk + p * size, size)
            n = i * pieces + p
            copies[i].append(pltpu.make_async_copy(mom.at[src, :], mom_to.at[dst, :], sems.at[0, n]))
            copies[i].append(
                pltpu.make_async_copy(grad.at[src, :], grad_to.at[dst, :], sems.at[1, n])
            )
    return copies


def start_all(copies):
    for row in copies:
        for c in row:
            c.start()


def project_kernel(n_head, part, following, is_first, n_in, ranks, mom, grad, *refs):
    ins, refs = refs[:n_in], list(refs)
    number = part[2]
    sems = refs.pop()
    ahead = []
    if is_first:
        right_sem, right, grad_in = refs.pop(), refs.pop(), refs.pop()
    if following:
        next_grad, next_mom = refs.pop(), refs.pop()
        ahead = row_copies(ranks, n_head, following, mom, grad, next_mom, next_grad, sems.at[1])
    if is_first:
        b_lo, b_hi = refs.pop(), refs.pop()
        total, out = refs.pop(), refs.pop()
        mom_in = total
        copies = row_copies(ranks, n_head, part, mom, grad, mom_in, grad_in, sems.at[0])
        fetch = pltpu.make_async_copy(ins[0], right, right_sem)
        start_all(copies[:1])
        fetch.start()
        start_all(copies[1:])
        fetch.wait()
        hi, lo = halves(right[...])
        b_hi[...] = hi
        b_lo[...] = lo
    else:
        total, out = refs.pop(), refs.pop()
        b_hi, b_lo, mom_in, grad_in = ins
        copies = [[]] * number
        start_all(ahead)
    chunk = total.shape[0] // number
    for i in range(number):
        for c in copies[i]:
            c.wait()
        if is_first and i == 0:
            start_all(ahead)
        rows = slice(i * chunk, (i + 1) * chunk)
        t = mom_in[rows, :] + grad_in[rows, :].astype(F32)
        total[rows, :] = t
        t_hi, t_lo = halves(t)
        acc = mm(t_hi, b_hi[...]) + (mm(t_hi, b_lo[...]) + mm(t_lo, b_hi[...]))
        out[rows, :] = acc.astype(out.dtype)
    for row in ahead:
        for c in row:
            c.wait()


def project(
    ranks, momentum, grad_q, ins, part, following, n_resp, n_head, dtype, after, weight=0
):
    is_first = len(ins) == 1
    rows, cols = momentum.shape
    chunk = rows // (n_resp * n_head)
    size = part[2] * chunk
    if is_first:
        right = ins[0]
        rank = right.shape[1]
        specs = [HBM]
    else:
        rank = ins[0].shape[1]
        specs = [VMEM] * 4
    out_shape = [jax.ShapeDtypeStruct((size, rank), dtype), jax.ShapeDtypeStruct((size, cols), F32)]
    if is_first:
        out_shape += [jax.ShapeDtypeStruct((cols, rank), BF16)] * 2
    if following:
        ahead = following[2] * chunk
        out_shape += [
            jax.ShapeDtypeStruct((ahead, cols), F32), jax.ShapeDtypeStruct((ahead, cols), BF16)
        ]
    scratch = [pltpu.SemaphoreType.DMA((2, 2, 2 * n_head))]
    if is_first:
        scratch = [
            pltpu.VMEM((size, cols), BF16), pltpu.VMEM((cols, rank), F32), pltpu.SemaphoreType.DMA
        ] + scratch
    outs = pl.pallas_call(
        functools.partial(project_kernel, n_head, part, following, is_first, len(ins)),
        in_specs=[SMEM, HBM, HBM] + specs + [ANY] * len(after),
        out_specs=[VMEM] * len(out_shape),
        scratch_shapes=scratch,
        out_shape=out_shape,
        compiler_params=params(14),
        name="project",
        cost_estimate=cost(weight),
    )(ranks, momentum, grad_q, *ins, *after)
    right = tuple(outs[2:4]) if is_first else tuple(ins[:2])
    return outs[0], outs[1], right + tuple(outs[-2:] if following else ())


def split_kernel(n_recv, number, own, *refs):
    recvs, outs = refs[:n_recv], refs[-number:]
    chunk = outs[0].shape[0]
    for i in range(number):
        rows = slice(i * chunk, (i + 1) * chunk)
        acc = own[rows, :]
        for r in recvs:
            acc = acc + r[rows, :].astype(F32)
        outs[i][...] = acc.astype(outs[i].dtype)


def split_sum(own, recvs, first, number):
    rows, rank = own.shape
    chunk = rows // number
    return pl.pallas_call(
        functools.partial(split_kernel, len(recvs), number),
        in_specs=[VMEM] * (1 + len(recvs)),
        out_specs=[VMEM] * number,
        out_shape=[
            jax.ShapeDtypeStruct((chunk, rank), BF16 if first + i else F32)
            for i in range(number)
        ],
        compiler_params=params(),
        name="split_sum",
        cost_estimate=cost(),
    )(own, *recvs)


def sum_kernel(n_parts, *refs):
    acc = refs[0][...].astype(F32)
    for r in refs[1:n_parts]:
        acc = acc + r[...].astype(F32)
    refs[-1][...] = acc.astype(refs[-1].dtype)


def sum_parts(parts, dtype, after=(), weight=0):
    shape = parts[0].shape
    return pl.pallas_call(
        functools.partial(sum_kernel, len(parts)),
        in_specs=[VMEM] * len(parts) + [ANY] * len(after),
        out_specs=VMEM,
        out_shape=jax.ShapeDtypeStruct(shape, dtype),
        compiler_params=params(),
        name="sum_parts",
        cost_estimate=cost(weight),
    )(*parts, *after)


def relay_kernel(n_parts, *refs):
    out = refs[-1]
    size = out.shape[0] // n_parts
    for i in range(n_parts):
        out[i * size : (i + 1) * size, :] = refs[i][...]


def relay(parts, after):
    rows, rank = parts[0].shape
    return pl.pallas_call(
        functools.partial(relay_kernel, len(parts)),
        in_specs=[VMEM] * len(parts) + [ANY] * len(after),
        out_specs=VMEM,
        out_shape=jax.ShapeDtypeStruct((len(parts) * rows, rank), parts[0].dtype),
        compiler_params=params(),
        name="relay",
        cost_estimate=cost(),
    )(*parts, *after)


def gram_kernel(n_chunks, *refs):
    chunks, (pcat, pcat_t, gram) = refs[:n_chunks], refs[-3:]
    at = 0
    for c in chunks:
        pcat[at : at + c.shape[0], :] = c[...]
        at += c.shape[0]
    p = pcat[...]
    pt = p.T
    pcat_t[...] = pt
    half = p.shape[1] // 2
    gram[:half, :] = mm(pt[:half, :], p[:, :half])
    low = mm(pt[half:, :], p)
    gram[half : 2 * half, :] = low[:, :half]
    gram[2 * half :, :] = low[:, half:]


def gather_gram(chunks, after):
    rank = chunks[0].shape[1]
    rows = sum(c.shape[0] for c in chunks)
    return pl.pallas_call(
        functools.partial(gram_kernel, len(chunks)),
        in_specs=[VMEM] * len(chunks) + [ANY] * len(after),
        out_specs=[VMEM] * 3,
        out_shape=[
            jax.ShapeDtypeStruct((rows, rank), BF16),
            jax.ShapeDtypeStruct((rank, rows), BF16),
            jax.ShapeDtypeStruct((3 * rank // 2, rank // 2), F32),
        ],
        compiler_params=params(8),
        name="gather_gram",
        cost_estimate=cost(),
    )(*chunks, *after)


def back_part_kernel(n_totals, pcat_t, *refs):
    totals, out = refs[:n_totals], refs[-1]
    seg = totals[0].shape[0]
    step = min(seg, 512)
    acc = None
    for j, total in enumerate(totals):
        for i in range(0, seg, step):
            t_hi, t_lo = halves(total[i : i + step, :])
            pt = pcat_t[:, j * seg + i : j * seg + i + step]
            part = mm(pt, t_hi) + mm(pt, t_lo)
            acc = part if acc is None else acc + part
    out[...] = acc.astype(BF16)


def back_part(pcat_t, totals, after):
    rank = pcat_t.shape[0]
    seg, cols = totals[0].shape
    rows = seg * len(totals)
    return pl.pallas_call(
        functools.partial(back_part_kernel, len(totals)),
        in_specs=[VMEM] * (1 + len(totals)) + [ANY] * len(after),
        out_specs=VMEM,
        out_shape=jax.ShapeDtypeStruct((rank, cols), BF16),
        compiler_params=params(14),
        name="back_part",
        cost_estimate=cost(5),
    )(pcat_t, *totals, *after)


def factor_panel(panel, off):
    shape = (PANEL, 128)
    d = {}
    for j in range(PANEL):
        col = jnp.broadcast_to(panel[:, off + j : off + j + 1], shape)
        for i in range(j, PANEL):
            d[i, j] = jnp.broadcast_to(col[i : i + 1, :], shape)
    low, inv = {}, {}
    for j in range(0, PANEL, 2):
        a, b, c = d[j, j], d[j + 1, j], d[j + 1, j + 1]
        first = lax.rsqrt(a)
        second = lax.rsqrt(a * c - b * b) * (a * first)
        inv[j, j], inv[j + 1, j + 1] = first, second
        low[j + 1, j] = b * first
        for i in range(j + 2, PANEL):
            low[i, j] = d[i, j] * first
            low[i, j + 1] = (d[i, j + 1] - low[i, j] * low[j + 1, j]) * second
        for k in range(j + 2, PANEL):
            for i in range(k, PANEL):
                d[i, k] = d[i, k] - (low[i, j] * low[k, j] + low[i, j + 1] * low[k, j + 1])
    for j in range(PANEL):
        for i in range(j + 1, PANEL):
            acc = low[i, j] * inv[j, j]
            for k in range(j + 1, i):
                acc = acc + low[i, k] * inv[k, j]
            inv[i, j] = -(acc * inv[i, i])
    return inv


def three_parts(x):
    a = x.astype(BF16)
    rest = x - a.astype(F32)
    b = rest.astype(BF16)
    return a, b, (rest - b.astype(F32)).astype(BF16)


def cholesky_kernel(n_parts, *refs):
    parts, out, work = refs[:n_parts], refs[n_parts], refs[n_parts + 1]
    n = out.shape[0]
    half = n // 2
    tiles = n // 128 + 1
    total = parts[0][...]
    for part in parts[1:]:
        total = total + part[...]
    low = total[half : 2 * half, :]
    work[:half, :half] = total[:half, :]
    work[half:, :half] = low
    work[:half, half:] = low.T
    work[half:, half:] = total[2 * half :, :]
    eye = lax.broadcasted_iota(jnp.int32, (n, n), 0) == lax.broadcasted_iota(jnp.int32, (n, n), 1)
    whole = work[...]
    diag = jnp.where(eye, whole, 0.0)
    across = lax.rsqrt(jnp.sum(diag, axis=0, keepdims=True))
    work[...] = whole * lax.rsqrt(jnp.sum(diag, axis=1, keepdims=True)) * across
    sub = lax.broadcasted_iota(jnp.int32, (PANEL, 128), 0)
    lane = lax.broadcasted_iota(jnp.int32, (PANEL, 128), 1)
    n_panels = OUTER // PANEL

    def step(o, carry):
        blk = [
            [work[p * PANEL : (p + 1) * PANEL, t * 128 : (t + 1) * 128] for t in range(tiles - 1)]
            + [jnp.where(lane == sub + p * PANEL, 1.0, 0.0).astype(F32)]
            for p in range(n_panels)
        ]
        for p in range(n_panels):
            off = p * PANEL
            inv = factor_panel(blk[p][0], off)
            rows_of = [
                [jnp.broadcast_to(blk[p][t][j : j + 1, :], (PANEL, 128)) for t in range(tiles)]
                for j in range(PANEL)
            ]
            new = [None] * tiles
            for j in range(PANEL):
                col = inv[PANEL - 1, j]
                for i in range(PANEL - 2, j - 1, -1):
                    col = jnp.where(sub == i, inv[i, j], col)
                if j:
                    col = jnp.where(sub < j, 0.0, col)
                for t in range(tiles):
                    term = col * rows_of[j][t]
                    new[t] = term if new[t] is None else new[t] + term
            blk[p] = new
            if p + 1 < n_panels:
                u_rows = [
                    [jnp.broadcast_to(new[t][j : j + 1, :], (PANEL, 128)) for t in range(tiles)]
                    for j in range(PANEL)
                ]
                for b in range(p + 1, n_panels):
                    lanes = [
                        jnp.broadcast_to(blk[b][0][:, off + m : off + m + 1], (PANEL, 128))
                        for m in range(PANEL)
                    ]
                    upd = list(blk[b])
                    for k in range(PANEL):
                        v = lanes[0] * inv[k, 0]
                        for m in range(1, k + 1):
                            v = v + lanes[m] * inv[k, m]
                        for t in range(tiles):
                            upd[t] = upd[t] - v * u_rows[k][t]
                    blk[b] = upd
        u = jnp.concatenate([jnp.concatenate(row, axis=1) for row in blk], axis=0)
        u = pltpu.roll(u, tiles * 128 - OUTER, 1)[:, :n]
        at = lax.broadcasted_iota(jnp.int32, (OUTER, n), 1)
        left = jnp.where(at < n - OUTER * (o + 1), u, 0.0)
        la, lb, lc = three_parts(left)
        ua, ub, uc = three_parts(u)
        lhs = jnp.concatenate([la, la, lb, la, lc, lb], axis=0)
        rhs = jnp.concatenate([ua, ub, ua, uc, ua, ub], axis=0)
        upd = mm(lhs.T, rhs)
        rest = work[OUTER:, :]
        lanes_at = lax.broadcasted_iota(jnp.int32, rest.shape, 1)
        rest = pltpu.roll(jnp.where(lanes_at < OUTER, 0.0, rest), n - OUTER, 1)
        work[: n - OUTER, :] = rest - upd[: n - OUTER, :]
        work[n - OUTER :, :] = u
        return carry

    lax.fori_loop(0, n // OUTER, step, 0)
    out[...] = work[...] * across


def inverse_factor(*parts):
    n = 2 * parts[0].shape[1]
    return pl.pallas_call(
        functools.partial(cholesky_kernel, len(parts)),
        in_specs=[VMEM] * len(parts),
        out_specs=VMEM,
        scratch_shapes=[pltpu.VMEM((n, n), F32)],
        out_shape=jax.ShapeDtypeStruct((n, n), F32),
        compiler_params=params(),
        name="inverse_factor",
        cost_estimate=cost(2),
    )(*parts)


def mm_three(a, b):
    a_hi, a_lo = halves(a)
    b_hi, b_lo = halves(b)
    return mm(a_hi, b_hi) + (mm(a_hi, b_lo) + mm(a_lo, b_hi))


def back_kernel(x, wa, wb, *refs):
    bt_out, y_out, s_out = refs[-3:]
    w = wa[...].astype(F32) + wb[...].astype(F32)
    bt = mm_three(x[...], w)
    bt_out[...] = bt
    s = jnp.sum(bt * bt, axis=1, keepdims=True)
    s_out[...] = jnp.broadcast_to(s, (s.shape[0], 128)).T[:8, :]
    y_out[...] = ((1.0 - momentum_keep) * mm(x[...].T.astype(BF16), bt.astype(BF16))).astype(BF16)


def back_full(x, wa, wb, after):
    rank, cols = wa.shape
    return pl.pallas_call(
        back_kernel,
        in_specs=[VMEM] * 3 + [ANY] * len(after),
        out_specs=[VMEM] * 3,
        out_shape=[
            jax.ShapeDtypeStruct((rank, cols), F32),
            jax.ShapeDtypeStruct((rank, cols), BF16),
            jax.ShapeDtypeStruct((8, rank), F32),
        ],
        compiler_params=params(),
        name="back_full",
        cost_estimate=cost(),
    )(x, wa, wb, *after)


def row_blocks(ranks, n_resp, n_head, chunk):
    return [
        pl.multiple_of(((ranks[0] ^ j) * n_head + (ranks[2] ^ k)) * chunk, chunk)
        for j in range(n_resp)
        for k in range(n_head)
    ]


def momentum_rows(blocks, pcat, y, totals, held, out, sems, begin, end):
    chunk = held.shape[0] // (end - begin)
    seg = totals[0].shape[0]
    copies = []
    for i in range(begin, end):
        rows = slice(i * chunk, (i + 1) * chunk)
        kept = slice((i - begin) * chunk, (i - begin + 1) * chunk)
        off = i * chunk % seg
        total = totals[(i - begin) * chunk // seg][off : off + chunk, :]
        held[kept, :] = total - mm(pcat[rows, :], y[...])
        copies.append(
            pltpu.make_async_copy(
                held.at[kept, :], out.at[pl.ds(blocks[i], chunk), :], sems.at[i - begin]
            )
        )
        copies[-1].start()
    return copies


def momentum_kernel(n_resp, n_head, n_totals, ranks, pcat, y, *refs):
    totals, refs = refs[:n_totals], refs[n_totals:]
    dq_parts, rg, refs = refs[:2], refs[2], refs[-7:]
    out, dq, resp_grad, token, held, sems, more = refs
    token[...] = jnp.zeros_like(token)
    width = dq_parts[0].shape[1]
    copies = [
        pltpu.make_async_copy(part, dq.at[:, pl.ds(i * width, width)], more.at[i])
        for i, part in enumerate(dq_parts)
    ]
    copies.append(pltpu.make_async_copy(rg, resp_grad, more.at[2]))
    n = n_resp * n_head
    blocks = row_blocks(ranks, n_resp, n_head, pcat.shape[0] // n)
    copies[2].start()
    moved = momentum_rows(blocks, pcat, y, totals, held, out, sems, 0, n // 2)
    for c in copies[:2]:
        c.start()
    for c in copies + moved:
        c.wait()


def new_momentum(ranks, pcat, totals, y, n_resp, n_head, dq_parts, rg, after):
    rows, rank = pcat.shape
    cols = totals[0].shape[1]
    length, width = dq_parts[0].shape
    return pl.pallas_call(
        functools.partial(momentum_kernel, n_resp, n_head, len(totals)),
        in_specs=[SMEM] + [VMEM] * (5 + len(totals)) + [ANY] * len(after),
        out_specs=[HBM, HBM, HBM, VMEM],
        scratch_shapes=[
            pltpu.VMEM((rows // 2, cols), F32),
            pltpu.SemaphoreType.DMA((n_resp * n_head // 2,)),
            pltpu.SemaphoreType.DMA((3,)),
        ],
        out_shape=[
            jax.ShapeDtypeStruct((rows, cols), F32),
            jax.ShapeDtypeStruct((length, 2 * width), BF16),
            jax.ShapeDtypeStruct(rg.shape, BF16),
            jax.ShapeDtypeStruct((8, 128), F32),
        ],
        compiler_params=params(12),
        name="new_momentum",
        cost_estimate=cost(5),
    )(ranks, pcat, y, *totals, *dq_parts, rg, *after)


def update_kernel(gain, n_resp, n_head, n_sums, n_totals, n_prompt, ranks, pcat, x, bt, y, *refs):
    sums, refs = refs[:n_sums], refs[n_sums:]
    totals, refs = refs[:n_totals], refs[n_totals:]
    prompts, refs = refs[:n_prompt], refs[n_prompt + 1 :]
    upd, basis_out, mom_out, prompt_out, held, held_mom, held_basis, held_prompt, sems, more = refs
    n = n_resp * n_head
    chunk = pcat.shape[0] // n
    blocks = row_blocks(ranks, n_resp, n_head, chunk)
    total = sums[0][...]
    for s in sums[1:]:
        total = total + s[...]
    scale = lax.rsqrt(total + norm_eps).T[:, :1]
    scaled = bt[...] * scale
    held_basis[...] = scaled.T
    acc = prompts[0][...]
    for p in prompts[1:]:
        acc = acc + p[...].astype(F32)
    held_prompt[...] = acc
    copies = [
        pltpu.make_async_copy(held_basis, basis_out, more.at[0]),
        pltpu.make_async_copy(held_prompt, prompt_out, more.at[1]),
    ]
    for c in copies:
        c.start()
    copies += momentum_rows(blocks, pcat, y, totals, held_mom, mom_out, sems.at[1], n // 2, n)
    z_hi, z_lo = halves(gain * mm_three(x[...].T, scaled))
    for i, at in enumerate(blocks):
        rows = slice(i * chunk, (i + 1) * chunk)
        p = pcat[rows, :]
        held[rows, :] = (mm(p, z_hi) + mm(p, z_lo)).astype(BF16)
        copies.append(
            pltpu.make_async_copy(held.at[rows, :], upd.at[pl.ds(at, chunk), :], sems.at[0, i])
        )
        copies[-1].start()
    for c in copies:
        c.wait()


def final_update(ranks, pcat, x, bt, y, sums, totals, prompts, momentum, gain, n_resp, n_head):
    rows, rank = pcat.shape
    cols = bt.shape[1]
    n_vmem = 4 + len(sums) + len(totals) + len(prompts)
    return pl.pallas_call(
        functools.partial(
            update_kernel, gain, n_resp, n_head, len(sums), len(totals), len(prompts)
        ),
        in_specs=[SMEM] + [VMEM] * n_vmem + [HBM],
        out_specs=[HBM] * 4,
        scratch_shapes=[
            pltpu.VMEM((rows, cols), BF16),
            pltpu.VMEM((rows // 2, cols), F32),
            pltpu.VMEM((cols, rank), F32),
            pltpu.VMEM(prompts[0].shape, F32),
            pltpu.SemaphoreType.DMA((2, n_resp * n_head)),
            pltpu.SemaphoreType.DMA((2,)),
        ],
        out_shape=[
            jax.ShapeDtypeStruct((rows, cols), BF16),
            jax.ShapeDtypeStruct((cols, rank), F32),
            jax.ShapeDtypeStruct((rows, cols), F32),
            jax.ShapeDtypeStruct(prompts[0].shape, F32),
        ],
        input_output_aliases={1 + n_vmem: 2},
        compiler_params=params(14),
        name="final_update",
        cost_estimate=cost(5),
    )(ranks, pcat, x, bt, y, *sums, *totals, *prompts, momentum)


def group_of(counts, response):
    group = jnp.int32(0)
    end = jnp.int32(0)
    for g in range(counts.shape[0]):
        end = end + counts[g]
        group = group + (end <= response).astype(jnp.int32)
    return group


def pack_kernel(*refs):
    keys, values, out = refs[0], refs[1], refs[-1]
    out[0] = keys[...]
    out[1] = values[...]


def pack_prompts(keys, values, after):
    return pl.pallas_call(
        pack_kernel,
        in_specs=[VMEM] * 2 + [ANY] * len(after),
        out_specs=VMEM,
        out_shape=jax.ShapeDtypeStruct((2,) + keys.shape, BF16),
        compiler_params=params(),
        name="pack_prompts",
        cost_estimate=cost(),
    )(keys, values, *after)


def select_kernel(n_resp, n_fsdp, ranks, counts, slots, *refs):
    stored, outs = refs[:n_resp], refs[-n_fsdp:]
    held = stored[0].shape[1]
    for k in range(n_fsdp):
        slot = slots[group_of(counts, ranks[0] * n_fsdp + (ranks[1] ^ k))]
        owner, local = slot // held, slot % held
        for j in range(n_resp):

            @pl.when(owner == (ranks[0] ^ j))
            def _():
                outs[k][0] = stored[j][0, local]
                outs[k][1] = stored[j][1, local]


def select_prompts(ranks, counts, slots, stored, n_fsdp, after):
    _, _, piece, width = stored[0].shape
    return pl.pallas_call(
        functools.partial(select_kernel, len(stored), n_fsdp),
        in_specs=[SMEM] * 3 + [VMEM] * len(stored) + [ANY] * len(after),
        out_specs=[VMEM] * n_fsdp,
        out_shape=[jax.ShapeDtypeStruct((2, piece, width), BF16)] * n_fsdp,
        compiler_params=params(),
        name="select_prompts",
        cost_estimate=cost(),
    )(ranks, counts, slots, *stored, *after)


def attention_kernel(
    n_fsdp, heads, last, ranks, counts, prompt_blocks, resp_blocks, q, sk, sv, go, *refs
):
    pieces, refs = refs[:n_fsdp], refs[n_fsdp:]
    keys, values, dk, dv = refs[-4:]
    n_out = 2 + n_fsdp if last else 3
    outs = refs[-4 - n_out : -4]
    dq = outs[0]
    piece = pieces[0].shape[1]
    cap = piece * n_fsdp
    length = q.shape[0]
    scale = HD ** (-0.5)
    for k in range(n_fsdp):
        rows = pl.ds(pl.multiple_of((ranks[1] ^ k) * piece, piece), piece)
        keys[rows, :] = pieces[k][0]
        values[rows, :] = pieces[k][1]
    keys[cap:, :] = sk[...]
    values[cap:, :] = sv[...]
    prompt_len = prompt_blocks[group_of(counts, ranks[0] * n_fsdp + ranks[1])] * 128
    resp_len = resp_blocks[0] * 128
    width = keys.shape[0]
    place = lax.broadcasted_iota(jnp.int32, (width, length), 0)
    pos = lax.broadcasted_iota(jnp.int32, (width, length), 1)
    inner = place - cap
    seen = ((place < cap) & (place < prompt_len)) | (
        (place >= cap) & (inner <= pos) & (inner < resp_len)
    )
    bias = jnp.where(seen, 0.0, -jnp.inf).astype(F32)
    live = lax.broadcasted_iota(jnp.int32, (length, HD), 0) < resp_len
    nt = (((1,), (1,)), ((), ()))
    kall = keys[...]
    vall = values[...]
    kt = kall.T
    if last:
        dk[...] = refs[0][...]
        dv[...] = refs[1][...]
    else:
        dk[...] = jnp.zeros_like(dk)
        dv[...] = jnp.zeros_like(dv)
    for i, h in enumerate(heads):
        cols = slice(h * HD, (h + 1) * HD)
        qh = q[:, cols]
        gh = jnp.where(live, go[:, cols], jnp.zeros((), BF16))
        logits = lax.dot_general(kall, qh, nt, preferred_element_type=F32) * scale + bias
        peak = jnp.max(logits, axis=0, keepdims=True)
        e = jnp.exp(logits - peak)
        w = (e * (1.0 / jnp.sum(e, axis=0, keepdims=True))).astype(BF16)
        dp = lax.dot_general(vall, gh, nt, preferred_element_type=F32)
        wf = w.astype(F32)
        diag = jnp.sum(wf * dp, axis=0, keepdims=True)
        ds = (wf * (dp - diag)).astype(BF16)
        dk[...] += mm(ds, qh)
        dv[...] += mm(w, gh)
        dq[:, i * HD : (i + 1) * HD] = (mm(kt, ds) * scale).T.astype(BF16)
    if last:
        own, sends = outs[1], outs[2:]
        own[0] = (dk[cap:, :] * scale).astype(BF16)
        own[1] = dv[cap:, :].astype(BF16)
        for k in range(n_fsdp):
            rows = pl.ds(pl.multiple_of((ranks[1] ^ k) * piece, piece), piece)
            sends[k][0] = (dk[rows, :] * scale).astype(sends[k].dtype)
            sends[k][1] = dv[rows, :].astype(sends[k].dtype)
    else:
        outs[1][...] = dk[...]
        outs[2][...] = dv[...]


def attention(heads, earlier, ranks, counts, prompt_blocks, resp_blocks, q, sk, sv, go, pieces, after):
    n_fsdp = len(pieces)
    piece = pieces[0].shape[1]
    length, width = q.shape
    cap = piece * n_fsdp
    total = cap + length
    last = earlier is not None
    dq_shape = jax.ShapeDtypeStruct((length, len(heads) * HD), BF16)
    if last:
        extra, specs = (earlier[1], earlier[2]), [VMEM] * 2
        out_shape = [dq_shape, jax.ShapeDtypeStruct((2, length, HD), BF16)] + [
            jax.ShapeDtypeStruct((2, piece, HD), BF16 if k else F32) for k in range(n_fsdp)
        ]
    else:
        extra, specs = (), []
        out_shape = [dq_shape] + [jax.ShapeDtypeStruct((total, HD), F32)] * 2
    return pl.pallas_call(
        functools.partial(attention_kernel, n_fsdp, heads, last),
        in_specs=[SMEM] * 4 + [VMEM] * (4 + n_fsdp) + specs + [ANY] * len(after),
        out_specs=[VMEM] * len(out_shape),
        scratch_shapes=[pltpu.VMEM((total, HD), BF16)] * 2 + [pltpu.VMEM((total, HD), F32)] * 2,
        out_shape=out_shape,
        compiler_params=params(12),
        name="attention",
        cost_estimate=cost(),
    )(ranks, counts, prompt_blocks, resp_blocks, q, sk, sv, go, *pieces, *extra, *after)


def by_slot_kernel(n_resp, n_fsdp, ranks, counts, slots, *refs):
    parts, outs = refs[:n_fsdp], refs[-n_resp:]
    held = outs[0].shape[1]
    slot_of = [
        slots[group_of(counts, ranks[0] * n_fsdp + (ranks[1] ^ k))] for k in range(n_fsdp)
    ]
    for j in range(n_resp):
        for local in range(held):
            slot = (ranks[0] ^ j) * held + local
            acc = jnp.zeros(parts[0].shape, F32)
            for k in range(n_fsdp):
                acc = acc + jnp.where(slot_of[k] == slot, parts[k][...].astype(F32), 0.0)
            outs[j][:, local] = acc.astype(outs[j].dtype)


def sum_by_slot(ranks, counts, slots, parts, n_resp, after):
    held = counts.shape[0] // n_resp
    _, piece, width = parts[0].shape
    return pl.pallas_call(
        functools.partial(by_slot_kernel, n_resp, len(parts)),
        in_specs=[SMEM] * 3 + [VMEM] * len(parts) + [ANY] * len(after),
        out_specs=[VMEM] * n_resp,
        out_shape=[
            jax.ShapeDtypeStruct((2, held, piece, width), BF16 if j else F32)
            for j in range(n_resp)
        ],
        compiler_params=params(),
        name="sum_by_slot",
        cost_estimate=cost(),
    )(ranks, counts, slots, *parts, *after)


def on_device(
    queries,
    self_keys,
    self_values,
    d_out,
    prompt_keys,
    prompt_values,
    counts,
    owner_slot,
    prompt_blocks,
    resp_blocks,
    grad_q,
    momentum,
    basis,
):
    n_resp, n_fsdp, n_head = (lax.axis_size(a) for a in ("resp", "fsdp", "head"))
    ranks = jnp.stack([lax.axis_index(a) for a in ("resp", "fsdp", "head")]).astype(jnp.int32)
    gain = math.sqrt(
        momentum.shape[0] * n_fsdp * momentum.shape[1] * n_resp * n_head / basis.shape[1]
    )

    in_hbm = [pltpu.with_memory_space_constraint(a, pltpu.HBM) for a in (momentum, grad_q, basis)]
    half = n_head // 2
    groups = [(half, half), (0, half)] if half else [(0, n_head)]

    mom_hbm, grad_hbm, basis_hbm = in_hbm
    order = [(j, *group) for group in groups for j in [*range(1, n_resp), 0]]
    nexts = dict(zip(order, order[1:] + [None]))
    totals, arrived, split, ins, after = {}, {}, {}, (basis_hbm,), ()
    for part in order:
        j, first, number = part
        value, totals[part[:2]], ins = project(
            ranks, mom_hbm, grad_hbm, ins, part, nexts[part], n_resp, n_head, BF16 if j else F32,
            after, 0 if j or first == 0 else 10,
        )
        after = ()
        if j:
            arrived.setdefault(first, []).append(swap(value, "resp", j))
            if part[1:] == groups[-1] and j == n_resp - 1:
                packed = pack_prompts(prompt_keys, prompt_values, (value,))
                stored = [packed] + [swap(packed, "resp", k) for k in range(1, n_resp)]
                outs = split_sum(owned, arrived[groups[0][0]], *groups[0])
                for i in range(groups[0][1]):
                    split[groups[0][0] + i] = outs[i]
                after = (outs[0],)
        elif part[1:] == groups[0] and len(groups) > 1:
            owned = value
        else:
            outs = split_sum(value, arrived[first], first, number)
            for i in range(number):
                split[first + i] = outs[i]
    totals = [totals[at] for at in sorted(totals)]
    chosen = select_prompts(
        ranks, counts, owner_slot, stored, n_fsdp, (split[1 % n_head],)
    )
    far_first = [k for first, number in groups for k in range(first, first + number) if k]
    summands = {k: swap(split[k], "head", k) for k in far_first}
    pieces = [chosen[0]] + [swap(chosen[k], "fsdp", k) for k in range(1, n_fsdp)]
    later = groups[-1][1] if len(groups) > 1 else 1
    far = sum_parts(
        [split[0]] + [summands[k] for k in range(later, n_head)], F32, (), 10
    )
    piece0 = sum_parts(
        [far] + [summands[k] for k in range(1, later)], BF16, tuple(pieces[1:])
    )

    along = {0: piece0}
    for k in range(1, later):
        along[k] = swap(piece0, "head", k)
    held_back = relay([piece0], (along[max(1, later) - 1],))
    for k in range(later, n_head):
        along[k] = swap(held_back if k > later else piece0, "head", k)

    n_q = queries.shape[1] // HD
    heads = [list(range(n_q // 2)), list(range(n_q // 2, n_q))]
    held = (
        ranks, counts, prompt_blocks, resp_blocks, queries, self_keys, self_values, d_out, pieces
    )
    last = n_head - 1
    earlier = attention(heads[0], None, *held, (along[max(1, later) - 1],))
    passed = [[swap(along[k], "resp", j) for k in range(later)] for j in range(1, n_resp)]
    before = (earlier[1], *[c for row in passed for c in row])
    mid = [relay([along[k]], before) for k in range(later, last)]
    for j in range(1, n_resp):
        passed[j - 1] += [swap(c, "resp", j) for c in mid]
    sent_last = relay([along[last]], (*before, *mid))
    chunks = [along[k] for k in range(n_head)]
    for j in range(1, n_resp):
        chunks += passed[j - 1] + [swap(sent_last, "resp", j)]
    dq_parts, resp_grad, *parts = attention(
        heads[1], earlier, *held, (sent_last, *[c for row in passed for c in row[later:]])
    )
    dq_parts = (earlier[0], dq_parts)
    pcat, pcat_t, gram = gather_gram(chunks, (parts[0],))

    bits = [1 << b for b in range(n_fsdp.bit_length() - 1)]
    w = back_part(pcat_t, totals, (gram,))
    for bit in bits[:-1]:
        gram = sum_parts([gram, swap(gram, "fsdp", bit)], F32, (), 3)
    gram_parts = (gram, swap(gram, "fsdp", bits[-1]))
    for bit in bits[:-1]:
        w = sum_parts([w, swap(w, "fsdp", bit)], BF16, (gram,), 5)
    w_other = swap(w, "fsdp", bits[-1])
    returned = [parts[0]] + [swap(parts[k], "fsdp", k) for k in range(1, n_fsdp)]
    x = inverse_factor(*gram_parts)
    bt, y, squares = back_full(x, w, w_other, tuple(returned[1:]))
    from_head = [swap(squares, "head", k) for k in range(1, n_head)]
    half = len(totals) // 2
    slots = sum_by_slot(ranks, counts, owner_slot, returned, n_resp, (squares,))
    prompts = [slots[0]] + [swap(slots[j], "resp", j) for j in range(1, n_resp)]
    squares = sum_parts([squares] + from_head, F32, (slots[-1],))
    sums = sum_parts(
        [squares] + [swap(squares, "resp", j) for j in range(1, n_resp)], F32
    )
    momentum_out, dq, resp_grad, _ = new_momentum(
        ranks, pcat, totals[:half], y, n_resp, n_head, dq_parts, resp_grad, (squares,)
    )
    update, basis_out, momentum_out, prompt_grad = final_update(
        ranks, pcat, x, bt, y, [sums], totals[half:], prompts, momentum_out, gain, n_resp, n_head
    )
    return (dq, resp_grad, prompt_grad, update, momentum_out, basis_out)


def solution(mesh):
    placed = (
        P(("resp", "fsdp"), "head"),
        P(("resp", "fsdp"), "head"),
        P(("resp", "fsdp"), "head"),
        P(("resp", "fsdp"), "head"),
        P("resp", "fsdp", "head"),
        P("resp", "fsdp", "head"),
        P(),
        P(),
        P(),
        P(("resp", "fsdp")),
        P("fsdp", ("resp", "head")),
        P("fsdp", ("resp", "head")),
        P(("resp", "head"), None),
    )
    return jax.shard_map(
        on_device,
        mesh=mesh,
        in_specs=placed,
        out_specs=(
            P(("resp", "fsdp"), "head"),
            P(None, ("resp", "fsdp"), "head"),
            P(None, "resp", "fsdp", "head"),
            P("fsdp", ("resp", "head")),
            P("fsdp", ("resp", "head")),
            P(("resp", "head"), None),
        ),
        check_vma=False,
    )
```

```python
import functools
import math

import jax
import jax.numpy as jnp
from jax import lax
from jax.experimental import pallas as pl
from jax.experimental.pallas import tpu as pltpu
from jax.sharding import PartitionSpec as P

HD = 128
PANEL = 8
OUTER = 32
MIB = 1 << 20

momentum_keep = 0.95
norm_eps = 1e-06

F32 = jnp.float32
BF16 = jnp.bfloat16
HIGHEST = lax.Precision.HIGHEST

SMEM = pl.BlockSpec(memory_space=pltpu.SMEM)
VMEM = pl.BlockSpec(memory_space=pltpu.VMEM)
ANY = pl.BlockSpec(memory_space=pl.ANY)
HBM = pl.BlockSpec(memory_space=pltpu.HBM)


def swap(value, axes, k):
    axes = (axes,) if isinstance(axes, str) else axes
    n = math.prod(lax.axis_size(a) for a in axes)
    return lax.ppermute(value, axes, [(i, i ^ k) for i in range(n)])


def params(mib=6):
    return pltpu.CompilerParams(vmem_limit_bytes=mib * MIB)


def cost(weight=0):
    return pl.CostEstimate(flops=1 + weight * 10**9, bytes_accessed=1, transcendentals=0)


def halves(x):
    hi = x.astype(BF16)
    return hi, (x - hi.astype(F32)).astype(BF16)


def mm(a, b):
    return jnp.dot(a, b, preferred_element_type=F32)


def mm_full(a, b):
    return jnp.dot(a, b, precision=HIGHEST, preferred_element_type=F32)


def row_copies(ranks, n_head, part, mom, grad, mom_to, grad_to, sems):
    j, first, number = part
    chunk = mom_to.shape[0] // number
    pieces = 2 if chunk % 32 == 0 else 1
    size = chunk // pieces
    copies = []
    for i in range(number):
        at = ((ranks[0] ^ j) * n_head + (ranks[2] ^ (first + i))) * chunk
        copies.append([])
        for p in range(pieces):
            src = pl.ds(pl.multiple_of(at + p * size, size), size)
            dst = pl.ds(i * chunk + p * size, size)
            n = i * pieces + p
            copies[i].append(pltpu.make_async_copy(mom.at[src, :], mom_to.at[dst, :], sems.at[0, n]))
            copies[i].append(
                pltpu.make_async_copy(grad.at[src, :], grad_to.at[dst, :], sems.at[1, n])
            )
    return copies


def start_all(copies):
    for row in copies:
        for c in row:
            c.start()


def project_kernel(n_head, part, following, is_first, n_in, ranks, mom, grad, *refs):
    ins, refs = refs[:n_in], list(refs)
    number = part[2]
    sems = refs.pop()
    ahead = []
    if is_first:
        right_sem, right, grad_in = refs.pop(), refs.pop(), refs.pop()
    if following:
        next_grad, next_mom = refs.pop(), refs.pop()
        ahead = row_copies(ranks, n_head, following, mom, grad, next_mom, next_grad, sems.at[1])
    if is_first:
        b_lo, b_hi = refs.pop(), refs.pop()
        total, out = refs.pop(), refs.pop()
        mom_in = total
        copies = row_copies(ranks, n_head, part, mom, grad, mom_in, grad_in, sems.at[0])
        fetch = pltpu.make_async_copy(ins[0], right, right_sem)
        start_all(copies[:1])
        fetch.start()
        start_all(copies[1:])
        fetch.wait()
        hi, lo = halves(right[...])
        b_hi[...] = hi
        b_lo[...] = lo
    else:
        total, out = refs.pop(), refs.pop()
        b_hi, b_lo, mom_in, grad_in = ins
        copies = [[]] * number
        start_all(ahead)
    chunk = total.shape[0] // number
    for i in range(number):
        for c in copies[i]:
            c.wait()
        if is_first and i == 0:
            start_all(ahead)
        rows = slice(i * chunk, (i + 1) * chunk)
        t = mom_in[rows, :] + grad_in[rows, :].astype(F32)
        total[rows, :] = t
        t_hi, t_lo = halves(t)
        acc = mm(t_hi, b_hi[...]) + (mm(t_hi, b_lo[...]) + mm(t_lo, b_hi[...]))
        out[rows, :] = acc.astype(out.dtype)
    for row in ahead:
        for c in row:
            c.wait()


def project(
    ranks, momentum, grad_q, ins, part, following, n_resp, n_head, dtype, after, weight=0
):
    is_first = len(ins) == 1
    rows, cols = momentum.shape
    chunk = rows // (n_resp * n_head)
    size = part[2] * chunk
    if is_first:
        right = ins[0]
        rank = right.shape[1]
        specs = [HBM]
    else:
        rank = ins[0].shape[1]
        specs = [VMEM] * 4
    out_shape = [jax.ShapeDtypeStruct((size, rank), dtype), jax.ShapeDtypeStruct((size, cols), F32)]
    if is_first:
        out_shape += [jax.ShapeDtypeStruct((cols, rank), BF16)] * 2
    if following:
        ahead = following[2] * chunk
        out_shape += [
            jax.ShapeDtypeStruct((ahead, cols), F32), jax.ShapeDtypeStruct((ahead, cols), BF16)
        ]
    scratch = [pltpu.SemaphoreType.DMA((2, 2, 2 * n_head))]
    if is_first:
        scratch = [
            pltpu.VMEM((size, cols), BF16), pltpu.VMEM((cols, rank), F32), pltpu.SemaphoreType.DMA
        ] + scratch
    outs = pl.pallas_call(
        functools.partial(project_kernel, n_head, part, following, is_first, len(ins)),
        in_specs=[SMEM, HBM, HBM] + specs + [ANY] * len(after),
        out_specs=[VMEM] * len(out_shape),
        scratch_shapes=scratch,
        out_shape=out_shape,
        compiler_params=params(14),
        name="project",
        cost_estimate=cost(weight),
    )(ranks, momentum, grad_q, *ins, *after)
    right = tuple(outs[2:4]) if is_first else tuple(ins[:2])
    return outs[0], outs[1], right + tuple(outs[-2:] if following else ())


def split_kernel(n_recv, number, own, *refs):
    recvs, outs = refs[:n_recv], refs[-number:]
    chunk = outs[0].shape[0]
    for i in range(number):
        rows = slice(i * chunk, (i + 1) * chunk)
        acc = own[rows, :]
        for r in recvs:
            acc = acc + r[rows, :].astype(F32)
        outs[i][...] = acc.astype(outs[i].dtype)


def split_sum(own, recvs, first, number):
    rows, rank = own.shape
    chunk = rows // number
    return pl.pallas_call(
        functools.partial(split_kernel, len(recvs), number),
        in_specs=[VMEM] * (1 + len(recvs)),
        out_specs=[VMEM] * number,
        out_shape=[
            jax.ShapeDtypeStruct((chunk, rank), BF16 if first + i else F32)
            for i in range(number)
        ],
        compiler_params=params(),
        name="split_sum",
        cost_estimate=cost(),
    )(own, *recvs)


def sum_kernel(n_parts, *refs):
    acc = refs[0][...].astype(F32)
    for r in refs[1:n_parts]:
        acc = acc + r[...].astype(F32)
    refs[-1][...] = acc.astype(refs[-1].dtype)


def sum_parts(parts, dtype, after=(), weight=0):
    shape = parts[0].shape
    return pl.pallas_call(
        functools.partial(sum_kernel, len(parts)),
        in_specs=[VMEM] * len(parts) + [ANY] * len(after),
        out_specs=VMEM,
        out_shape=jax.ShapeDtypeStruct(shape, dtype),
        compiler_params=params(),
        name="sum_parts",
        cost_estimate=cost(weight),
    )(*parts, *after)


def relay_kernel(n_parts, *refs):
    out = refs[-1]
    size = out.shape[0] // n_parts
    for i in range(n_parts):
        out[i * size : (i + 1) * size, :] = refs[i][...]


def relay(parts, after):
    rows, rank = parts[0].shape
    return pl.pallas_call(
        functools.partial(relay_kernel, len(parts)),
        in_specs=[VMEM] * len(parts) + [ANY] * len(after),
        out_specs=VMEM,
        out_shape=jax.ShapeDtypeStruct((len(parts) * rows, rank), parts[0].dtype),
        compiler_params=params(),
        name="relay",
        cost_estimate=cost(),
    )(*parts, *after)


def gram_kernel(n_chunks, *refs):
    chunks, (pcat, pcat_t, gram) = refs[:n_chunks], refs[-3:]
    at = 0
    for c in chunks:
        pcat[at : at + c.shape[0], :] = c[...]
        at += c.shape[0]
    p = pcat[...]
    pt = p.T
    pcat_t[...] = pt
    half = p.shape[1] // 2
    gram[:half, :] = mm(pt[:half, :], p[:, :half])
    low = mm(pt[half:, :], p)
    gram[half : 2 * half, :] = low[:, :half]
    gram[2 * half :, :] = low[:, half:]


def gather_gram(chunks, after):
    rank = chunks[0].shape[1]
    rows = sum(c.shape[0] for c in chunks)
    return pl.pallas_call(
        functools.partial(gram_kernel, len(chunks)),
        in_specs=[VMEM] * len(chunks) + [ANY] * len(after),
        out_specs=[VMEM] * 3,
        out_shape=[
            jax.ShapeDtypeStruct((rows, rank), BF16),
            jax.ShapeDtypeStruct((rank, rows), BF16),
            jax.ShapeDtypeStruct((3 * rank // 2, rank // 2), F32),
        ],
        compiler_params=params(8),
        name="gather_gram",
        cost_estimate=cost(),
    )(*chunks, *after)


def back_part_kernel(n_totals, pcat_t, *refs):
    totals, out = refs[:n_totals], refs[-1]
    seg = totals[0].shape[0]
    step = min(seg, 512)
    acc = None
    for j, total in enumerate(totals):
        for i in range(0, seg, step):
            t_hi, t_lo = halves(total[i : i + step, :])
            pt = pcat_t[:, j * seg + i : j * seg + i + step]
            part = mm(pt, t_hi) + mm(pt, t_lo)
            acc = part if acc is None else acc + part
    out[...] = acc.astype(BF16)


def back_part(pcat_t, totals, after):
    rank = pcat_t.shape[0]
    seg, cols = totals[0].shape
    rows = seg * len(totals)
    return pl.pallas_call(
        functools.partial(back_part_kernel, len(totals)),
        in_specs=[VMEM] * (1 + len(totals)) + [ANY] * len(after),
        out_specs=VMEM,
        out_shape=jax.ShapeDtypeStruct((rank, cols), BF16),
        compiler_params=params(14),
        name="back_part",
        cost_estimate=cost(5),
    )(pcat_t, *totals, *after)


def factor_panel(panel, off):
    shape = (PANEL, 128)
    d = {}
    for j in range(PANEL):
        col = jnp.broadcast_to(panel[:, off + j : off + j + 1], shape)
        for i in range(j, PANEL):
            d[i, j] = jnp.broadcast_to(col[i : i + 1, :], shape)
    low, inv = {}, {}
    for j in range(0, PANEL, 2):
        a, b, c = d[j, j], d[j + 1, j], d[j + 1, j + 1]
        first = lax.rsqrt(a)
        second = lax.rsqrt(a * c - b * b) * (a * first)
        inv[j, j], inv[j + 1, j + 1] = first, second
        low[j + 1, j] = b * first
        for i in range(j + 2, PANEL):
            low[i, j] = d[i, j] * first
            low[i, j + 1] = (d[i, j + 1] - low[i, j] * low[j + 1, j]) * second
        for k in range(j + 2, PANEL):
            for i in range(k, PANEL):
                d[i, k] = d[i, k] - (low[i, j] * low[k, j] + low[i, j + 1] * low[k, j + 1])
    for j in range(PANEL):
        for i in range(j + 1, PANEL):
            acc = low[i, j] * inv[j, j]
            for k in range(j + 1, i):
                acc = acc + low[i, k] * inv[k, j]
            inv[i, j] = -(acc * inv[i, i])
    return inv


def three_parts(x):
    a = x.astype(BF16)
    rest = x - a.astype(F32)
    b = rest.astype(BF16)
    return a, b, (rest - b.astype(F32)).astype(BF16)


def cholesky_kernel(n_parts, *refs):
    parts, out, work = refs[:n_parts], refs[n_parts], refs[n_parts + 1]
    n = out.shape[0]
    half = n // 2
    tiles = n // 128 + 1
    total = parts[0][...]
    for part in parts[1:]:
        total = total + part[...]
    low = total[half : 2 * half, :]
    work[:half, :half] = total[:half, :]
    work[half:, :half] = low
    work[:half, half:] = low.T
    work[half:, half:] = total[2 * half :, :]
    eye = lax.broadcasted_iota(jnp.int32, (n, n), 0) == lax.broadcasted_iota(jnp.int32, (n, n), 1)
    whole = work[...]
    diag = jnp.where(eye, whole, 0.0)
    across = lax.rsqrt(jnp.sum(diag, axis=0, keepdims=True))
    work[...] = whole * lax.rsqrt(jnp.sum(diag, axis=1, keepdims=True)) * across
    sub = lax.broadcasted_iota(jnp.int32, (PANEL, 128), 0)
    lane = lax.broadcasted_iota(jnp.int32, (PANEL, 128), 1)
    n_panels = OUTER // PANEL

    def step(o, carry):
        blk = [
            [work[p * PANEL : (p + 1) * PANEL, t * 128 : (t + 1) * 128] for t in range(tiles - 1)]
            + [jnp.where(lane == sub + p * PANEL, 1.0, 0.0).astype(F32)]
            for p in range(n_panels)
        ]
        for p in range(n_panels):
            off = p * PANEL
            inv = factor_panel(blk[p][0], off)
            rows_of = [
                [jnp.broadcast_to(blk[p][t][j : j + 1, :], (PANEL, 128)) for t in range(tiles)]
                for j in range(PANEL)
            ]
            new = [None] * tiles
            for j in range(PANEL):
                col = inv[PANEL - 1, j]
                for i in range(PANEL - 2, j - 1, -1):
                    col = jnp.where(sub == i, inv[i, j], col)
                if j:
                    col = jnp.where(sub < j, 0.0, col)
                for t in range(tiles):
                    term = col * rows_of[j][t]
                    new[t] = term if new[t] is None else new[t] + term
            blk[p] = new
            if p + 1 < n_panels:
                u_rows = [
                    [jnp.broadcast_to(new[t][j : j + 1, :], (PANEL, 128)) for t in range(tiles)]
                    for j in range(PANEL)
                ]
                for b in range(p + 1, n_panels):
                    lanes = [
                        jnp.broadcast_to(blk[b][0][:, off + m : off + m + 1], (PANEL, 128))
                        for m in range(PANEL)
                    ]
                    upd = list(blk[b])
                    for k in range(PANEL):
                        v = lanes[0] * inv[k, 0]
                        for m in range(1, k + 1):
                            v = v + lanes[m] * inv[k, m]
                        for t in range(tiles):
                            upd[t] = upd[t] - v * u_rows[k][t]
                    blk[b] = upd
        u = jnp.concatenate([jnp.concatenate(row, axis=1) for row in blk], axis=0)
        u = pltpu.roll(u, tiles * 128 - OUTER, 1)[:, :n]
        at = lax.broadcasted_iota(jnp.int32, (OUTER, n), 1)
        left = jnp.where(at < n - OUTER * (o + 1), u, 0.0)
        la, lb, lc = three_parts(left)
        ua, ub, uc = three_parts(u)
        lhs = jnp.concatenate([la, la, lb, la, lc, lb], axis=0)
        rhs = jnp.concatenate([ua, ub, ua, uc, ua, ub], axis=0)
        upd = mm(lhs.T, rhs)
        rest = work[OUTER:, :]
        lanes_at = lax.broadcasted_iota(jnp.int32, rest.shape, 1)
        rest = pltpu.roll(jnp.where(lanes_at < OUTER, 0.0, rest), n - OUTER, 1)
        work[: n - OUTER, :] = rest - upd[: n - OUTER, :]
        work[n - OUTER :, :] = u
        return carry

    lax.fori_loop(0, n // OUTER, step, 0)
    out[...] = work[...] * across


def inverse_factor(*parts):
    n = 2 * parts[0].shape[1]
    return pl.pallas_call(
        functools.partial(cholesky_kernel, len(parts)),
        in_specs=[VMEM] * len(parts),
        out_specs=VMEM,
        scratch_shapes=[pltpu.VMEM((n, n), F32)],
        out_shape=jax.ShapeDtypeStruct((n, n), F32),
        compiler_params=params(),
        name="inverse_factor",
        cost_estimate=cost(2),
    )(*parts)


def mm_three(a, b):
    a_hi, a_lo = halves(a)
    b_hi, b_lo = halves(b)
    return mm(a_hi, b_hi) + (mm(a_hi, b_lo) + mm(a_lo, b_hi))


def back_kernel(x, wa, wb, *refs):
    bt_out, y_out, s_out = refs[-3:]
    w = wa[...].astype(F32) + wb[...].astype(F32)
    bt = mm_three(x[...], w)
    bt_out[...] = bt
    s = jnp.sum(bt * bt, axis=1, keepdims=True)
    s_out[...] = jnp.broadcast_to(s, (s.shape[0], 128)).T[:8, :]
    y_out[...] = ((1.0 - momentum_keep) * mm(x[...].T.astype(BF16), bt.astype(BF16))).astype(BF16)


def back_full(x, wa, wb, after):
    rank, cols = wa.shape
    return pl.pallas_call(
        back_kernel,
        in_specs=[VMEM] * 3 + [ANY] * len(after),
        out_specs=[VMEM] * 3,
        out_shape=[
            jax.ShapeDtypeStruct((rank, cols), F32),
            jax.ShapeDtypeStruct((rank, cols), BF16),
            jax.ShapeDtypeStruct((8, rank), F32),
        ],
        compiler_params=params(),
        name="back_full",
        cost_estimate=cost(),
    )(x, wa, wb, *after)


def row_blocks(ranks, n_resp, n_head, chunk):
    return [
        pl.multiple_of(((ranks[0] ^ j) * n_head + (ranks[2] ^ k)) * chunk, chunk)
        for j in range(n_resp)
        for k in range(n_head)
    ]


def momentum_rows(blocks, pcat, y, totals, held, out, sems, begin, end):
    chunk = held.shape[0] // (end - begin)
    seg = totals[0].shape[0]
    copies = []
    for i in range(begin, end):
        rows = slice(i * chunk, (i + 1) * chunk)
        kept = slice((i - begin) * chunk, (i - begin + 1) * chunk)
        off = i * chunk % seg
        total = totals[(i - begin) * chunk // seg][off : off + chunk, :]
        held[kept, :] = total - mm(pcat[rows, :], y[...])
        copies.append(
            pltpu.make_async_copy(
                held.at[kept, :], out.at[pl.ds(blocks[i], chunk), :], sems.at[i - begin]
            )
        )
        copies[-1].start()
    return copies


def momentum_kernel(n_resp, n_head, n_totals, ranks, pcat, y, *refs):
    totals, refs = refs[:n_totals], refs[n_totals:]
    dq_parts, rg, refs = refs[:2], refs[2], refs[-7:]
    out, dq, resp_grad, token, held, sems, more = refs
    token[...] = jnp.zeros_like(token)
    width = dq_parts[0].shape[1]
    copies = [
        pltpu.make_async_copy(part, dq.at[:, pl.ds(i * width, width)], more.at[i])
        for i, part in enumerate(dq_parts)
    ]
    copies.append(pltpu.make_async_copy(rg, resp_grad, more.at[2]))
    n = n_resp * n_head
    blocks = row_blocks(ranks, n_resp, n_head, pcat.shape[0] // n)
    copies[2].start()
    moved = momentum_rows(blocks, pcat, y, totals, held, out, sems, 0, n // 2)
    for c in copies[:2]:
        c.start()
    for c in copies + moved:
        c.wait()


def new_momentum(ranks, pcat, totals, y, n_resp, n_head, dq_parts, rg, after):
    rows, rank = pcat.shape
    cols = totals[0].shape[1]
    length, width = dq_parts[0].shape
    return pl.pallas_call(
        functools.partial(momentum_kernel, n_resp, n_head, len(totals)),
        in_specs=[SMEM] + [VMEM] * (5 + len(totals)) + [ANY] * len(after),
        out_specs=[HBM, HBM, HBM, VMEM],
        scratch_shapes=[
            pltpu.VMEM((rows // 2, cols), F32),
            pltpu.SemaphoreType.DMA((n_resp * n_head // 2,)),
            pltpu.SemaphoreType.DMA((3,)),
        ],
        out_shape=[
            jax.ShapeDtypeStruct((rows, cols), F32),
            jax.ShapeDtypeStruct((length, 2 * width), BF16),
            jax.ShapeDtypeStruct(rg.shape, BF16),
            jax.ShapeDtypeStruct((8, 128), F32),
        ],
        compiler_params=params(12),
        name="new_momentum",
        cost_estimate=cost(5),
    )(ranks, pcat, y, *totals, *dq_parts, rg, *after)


def update_kernel(gain, n_resp, n_head, n_sums, n_totals, n_prompt, ranks, pcat, x, bt, y, *refs):
    sums, refs = refs[:n_sums], refs[n_sums:]
    totals, refs = refs[:n_totals], refs[n_totals:]
    prompts, refs = refs[:n_prompt], refs[n_prompt + 1 :]
    upd, basis_out, mom_out, prompt_out, held, held_mom, held_basis, held_prompt, sems, more = refs
    n = n_resp * n_head
    chunk = pcat.shape[0] // n
    blocks = row_blocks(ranks, n_resp, n_head, chunk)
    total = sums[0][...]
    for s in sums[1:]:
        total = total + s[...]
    scale = lax.rsqrt(total + norm_eps).T[:, :1]
    scaled = bt[...] * scale
    held_basis[...] = scaled.T
    acc = prompts[0][...]
    for p in prompts[1:]:
        acc = acc + p[...].astype(F32)
    held_prompt[...] = acc
    copies = [
        pltpu.make_async_copy(held_basis, basis_out, more.at[0]),
        pltpu.make_async_copy(held_prompt, prompt_out, more.at[1]),
    ]
    for c in copies:
        c.start()
    copies += momentum_rows(blocks, pcat, y, totals, held_mom, mom_out, sems.at[1], n // 2, n)
    z_hi, z_lo = halves(gain * mm_three(x[...].T, scaled))
    for i, at in enumerate(blocks):
        rows = slice(i * chunk, (i + 1) * chunk)
        p = pcat[rows, :]
        held[rows, :] = (mm(p, z_hi) + mm(p, z_lo)).astype(BF16)
        copies.append(
            pltpu.make_async_copy(held.at[rows, :], upd.at[pl.ds(at, chunk), :], sems.at[0, i])
        )
        copies[-1].start()
    for c in copies:
        c.wait()


def final_update(ranks, pcat, x, bt, y, sums, totals, prompts, momentum, gain, n_resp, n_head):
    rows, rank = pcat.shape
    cols = bt.shape[1]
    n_vmem = 4 + len(sums) + len(totals) + len(prompts)
    return pl.pallas_call(
        functools.partial(
            update_kernel, gain, n_resp, n_head, len(sums), len(totals), len(prompts)
        ),
        in_specs=[SMEM] + [VMEM] * n_vmem + [HBM],
        out_specs=[HBM] * 4,
        scratch_shapes=[
            pltpu.VMEM((rows, cols), BF16),
            pltpu.VMEM((rows // 2, cols), F32),
            pltpu.VMEM((cols, rank), F32),
            pltpu.VMEM(prompts[0].shape, F32),
            pltpu.SemaphoreType.DMA((2, n_resp * n_head)),
            pltpu.SemaphoreType.DMA((2,)),
        ],
        out_shape=[
            jax.ShapeDtypeStruct((rows, cols), BF16),
            jax.ShapeDtypeStruct((cols, rank), F32),
            jax.ShapeDtypeStruct((rows, cols), F32),
            jax.ShapeDtypeStruct(prompts[0].shape, F32),
        ],
        input_output_aliases={1 + n_vmem: 2},
        compiler_params=params(14),
        name="final_update",
        cost_estimate=cost(5),
    )(ranks, pcat, x, bt, y, *sums, *totals, *prompts, momentum)


def group_of(counts, response):
    group = jnp.int32(0)
    end = jnp.int32(0)
    for g in range(counts.shape[0]):
        end = end + counts[g]
        group = group + (end <= response).astype(jnp.int32)
    return group


def pack_kernel(*refs):
    keys, values, out = refs[0], refs[1], refs[-1]
    out[0] = keys[...]
    out[1] = values[...]


def pack_prompts(keys, values, after):
    return pl.pallas_call(
        pack_kernel,
        in_specs=[VMEM] * 2 + [ANY] * len(after),
        out_specs=VMEM,
        out_shape=jax.ShapeDtypeStruct((2,) + keys.shape, BF16),
        compiler_params=params(),
        name="pack_prompts",
        cost_estimate=cost(),
    )(keys, values, *after)


def select_kernel(n_resp, n_fsdp, ranks, counts, slots, *refs):
    stored, outs = refs[:n_resp], refs[-n_fsdp:]
    held = stored[0].shape[1]
    for k in range(n_fsdp):
        slot = slots[group_of(counts, ranks[0] * n_fsdp + (ranks[1] ^ k))]
        owner, local = slot // held, slot % held
        for j in range(n_resp):

            @pl.when(owner == (ranks[0] ^ j))
            def _():
                outs[k][0] = stored[j][0, local]
                outs[k][1] = stored[j][1, local]


def select_prompts(ranks, counts, slots, stored, n_fsdp, after):
    _, _, piece, width = stored[0].shape
    return pl.pallas_call(
        functools.partial(select_kernel, len(stored), n_fsdp),
        in_specs=[SMEM] * 3 + [VMEM] * len(stored) + [ANY] * len(after),
        out_specs=[VMEM] * n_fsdp,
        out_shape=[jax.ShapeDtypeStruct((2, piece, width), BF16)] * n_fsdp,
        compiler_params=params(),
        name="select_prompts",
        cost_estimate=cost(),
    )(ranks, counts, slots, *stored, *after)


def attention_kernel(
    n_fsdp, heads, last, ranks, counts, prompt_blocks, resp_blocks, q, sk, sv, go, *refs
):
    pieces, refs = refs[:n_fsdp], refs[n_fsdp:]
    keys, values, dk, dv = refs[-4:]
    n_out = 2 + n_fsdp if last else 3
    outs = refs[-4 - n_out : -4]
    dq = outs[0]
    piece = pieces[0].shape[1]
    cap = piece * n_fsdp
    length = q.shape[0]
    scale = HD ** (-0.5)
    for k in range(n_fsdp):
        rows = pl.ds(pl.multiple_of((ranks[1] ^ k) * piece, piece), piece)
        keys[rows, :] = pieces[k][0]
        values[rows, :] = pieces[k][1]
    keys[cap:, :] = sk[...]
    values[cap:, :] = sv[...]
    prompt_len = prompt_blocks[group_of(counts, ranks[0] * n_fsdp + ranks[1])] * 128
    resp_len = resp_blocks[0] * 128
    width = keys.shape[0]
    place = lax.broadcasted_iota(jnp.int32, (width, length), 0)
    pos = lax.broadcasted_iota(jnp.int32, (width, length), 1)
    inner = place - cap
    seen = ((place < cap) & (place < prompt_len)) | (
        (place >= cap) & (inner <= pos) & (inner < resp_len)
    )
    bias = jnp.where(seen, 0.0, -jnp.inf).astype(F32)
    live = lax.broadcasted_iota(jnp.int32, (length, HD), 0) < resp_len
    nt = (((1,), (1,)), ((), ()))
    kall = keys[...]
    vall = values[...]
    kt = kall.T
    if last:
        dk[...] = refs[0][...]
        dv[...] = refs[1][...]
    else:
        dk[...] = jnp.zeros_like(dk)
        dv[...] = jnp.zeros_like(dv)
    for i, h in enumerate(heads):
        cols = slice(h * HD, (h + 1) * HD)
        qh = q[:, cols]
        gh = jnp.where(live, go[:, cols], jnp.zeros((), BF16))
        logits = lax.dot_general(kall, qh, nt, preferred_element_type=F32) * scale + bias
        peak = jnp.max(logits, axis=0, keepdims=True)
        e = jnp.exp(logits - peak)
        w = (e * (1.0 / jnp.sum(e, axis=0, keepdims=True))).astype(BF16)
        dp = lax.dot_general(vall, gh, nt, preferred_element_type=F32)
        wf = w.astype(F32)
        diag = jnp.sum(wf * dp, axis=0, keepdims=True)
        ds = (wf * (dp - diag)).astype(BF16)
        dk[...] += mm(ds, qh)
        dv[...] += mm(w, gh)
        dq[:, i * HD : (i + 1) * HD] = (mm(kt, ds) * scale).T.astype(BF16)
    if last:
        own, sends = outs[1], outs[2:]
        own[0] = (dk[cap:, :] * scale).astype(BF16)
        own[1] = dv[cap:, :].astype(BF16)
        for k in range(n_fsdp):
            rows = pl.ds(pl.multiple_of((ranks[1] ^ k) * piece, piece), piece)
            sends[k][0] = (dk[rows, :] * scale).astype(sends[k].dtype)
            sends[k][1] = dv[rows, :].astype(sends[k].dtype)
    else:
        outs[1][...] = dk[...]
        outs[2][...] = dv[...]


def attention(heads, earlier, ranks, counts, prompt_blocks, resp_blocks, q, sk, sv, go, pieces, after):
    n_fsdp = len(pieces)
    piece = pieces[0].shape[1]
    length, width = q.shape
    cap = piece * n_fsdp
    total = cap + length
    last = earlier is not None
    dq_shape = jax.ShapeDtypeStruct((length, len(heads) * HD), BF16)
    if last:
        extra, specs = (earlier[1], earlier[2]), [VMEM] * 2
        out_shape = [dq_shape, jax.ShapeDtypeStruct((2, length, HD), BF16)] + [
            jax.ShapeDtypeStruct((2, piece, HD), BF16 if k else F32) for k in range(n_fsdp)
        ]
    else:
        extra, specs = (), []
        out_shape = [dq_shape] + [jax.ShapeDtypeStruct((total, HD), F32)] * 2
    return pl.pallas_call(
        functools.partial(attention_kernel, n_fsdp, heads, last),
        in_specs=[SMEM] * 4 + [VMEM] * (4 + n_fsdp) + specs + [ANY] * len(after),
        out_specs=[VMEM] * len(out_shape),
        scratch_shapes=[pltpu.VMEM((total, HD), BF16)] * 2 + [pltpu.VMEM((total, HD), F32)] * 2,
        out_shape=out_shape,
        compiler_params=params(12),
        name="attention",
        cost_estimate=cost(),
    )(ranks, counts, prompt_blocks, resp_blocks, q, sk, sv, go, *pieces, *extra, *after)


def by_slot_kernel(n_resp, n_fsdp, ranks, counts, slots, *refs):
    parts, outs = refs[:n_fsdp], refs[-n_resp:]
    held = outs[0].shape[1]
    slot_of = [
        slots[group_of(counts, ranks[0] * n_fsdp + (ranks[1] ^ k))] for k in range(n_fsdp)
    ]
    for j in range(n_resp):
        for local in range(held):
            slot = (ranks[0] ^ j) * held + local
            acc = jnp.zeros(parts[0].shape, F32)
            for k in range(n_fsdp):
                acc = acc + jnp.where(slot_of[k] == slot, parts[k][...].astype(F32), 0.0)
            outs[j][:, local] = acc.astype(outs[j].dtype)


def sum_by_slot(ranks, counts, slots, parts, n_resp, after):
    held = counts.shape[0] // n_resp
    _, piece, width = parts[0].shape
    return pl.pallas_call(
        functools.partial(by_slot_kernel, n_resp, len(parts)),
        in_specs=[SMEM] * 3 + [VMEM] * len(parts) + [ANY] * len(after),
        out_specs=[VMEM] * n_resp,
        out_shape=[
            jax.ShapeDtypeStruct((2, held, piece, width), BF16 if j else F32)
            for j in range(n_resp)
        ],
        compiler_params=params(),
        name="sum_by_slot",
        cost_estimate=cost(),
    )(ranks, counts, slots, *parts, *after)


def on_device(
    queries,
    self_keys,
    self_values,
    d_out,
    prompt_keys,
    prompt_values,
    counts,
    owner_slot,
    prompt_blocks,
    resp_blocks,
    grad_q,
    momentum,
    basis,
):
    n_resp, n_fsdp, n_head = (lax.axis_size(a) for a in ("resp", "fsdp", "head"))
    ranks = jnp.stack([lax.axis_index(a) for a in ("resp", "fsdp", "head")]).astype(jnp.int32)
    gain = math.sqrt(
        momentum.shape[0] * n_fsdp * momentum.shape[1] * n_resp * n_head / basis.shape[1]
    )

    in_hbm = [pltpu.with_memory_space_constraint(a, pltpu.HBM) for a in (momentum, grad_q, basis)]
    half = n_head // 2
    groups = [(half, half), (0, half)] if half else [(0, n_head)]

    mom_hbm, grad_hbm, basis_hbm = in_hbm
    order = [(j, *group) for group in groups for j in [*range(1, n_resp), 0]]
    nexts = dict(zip(order, order[1:] + [None]))
    totals, arrived, split, ins, after = {}, {}, {}, (basis_hbm,), ()
    for part in order:
        j, first, number = part
        value, totals[part[:2]], ins = project(
            ranks, mom_hbm, grad_hbm, ins, part, nexts[part], n_resp, n_head, BF16 if j else F32,
            after, 0 if j or first == 0 else 10,
        )
        after = ()
        if j:
            arrived.setdefault(first, []).append(swap(value, "resp", j))
            if part[1:] == groups[-1] and j == n_resp - 1:
                packed = pack_prompts(prompt_keys, prompt_values, (value,))
                stored = [packed] + [swap(packed, "resp", k) for k in range(1, n_resp)]
                outs = split_sum(owned, arrived[groups[0][0]], *groups[0])
                for i in range(groups[0][1]):
                    split[groups[0][0] + i] = outs[i]
                after = (outs[0],)
        elif part[1:] == groups[0] and len(groups) > 1:
            owned = value
        else:
            outs = split_sum(value, arrived[first], first, number)
            for i in range(number):
                split[first + i] = outs[i]
    totals = [totals[at] for at in sorted(totals)]
    chosen = select_prompts(
        ranks, counts, owner_slot, stored, n_fsdp, (split[1 % n_head],)
    )
    far_first = [k for first, number in groups for k in range(first, first + number) if k]
    summands = {k: swap(split[k], "head", k) for k in far_first}
    pieces = [chosen[0]] + [swap(chosen[k], "fsdp", k) for k in range(1, n_fsdp)]
    later = groups[-1][1] if len(groups) > 1 else 1
    far = sum_parts(
        [split[0]] + [summands[k] for k in range(later, n_head)], F32, (), 10
    )
    piece0 = sum_parts(
        [far] + [summands[k] for k in range(1, later)], BF16, tuple(pieces[1:])
    )

    n_q = queries.shape[1] // HD
    heads = [list(range(n_q // 2)), list(range(n_q // 2, n_q))]
    held = (
        ranks, counts, prompt_blocks, resp_blocks, queries, self_keys, self_values, d_out, pieces
    )
    along = {0: piece0}
    for k in range(1, n_head):
        if not k & (k - 1):
            along[k] = swap(piece0, "head", k)
    earlier = attention(heads[0], None, *held, (piece0,))
    hops = {}
    for k in range(1, n_head):
        low = k & -k
        if k != low:
            if k - low not in hops:
                hops[k - low] = relay([along[k - low]], (earlier[1],))
            along[k] = swap(hops[k - low], "head", low)
    last = n_head - 1
    passed = [
        [swap(hops.get(k, along[k]), "resp", j) for k in range(last)] for j in range(1, n_resp)
    ]
    sent_last = relay([along[last]], (earlier[1], *[c for row in passed for c in row]))
    chunks = [along[k] for k in range(n_head)]
    for j in range(1, n_resp):
        chunks += passed[j - 1] + [swap(sent_last, "resp", j)]
    dq_parts, resp_grad, *parts = attention(heads[1], earlier, *held, (sent_last,))
    dq_parts = (earlier[0], dq_parts)
    pcat, pcat_t, gram = gather_gram(chunks, (parts[0],))

    bits = [1 << b for b in range(n_fsdp.bit_length() - 1)]
    w = back_part(pcat_t, totals, (gram,))
    for bit in bits[:-1]:
        gram = sum_parts([gram, swap(gram, "fsdp", bit)], F32, (), 3)
    gram_parts = (gram, swap(gram, "fsdp", bits[-1]))
    for bit in bits[:-1]:
        w = sum_parts([w, swap(w, "fsdp", bit)], BF16, (gram,), 5)
    w_other = swap(w, "fsdp", bits[-1])
    returned = [parts[0]] + [swap(parts[k], "fsdp", k) for k in range(1, n_fsdp)]
    x = inverse_factor(*gram_parts)
    bt, y, squares = back_full(x, w, w_other, tuple(returned[1:]))
    from_head = [swap(squares, "head", k) for k in range(1, n_head)]
    half = len(totals) // 2
    slots = sum_by_slot(ranks, counts, owner_slot, returned, n_resp, (squares,))
    prompts = [slots[0]] + [swap(slots[j], "resp", j) for j in range(1, n_resp)]
    squares = sum_parts([squares] + from_head, F32, (slots[-1],))
    sums = sum_parts(
        [squares] + [swap(squares, "resp", j) for j in range(1, n_resp)], F32
    )
    momentum_out, dq, resp_grad, _ = new_momentum(
        ranks, pcat, totals[:half], y, n_resp, n_head, dq_parts, resp_grad, (squares,)
    )
    update, basis_out, momentum_out, prompt_grad = final_update(
        ranks, pcat, x, bt, y, [sums], totals[half:], prompts, momentum_out, gain, n_resp, n_head
    )
    return (dq, resp_grad, prompt_grad, update, momentum_out, basis_out)


def solution(mesh):
    placed = (
        P(("resp", "fsdp"), "head"),
        P(("resp", "fsdp"), "head"),
        P(("resp", "fsdp"), "head"),
        P(("resp", "fsdp"), "head"),
        P("resp", "fsdp", "head"),
        P("resp", "fsdp", "head"),
        P(),
        P(),
        P(),
        P(("resp", "fsdp")),
        P("fsdp", ("resp", "head")),
        P("fsdp", ("resp", "head")),
        P(("resp", "head"), None),
    )
    return jax.shard_map(
        on_device,
        mesh=mesh,
        in_specs=placed,
        out_specs=(
            P(("resp", "fsdp"), "head"),
            P(None, ("resp", "fsdp"), "head"),
            P(None, "resp", "fsdp", "head"),
            P("fsdp", ("resp", "head")),
            P("fsdp", ("resp", "head")),
            P(("resp", "head"), None),
        ),
        check_vma=False,
    )
```

```python
import functools
import math

import jax
import jax.numpy as jnp
from jax import lax
from jax.experimental import pallas as pl
from jax.experimental.pallas import tpu as pltpu
from jax.sharding import PartitionSpec as P

HD = 128
PANEL = 8
OUTER = 32
MIB = 1 << 20

momentum_keep = 0.95
norm_eps = 1e-06

F32 = jnp.float32
BF16 = jnp.bfloat16
HIGHEST = lax.Precision.HIGHEST

SMEM = pl.BlockSpec(memory_space=pltpu.SMEM)
VMEM = pl.BlockSpec(memory_space=pltpu.VMEM)
ANY = pl.BlockSpec(memory_space=pl.ANY)
HBM = pl.BlockSpec(memory_space=pltpu.HBM)


def swap(value, axes, k):
    axes = (axes,) if isinstance(axes, str) else axes
    n = math.prod(lax.axis_size(a) for a in axes)
    return lax.ppermute(value, axes, [(i, i ^ k) for i in range(n)])


def params(mib=6):
    return pltpu.CompilerParams(vmem_limit_bytes=mib * MIB)


def cost(weight=0):
    return pl.CostEstimate(flops=1 + weight * 10**9, bytes_accessed=1, transcendentals=0)


def halves(x):
    hi = x.astype(BF16)
    return hi, (x - hi.astype(F32)).astype(BF16)


def mm(a, b):
    return jnp.dot(a, b, preferred_element_type=F32)


def mm_full(a, b):
    return jnp.dot(a, b, precision=HIGHEST, preferred_element_type=F32)


def row_copies(ranks, n_head, part, mom, grad, mom_to, grad_to, sems):
    j, first, number = part
    chunk = mom_to.shape[0] // number
    pieces = 2 if chunk % 32 == 0 else 1
    size = chunk // pieces
    copies = []
    for i in range(number):
        at = ((ranks[0] ^ j) * n_head + (ranks[2] ^ (first + i))) * chunk
        copies.append([])
        for p in range(pieces):
            src = pl.ds(pl.multiple_of(at + p * size, size), size)
            dst = pl.ds(i * chunk + p * size, size)
            n = i * pieces + p
            copies[i].append(pltpu.make_async_copy(mom.at[src, :], mom_to.at[dst, :], sems.at[0, n]))
            copies[i].append(
                pltpu.make_async_copy(grad.at[src, :], grad_to.at[dst, :], sems.at[1, n])
            )
    return copies


def start_all(copies):
    for row in copies:
        for c in row:
            c.start()


def project_kernel(n_head, part, following, is_first, n_in, ranks, mom, grad, *refs):
    ins, refs = refs[:n_in], list(refs)
    number = part[2]
    sems = refs.pop()
    ahead = []
    if is_first:
        right_sem, right, grad_in = refs.pop(), refs.pop(), refs.pop()
    if following:
        next_grad, next_mom = refs.pop(), refs.pop()
        ahead = row_copies(ranks, n_head, following, mom, grad, next_mom, next_grad, sems.at[1])
    if is_first:
        b_lo, b_hi = refs.pop(), refs.pop()
        total, out = refs.pop(), refs.pop()
        mom_in = total
        copies = row_copies(ranks, n_head, part, mom, grad, mom_in, grad_in, sems.at[0])
        fetch = pltpu.make_async_copy(ins[0], right, right_sem)
        start_all(copies[:1])
        fetch.start()
        start_all(copies[1:])
        fetch.wait()
        hi, lo = halves(right[...])
        b_hi[...] = hi
        b_lo[...] = lo
    else:
        total, out = refs.pop(), refs.pop()
        b_hi, b_lo, mom_in, grad_in = ins
        copies = [[]] * number
        start_all(ahead)
    chunk = total.shape[0] // number
    for i in range(number):
        for c in copies[i]:
            c.wait()
        if is_first and i == 0:
            start_all(ahead)
        rows = slice(i * chunk, (i + 1) * chunk)
        t = mom_in[rows, :] + grad_in[rows, :].astype(F32)
        total[rows, :] = t
        t_hi, t_lo = halves(t)
        acc = mm(t_hi, b_hi[...]) + (mm(t_hi, b_lo[...]) + mm(t_lo, b_hi[...]))
        out[rows, :] = acc.astype(out.dtype)
    for row in ahead:
        for c in row:
            c.wait()


def project(
    ranks, momentum, grad_q, ins, part, following, n_resp, n_head, dtype, after, weight=0
):
    is_first = len(ins) == 1
    rows, cols = momentum.shape
    chunk = rows // (n_resp * n_head)
    size = part[2] * chunk
    if is_first:
        right = ins[0]
        rank = right.shape[1]
        specs = [HBM]
    else:
        rank = ins[0].shape[1]
        specs = [VMEM] * 4
    out_shape = [jax.ShapeDtypeStruct((size, rank), dtype), jax.ShapeDtypeStruct((size, cols), F32)]
    if is_first:
        out_shape += [jax.ShapeDtypeStruct((cols, rank), BF16)] * 2
    if following:
        ahead = following[2] * chunk
        out_shape += [
            jax.ShapeDtypeStruct((ahead, cols), F32), jax.ShapeDtypeStruct((ahead, cols), BF16)
        ]
    scratch = [pltpu.SemaphoreType.DMA((2, 2, 2 * n_head))]
    if is_first:
        scratch = [
            pltpu.VMEM((size, cols), BF16), pltpu.VMEM((cols, rank), F32), pltpu.SemaphoreType.DMA
        ] + scratch
    outs = pl.pallas_call(
        functools.partial(project_kernel, n_head, part, following, is_first, len(ins)),
        in_specs=[SMEM, HBM, HBM] + specs + [ANY] * len(after),
        out_specs=[VMEM] * len(out_shape),
        scratch_shapes=scratch,
        out_shape=out_shape,
        compiler_params=params(14),
        name="project",
        cost_estimate=cost(weight),
    )(ranks, momentum, grad_q, *ins, *after)
    right = tuple(outs[2:4]) if is_first else tuple(ins[:2])
    return outs[0], outs[1], right + tuple(outs[-2:] if following else ())


def split_kernel(n_recv, number, own, *refs):
    recvs, outs = refs[:n_recv], refs[-number:]
    chunk = outs[0].shape[0]
    for i in range(number):
        rows = slice(i * chunk, (i + 1) * chunk)
        acc = own[rows, :]
        for r in recvs:
            acc = acc + r[rows, :].astype(F32)
        outs[i][...] = acc.astype(outs[i].dtype)


def split_sum(own, recvs, first, number):
    rows, rank = own.shape
    chunk = rows // number
    return pl.pallas_call(
        functools.partial(split_kernel, len(recvs), number),
        in_specs=[VMEM] * (1 + len(recvs)),
        out_specs=[VMEM] * number,
        out_shape=[
            jax.ShapeDtypeStruct((chunk, rank), BF16 if (first + i) % 2 else F32)
            for i in range(number)
        ],
        compiler_params=params(),
        name="split_sum",
        cost_estimate=cost(),
    )(own, *recvs)


def sum_kernel(n_parts, *refs):
    acc = refs[0][...].astype(F32)
    for r in refs[1:n_parts]:
        acc = acc + r[...].astype(F32)
    refs[-1][...] = acc.astype(refs[-1].dtype)


def sum_parts(parts, dtype, after=(), weight=0):
    shape = parts[0].shape
    return pl.pallas_call(
        functools.partial(sum_kernel, len(parts)),
        in_specs=[VMEM] * len(parts) + [ANY] * len(after),
        out_specs=VMEM,
        out_shape=jax.ShapeDtypeStruct(shape, dtype),
        compiler_params=params(),
        name="sum_parts",
        cost_estimate=cost(weight),
    )(*parts, *after)


def relay_kernel(n_parts, *refs):
    out = refs[-1]
    size = out.shape[0] // n_parts
    for i in range(n_parts):
        out[i * size : (i + 1) * size, :] = refs[i][...]


def relay(parts, after):
    rows, rank = parts[0].shape
    return pl.pallas_call(
        functools.partial(relay_kernel, len(parts)),
        in_specs=[VMEM] * len(parts) + [ANY] * len(after),
        out_specs=VMEM,
        out_shape=jax.ShapeDtypeStruct((len(parts) * rows, rank), parts[0].dtype),
        compiler_params=params(),
        name="relay",
        cost_estimate=cost(),
    )(*parts, *after)


def gram_kernel(n_chunks, *refs):
    chunks, (pcat, pcat_t, gram) = refs[:n_chunks], refs[-3:]
    at = 0
    for c in chunks:
        pcat[at : at + c.shape[0], :] = c[...]
        at += c.shape[0]
    p = pcat[...]
    pt = p.T
    pcat_t[...] = pt
    half = p.shape[1] // 2
    gram[:half, :] = mm(pt[:half, :], p[:, :half])
    low = mm(pt[half:, :], p)
    gram[half : 2 * half, :] = low[:, :half]
    gram[2 * half :, :] = low[:, half:]


def gather_gram(chunks, after):
    rank = chunks[0].shape[1]
    rows = sum(c.shape[0] for c in chunks)
    return pl.pallas_call(
        functools.partial(gram_kernel, len(chunks)),
        in_specs=[VMEM] * len(chunks) + [ANY] * len(after),
        out_specs=[VMEM] * 3,
        out_shape=[
            jax.ShapeDtypeStruct((rows, rank), BF16),
            jax.ShapeDtypeStruct((rank, rows), BF16),
            jax.ShapeDtypeStruct((3 * rank // 2, rank // 2), F32),
        ],
        compiler_params=params(8),
        name="gather_gram",
        cost_estimate=cost(),
    )(*chunks, *after)


def back_part_kernel(n_totals, pcat_t, *refs):
    totals, out = refs[:n_totals], refs[-1]
    seg = totals[0].shape[0]
    step = min(seg, 512)
    acc = None
    for j, total in enumerate(totals):
        for i in range(0, seg, step):
            t_hi, t_lo = halves(total[i : i + step, :])
            pt = pcat_t[:, j * seg + i : j * seg + i + step]
            part = mm(pt, t_hi) + mm(pt, t_lo)
            acc = part if acc is None else acc + part
    out[...] = acc.astype(BF16)


def back_part(pcat_t, totals, after):
    rank = pcat_t.shape[0]
    seg, cols = totals[0].shape
    rows = seg * len(totals)
    return pl.pallas_call(
        functools.partial(back_part_kernel, len(totals)),
        in_specs=[VMEM] * (1 + len(totals)) + [ANY] * len(after),
        out_specs=VMEM,
        out_shape=jax.ShapeDtypeStruct((rank, cols), BF16),
        compiler_params=params(14),
        name="back_part",
        cost_estimate=cost(5),
    )(pcat_t, *totals, *after)


def factor_panel(panel, off):
    shape = (PANEL, 128)
    d = {}
    for j in range(PANEL):
        col = jnp.broadcast_to(panel[:, off + j : off + j + 1], shape)
        for i in range(j, PANEL):
            d[i, j] = jnp.broadcast_to(col[i : i + 1, :], shape)
    low, inv = {}, {}
    for j in range(0, PANEL, 2):
        a, b, c = d[j, j], d[j + 1, j], d[j + 1, j + 1]
        first = lax.rsqrt(a)
        second = lax.rsqrt(a * c - b * b) * (a * first)
        inv[j, j], inv[j + 1, j + 1] = first, second
        low[j + 1, j] = b * first
        for i in range(j + 2, PANEL):
            low[i, j] = d[i, j] * first
            low[i, j + 1] = (d[i, j + 1] - low[i, j] * low[j + 1, j]) * second
        for k in range(j + 2, PANEL):
            for i in range(k, PANEL):
                d[i, k] = d[i, k] - (low[i, j] * low[k, j] + low[i, j + 1] * low[k, j + 1])
    for j in range(PANEL):
        for i in range(j + 1, PANEL):
            acc = low[i, j] * inv[j, j]
            for k in range(j + 1, i):
                acc = acc + low[i, k] * inv[k, j]
            inv[i, j] = -(acc * inv[i, i])
    return inv


def three_parts(x):
    a = x.astype(BF16)
    rest = x - a.astype(F32)
    b = rest.astype(BF16)
    return a, b, (rest - b.astype(F32)).astype(BF16)


def cholesky_kernel(n_parts, *refs):
    parts, out, work = refs[:n_parts], refs[n_parts], refs[n_parts + 1]
    n = out.shape[0]
    half = n // 2
    tiles = n // 128 + 1
    total = parts[0][...]
    for part in parts[1:]:
        total = total + part[...]
    low = total[half : 2 * half, :]
    work[:half, :half] = total[:half, :]
    work[half:, :half] = low
    work[:half, half:] = low.T
    work[half:, half:] = total[2 * half :, :]
    eye = lax.broadcasted_iota(jnp.int32, (n, n), 0) == lax.broadcasted_iota(jnp.int32, (n, n), 1)
    whole = work[...]
    diag = jnp.where(eye, whole, 0.0)
    across = lax.rsqrt(jnp.sum(diag, axis=0, keepdims=True))
    work[...] = whole * lax.rsqrt(jnp.sum(diag, axis=1, keepdims=True)) * across
    sub = lax.broadcasted_iota(jnp.int32, (PANEL, 128), 0)
    lane = lax.broadcasted_iota(jnp.int32, (PANEL, 128), 1)
    n_panels = OUTER // PANEL

    def step(o, carry):
        blk = [
            [work[p * PANEL : (p + 1) * PANEL, t * 128 : (t + 1) * 128] for t in range(tiles - 1)]
            + [jnp.where(lane == sub + p * PANEL, 1.0, 0.0).astype(F32)]
            for p in range(n_panels)
        ]
        for p in range(n_panels):
            off = p * PANEL
            inv = factor_panel(blk[p][0], off)
            rows_of = [
                [jnp.broadcast_to(blk[p][t][j : j + 1, :], (PANEL, 128)) for t in range(tiles)]
                for j in range(PANEL)
            ]
            new = [None] * tiles
            for j in range(PANEL):
                col = inv[PANEL - 1, j]
                for i in range(PANEL - 2, j - 1, -1):
                    col = jnp.where(sub == i, inv[i, j], col)
                if j:
                    col = jnp.where(sub < j, 0.0, col)
                for t in range(tiles):
                    term = col * rows_of[j][t]
                    new[t] = term if new[t] is None else new[t] + term
            blk[p] = new
            if p + 1 < n_panels:
                u_rows = [
                    [jnp.broadcast_to(new[t][j : j + 1, :], (PANEL, 128)) for t in range(tiles)]
                    for j in range(PANEL)
                ]
                for b in range(p + 1, n_panels):
                    lanes = [
                        jnp.broadcast_to(blk[b][0][:, off + m : off + m + 1], (PANEL, 128))
                        for m in range(PANEL)
                    ]
                    upd = list(blk[b])
                    for k in range(PANEL):
                        v = lanes[0] * inv[k, 0]
                        for m in range(1, k + 1):
                            v = v + lanes[m] * inv[k, m]
                        for t in range(tiles):
                            upd[t] = upd[t] - v * u_rows[k][t]
                    blk[b] = upd
        u = jnp.concatenate([jnp.concatenate(row, axis=1) for row in blk], axis=0)
        u = pltpu.roll(u, tiles * 128 - OUTER, 1)[:, :n]
        at = lax.broadcasted_iota(jnp.int32, (OUTER, n), 1)
        left = jnp.where(at < n - OUTER * (o + 1), u, 0.0)
        la, lb, lc = three_parts(left)
        ua, ub, uc = three_parts(u)
        lhs = jnp.concatenate([la, la, lb, la, lc, lb], axis=0)
        rhs = jnp.concatenate([ua, ub, ua, uc, ua, ub], axis=0)
        upd = mm(lhs.T, rhs)
        rest = work[OUTER:, :]
        lanes_at = lax.broadcasted_iota(jnp.int32, rest.shape, 1)
        rest = pltpu.roll(jnp.where(lanes_at < OUTER, 0.0, rest), n - OUTER, 1)
        work[: n - OUTER, :] = rest - upd[: n - OUTER, :]
        work[n - OUTER :, :] = u
        return carry

    lax.fori_loop(0, n // OUTER, step, 0)
    out[...] = work[...] * across


def inverse_factor(*parts):
    n = 2 * parts[0].shape[1]
    return pl.pallas_call(
        functools.partial(cholesky_kernel, len(parts)),
        in_specs=[VMEM] * len(parts),
        out_specs=VMEM,
        scratch_shapes=[pltpu.VMEM((n, n), F32)],
        out_shape=jax.ShapeDtypeStruct((n, n), F32),
        compiler_params=params(),
        name="inverse_factor",
        cost_estimate=cost(2),
    )(*parts)


def mm_three(a, b):
    a_hi, a_lo = halves(a)
    b_hi, b_lo = halves(b)
    return mm(a_hi, b_hi) + (mm(a_hi, b_lo) + mm(a_lo, b_hi))


def back_kernel(x, wa, wb, *refs):
    bt_out, y_out, s_out = refs[-3:]
    w = wa[...].astype(F32) + wb[...].astype(F32)
    bt = mm_three(x[...], w)
    bt_out[...] = bt
    s = jnp.sum(bt * bt, axis=1, keepdims=True)
    s_out[...] = jnp.broadcast_to(s, (s.shape[0], 128)).T[:8, :]
    y_out[...] = ((1.0 - momentum_keep) * mm(x[...].T.astype(BF16), bt.astype(BF16))).astype(BF16)


def back_full(x, wa, wb, after):
    rank, cols = wa.shape
    return pl.pallas_call(
        back_kernel,
        in_specs=[VMEM] * 3 + [ANY] * len(after),
        out_specs=[VMEM] * 3,
        out_shape=[
            jax.ShapeDtypeStruct((rank, cols), F32),
            jax.ShapeDtypeStruct((rank, cols), BF16),
            jax.ShapeDtypeStruct((8, rank), F32),
        ],
        compiler_params=params(),
        name="back_full",
        cost_estimate=cost(),
    )(x, wa, wb, *after)


def row_blocks(ranks, n_resp, n_head, chunk):
    return [
        pl.multiple_of(((ranks[0] ^ j) * n_head + (ranks[2] ^ k)) * chunk, chunk)
        for j in range(n_resp)
        for k in range(n_head)
    ]


def momentum_rows(blocks, pcat, y, totals, held, out, sems, begin, end):
    chunk = held.shape[0] // (end - begin)
    seg = totals[0].shape[0]
    copies = []
    for i in range(begin, end):
        rows = slice(i * chunk, (i + 1) * chunk)
        kept = slice((i - begin) * chunk, (i - begin + 1) * chunk)
        off = i * chunk % seg
        total = totals[(i - begin) * chunk // seg][off : off + chunk, :]
        held[kept, :] = total - mm(pcat[rows, :], y[...])
        copies.append(
            pltpu.make_async_copy(
                held.at[kept, :], out.at[pl.ds(blocks[i], chunk), :], sems.at[i - begin]
            )
        )
        copies[-1].start()
    return copies


def momentum_kernel(n_resp, n_head, n_totals, ranks, pcat, y, *refs):
    totals, refs = refs[:n_totals], refs[n_totals:]
    dq_parts, rg, refs = refs[:2], refs[2], refs[-7:]
    out, dq, resp_grad, token, held, sems, more = refs
    token[...] = jnp.zeros_like(token)
    width = dq_parts[0].shape[1]
    copies = [
        pltpu.make_async_copy(part, dq.at[:, pl.ds(i * width, width)], more.at[i])
        for i, part in enumerate(dq_parts)
    ]
    copies.append(pltpu.make_async_copy(rg, resp_grad, more.at[2]))
    n = n_resp * n_head
    blocks = row_blocks(ranks, n_resp, n_head, pcat.shape[0] // n)
    copies[2].start()
    moved = momentum_rows(blocks, pcat, y, totals, held, out, sems, 0, n // 2)
    for c in copies[:2]:
        c.start()
    for c in copies + moved:
        c.wait()


def new_momentum(ranks, pcat, totals, y, n_resp, n_head, dq_parts, rg, after):
    rows, rank = pcat.shape
    cols = totals[0].shape[1]
    length, width = dq_parts[0].shape
    return pl.pallas_call(
        functools.partial(momentum_kernel, n_resp, n_head, len(totals)),
        in_specs=[SMEM] + [VMEM] * (5 + len(totals)) + [ANY] * len(after),
        out_specs=[HBM, HBM, HBM, VMEM],
        scratch_shapes=[
            pltpu.VMEM((rows // 2, cols), F32),
            pltpu.SemaphoreType.DMA((n_resp * n_head // 2,)),
            pltpu.SemaphoreType.DMA((3,)),
        ],
        out_shape=[
            jax.ShapeDtypeStruct((rows, cols), F32),
            jax.ShapeDtypeStruct((length, 2 * width), BF16),
            jax.ShapeDtypeStruct(rg.shape, BF16),
            jax.ShapeDtypeStruct((8, 128), F32),
        ],
        compiler_params=params(12),
        name="new_momentum",
        cost_estimate=cost(5),
    )(ranks, pcat, y, *totals, *dq_parts, rg, *after)


def update_kernel(gain, n_resp, n_head, n_sums, n_totals, n_prompt, ranks, pcat, x, bt, y, *refs):
    sums, refs = refs[:n_sums], refs[n_sums:]
    totals, refs = refs[:n_totals], refs[n_totals:]
    prompts, refs = refs[:n_prompt], refs[n_prompt + 1 :]
    upd, basis_out, mom_out, prompt_out, held, held_mom, held_basis, held_prompt, sems, more = refs
    n = n_resp * n_head
    chunk = pcat.shape[0] // n
    blocks = row_blocks(ranks, n_resp, n_head, chunk)
    total = sums[0][...]
    for s in sums[1:]:
        total = total + s[...]
    scale = lax.rsqrt(total + norm_eps).T[:, :1]
    scaled = bt[...] * scale
    held_basis[...] = scaled.T
    acc = prompts[0][...]
    for p in prompts[1:]:
        acc = acc + p[...].astype(F32)
    held_prompt[...] = acc
    copies = [
        pltpu.make_async_copy(held_basis, basis_out, more.at[0]),
        pltpu.make_async_copy(held_prompt, prompt_out, more.at[1]),
    ]
    for c in copies:
        c.start()
    copies += momentum_rows(blocks, pcat, y, totals, held_mom, mom_out, sems.at[1], n // 2, n)
    z_hi, z_lo = halves(gain * mm_three(x[...].T, scaled))
    for i, at in enumerate(blocks):
        rows = slice(i * chunk, (i + 1) * chunk)
        p = pcat[rows, :]
        held[rows, :] = (mm(p, z_hi) + mm(p, z_lo)).astype(BF16)
        copies.append(
            pltpu.make_async_copy(held.at[rows, :], upd.at[pl.ds(at, chunk), :], sems.at[0, i])
        )
        copies[-1].start()
    for c in copies:
        c.wait()


def final_update(ranks, pcat, x, bt, y, sums, totals, prompts, momentum, gain, n_resp, n_head):
    rows, rank = pcat.shape
    cols = bt.shape[1]
    n_vmem = 4 + len(sums) + len(totals) + len(prompts)
    return pl.pallas_call(
        functools.partial(
            update_kernel, gain, n_resp, n_head, len(sums), len(totals), len(prompts)
        ),
        in_specs=[SMEM] + [VMEM] * n_vmem + [HBM],
        out_specs=[HBM] * 4,
        scratch_shapes=[
            pltpu.VMEM((rows, cols), BF16),
            pltpu.VMEM((rows // 2, cols), F32),
            pltpu.VMEM((cols, rank), F32),
            pltpu.VMEM(prompts[0].shape, F32),
            pltpu.SemaphoreType.DMA((2, n_resp * n_head)),
            pltpu.SemaphoreType.DMA((2,)),
        ],
        out_shape=[
            jax.ShapeDtypeStruct((rows, cols), BF16),
            jax.ShapeDtypeStruct((cols, rank), F32),
            jax.ShapeDtypeStruct((rows, cols), F32),
            jax.ShapeDtypeStruct(prompts[0].shape, F32),
        ],
        input_output_aliases={1 + n_vmem: 2},
        compiler_params=params(14),
        name="final_update",
        cost_estimate=cost(5),
    )(ranks, pcat, x, bt, y, *sums, *totals, *prompts, momentum)


def group_of(counts, response):
    group = jnp.int32(0)
    end = jnp.int32(0)
    for g in range(counts.shape[0]):
        end = end + counts[g]
        group = group + (end <= response).astype(jnp.int32)
    return group


def pack_kernel(*refs):
    keys, values, out = refs[0], refs[1], refs[-1]
    out[0] = keys[...]
    out[1] = values[...]


def pack_prompts(keys, values, after):
    return pl.pallas_call(
        pack_kernel,
        in_specs=[VMEM] * 2 + [ANY] * len(after),
        out_specs=VMEM,
        out_shape=jax.ShapeDtypeStruct((2,) + keys.shape, BF16),
        compiler_params=params(),
        name="pack_prompts",
        cost_estimate=cost(),
    )(keys, values, *after)


def select_kernel(n_resp, n_fsdp, ranks, counts, slots, *refs):
    stored, outs = refs[:n_resp], refs[-n_fsdp:]
    held = stored[0].shape[1]
    for k in range(n_fsdp):
        slot = slots[group_of(counts, ranks[0] * n_fsdp + (ranks[1] ^ k))]
        owner, local = slot // held, slot % held
        for j in range(n_resp):

            @pl.when(owner == (ranks[0] ^ j))
            def _():
                outs[k][0] = stored[j][0, local]
                outs[k][1] = stored[j][1, local]


def select_prompts(ranks, counts, slots, stored, n_fsdp, after):
    _, _, piece, width = stored[0].shape
    return pl.pallas_call(
        functools.partial(select_kernel, len(stored), n_fsdp),
        in_specs=[SMEM] * 3 + [VMEM] * len(stored) + [ANY] * len(after),
        out_specs=[VMEM] * n_fsdp,
        out_shape=[jax.ShapeDtypeStruct((2, piece, width), BF16)] * n_fsdp,
        compiler_params=params(),
        name="select_prompts",
        cost_estimate=cost(),
    )(ranks, counts, slots, *stored, *after)


def attention_kernel(
    n_fsdp, heads, last, ranks, counts, prompt_blocks, resp_blocks, q, sk, sv, go, *refs
):
    pieces, refs = refs[:n_fsdp], refs[n_fsdp:]
    keys, values, dk, dv = refs[-4:]
    n_out = 2 + n_fsdp if last else 3
    outs = refs[-4 - n_out : -4]
    dq = outs[0]
    piece = pieces[0].shape[1]
    cap = piece * n_fsdp
    length = q.shape[0]
    scale = HD ** (-0.5)
    for k in range(n_fsdp):
        rows = pl.ds(pl.multiple_of((ranks[1] ^ k) * piece, piece), piece)
        keys[rows, :] = pieces[k][0]
        values[rows, :] = pieces[k][1]
    keys[cap:, :] = sk[...]
    values[cap:, :] = sv[...]
    prompt_len = prompt_blocks[group_of(counts, ranks[0] * n_fsdp + ranks[1])] * 128
    resp_len = resp_blocks[0] * 128
    width = keys.shape[0]
    place = lax.broadcasted_iota(jnp.int32, (width, length), 0)
    pos = lax.broadcasted_iota(jnp.int32, (width, length), 1)
    inner = place - cap
    seen = ((place < cap) & (place < prompt_len)) | (
        (place >= cap) & (inner <= pos) & (inner < resp_len)
    )
    bias = jnp.where(seen, 0.0, -jnp.inf).astype(F32)
    live = lax.broadcasted_iota(jnp.int32, (length, HD), 0) < resp_len
    nt = (((1,), (1,)), ((), ()))
    kall = keys[...]
    vall = values[...]
    kt = kall.T
    if last:
        dk[...] = refs[0][...]
        dv[...] = refs[1][...]
    else:
        dk[...] = jnp.zeros_like(dk)
        dv[...] = jnp.zeros_like(dv)
    for i, h in enumerate(heads):
        cols = slice(h * HD, (h + 1) * HD)
        qh = q[:, cols]
        gh = jnp.where(live, go[:, cols], jnp.zeros((), BF16))
        logits = lax.dot_general(kall, qh, nt, preferred_element_type=F32) * scale + bias
        peak = jnp.max(logits, axis=0, keepdims=True)
        e = jnp.exp(logits - peak)
        w = (e * (1.0 / jnp.sum(e, axis=0, keepdims=True))).astype(BF16)
        dp = lax.dot_general(vall, gh, nt, preferred_element_type=F32)
        wf = w.astype(F32)
        diag = jnp.sum(wf * dp, axis=0, keepdims=True)
        ds = (wf * (dp - diag)).astype(BF16)
        dk[...] += mm(ds, qh)
        dv[...] += mm(w, gh)
        dq[:, i * HD : (i + 1) * HD] = (mm(kt, ds) * scale).T.astype(BF16)
    if last:
        own, sends = outs[1], outs[2:]
        own[0] = (dk[cap:, :] * scale).astype(BF16)
        own[1] = dv[cap:, :].astype(BF16)
        for k in range(n_fsdp):
            rows = pl.ds(pl.multiple_of((ranks[1] ^ k) * piece, piece), piece)
            sends[k][0] = (dk[rows, :] * scale).astype(sends[k].dtype)
            sends[k][1] = dv[rows, :].astype(sends[k].dtype)
    else:
        outs[1][...] = dk[...]
        outs[2][...] = dv[...]


def attention(heads, earlier, ranks, counts, prompt_blocks, resp_blocks, q, sk, sv, go, pieces, after):
    n_fsdp = len(pieces)
    piece = pieces[0].shape[1]
    length, width = q.shape
    cap = piece * n_fsdp
    total = cap + length
    last = earlier is not None
    dq_shape = jax.ShapeDtypeStruct((length, len(heads) * HD), BF16)
    if last:
        extra, specs = (earlier[1], earlier[2]), [VMEM] * 2
        out_shape = [dq_shape, jax.ShapeDtypeStruct((2, length, HD), BF16)] + [
            jax.ShapeDtypeStruct((2, piece, HD), BF16 if k else F32) for k in range(n_fsdp)
        ]
    else:
        extra, specs = (), []
        out_shape = [dq_shape] + [jax.ShapeDtypeStruct((total, HD), F32)] * 2
    return pl.pallas_call(
        functools.partial(attention_kernel, n_fsdp, heads, last),
        in_specs=[SMEM] * 4 + [VMEM] * (4 + n_fsdp) + specs + [ANY] * len(after),
        out_specs=[VMEM] * len(out_shape),
        scratch_shapes=[pltpu.VMEM((total, HD), BF16)] * 2 + [pltpu.VMEM((total, HD), F32)] * 2,
        out_shape=out_shape,
        compiler_params=params(12),
        name="attention",
        cost_estimate=cost(),
    )(ranks, counts, prompt_blocks, resp_blocks, q, sk, sv, go, *pieces, *extra, *after)


def by_slot_kernel(n_resp, n_fsdp, ranks, counts, slots, *refs):
    parts, outs = refs[:n_fsdp], refs[-n_resp:]
    held = outs[0].shape[1]
    slot_of = [
        slots[group_of(counts, ranks[0] * n_fsdp + (ranks[1] ^ k))] for k in range(n_fsdp)
    ]
    for j in range(n_resp):
        for local in range(held):
            slot = (ranks[0] ^ j) * held + local
            acc = jnp.zeros(parts[0].shape, F32)
            for k in range(n_fsdp):
                acc = acc + jnp.where(slot_of[k] == slot, parts[k][...].astype(F32), 0.0)
            outs[j][:, local] = acc.astype(outs[j].dtype)


def sum_by_slot(ranks, counts, slots, parts, n_resp, after):
    held = counts.shape[0] // n_resp
    _, piece, width = parts[0].shape
    return pl.pallas_call(
        functools.partial(by_slot_kernel, n_resp, len(parts)),
        in_specs=[SMEM] * 3 + [VMEM] * len(parts) + [ANY] * len(after),
        out_specs=[VMEM] * n_resp,
        out_shape=[
            jax.ShapeDtypeStruct((2, held, piece, width), BF16 if j else F32)
            for j in range(n_resp)
        ],
        compiler_params=params(),
        name="sum_by_slot",
        cost_estimate=cost(),
    )(ranks, counts, slots, *parts, *after)


def on_device(
    queries,
    self_keys,
    self_values,
    d_out,
    prompt_keys,
    prompt_values,
    counts,
    owner_slot,
    prompt_blocks,
    resp_blocks,
    grad_q,
    momentum,
    basis,
):
    n_resp, n_fsdp, n_head = (lax.axis_size(a) for a in ("resp", "fsdp", "head"))
    ranks = jnp.stack([lax.axis_index(a) for a in ("resp", "fsdp", "head")]).astype(jnp.int32)
    gain = math.sqrt(
        momentum.shape[0] * n_fsdp * momentum.shape[1] * n_resp * n_head / basis.shape[1]
    )

    in_hbm = [pltpu.with_memory_space_constraint(a, pltpu.HBM) for a in (momentum, grad_q, basis)]
    half = n_head // 2
    groups = [(half, half), (0, half)] if half else [(0, n_head)]

    mom_hbm, grad_hbm, basis_hbm = in_hbm
    order = [(j, *group) for group in groups for j in [*range(1, n_resp), 0]]
    nexts = dict(zip(order, order[1:] + [None]))
    totals, arrived, split, ins, after = {}, {}, {}, (basis_hbm,), ()
    for part in order:
        j, first, number = part
        value, totals[part[:2]], ins = project(
            ranks, mom_hbm, grad_hbm, ins, part, nexts[part], n_resp, n_head, BF16 if j else F32,
            after, 0 if j or first == 0 else 10,
        )
        after = ()
        if j:
            arrived.setdefault(first, []).append(swap(value, "resp", j))
            if part[1:] == groups[-1] and j == n_resp - 1:
                packed = pack_prompts(prompt_keys, prompt_values, (value,))
                stored = [packed] + [swap(packed, "resp", k) for k in range(1, n_resp)]
                outs = split_sum(owned, arrived[groups[0][0]], *groups[0])
                for i in range(groups[0][1]):
                    split[groups[0][0] + i] = outs[i]
                after = (outs[-1],)
        elif part[1:] == groups[0] and len(groups) > 1:
            owned = value
        else:
            outs = split_sum(value, arrived[first], first, number)
            for i in range(number):
                split[first + i] = outs[i]
    totals = [totals[at] for at in sorted(totals)]
    chosen = select_prompts(
        ranks, counts, owner_slot, stored, n_fsdp, (split[1 % n_head],)
    )
    pieces = [chosen[0]] + [swap(chosen[k], "fsdp", k) for k in range(1, n_fsdp)]
    pending, arriving, bit = {k: split[k] for k in range(1, n_head)}, [], 1
    while bit < n_head:
        for k in sorted(pending):
            if k & -k == bit:
                received = swap(pending.pop(k), "head", bit)
                if k == bit:
                    arriving.append(received)
                else:
                    pending[k - bit] = sum_parts([pending[k - bit], received], BF16, (), 0)
        bit *= 2
    far = sum_parts([split[0], arriving[-1]], F32, (), 10)
    piece0 = sum_parts([far, *arriving[:-1]], BF16, tuple(pieces[1:]))

    n_q = queries.shape[1] // HD
    heads = [list(range(n_q // 2)), list(range(n_q // 2, n_q))]
    held = (
        ranks, counts, prompt_blocks, resp_blocks, queries, self_keys, self_values, d_out, pieces
    )
    along = {0: piece0}
    for k in range(1, n_head):
        if not k & (k - 1):
            along[k] = swap(piece0, "head", k)
    earlier = attention(heads[0], None, *held, (piece0,))
    hops = {}
    for k in range(1, n_head):
        low = k & -k
        if k != low:
            if k - low not in hops:
                hops[k - low] = relay([along[k - low]], (earlier[1],))
            along[k] = swap(hops[k - low], "head", low)
    last = n_head - 1
    passed = [[swap(hops.get(k, along[k]), "resp", j) for k in range(last)] for j in range(1, n_resp)]
    dq_parts, resp_grad, *parts = attention(heads[1], earlier, *held, tuple(hops.values()))
    sent_last = relay([along[last]], (parts[0], *[c for row in passed for c in row]))
    chunks = [along[k] for k in range(n_head)]
    for j in range(1, n_resp):
        chunks += passed[j - 1] + [swap(sent_last, "resp", j)]
    dq_parts = (earlier[0], dq_parts)
    pcat, pcat_t, gram = gather_gram(chunks, ())

    bits = [1 << b for b in range(n_fsdp.bit_length() - 1)]
    returned = [parts[0]] + [swap(parts[k], "fsdp", k) for k in range(1, n_fsdp)]
    w = back_part(pcat_t, totals, (gram, *returned[1:]))
    for bit in bits[:-1]:
        gram = sum_parts([gram, swap(gram, "fsdp", bit)], F32, (), 3)
    gram_parts = (gram, swap(gram, "fsdp", bits[-1]))
    for bit in bits[:-1]:
        w = sum_parts([w, swap(w, "fsdp", bit)], BF16, (gram,), 5)
    w_other = swap(w, "fsdp", bits[-1])
    x = inverse_factor(*gram_parts)
    bt, y, squares = back_full(x, w, w_other, tuple(returned[1:]))
    from_head = [swap(squares, "head", k) for k in range(1, n_head)]
    half = len(totals) // 2
    slots = sum_by_slot(ranks, counts, owner_slot, returned, n_resp, (squares,))
    prompts = [slots[0]] + [swap(slots[j], "resp", j) for j in range(1, n_resp)]
    squares = sum_parts([squares] + from_head, F32, (slots[-1],))
    sums = sum_parts(
        [squares] + [swap(squares, "resp", j) for j in range(1, n_resp)], F32
    )
    momentum_out, dq, resp_grad, _ = new_momentum(
        ranks, pcat, totals[:half], y, n_resp, n_head, dq_parts, resp_grad, (squares,)
    )
    update, basis_out, momentum_out, prompt_grad = final_update(
        ranks, pcat, x, bt, y, [sums], totals[half:], prompts, momentum_out, gain, n_resp, n_head
    )
    return (dq, resp_grad, prompt_grad, update, momentum_out, basis_out)


def solution(mesh):
    placed = (
        P(("resp", "fsdp"), "head"),
        P(("resp", "fsdp"), "head"),
        P(("resp", "fsdp"), "head"),
        P(("resp", "fsdp"), "head"),
        P("resp", "fsdp", "head"),
        P("resp", "fsdp", "head"),
        P(),
        P(),
        P(),
        P(("resp", "fsdp")),
        P("fsdp", ("resp", "head")),
        P("fsdp", ("resp", "head")),
        P(("resp", "head"), None),
    )
    return jax.shard_map(
        on_device,
        mesh=mesh,
        in_specs=placed,
        out_specs=(
            P(("resp", "fsdp"), "head"),
            P(None, ("resp", "fsdp"), "head"),
            P(None, "resp", "fsdp", "head"),
            P("fsdp", ("resp", "head")),
            P("fsdp", ("resp", "head")),
            P(("resp", "head"), None),
        ),
        check_vma=False,
    )
```

```python
import functools
import math

import jax
import jax.numpy as jnp
from jax import lax
from jax.experimental import pallas as pl
from jax.experimental.pallas import tpu as pltpu
from jax.sharding import PartitionSpec as P

HD = 128
PANEL = 8
OUTER = 32
MIB = 1 << 20

momentum_keep = 0.95
norm_eps = 1e-06

F32 = jnp.float32
BF16 = jnp.bfloat16
HIGHEST = lax.Precision.HIGHEST

SMEM = pl.BlockSpec(memory_space=pltpu.SMEM)
VMEM = pl.BlockSpec(memory_space=pltpu.VMEM)
ANY = pl.BlockSpec(memory_space=pl.ANY)
HBM = pl.BlockSpec(memory_space=pltpu.HBM)


def swap(value, axes, k):
    axes = (axes,) if isinstance(axes, str) else axes
    n = math.prod(lax.axis_size(a) for a in axes)
    return lax.ppermute(value, axes, [(i, i ^ k) for i in range(n)])


def params(mib=6):
    return pltpu.CompilerParams(vmem_limit_bytes=mib * MIB)


def cost(weight=0):
    return pl.CostEstimate(flops=1 + weight * 10**9, bytes_accessed=1, transcendentals=0)


def halves(x):
    hi = x.astype(BF16)
    return hi, (x - hi.astype(F32)).astype(BF16)


def mm(a, b):
    return jnp.dot(a, b, preferred_element_type=F32)


def mm_full(a, b):
    return jnp.dot(a, b, precision=HIGHEST, preferred_element_type=F32)


def row_copies(ranks, n_head, part, mom, grad, mom_to, grad_to, sems):
    j, first, number = part
    chunk = mom_to.shape[0] // number
    pieces = 2 if chunk % 32 == 0 else 1
    size = chunk // pieces
    copies = []
    for i in range(number):
        at = ((ranks[0] ^ j) * n_head + (ranks[2] ^ (first + i))) * chunk
        copies.append([])
        for p in range(pieces):
            src = pl.ds(pl.multiple_of(at + p * size, size), size)
            dst = pl.ds(i * chunk + p * size, size)
            n = i * pieces + p
            copies[i].append(pltpu.make_async_copy(mom.at[src, :], mom_to.at[dst, :], sems.at[0, n]))
            copies[i].append(
                pltpu.make_async_copy(grad.at[src, :], grad_to.at[dst, :], sems.at[1, n])
            )
    return copies


def start_all(copies):
    for row in copies:
        for c in row:
            c.start()


def project_kernel(n_head, part, following, is_first, n_in, ranks, mom, grad, *refs):
    ins, refs = refs[:n_in], list(refs)
    number = part[2]
    sems = refs.pop()
    ahead = []
    if is_first:
        right_sem, right, grad_in = refs.pop(), refs.pop(), refs.pop()
    if following:
        next_grad, next_mom = refs.pop(), refs.pop()
        ahead = row_copies(ranks, n_head, following, mom, grad, next_mom, next_grad, sems.at[1])
    if is_first:
        b_lo, b_hi = refs.pop(), refs.pop()
        total, out = refs.pop(), refs.pop()
        mom_in = total
        copies = row_copies(ranks, n_head, part, mom, grad, mom_in, grad_in, sems.at[0])
        fetch = pltpu.make_async_copy(ins[0], right, right_sem)
        start_all(copies[:1])
        fetch.start()
        start_all(copies[1:])
        fetch.wait()
        hi, lo = halves(right[...])
        b_hi[...] = hi
        b_lo[...] = lo
    else:
        total, out = refs.pop(), refs.pop()
        b_hi, b_lo, mom_in, grad_in = ins
        copies = [[]] * number
        start_all(ahead)
    chunk = total.shape[0] // number
    for i in range(number):
        for c in copies[i]:
            c.wait()
        if is_first and i == 0:
            start_all(ahead)
        rows = slice(i * chunk, (i + 1) * chunk)
        t = mom_in[rows, :] + grad_in[rows, :].astype(F32)
        total[rows, :] = t
        t_hi, t_lo = halves(t)
        acc = mm(t_hi, b_hi[...]) + (mm(t_hi, b_lo[...]) + mm(t_lo, b_hi[...]))
        out[rows, :] = acc.astype(out.dtype)
    for row in ahead:
        for c in row:
            c.wait()


def project(
    ranks, momentum, grad_q, ins, part, following, n_resp, n_head, dtype, after, weight=0
):
    is_first = len(ins) == 1
    rows, cols = momentum.shape
    chunk = rows // (n_resp * n_head)
    size = part[2] * chunk
    if is_first:
        right = ins[0]
        rank = right.shape[1]
        specs = [HBM]
    else:
        rank = ins[0].shape[1]
        specs = [VMEM] * 4
    out_shape = [jax.ShapeDtypeStruct((size, rank), dtype), jax.ShapeDtypeStruct((size, cols), F32)]
    if is_first:
        out_shape += [jax.ShapeDtypeStruct((cols, rank), BF16)] * 2
    if following:
        ahead = following[2] * chunk
        out_shape += [
            jax.ShapeDtypeStruct((ahead, cols), F32), jax.ShapeDtypeStruct((ahead, cols), BF16)
        ]
    scratch = [pltpu.SemaphoreType.DMA((2, 2, 2 * n_head))]
    if is_first:
        scratch = [
            pltpu.VMEM((size, cols), BF16), pltpu.VMEM((cols, rank), F32), pltpu.SemaphoreType.DMA
        ] + scratch
    outs = pl.pallas_call(
        functools.partial(project_kernel, n_head, part, following, is_first, len(ins)),
        in_specs=[SMEM, HBM, HBM] + specs + [ANY] * len(after),
        out_specs=[VMEM] * len(out_shape),
        scratch_shapes=scratch,
        out_shape=out_shape,
        compiler_params=params(14),
        name="project",
        cost_estimate=cost(weight),
    )(ranks, momentum, grad_q, *ins, *after)
    right = tuple(outs[2:4]) if is_first else tuple(ins[:2])
    return outs[0], outs[1], right + tuple(outs[-2:] if following else ())


def split_kernel(n_recv, number, own, *refs):
    recvs, outs = refs[:n_recv], refs[-number:]
    chunk = outs[0].shape[0]
    for i in range(number):
        rows = slice(i * chunk, (i + 1) * chunk)
        acc = own[rows, :]
        for r in recvs:
            acc = acc + r[rows, :].astype(F32)
        outs[i][...] = acc.astype(outs[i].dtype)


def split_sum(own, recvs, first, number):
    rows, rank = own.shape
    chunk = rows // number
    return pl.pallas_call(
        functools.partial(split_kernel, len(recvs), number),
        in_specs=[VMEM] * (1 + len(recvs)),
        out_specs=[VMEM] * number,
        out_shape=[
            jax.ShapeDtypeStruct((chunk, rank), BF16 if first + i else F32)
            for i in range(number)
        ],
        compiler_params=params(),
        name="split_sum",
        cost_estimate=cost(),
    )(own, *recvs)


def sum_kernel(n_parts, *refs):
    acc = refs[0][...].astype(F32)
    for r in refs[1:n_parts]:
        acc = acc + r[...].astype(F32)
    refs[-1][...] = acc.astype(refs[-1].dtype)


def sum_parts(parts, dtype, after=(), weight=0):
    shape = parts[0].shape
    return pl.pallas_call(
        functools.partial(sum_kernel, len(parts)),
        in_specs=[VMEM] * len(parts) + [ANY] * len(after),
        out_specs=VMEM,
        out_shape=jax.ShapeDtypeStruct(shape, dtype),
        compiler_params=params(),
        name="sum_parts",
        cost_estimate=cost(weight),
    )(*parts, *after)


def relay_kernel(n_parts, *refs):
    out = refs[-1]
    size = out.shape[0] // n_parts
    for i in range(n_parts):
        out[i * size : (i + 1) * size, :] = refs[i][...]


def relay(parts, after):
    rows, rank = parts[0].shape
    return pl.pallas_call(
        functools.partial(relay_kernel, len(parts)),
        in_specs=[VMEM] * len(parts) + [ANY] * len(after),
        out_specs=VMEM,
        out_shape=jax.ShapeDtypeStruct((len(parts) * rows, rank), parts[0].dtype),
        compiler_params=params(),
        name="relay",
        cost_estimate=cost(),
    )(*parts, *after)


def gram_kernel(n_chunks, *refs):
    chunks, (pcat, pcat_t, gram) = refs[:n_chunks], refs[-3:]
    at = 0
    for c in chunks:
        pcat[at : at + c.shape[0], :] = c[...]
        at += c.shape[0]
    p = pcat[...]
    pt = p.T
    pcat_t[...] = pt
    half = p.shape[1] // 2
    gram[:half, :] = mm(pt[:half, :], p[:, :half])
    low = mm(pt[half:, :], p)
    gram[half : 2 * half, :] = low[:, :half]
    gram[2 * half :, :] = low[:, half:]


def gather_gram(chunks, after):
    rank = chunks[0].shape[1]
    rows = sum(c.shape[0] for c in chunks)
    return pl.pallas_call(
        functools.partial(gram_kernel, len(chunks)),
        in_specs=[VMEM] * len(chunks) + [ANY] * len(after),
        out_specs=[VMEM] * 3,
        out_shape=[
            jax.ShapeDtypeStruct((rows, rank), BF16),
            jax.ShapeDtypeStruct((rank, rows), BF16),
            jax.ShapeDtypeStruct((3 * rank // 2, rank // 2), F32),
        ],
        compiler_params=params(8),
        name="gather_gram",
        cost_estimate=cost(),
    )(*chunks, *after)


def back_part_kernel(n_totals, pcat_t, *refs):
    totals, out = refs[:n_totals], refs[-1]
    seg = totals[0].shape[0]
    step = min(seg, 512)
    acc = None
    for j, total in enumerate(totals):
        for i in range(0, seg, step):
            t_hi, t_lo = halves(total[i : i + step, :])
            pt = pcat_t[:, j * seg + i : j * seg + i + step]
            part = mm(pt, t_hi) + mm(pt, t_lo)
            acc = part if acc is None else acc + part
    out[...] = acc.astype(BF16)


def back_part(pcat_t, totals, after):
    rank = pcat_t.shape[0]
    seg, cols = totals[0].shape
    rows = seg * len(totals)
    return pl.pallas_call(
        functools.partial(back_part_kernel, len(totals)),
        in_specs=[VMEM] * (1 + len(totals)) + [ANY] * len(after),
        out_specs=VMEM,
        out_shape=jax.ShapeDtypeStruct((rank, cols), BF16),
        compiler_params=params(14),
        name="back_part",
        cost_estimate=cost(5),
    )(pcat_t, *totals, *after)


def factor_panel(panel, off):
    shape = (PANEL, 128)
    d = {}
    for j in range(PANEL):
        col = jnp.broadcast_to(panel[:, off + j : off + j + 1], shape)
        for i in range(j, PANEL):
            d[i, j] = jnp.broadcast_to(col[i : i + 1, :], shape)
    low, inv = {}, {}
    for j in range(0, PANEL, 2):
        a, b, c = d[j, j], d[j + 1, j], d[j + 1, j + 1]
        first = lax.rsqrt(a)
        second = lax.rsqrt(a * c - b * b) * (a * first)
        inv[j, j], inv[j + 1, j + 1] = first, second
        low[j + 1, j] = b * first
        for i in range(j + 2, PANEL):
            low[i, j] = d[i, j] * first
            low[i, j + 1] = (d[i, j + 1] - low[i, j] * low[j + 1, j]) * second
        for k in range(j + 2, PANEL):
            for i in range(k, PANEL):
                d[i, k] = d[i, k] - (low[i, j] * low[k, j] + low[i, j + 1] * low[k, j + 1])
    for j in range(PANEL):
        for i in range(j + 1, PANEL):
            acc = low[i, j] * inv[j, j]
            for k in range(j + 1, i):
                acc = acc + low[i, k] * inv[k, j]
            inv[i, j] = -(acc * inv[i, i])
    return inv


def three_parts(x):
    a = x.astype(BF16)
    rest = x - a.astype(F32)
    b = rest.astype(BF16)
    return a, b, (rest - b.astype(F32)).astype(BF16)


def cholesky_kernel(n_parts, *refs):
    parts, out, work = refs[:n_parts], refs[n_parts], refs[n_parts + 1]
    n = out.shape[0]
    half = n // 2
    tiles = n // 128 + 1
    total = parts[0][...]
    for part in parts[1:]:
        total = total + part[...]
    low = total[half : 2 * half, :]
    work[:half, :half] = total[:half, :]
    work[half:, :half] = low
    work[:half, half:] = low.T
    work[half:, half:] = total[2 * half :, :]
    eye = lax.broadcasted_iota(jnp.int32, (n, n), 0) == lax.broadcasted_iota(jnp.int32, (n, n), 1)
    whole = work[...]
    diag = jnp.where(eye, whole, 0.0)
    across = lax.rsqrt(jnp.sum(diag, axis=0, keepdims=True))
    work[...] = whole * lax.rsqrt(jnp.sum(diag, axis=1, keepdims=True)) * across
    sub = lax.broadcasted_iota(jnp.int32, (PANEL, 128), 0)
    lane = lax.broadcasted_iota(jnp.int32, (PANEL, 128), 1)
    n_panels = OUTER // PANEL

    def step(o, carry):
        blk = [
            [work[p * PANEL : (p + 1) * PANEL, t * 128 : (t + 1) * 128] for t in range(tiles - 1)]
            + [jnp.where(lane == sub + p * PANEL, 1.0, 0.0).astype(F32)]
            for p in range(n_panels)
        ]
        for p in range(n_panels):
            off = p * PANEL
            inv = factor_panel(blk[p][0], off)
            rows_of = [
                [jnp.broadcast_to(blk[p][t][j : j + 1, :], (PANEL, 128)) for t in range(tiles)]
                for j in range(PANEL)
            ]
            new = [None] * tiles
            for j in range(PANEL):
                col = inv[PANEL - 1, j]
                for i in range(PANEL - 2, j - 1, -1):
                    col = jnp.where(sub == i, inv[i, j], col)
                if j:
                    col = jnp.where(sub < j, 0.0, col)
                for t in range(tiles):
                    term = col * rows_of[j][t]
                    new[t] = term if new[t] is None else new[t] + term
            blk[p] = new
            if p + 1 < n_panels:
                u_rows = [
                    [jnp.broadcast_to(new[t][j : j + 1, :], (PANEL, 128)) for t in range(tiles)]
                    for j in range(PANEL)
                ]
                for b in range(p + 1, n_panels):
                    lanes = [
                        jnp.broadcast_to(blk[b][0][:, off + m : off + m + 1], (PANEL, 128))
                        for m in range(PANEL)
                    ]
                    upd = list(blk[b])
                    for k in range(PANEL):
                        v = lanes[0] * inv[k, 0]
                        for m in range(1, k + 1):
                            v = v + lanes[m] * inv[k, m]
                        for t in range(tiles):
                            upd[t] = upd[t] - v * u_rows[k][t]
                    blk[b] = upd
        u = jnp.concatenate([jnp.concatenate(row, axis=1) for row in blk], axis=0)
        u = pltpu.roll(u, tiles * 128 - OUTER, 1)[:, :n]
        at = lax.broadcasted_iota(jnp.int32, (OUTER, n), 1)
        left = jnp.where(at < n - OUTER * (o + 1), u, 0.0)
        la, lb, lc = three_parts(left)
        ua, ub, uc = three_parts(u)
        lhs = jnp.concatenate([la, la, lb, la, lc, lb], axis=0)
        rhs = jnp.concatenate([ua, ub, ua, uc, ua, ub], axis=0)
        upd = mm(lhs.T, rhs)
        rest = work[OUTER:, :]
        lanes_at = lax.broadcasted_iota(jnp.int32, rest.shape, 1)
        rest = pltpu.roll(jnp.where(lanes_at < OUTER, 0.0, rest), n - OUTER, 1)
        work[: n - OUTER, :] = rest - upd[: n - OUTER, :]
        work[n - OUTER :, :] = u
        return carry

    lax.fori_loop(0, n // OUTER, step, 0)
    out[...] = work[...] * across


def inverse_factor(*parts):
    n = 2 * parts[0].shape[1]
    return pl.pallas_call(
        functools.partial(cholesky_kernel, len(parts)),
        in_specs=[VMEM] * len(parts),
        out_specs=VMEM,
        scratch_shapes=[pltpu.VMEM((n, n), F32)],
        out_shape=jax.ShapeDtypeStruct((n, n), F32),
        compiler_params=params(),
        name="inverse_factor",
        cost_estimate=cost(2),
    )(*parts)


def mm_three(a, b):
    a_hi, a_lo = halves(a)
    b_hi, b_lo = halves(b)
    return mm(a_hi, b_hi) + (mm(a_hi, b_lo) + mm(a_lo, b_hi))


def back_kernel(x, wa, wb, *refs):
    bt_out, y_out, s_out = refs[-3:]
    w = wa[...].astype(F32) + wb[...].astype(F32)
    bt = mm_three(x[...], w)
    bt_out[...] = bt
    s = jnp.sum(bt * bt, axis=1, keepdims=True)
    s_out[...] = jnp.broadcast_to(s, (s.shape[0], 128)).T[:8, :]
    y_out[...] = ((1.0 - momentum_keep) * mm(x[...].T.astype(BF16), bt.astype(BF16))).astype(BF16)


def back_full(x, wa, wb, after):
    rank, cols = wa.shape
    return pl.pallas_call(
        back_kernel,
        in_specs=[VMEM] * 3 + [ANY] * len(after),
        out_specs=[VMEM] * 3,
        out_shape=[
            jax.ShapeDtypeStruct((rank, cols), F32),
            jax.ShapeDtypeStruct((rank, cols), BF16),
            jax.ShapeDtypeStruct((8, rank), F32),
        ],
        compiler_params=params(),
        name="back_full",
        cost_estimate=cost(),
    )(x, wa, wb, *after)


def row_blocks(ranks, n_resp, n_head, chunk):
    return [
        pl.multiple_of(((ranks[0] ^ j) * n_head + (ranks[2] ^ k)) * chunk, chunk)
        for j in range(n_resp)
        for k in range(n_head)
    ]


def momentum_rows(blocks, pcat, y, totals, held, out, sems, begin, end):
    chunk = held.shape[0] // (end - begin)
    seg = totals[0].shape[0]
    copies = []
    for i in range(begin, end):
        rows = slice(i * chunk, (i + 1) * chunk)
        kept = slice((i - begin) * chunk, (i - begin + 1) * chunk)
        off = i * chunk % seg
        total = totals[(i - begin) * chunk // seg][off : off + chunk, :]
        held[kept, :] = total - mm(pcat[rows, :], y[...])
        copies.append(
            pltpu.make_async_copy(
                held.at[kept, :], out.at[pl.ds(blocks[i], chunk), :], sems.at[i - begin]
            )
        )
        copies[-1].start()
    return copies


def momentum_kernel(n_resp, n_head, n_totals, ranks, pcat, y, *refs):
    totals, refs = refs[:n_totals], refs[n_totals:]
    dq_parts, rg, refs = refs[:2], refs[2], refs[-7:]
    out, dq, resp_grad, token, held, sems, more = refs
    token[...] = jnp.zeros_like(token)
    width = dq_parts[0].shape[1]
    copies = [
        pltpu.make_async_copy(part, dq.at[:, pl.ds(i * width, width)], more.at[i])
        for i, part in enumerate(dq_parts)
    ]
    copies.append(pltpu.make_async_copy(rg, resp_grad, more.at[2]))
    n = n_resp * n_head
    blocks = row_blocks(ranks, n_resp, n_head, pcat.shape[0] // n)
    copies[2].start()
    moved = momentum_rows(blocks, pcat, y, totals, held, out, sems, 0, n // 2)
    for c in copies[:2]:
        c.start()
    for c in copies + moved:
        c.wait()


def new_momentum(ranks, pcat, totals, y, n_resp, n_head, dq_parts, rg, after):
    rows, rank = pcat.shape
    cols = totals[0].shape[1]
    length, width = dq_parts[0].shape
    return pl.pallas_call(
        functools.partial(momentum_kernel, n_resp, n_head, len(totals)),
        in_specs=[SMEM] + [VMEM] * (5 + len(totals)) + [ANY] * len(after),
        out_specs=[HBM, HBM, HBM, VMEM],
        scratch_shapes=[
            pltpu.VMEM((rows // 2, cols), F32),
            pltpu.SemaphoreType.DMA((n_resp * n_head // 2,)),
            pltpu.SemaphoreType.DMA((3,)),
        ],
        out_shape=[
            jax.ShapeDtypeStruct((rows, cols), F32),
            jax.ShapeDtypeStruct((length, 2 * width), BF16),
            jax.ShapeDtypeStruct(rg.shape, BF16),
            jax.ShapeDtypeStruct((8, 128), F32),
        ],
        compiler_params=params(12),
        name="new_momentum",
        cost_estimate=cost(5),
    )(ranks, pcat, y, *totals, *dq_parts, rg, *after)


def update_kernel(gain, n_resp, n_head, n_sums, n_totals, n_prompt, ranks, pcat, x, bt, y, *refs):
    sums, refs = refs[:n_sums], refs[n_sums:]
    totals, refs = refs[:n_totals], refs[n_totals:]
    prompts, refs = refs[:n_prompt], refs[n_prompt + 1 :]
    upd, basis_out, mom_out, prompt_out, held, held_mom, held_basis, held_prompt, sems, more = refs
    n = n_resp * n_head
    chunk = pcat.shape[0] // n
    blocks = row_blocks(ranks, n_resp, n_head, chunk)
    total = sums[0][...]
    for s in sums[1:]:
        total = total + s[...]
    scale = lax.rsqrt(total + norm_eps).T[:, :1]
    scaled = bt[...] * scale
    held_basis[...] = scaled.T
    acc = prompts[0][...]
    for p in prompts[1:]:
        acc = acc + p[...].astype(F32)
    held_prompt[...] = acc
    copies = [
        pltpu.make_async_copy(held_basis, basis_out, more.at[0]),
        pltpu.make_async_copy(held_prompt, prompt_out, more.at[1]),
    ]
    for c in copies:
        c.start()
    copies += momentum_rows(blocks, pcat, y, totals, held_mom, mom_out, sems.at[1], n // 2, n)
    z_hi, z_lo = halves(gain * mm_three(x[...].T, scaled))
    for i, at in enumerate(blocks):
        rows = slice(i * chunk, (i + 1) * chunk)
        p = pcat[rows, :]
        held[rows, :] = (mm(p, z_hi) + mm(p, z_lo)).astype(BF16)
        copies.append(
            pltpu.make_async_copy(held.at[rows, :], upd.at[pl.ds(at, chunk), :], sems.at[0, i])
        )
        copies[-1].start()
    for c in copies:
        c.wait()


def final_update(ranks, pcat, x, bt, y, sums, totals, prompts, momentum, gain, n_resp, n_head):
    rows, rank = pcat.shape
    cols = bt.shape[1]
    n_vmem = 4 + len(sums) + len(totals) + len(prompts)
    return pl.pallas_call(
        functools.partial(
            update_kernel, gain, n_resp, n_head, len(sums), len(totals), len(prompts)
        ),
        in_specs=[SMEM] + [VMEM] * n_vmem + [HBM],
        out_specs=[HBM] * 4,
        scratch_shapes=[
            pltpu.VMEM((rows, cols), BF16),
            pltpu.VMEM((rows // 2, cols), F32),
            pltpu.VMEM((cols, rank), F32),
            pltpu.VMEM(prompts[0].shape, F32),
            pltpu.SemaphoreType.DMA((2, n_resp * n_head)),
            pltpu.SemaphoreType.DMA((2,)),
        ],
        out_shape=[
            jax.ShapeDtypeStruct((rows, cols), BF16),
            jax.ShapeDtypeStruct((cols, rank), F32),
            jax.ShapeDtypeStruct((rows, cols), F32),
            jax.ShapeDtypeStruct(prompts[0].shape, F32),
        ],
        input_output_aliases={1 + n_vmem: 2},
        compiler_params=params(14),
        name="final_update",
        cost_estimate=cost(5),
    )(ranks, pcat, x, bt, y, *sums, *totals, *prompts, momentum)


def group_of(counts, response):
    group = jnp.int32(0)
    end = jnp.int32(0)
    for g in range(counts.shape[0]):
        end = end + counts[g]
        group = group + (end <= response).astype(jnp.int32)
    return group


def pack_kernel(*refs):
    keys, values, out = refs[0], refs[1], refs[-1]
    out[0] = keys[...]
    out[1] = values[...]


def pack_prompts(keys, values, after):
    return pl.pallas_call(
        pack_kernel,
        in_specs=[VMEM] * 2 + [ANY] * len(after),
        out_specs=VMEM,
        out_shape=jax.ShapeDtypeStruct((2,) + keys.shape, BF16),
        compiler_params=params(),
        name="pack_prompts",
        cost_estimate=cost(),
    )(keys, values, *after)


def select_kernel(n_resp, n_fsdp, ranks, counts, slots, *refs):
    stored, outs = refs[:n_resp], refs[-n_fsdp:]
    held = stored[0].shape[1]
    for k in range(n_fsdp):
        slot = slots[group_of(counts, ranks[0] * n_fsdp + (ranks[1] ^ k))]
        owner, local = slot // held, slot % held
        for j in range(n_resp):

            @pl.when(owner == (ranks[0] ^ j))
            def _():
                outs[k][0] = stored[j][0, local]
                outs[k][1] = stored[j][1, local]


def select_prompts(ranks, counts, slots, stored, n_fsdp, after):
    _, _, piece, width = stored[0].shape
    return pl.pallas_call(
        functools.partial(select_kernel, len(stored), n_fsdp),
        in_specs=[SMEM] * 3 + [VMEM] * len(stored) + [ANY] * len(after),
        out_specs=[VMEM] * n_fsdp,
        out_shape=[jax.ShapeDtypeStruct((2, piece, width), BF16)] * n_fsdp,
        compiler_params=params(),
        name="select_prompts",
        cost_estimate=cost(),
    )(ranks, counts, slots, *stored, *after)


def attention_kernel(
    n_fsdp, heads, last, ranks, counts, prompt_blocks, resp_blocks, q, sk, sv, go, *refs
):
    pieces, refs = refs[:n_fsdp], refs[n_fsdp:]
    keys, values, dk, dv = refs[-4:]
    n_out = 2 + n_fsdp if last else 3
    outs = refs[-4 - n_out : -4]
    dq = outs[0]
    piece = pieces[0].shape[1]
    cap = piece * n_fsdp
    length = q.shape[0]
    scale = HD ** (-0.5)
    for k in range(n_fsdp):
        rows = pl.ds(pl.multiple_of((ranks[1] ^ k) * piece, piece), piece)
        keys[rows, :] = pieces[k][0]
        values[rows, :] = pieces[k][1]
    keys[cap:, :] = sk[...]
    values[cap:, :] = sv[...]
    prompt_len = prompt_blocks[group_of(counts, ranks[0] * n_fsdp + ranks[1])] * 128
    resp_len = resp_blocks[0] * 128
    width = keys.shape[0]
    place = lax.broadcasted_iota(jnp.int32, (width, length), 0)
    pos = lax.broadcasted_iota(jnp.int32, (width, length), 1)
    inner = place - cap
    seen = ((place < cap) & (place < prompt_len)) | (
        (place >= cap) & (inner <= pos) & (inner < resp_len)
    )
    bias = jnp.where(seen, 0.0, -jnp.inf).astype(F32)
    live = lax.broadcasted_iota(jnp.int32, (length, HD), 0) < resp_len
    nt = (((1,), (1,)), ((), ()))
    kall = keys[...]
    vall = values[...]
    kt = kall.T
    if last:
        dk[...] = refs[0][...]
        dv[...] = refs[1][...]
    else:
        dk[...] = jnp.zeros_like(dk)
        dv[...] = jnp.zeros_like(dv)
    for i, h in enumerate(heads):
        cols = slice(h * HD, (h + 1) * HD)
        qh = q[:, cols]
        gh = jnp.where(live, go[:, cols], jnp.zeros((), BF16))
        logits = lax.dot_general(kall, qh, nt, preferred_element_type=F32) * scale + bias
        peak = jnp.max(logits, axis=0, keepdims=True)
        e = jnp.exp(logits - peak)
        w = (e * (1.0 / jnp.sum(e, axis=0, keepdims=True))).astype(BF16)
        dp = lax.dot_general(vall, gh, nt, preferred_element_type=F32)
        wf = w.astype(F32)
        diag = jnp.sum(wf * dp, axis=0, keepdims=True)
        ds = (wf * (dp - diag)).astype(BF16)
        dk[...] += mm(ds, qh)
        dv[...] += mm(w, gh)
        dq[:, i * HD : (i + 1) * HD] = (mm(kt, ds) * scale).T.astype(BF16)
    if last:
        own, sends = outs[1], outs[2:]
        own[0] = (dk[cap:, :] * scale).astype(BF16)
        own[1] = dv[cap:, :].astype(BF16)
        for k in range(n_fsdp):
            rows = pl.ds(pl.multiple_of((ranks[1] ^ k) * piece, piece), piece)
            sends[k][0] = (dk[rows, :] * scale).astype(sends[k].dtype)
            sends[k][1] = dv[rows, :].astype(sends[k].dtype)
    else:
        outs[1][...] = dk[...]
        outs[2][...] = dv[...]


def attention(heads, earlier, ranks, counts, prompt_blocks, resp_blocks, q, sk, sv, go, pieces, after):
    n_fsdp = len(pieces)
    piece = pieces[0].shape[1]
    length, width = q.shape
    cap = piece * n_fsdp
    total = cap + length
    last = earlier is not None
    dq_shape = jax.ShapeDtypeStruct((length, len(heads) * HD), BF16)
    if last:
        extra, specs = (earlier[1], earlier[2]), [VMEM] * 2
        out_shape = [dq_shape, jax.ShapeDtypeStruct((2, length, HD), BF16)] + [
            jax.ShapeDtypeStruct((2, piece, HD), BF16 if k else F32) for k in range(n_fsdp)
        ]
    else:
        extra, specs = (), []
        out_shape = [dq_shape] + [jax.ShapeDtypeStruct((total, HD), F32)] * 2
    return pl.pallas_call(
        functools.partial(attention_kernel, n_fsdp, heads, last),
        in_specs=[SMEM] * 4 + [VMEM] * (4 + n_fsdp) + specs + [ANY] * len(after),
        out_specs=[VMEM] * len(out_shape),
        scratch_shapes=[pltpu.VMEM((total, HD), BF16)] * 2 + [pltpu.VMEM((total, HD), F32)] * 2,
        out_shape=out_shape,
        compiler_params=params(12),
        name="attention",
        cost_estimate=cost(),
    )(ranks, counts, prompt_blocks, resp_blocks, q, sk, sv, go, *pieces, *extra, *after)


def by_slot_kernel(n_resp, n_fsdp, ranks, counts, slots, *refs):
    parts, outs = refs[:n_fsdp], refs[-n_resp:]
    held = outs[0].shape[1]
    slot_of = [
        slots[group_of(counts, ranks[0] * n_fsdp + (ranks[1] ^ k))] for k in range(n_fsdp)
    ]
    for j in range(n_resp):
        for local in range(held):
            slot = (ranks[0] ^ j) * held + local
            acc = jnp.zeros(parts[0].shape, F32)
            for k in range(n_fsdp):
                acc = acc + jnp.where(slot_of[k] == slot, parts[k][...].astype(F32), 0.0)
            outs[j][:, local] = acc.astype(outs[j].dtype)


def sum_by_slot(ranks, counts, slots, parts, n_resp, after):
    held = counts.shape[0] // n_resp
    _, piece, width = parts[0].shape
    return pl.pallas_call(
        functools.partial(by_slot_kernel, n_resp, len(parts)),
        in_specs=[SMEM] * 3 + [VMEM] * len(parts) + [ANY] * len(after),
        out_specs=[VMEM] * n_resp,
        out_shape=[
            jax.ShapeDtypeStruct((2, held, piece, width), BF16 if j else F32)
            for j in range(n_resp)
        ],
        compiler_params=params(),
        name="sum_by_slot",
        cost_estimate=cost(),
    )(ranks, counts, slots, *parts, *after)


def on_device(
    queries,
    self_keys,
    self_values,
    d_out,
    prompt_keys,
    prompt_values,
    counts,
    owner_slot,
    prompt_blocks,
    resp_blocks,
    grad_q,
    momentum,
    basis,
):
    n_resp, n_fsdp, n_head = (lax.axis_size(a) for a in ("resp", "fsdp", "head"))
    ranks = jnp.stack([lax.axis_index(a) for a in ("resp", "fsdp", "head")]).astype(jnp.int32)
    gain = math.sqrt(
        momentum.shape[0] * n_fsdp * momentum.shape[1] * n_resp * n_head / basis.shape[1]
    )

    in_hbm = [pltpu.with_memory_space_constraint(a, pltpu.HBM) for a in (momentum, grad_q, basis)]
    half = n_head // 2
    groups = [(half, half), (0, half)] if half else [(0, n_head)]

    mom_hbm, grad_hbm, basis_hbm = in_hbm
    order = [(j, *group) for group in groups for j in [*range(1, n_resp), 0]]
    nexts = dict(zip(order, order[1:] + [None]))
    totals, arrived, split, ins, after = {}, {}, {}, (basis_hbm,), ()
    for part in order:
        j, first, number = part
        value, totals[part[:2]], ins = project(
            ranks, mom_hbm, grad_hbm, ins, part, nexts[part], n_resp, n_head, BF16 if j else F32,
            after, 0 if j or first == 0 else 10,
        )
        after = ()
        if j:
            arrived.setdefault(first, []).append(swap(value, "resp", j))
            if part[1:] == groups[-1] and j == n_resp - 1:
                packed = pack_prompts(prompt_keys, prompt_values, (value,))
                stored = [packed] + [swap(packed, "resp", k) for k in range(1, n_resp)]
                outs = split_sum(owned, arrived[groups[0][0]], *groups[0])
                for i in range(groups[0][1]):
                    split[groups[0][0] + i] = outs[i]
                after = (outs[0],)
        elif part[1:] == groups[0] and len(groups) > 1:
            owned = value
        else:
            outs = split_sum(value, arrived[first], first, number)
            for i in range(number):
                split[first + i] = outs[i]
    totals = [totals[at] for at in sorted(totals)]
    chosen = select_prompts(
        ranks, counts, owner_slot, stored, n_fsdp, (split[1 % n_head],)
    )
    far_first = [k for first, number in groups for k in range(first, first + number) if k]
    summands = {k: swap(split[k], "head", k) for k in far_first}
    pieces = [chosen[0]] + [swap(chosen[k], "fsdp", k) for k in range(1, n_fsdp)]
    later = groups[-1][1] if len(groups) > 1 else 1
    far = sum_parts(
        [split[0]] + [summands[k] for k in range(later, n_head)], F32, (), 10
    )
    piece0 = sum_parts(
        [far] + [summands[k] for k in range(1, later)], BF16, tuple(pieces[1:])
    )

    n_q = queries.shape[1] // HD
    heads = [list(range(n_q // 2)), list(range(n_q // 2, n_q))]
    held = (
        ranks, counts, prompt_blocks, resp_blocks, queries, self_keys, self_values, d_out, pieces
    )
    along = {0: piece0}
    for k in range(1, n_head):
        if not k & (k - 1):
            along[k] = swap(piece0, "head", k)
    earlier = attention(heads[0], None, *held, (piece0,))
    hops = {}
    for k in range(1, n_head):
        low = k & -k
        if k != low:
            if k - low not in hops:
                hops[k - low] = relay([along[k - low]], (earlier[1],))
            along[k] = swap(hops[k - low], "head", low)
    last = n_head - 1
    passed = [[swap(hops.get(k, along[k]), "resp", j) for k in range(last)] for j in range(1, n_resp)]
    dq_parts, resp_grad, *parts = attention(heads[1], earlier, *held, tuple(hops.values()))
    sent_last = relay([along[last]], (parts[0], *[c for row in passed for c in row[:later]]))
    chunks = [along[k] for k in range(n_head)]
    for j in range(1, n_resp):
        chunks += passed[j - 1] + [swap(sent_last, "resp", j)]
    dq_parts = (earlier[0], dq_parts)
    pcat, pcat_t, gram = gather_gram(chunks, ())

    bits = [1 << b for b in range(n_fsdp.bit_length() - 1)]
    returned = [parts[0]] + [swap(parts[k], "fsdp", k) for k in range(1, n_fsdp)]
    w = back_part(pcat_t, totals, (gram, *returned[1:]))
    for bit in bits[:-1]:
        gram = sum_parts([gram, swap(gram, "fsdp", bit)], F32, (), 3)
    gram_parts = (gram, swap(gram, "fsdp", bits[-1]))
    for bit in bits[:-1]:
        w = sum_parts([w, swap(w, "fsdp", bit)], BF16, (gram_parts[1],), 0)
    w_other = swap(w, "fsdp", bits[-1])
    x = inverse_factor(*gram_parts)
    bt, y, squares = back_full(x, w, w_other, tuple(returned[1:]))
    from_head = [swap(squares, "head", k) for k in range(1, n_head)]
    half = len(totals) // 2
    slots = sum_by_slot(ranks, counts, owner_slot, returned, n_resp, (squares,))
    prompts = [slots[0]] + [swap(slots[j], "resp", j) for j in range(1, n_resp)]
    squares = sum_parts([squares] + from_head, F32, (slots[-1],))
    sums = sum_parts(
        [squares] + [swap(squares, "resp", j) for j in range(1, n_resp)], F32
    )
    momentum_out, dq, resp_grad, _ = new_momentum(
        ranks, pcat, totals[:half], y, n_resp, n_head, dq_parts, resp_grad, (squares,)
    )
    update, basis_out, momentum_out, prompt_grad = final_update(
        ranks, pcat, x, bt, y, [sums], totals[half:], prompts, momentum_out, gain, n_resp, n_head
    )
    return (dq, resp_grad, prompt_grad, update, momentum_out, basis_out)


def solution(mesh):
    placed = (
        P(("resp", "fsdp"), "head"),
        P(("resp", "fsdp"), "head"),
        P(("resp", "fsdp"), "head"),
        P(("resp", "fsdp"), "head"),
        P("resp", "fsdp", "head"),
        P("resp", "fsdp", "head"),
        P(),
        P(),
        P(),
        P(("resp", "fsdp")),
        P("fsdp", ("resp", "head")),
        P("fsdp", ("resp", "head")),
        P(("resp", "head"), None),
    )
    return jax.shard_map(
        on_device,
        mesh=mesh,
        in_specs=placed,
        out_specs=(
            P(("resp", "fsdp"), "head"),
            P(None, ("resp", "fsdp"), "head"),
            P(None, "resp", "fsdp", "head"),
            P("fsdp", ("resp", "head")),
            P("fsdp", ("resp", "head")),
            P(("resp", "head"), None),
        ),
        check_vma=False,
    )
```

```python
import functools
import math

import jax
import jax.numpy as jnp
from jax import lax
from jax.experimental import pallas as pl
from jax.experimental.pallas import tpu as pltpu
from jax.sharding import PartitionSpec as P

HD = 128
PANEL = 8
OUTER = 32
MIB = 1 << 20

momentum_keep = 0.95
norm_eps = 1e-06

F32 = jnp.float32
BF16 = jnp.bfloat16
HIGHEST = lax.Precision.HIGHEST

SMEM = pl.BlockSpec(memory_space=pltpu.SMEM)
VMEM = pl.BlockSpec(memory_space=pltpu.VMEM)
ANY = pl.BlockSpec(memory_space=pl.ANY)
HBM = pl.BlockSpec(memory_space=pltpu.HBM)


def swap(value, axes, k):
    axes = (axes,) if isinstance(axes, str) else axes
    n = math.prod(lax.axis_size(a) for a in axes)
    return lax.ppermute(value, axes, [(i, i ^ k) for i in range(n)])


def params(mib=6):
    return pltpu.CompilerParams(vmem_limit_bytes=mib * MIB)


def cost(weight=0):
    return pl.CostEstimate(flops=1 + weight * 10**9, bytes_accessed=1, transcendentals=0)


def halves(x):
    hi = x.astype(BF16)
    return hi, (x - hi.astype(F32)).astype(BF16)


def mm(a, b):
    return jnp.dot(a, b, preferred_element_type=F32)


def mm_full(a, b):
    return jnp.dot(a, b, precision=HIGHEST, preferred_element_type=F32)


def row_copies(ranks, n_head, part, mom, grad, mom_to, grad_to, sems):
    j, first, number = part
    chunk = mom_to.shape[0] // number
    pieces = 2 if chunk % 32 == 0 else 1
    size = chunk // pieces
    copies = []
    for i in range(number):
        at = ((ranks[0] ^ j) * n_head + (ranks[2] ^ (first + i))) * chunk
        copies.append([])
        for p in range(pieces):
            src = pl.ds(pl.multiple_of(at + p * size, size), size)
            dst = pl.ds(i * chunk + p * size, size)
            n = i * pieces + p
            copies[i].append(pltpu.make_async_copy(mom.at[src, :], mom_to.at[dst, :], sems.at[0, n]))
            copies[i].append(
                pltpu.make_async_copy(grad.at[src, :], grad_to.at[dst, :], sems.at[1, n])
            )
    return copies


def start_all(copies):
    for row in copies:
        for c in row:
            c.start()


def project_kernel(n_head, part, following, is_first, n_in, ranks, mom, grad, *refs):
    ins, refs = refs[:n_in], list(refs)
    number = part[2]
    sems = refs.pop()
    ahead = []
    if is_first:
        right_sem, right, grad_in = refs.pop(), refs.pop(), refs.pop()
    if following:
        next_grad, next_mom = refs.pop(), refs.pop()
        ahead = row_copies(ranks, n_head, following, mom, grad, next_mom, next_grad, sems.at[1])
    if is_first:
        b_lo, b_hi = refs.pop(), refs.pop()
        total, out = refs.pop(), refs.pop()
        mom_in = total
        copies = row_copies(ranks, n_head, part, mom, grad, mom_in, grad_in, sems.at[0])
        fetch = pltpu.make_async_copy(ins[0], right, right_sem)
        start_all(copies[:1])
        fetch.start()
        start_all(copies[1:])
        fetch.wait()
        hi, lo = halves(right[...])
        b_hi[...] = hi
        b_lo[...] = lo
    else:
        total, out = refs.pop(), refs.pop()
        b_hi, b_lo, mom_in, grad_in = ins
        copies = [[]] * number
        start_all(ahead)
    chunk = total.shape[0] // number
    for i in range(number):
        for c in copies[i]:
            c.wait()
        if is_first and i == 0:
            start_all(ahead)
        rows = slice(i * chunk, (i + 1) * chunk)
        t = mom_in[rows, :] + grad_in[rows, :].astype(F32)
        total[rows, :] = t
        t_hi, t_lo = halves(t)
        acc = mm(t_hi, b_hi[...]) + (mm(t_hi, b_lo[...]) + mm(t_lo, b_hi[...]))
        out[rows, :] = acc.astype(out.dtype)
    for row in ahead:
        for c in row:
            c.wait()


def project(
    ranks, momentum, grad_q, ins, part, following, n_resp, n_head, dtype, after, weight=0
):
    is_first = len(ins) == 1
    rows, cols = momentum.shape
    chunk = rows // (n_resp * n_head)
    size = part[2] * chunk
    if is_first:
        right = ins[0]
        rank = right.shape[1]
        specs = [HBM]
    else:
        rank = ins[0].shape[1]
        specs = [VMEM] * 4
    out_shape = [jax.ShapeDtypeStruct((size, rank), dtype), jax.ShapeDtypeStruct((size, cols), F32)]
    if is_first:
        out_shape += [jax.ShapeDtypeStruct((cols, rank), BF16)] * 2
    if following:
        ahead = following[2] * chunk
        out_shape += [
            jax.ShapeDtypeStruct((ahead, cols), F32), jax.ShapeDtypeStruct((ahead, cols), BF16)
        ]
    scratch = [pltpu.SemaphoreType.DMA((2, 2, 2 * n_head))]
    if is_first:
        scratch = [
            pltpu.VMEM((size, cols), BF16), pltpu.VMEM((cols, rank), F32), pltpu.SemaphoreType.DMA
        ] + scratch
    outs = pl.pallas_call(
        functools.partial(project_kernel, n_head, part, following, is_first, len(ins)),
        in_specs=[SMEM, HBM, HBM] + specs + [ANY] * len(after),
        out_specs=[VMEM] * len(out_shape),
        scratch_shapes=scratch,
        out_shape=out_shape,
        compiler_params=params(14),
        name="project",
        cost_estimate=cost(weight),
    )(ranks, momentum, grad_q, *ins, *after)
    right = tuple(outs[2:4]) if is_first else tuple(ins[:2])
    return outs[0], outs[1], right + tuple(outs[-2:] if following else ())


def split_kernel(n_recv, number, own, *refs):
    recvs, outs = refs[:n_recv], refs[-number:]
    chunk = outs[0].shape[0]
    for i in range(number):
        rows = slice(i * chunk, (i + 1) * chunk)
        acc = own[rows, :]
        for r in recvs:
            acc = acc + r[rows, :].astype(F32)
        outs[i][...] = acc.astype(outs[i].dtype)


def split_sum(own, recvs, first, number):
    rows, rank = own.shape
    chunk = rows // number
    return pl.pallas_call(
        functools.partial(split_kernel, len(recvs), number),
        in_specs=[VMEM] * (1 + len(recvs)),
        out_specs=[VMEM] * number,
        out_shape=[
            jax.ShapeDtypeStruct((chunk, rank), BF16 if first + i else F32)
            for i in range(number)
        ],
        compiler_params=params(),
        name="split_sum",
        cost_estimate=cost(),
    )(own, *recvs)


def sum_kernel(n_parts, *refs):
    acc = refs[0][...].astype(F32)
    for r in refs[1:n_parts]:
        acc = acc + r[...].astype(F32)
    refs[-1][...] = acc.astype(refs[-1].dtype)


def sum_parts(parts, dtype, after=(), weight=0):
    shape = parts[0].shape
    return pl.pallas_call(
        functools.partial(sum_kernel, len(parts)),
        in_specs=[VMEM] * len(parts) + [ANY] * len(after),
        out_specs=VMEM,
        out_shape=jax.ShapeDtypeStruct(shape, dtype),
        compiler_params=params(),
        name="sum_parts",
        cost_estimate=cost(weight),
    )(*parts, *after)


def relay_kernel(n_parts, *refs):
    out = refs[-1]
    size = out.shape[0] // n_parts
    for i in range(n_parts):
        out[i * size : (i + 1) * size, :] = refs[i][...]


def relay(parts, after):
    rows, rank = parts[0].shape
    return pl.pallas_call(
        functools.partial(relay_kernel, len(parts)),
        in_specs=[VMEM] * len(parts) + [ANY] * len(after),
        out_specs=VMEM,
        out_shape=jax.ShapeDtypeStruct((len(parts) * rows, rank), parts[0].dtype),
        compiler_params=params(),
        name="relay",
        cost_estimate=cost(),
    )(*parts, *after)


def gram_kernel(n_chunks, *refs):
    chunks, (pcat, pcat_t, gram) = refs[:n_chunks], refs[-3:]
    at = 0
    for c in chunks:
        pcat[at : at + c.shape[0], :] = c[...]
        at += c.shape[0]
    p = pcat[...]
    pt = p.T
    pcat_t[...] = pt
    half = p.shape[1] // 2
    gram[:half, :] = mm(pt[:half, :], p[:, :half])
    low = mm(pt[half:, :], p)
    gram[half : 2 * half, :] = low[:, :half]
    gram[2 * half :, :] = low[:, half:]


def gather_gram(chunks, after):
    rank = chunks[0].shape[1]
    rows = sum(c.shape[0] for c in chunks)
    return pl.pallas_call(
        functools.partial(gram_kernel, len(chunks)),
        in_specs=[VMEM] * len(chunks) + [ANY] * len(after),
        out_specs=[VMEM] * 3,
        out_shape=[
            jax.ShapeDtypeStruct((rows, rank), BF16),
            jax.ShapeDtypeStruct((rank, rows), BF16),
            jax.ShapeDtypeStruct((3 * rank // 2, rank // 2), F32),
        ],
        compiler_params=params(8),
        name="gather_gram",
        cost_estimate=cost(),
    )(*chunks, *after)


def back_part_kernel(n_totals, pcat_t, *refs):
    totals, out = refs[:n_totals], refs[-1]
    seg = totals[0].shape[0]
    step = min(seg, 512)
    acc = None
    for j, total in enumerate(totals):
        for i in range(0, seg, step):
            t_hi, t_lo = halves(total[i : i + step, :])
            pt = pcat_t[:, j * seg + i : j * seg + i + step]
            part = mm(pt, t_hi) + mm(pt, t_lo)
            acc = part if acc is None else acc + part
    out[...] = acc.astype(BF16)


def back_part(pcat_t, totals, after):
    rank = pcat_t.shape[0]
    seg, cols = totals[0].shape
    rows = seg * len(totals)
    return pl.pallas_call(
        functools.partial(back_part_kernel, len(totals)),
        in_specs=[VMEM] * (1 + len(totals)) + [ANY] * len(after),
        out_specs=VMEM,
        out_shape=jax.ShapeDtypeStruct((rank, cols), BF16),
        compiler_params=params(14),
        name="back_part",
        cost_estimate=cost(5),
    )(pcat_t, *totals, *after)


def factor_panel(panel, off):
    shape = (PANEL, 128)
    d = {}
    for j in range(PANEL):
        col = jnp.broadcast_to(panel[:, off + j : off + j + 1], shape)
        for i in range(j, PANEL):
            d[i, j] = jnp.broadcast_to(col[i : i + 1, :], shape)
    low, inv = {}, {}
    for j in range(0, PANEL, 2):
        a, b, c = d[j, j], d[j + 1, j], d[j + 1, j + 1]
        first = lax.rsqrt(a)
        second = lax.rsqrt(a * c - b * b) * (a * first)
        inv[j, j], inv[j + 1, j + 1] = first, second
        low[j + 1, j] = b * first
        for i in range(j + 2, PANEL):
            low[i, j] = d[i, j] * first
            low[i, j + 1] = (d[i, j + 1] - low[i, j] * low[j + 1, j]) * second
        for k in range(j + 2, PANEL):
            for i in range(k, PANEL):
                d[i, k] = d[i, k] - (low[i, j] * low[k, j] + low[i, j + 1] * low[k, j + 1])
    for j in range(PANEL):
        for i in range(j + 1, PANEL):
            acc = low[i, j] * inv[j, j]
            for k in range(j + 1, i):
                acc = acc + low[i, k] * inv[k, j]
            inv[i, j] = -(acc * inv[i, i])
    return inv


def three_parts(x):
    a = x.astype(BF16)
    rest = x - a.astype(F32)
    b = rest.astype(BF16)
    return a, b, (rest - b.astype(F32)).astype(BF16)


def cholesky_kernel(n_parts, *refs):
    parts, out, work = refs[:n_parts], refs[n_parts], refs[n_parts + 1]
    n = out.shape[0]
    half = n // 2
    tiles = n // 128 + 1
    total = parts[0][...]
    for part in parts[1:]:
        total = total + part[...]
    low = total[half : 2 * half, :]
    work[:half, :half] = total[:half, :]
    work[half:, :half] = low
    work[:half, half:] = low.T
    work[half:, half:] = total[2 * half :, :]
    eye = lax.broadcasted_iota(jnp.int32, (n, n), 0) == lax.broadcasted_iota(jnp.int32, (n, n), 1)
    whole = work[...]
    diag = jnp.where(eye, whole, 0.0)
    across = lax.rsqrt(jnp.sum(diag, axis=0, keepdims=True))
    work[...] = whole * lax.rsqrt(jnp.sum(diag, axis=1, keepdims=True)) * across
    sub = lax.broadcasted_iota(jnp.int32, (PANEL, 128), 0)
    lane = lax.broadcasted_iota(jnp.int32, (PANEL, 128), 1)
    n_panels = OUTER // PANEL

    def step(o, carry):
        blk = [
            [work[p * PANEL : (p + 1) * PANEL, t * 128 : (t + 1) * 128] for t in range(tiles - 1)]
            + [jnp.where(lane == sub + p * PANEL, 1.0, 0.0).astype(F32)]
            for p in range(n_panels)
        ]
        for p in range(n_panels):
            off = p * PANEL
            inv = factor_panel(blk[p][0], off)
            rows_of = [
                [jnp.broadcast_to(blk[p][t][j : j + 1, :], (PANEL, 128)) for t in range(tiles)]
                for j in range(PANEL)
            ]
            new = [None] * tiles
            for j in range(PANEL):
                col = inv[PANEL - 1, j]
                for i in range(PANEL - 2, j - 1, -1):
                    col = jnp.where(sub == i, inv[i, j], col)
                if j:
                    col = jnp.where(sub < j, 0.0, col)
                for t in range(tiles):
                    term = col * rows_of[j][t]
                    new[t] = term if new[t] is None else new[t] + term
            blk[p] = new
            if p + 1 < n_panels:
                u_rows = [
                    [jnp.broadcast_to(new[t][j : j + 1, :], (PANEL, 128)) for t in range(tiles)]
                    for j in range(PANEL)
                ]
                for b in range(p + 1, n_panels):
                    lanes = [
                        jnp.broadcast_to(blk[b][0][:, off + m : off + m + 1], (PANEL, 128))
                        for m in range(PANEL)
                    ]
                    upd = list(blk[b])
                    for k in range(PANEL):
                        v = lanes[0] * inv[k, 0]
                        for m in range(1, k + 1):
                            v = v + lanes[m] * inv[k, m]
                        for t in range(tiles):
                            upd[t] = upd[t] - v * u_rows[k][t]
                    blk[b] = upd
        u = jnp.concatenate([jnp.concatenate(row, axis=1) for row in blk], axis=0)
        u = pltpu.roll(u, tiles * 128 - OUTER, 1)[:, :n]
        at = lax.broadcasted_iota(jnp.int32, (OUTER, n), 1)
        left = jnp.where(at < n - OUTER * (o + 1), u, 0.0)
        la, lb, lc = three_parts(left)
        ua, ub, uc = three_parts(u)
        lhs = jnp.concatenate([la, la, lb, la, lc, lb], axis=0)
        rhs = jnp.concatenate([ua, ub, ua, uc, ua, ub], axis=0)
        upd = mm(lhs.T, rhs)
        rest = work[OUTER:, :]
        lanes_at = lax.broadcasted_iota(jnp.int32, rest.shape, 1)
        rest = pltpu.roll(jnp.where(lanes_at < OUTER, 0.0, rest), n - OUTER, 1)
        work[: n - OUTER, :] = rest - upd[: n - OUTER, :]
        work[n - OUTER :, :] = u
        return carry

    lax.fori_loop(0, n // OUTER, step, 0)
    out[...] = work[...] * across


def inverse_factor(*parts):
    n = 2 * parts[0].shape[1]
    return pl.pallas_call(
        functools.partial(cholesky_kernel, len(parts)),
        in_specs=[VMEM] * len(parts),
        out_specs=VMEM,
        scratch_shapes=[pltpu.VMEM((n, n), F32)],
        out_shape=jax.ShapeDtypeStruct((n, n), F32),
        compiler_params=params(),
        name="inverse_factor",
        cost_estimate=cost(2),
    )(*parts)


def mm_three(a, b):
    a_hi, a_lo = halves(a)
    b_hi, b_lo = halves(b)
    return mm(a_hi, b_hi) + (mm(a_hi, b_lo) + mm(a_lo, b_hi))


def back_kernel(x, wa, wb, *refs):
    bt_out, y_out, s_out = refs[-3:]
    w = wa[...].astype(F32) + wb[...].astype(F32)
    bt = mm_three(x[...], w)
    bt_out[...] = bt
    s = jnp.sum(bt * bt, axis=1, keepdims=True)
    s_out[...] = jnp.broadcast_to(s, (s.shape[0], 128)).T[:8, :]
    y_out[...] = ((1.0 - momentum_keep) * mm(x[...].T.astype(BF16), bt.astype(BF16))).astype(BF16)


def back_full(x, wa, wb, after):
    rank, cols = wa.shape
    return pl.pallas_call(
        back_kernel,
        in_specs=[VMEM] * 3 + [ANY] * len(after),
        out_specs=[VMEM] * 3,
        out_shape=[
            jax.ShapeDtypeStruct((rank, cols), F32),
            jax.ShapeDtypeStruct((rank, cols), BF16),
            jax.ShapeDtypeStruct((8, rank), F32),
        ],
        compiler_params=params(),
        name="back_full",
        cost_estimate=cost(),
    )(x, wa, wb, *after)


def row_blocks(ranks, n_resp, n_head, chunk):
    return [
        pl.multiple_of(((ranks[0] ^ j) * n_head + (ranks[2] ^ k)) * chunk, chunk)
        for j in range(n_resp)
        for k in range(n_head)
    ]


def momentum_rows(blocks, pcat, y, totals, held, out, sems, begin, end):
    chunk = held.shape[0] // (end - begin)
    seg = totals[0].shape[0]
    copies = []
    for i in range(begin, end):
        rows = slice(i * chunk, (i + 1) * chunk)
        kept = slice((i - begin) * chunk, (i - begin + 1) * chunk)
        off = i * chunk % seg
        total = totals[(i - begin) * chunk // seg][off : off + chunk, :]
        held[kept, :] = total - mm(pcat[rows, :], y[...])
        copies.append(
            pltpu.make_async_copy(
                held.at[kept, :], out.at[pl.ds(blocks[i], chunk), :], sems.at[i - begin]
            )
        )
        copies[-1].start()
    return copies


def momentum_kernel(n_resp, n_head, n_totals, ranks, pcat, y, *refs):
    totals, refs = refs[:n_totals], refs[n_totals:]
    dq_parts, rg, refs = refs[:2], refs[2], refs[-7:]
    out, dq, resp_grad, token, held, sems, more = refs
    token[...] = jnp.zeros_like(token)
    width = dq_parts[0].shape[1]
    copies = [
        pltpu.make_async_copy(part, dq.at[:, pl.ds(i * width, width)], more.at[i])
        for i, part in enumerate(dq_parts)
    ]
    copies.append(pltpu.make_async_copy(rg, resp_grad, more.at[2]))
    n = n_resp * n_head
    blocks = row_blocks(ranks, n_resp, n_head, pcat.shape[0] // n)
    copies[2].start()
    moved = momentum_rows(blocks, pcat, y, totals, held, out, sems, 0, n // 2)
    for c in copies[:2]:
        c.start()
    for c in copies + moved:
        c.wait()


def new_momentum(ranks, pcat, totals, y, n_resp, n_head, dq_parts, rg, after):
    rows, rank = pcat.shape
    cols = totals[0].shape[1]
    length, width = dq_parts[0].shape
    return pl.pallas_call(
        functools.partial(momentum_kernel, n_resp, n_head, len(totals)),
        in_specs=[SMEM] + [VMEM] * (5 + len(totals)) + [ANY] * len(after),
        out_specs=[HBM, HBM, HBM, VMEM],
        scratch_shapes=[
            pltpu.VMEM((rows // 2, cols), F32),
            pltpu.SemaphoreType.DMA((n_resp * n_head // 2,)),
            pltpu.SemaphoreType.DMA((3,)),
        ],
        out_shape=[
            jax.ShapeDtypeStruct((rows, cols), F32),
            jax.ShapeDtypeStruct((length, 2 * width), BF16),
            jax.ShapeDtypeStruct(rg.shape, BF16),
            jax.ShapeDtypeStruct((8, 128), F32),
        ],
        compiler_params=params(12),
        name="new_momentum",
        cost_estimate=cost(5),
    )(ranks, pcat, y, *totals, *dq_parts, rg, *after)


def update_kernel(gain, n_resp, n_head, n_sums, n_totals, n_prompt, ranks, pcat, x, bt, y, *refs):
    sums, refs = refs[:n_sums], refs[n_sums:]
    totals, refs = refs[:n_totals], refs[n_totals:]
    prompts, refs = refs[:n_prompt], refs[n_prompt + 1 :]
    upd, basis_out, mom_out, prompt_out, held, held_mom, held_basis, held_prompt, sems, more = refs
    n = n_resp * n_head
    chunk = pcat.shape[0] // n
    blocks = row_blocks(ranks, n_resp, n_head, chunk)
    total = sums[0][...]
    for s in sums[1:]:
        total = total + s[...]
    scale = lax.rsqrt(total + norm_eps).T[:, :1]
    scaled = bt[...] * scale
    held_basis[...] = scaled.T
    acc = prompts[0][...]
    for p in prompts[1:]:
        acc = acc + p[...].astype(F32)
    held_prompt[...] = acc
    copies = [
        pltpu.make_async_copy(held_basis, basis_out, more.at[0]),
        pltpu.make_async_copy(held_prompt, prompt_out, more.at[1]),
    ]
    for c in copies:
        c.start()
    copies += momentum_rows(blocks, pcat, y, totals, held_mom, mom_out, sems.at[1], n // 2, n)
    z_hi, z_lo = halves(gain * mm_three(x[...].T, scaled))
    for i, at in enumerate(blocks):
        rows = slice(i * chunk, (i + 1) * chunk)
        p = pcat[rows, :]
        held[rows, :] = (mm(p, z_hi) + mm(p, z_lo)).astype(BF16)
        copies.append(
            pltpu.make_async_copy(held.at[rows, :], upd.at[pl.ds(at, chunk), :], sems.at[0, i])
        )
        copies[-1].start()
    for c in copies:
        c.wait()


def final_update(ranks, pcat, x, bt, y, sums, totals, prompts, momentum, gain, n_resp, n_head):
    rows, rank = pcat.shape
    cols = bt.shape[1]
    n_vmem = 4 + len(sums) + len(totals) + len(prompts)
    return pl.pallas_call(
        functools.partial(
            update_kernel, gain, n_resp, n_head, len(sums), len(totals), len(prompts)
        ),
        in_specs=[SMEM] + [VMEM] * n_vmem + [HBM],
        out_specs=[HBM] * 4,
        scratch_shapes=[
            pltpu.VMEM((rows, cols), BF16),
            pltpu.VMEM((rows // 2, cols), F32),
            pltpu.VMEM((cols, rank), F32),
            pltpu.VMEM(prompts[0].shape, F32),
            pltpu.SemaphoreType.DMA((2, n_resp * n_head)),
            pltpu.SemaphoreType.DMA((2,)),
        ],
        out_shape=[
            jax.ShapeDtypeStruct((rows, cols), BF16),
            jax.ShapeDtypeStruct((cols, rank), F32),
            jax.ShapeDtypeStruct((rows, cols), F32),
            jax.ShapeDtypeStruct(prompts[0].shape, F32),
        ],
        input_output_aliases={1 + n_vmem: 2},
        compiler_params=params(14),
        name="final_update",
        cost_estimate=cost(5),
    )(ranks, pcat, x, bt, y, *sums, *totals, *prompts, momentum)


def group_of(counts, response):
    group = jnp.int32(0)
    end = jnp.int32(0)
    for g in range(counts.shape[0]):
        end = end + counts[g]
        group = group + (end <= response).astype(jnp.int32)
    return group


def pack_kernel(*refs):
    keys, values, out = refs[0], refs[1], refs[-1]
    out[0] = keys[...]
    out[1] = values[...]


def pack_prompts(keys, values, after):
    return pl.pallas_call(
        pack_kernel,
        in_specs=[VMEM] * 2 + [ANY] * len(after),
        out_specs=VMEM,
        out_shape=jax.ShapeDtypeStruct((2,) + keys.shape, BF16),
        compiler_params=params(),
        name="pack_prompts",
        cost_estimate=cost(),
    )(keys, values, *after)


def select_kernel(n_resp, n_fsdp, ranks, counts, slots, *refs):
    stored, outs = refs[:n_resp], refs[-n_fsdp:]
    held = stored[0].shape[1]
    for k in range(n_fsdp):
        slot = slots[group_of(counts, ranks[0] * n_fsdp + (ranks[1] ^ k))]
        owner, local = slot // held, slot % held
        for j in range(n_resp):

            @pl.when(owner == (ranks[0] ^ j))
            def _():
                outs[k][0] = stored[j][0, local]
                outs[k][1] = stored[j][1, local]


def select_prompts(ranks, counts, slots, stored, n_fsdp, after):
    _, _, piece, width = stored[0].shape
    return pl.pallas_call(
        functools.partial(select_kernel, len(stored), n_fsdp),
        in_specs=[SMEM] * 3 + [VMEM] * len(stored) + [ANY] * len(after),
        out_specs=[VMEM] * n_fsdp,
        out_shape=[jax.ShapeDtypeStruct((2, piece, width), BF16)] * n_fsdp,
        compiler_params=params(),
        name="select_prompts",
        cost_estimate=cost(),
    )(ranks, counts, slots, *stored, *after)


def attention_kernel(
    n_fsdp, heads, last, ranks, counts, prompt_blocks, resp_blocks, q, sk, sv, go, *refs
):
    pieces, refs = refs[:n_fsdp], refs[n_fsdp:]
    keys, values, dk, dv = refs[-4:]
    n_out = 2 + n_fsdp if last else 3
    outs = refs[-4 - n_out : -4]
    dq = outs[0]
    piece = pieces[0].shape[1]
    cap = piece * n_fsdp
    length = q.shape[0]
    scale = HD ** (-0.5)
    for k in range(n_fsdp):
        rows = pl.ds(pl.multiple_of((ranks[1] ^ k) * piece, piece), piece)
        keys[rows, :] = pieces[k][0]
        values[rows, :] = pieces[k][1]
    keys[cap:, :] = sk[...]
    values[cap:, :] = sv[...]
    prompt_len = prompt_blocks[group_of(counts, ranks[0] * n_fsdp + ranks[1])] * 128
    resp_len = resp_blocks[0] * 128
    width = keys.shape[0]
    place = lax.broadcasted_iota(jnp.int32, (width, length), 0)
    pos = lax.broadcasted_iota(jnp.int32, (width, length), 1)
    inner = place - cap
    seen = ((place < cap) & (place < prompt_len)) | (
        (place >= cap) & (inner <= pos) & (inner < resp_len)
    )
    bias = jnp.where(seen, 0.0, -jnp.inf).astype(F32)
    live = lax.broadcasted_iota(jnp.int32, (length, HD), 0) < resp_len
    nt = (((1,), (1,)), ((), ()))
    kall = keys[...]
    vall = values[...]
    kt = kall.T
    if last:
        dk[...] = refs[0][...]
        dv[...] = refs[1][...]
    else:
        dk[...] = jnp.zeros_like(dk)
        dv[...] = jnp.zeros_like(dv)
    for i, h in enumerate(heads):
        cols = slice(h * HD, (h + 1) * HD)
        qh = q[:, cols]
        gh = jnp.where(live, go[:, cols], jnp.zeros((), BF16))
        logits = lax.dot_general(kall, qh, nt, preferred_element_type=F32) * scale + bias
        peak = jnp.max(logits, axis=0, keepdims=True)
        e = jnp.exp(logits - peak)
        w = (e * (1.0 / jnp.sum(e, axis=0, keepdims=True))).astype(BF16)
        dp = lax.dot_general(vall, gh, nt, preferred_element_type=F32)
        wf = w.astype(F32)
        diag = jnp.sum(wf * dp, axis=0, keepdims=True)
        ds = (wf * (dp - diag)).astype(BF16)
        dk[...] += mm(ds, qh)
        dv[...] += mm(w, gh)
        dq[:, i * HD : (i + 1) * HD] = (mm(kt, ds) * scale).T.astype(BF16)
    if last:
        own, sends = outs[1], outs[2:]
        own[0] = (dk[cap:, :] * scale).astype(BF16)
        own[1] = dv[cap:, :].astype(BF16)
        for k in range(n_fsdp):
            rows = pl.ds(pl.multiple_of((ranks[1] ^ k) * piece, piece), piece)
            sends[k][0] = (dk[rows, :] * scale).astype(sends[k].dtype)
            sends[k][1] = dv[rows, :].astype(sends[k].dtype)
    else:
        outs[1][...] = dk[...]
        outs[2][...] = dv[...]


def attention(heads, earlier, ranks, counts, prompt_blocks, resp_blocks, q, sk, sv, go, pieces, after):
    n_fsdp = len(pieces)
    piece = pieces[0].shape[1]
    length, width = q.shape
    cap = piece * n_fsdp
    total = cap + length
    last = earlier is not None
    dq_shape = jax.ShapeDtypeStruct((length, len(heads) * HD), BF16)
    if last:
        extra, specs = (earlier[1], earlier[2]), [VMEM] * 2
        out_shape = [dq_shape, jax.ShapeDtypeStruct((2, length, HD), BF16)] + [
            jax.ShapeDtypeStruct((2, piece, HD), BF16 if k else F32) for k in range(n_fsdp)
        ]
    else:
        extra, specs = (), []
        out_shape = [dq_shape] + [jax.ShapeDtypeStruct((total, HD), F32)] * 2
    return pl.pallas_call(
        functools.partial(attention_kernel, n_fsdp, heads, last),
        in_specs=[SMEM] * 4 + [VMEM] * (4 + n_fsdp) + specs + [ANY] * len(after),
        out_specs=[VMEM] * len(out_shape),
        scratch_shapes=[pltpu.VMEM((total, HD), BF16)] * 2 + [pltpu.VMEM((total, HD), F32)] * 2,
        out_shape=out_shape,
        compiler_params=params(12),
        name="attention",
        cost_estimate=cost(),
    )(ranks, counts, prompt_blocks, resp_blocks, q, sk, sv, go, *pieces, *extra, *after)


def by_slot_kernel(n_resp, n_fsdp, ranks, counts, slots, *refs):
    parts, outs = refs[:n_fsdp], refs[-n_resp:]
    held = outs[0].shape[1]
    slot_of = [
        slots[group_of(counts, ranks[0] * n_fsdp + (ranks[1] ^ k))] for k in range(n_fsdp)
    ]
    for j in range(n_resp):
        for local in range(held):
            slot = (ranks[0] ^ j) * held + local
            acc = jnp.zeros(parts[0].shape, F32)
            for k in range(n_fsdp):
                acc = acc + jnp.where(slot_of[k] == slot, parts[k][...].astype(F32), 0.0)
            outs[j][:, local] = acc.astype(outs[j].dtype)


def sum_by_slot(ranks, counts, slots, parts, n_resp, after):
    held = counts.shape[0] // n_resp
    _, piece, width = parts[0].shape
    return pl.pallas_call(
        functools.partial(by_slot_kernel, n_resp, len(parts)),
        in_specs=[SMEM] * 3 + [VMEM] * len(parts) + [ANY] * len(after),
        out_specs=[VMEM] * n_resp,
        out_shape=[
            jax.ShapeDtypeStruct((2, held, piece, width), BF16 if j else F32)
            for j in range(n_resp)
        ],
        compiler_params=params(),
        name="sum_by_slot",
        cost_estimate=cost(),
    )(ranks, counts, slots, *parts, *after)


def on_device(
    queries,
    self_keys,
    self_values,
    d_out,
    prompt_keys,
    prompt_values,
    counts,
    owner_slot,
    prompt_blocks,
    resp_blocks,
    grad_q,
    momentum,
    basis,
):
    n_resp, n_fsdp, n_head = (lax.axis_size(a) for a in ("resp", "fsdp", "head"))
    ranks = jnp.stack([lax.axis_index(a) for a in ("resp", "fsdp", "head")]).astype(jnp.int32)
    gain = math.sqrt(
        momentum.shape[0] * n_fsdp * momentum.shape[1] * n_resp * n_head / basis.shape[1]
    )

    in_hbm = [pltpu.with_memory_space_constraint(a, pltpu.HBM) for a in (momentum, grad_q, basis)]
    half = n_head // 2
    groups = [(half, half), (0, half)] if half else [(0, n_head)]

    mom_hbm, grad_hbm, basis_hbm = in_hbm
    order = [(j, *group) for group in groups for j in [*range(1, n_resp), 0]]
    nexts = dict(zip(order, order[1:] + [None]))
    totals, arrived, split, ins, after = {}, {}, {}, (basis_hbm,), ()
    for part in order:
        j, first, number = part
        value, totals[part[:2]], ins = project(
            ranks, mom_hbm, grad_hbm, ins, part, nexts[part], n_resp, n_head, BF16 if j else F32,
            after, 0 if j or first == 0 else 10,
        )
        after = ()
        if j:
            arrived.setdefault(first, []).append(swap(value, "resp", j))
            if part[1:] == groups[-1] and j == n_resp - 1:
                packed = pack_prompts(prompt_keys, prompt_values, (value,))
                stored = [packed] + [swap(packed, "resp", k) for k in range(1, n_resp)]
                outs = split_sum(owned, arrived[groups[0][0]], *groups[0])
                for i in range(groups[0][1]):
                    split[groups[0][0] + i] = outs[i]
                after = (outs[0],)
        elif part[1:] == groups[0] and len(groups) > 1:
            owned = value
        else:
            outs = split_sum(value, arrived[first], first, number)
            for i in range(number):
                split[first + i] = outs[i]
    totals = [totals[at] for at in sorted(totals)]
    chosen = select_prompts(
        ranks, counts, owner_slot, stored, n_fsdp, (split[1 % n_head],)
    )
    far_first = [k for first, number in groups for k in range(first, first + number) if k]
    summands = {k: swap(split[k], "head", k) for k in far_first}
    pieces = [chosen[0]] + [swap(chosen[k], "fsdp", k) for k in range(1, n_fsdp)]
    later = groups[-1][1] if len(groups) > 1 else 1
    far = sum_parts(
        [split[0]] + [summands[k] for k in range(later, n_head)], F32, (), 10
    )
    piece0 = sum_parts(
        [far] + [summands[k] for k in range(1, later)], BF16, tuple(pieces[1:])
    )

    n_q = queries.shape[1] // HD
    heads = [list(range(n_q // 2)), list(range(n_q // 2, n_q))]
    held = (
        ranks, counts, prompt_blocks, resp_blocks, queries, self_keys, self_values, d_out, pieces
    )
    along = {0: piece0}
    for k in range(1, n_head):
        if not k & (k - 1):
            along[k] = swap(piece0, "head", k)
    earlier = attention(heads[0], None, *held, (piece0,))
    hops = {}
    for k in range(1, n_head):
        low = k & -k
        if k != low:
            if k - low not in hops:
                hops[k - low] = relay([along[k - low]], (earlier[1],))
            along[k] = swap(hops[k - low], "head", low)
    last = n_head - 1
    passed = [[swap(hops.get(k, along[k]), "resp", j) for k in range(last)] for j in range(1, n_resp)]
    dq_parts, resp_grad, *parts = attention(heads[1], earlier, *held, tuple(hops.values()))
    sent_last = relay([along[last]], (parts[0], *[c for row in passed for c in row[:later]]))
    chunks = [along[k] for k in range(n_head)]
    for j in range(1, n_resp):
        chunks += passed[j - 1] + [swap(sent_last, "resp", j)]
    dq_parts = (earlier[0], dq_parts)
    pcat, pcat_t, gram = gather_gram(chunks, ())

    bits = [1 << b for b in range(n_fsdp.bit_length() - 1)]
    returned = [parts[0]] + [swap(parts[k], "fsdp", k) for k in range(1, n_fsdp)]
    w = back_part(pcat_t, totals, (gram, *returned[1:]))
    for bit in bits[:-1]:
        gram = sum_parts([gram, swap(gram, "fsdp", bit)], F32, (), 3)
    gram_parts = (gram, swap(gram, "fsdp", bits[-1]))
    for bit in bits[:-1]:
        w = sum_parts([w, swap(w, "fsdp", bit)], BF16, (gram,), 5)
    w_other = swap(w, "fsdp", bits[-1])
    x = inverse_factor(*gram_parts)
    bt, y, squares = back_full(x, w, w_other, tuple(returned[1:]))
    from_head = [swap(squares, "head", k) for k in range(1, n_head)]
    half = len(totals) // 2
    slots = sum_by_slot(ranks, counts, owner_slot, returned, n_resp, (squares,))
    prompts = [slots[0]] + [swap(slots[j], "resp", j) for j in range(1, n_resp)]
    squares = sum_parts([squares] + from_head, F32, (slots[-1],))
    sums = sum_parts(
        [squares] + [swap(squares, "resp", j) for j in range(1, n_resp)], F32
    )
    momentum_out, dq, resp_grad, _ = new_momentum(
        ranks, pcat, totals[:half], y, n_resp, n_head, dq_parts, resp_grad, (squares,)
    )
    update, basis_out, momentum_out, prompt_grad = final_update(
        ranks, pcat, x, bt, y, [sums], totals[half:], prompts, momentum_out, gain, n_resp, n_head
    )
    return (dq, resp_grad, prompt_grad, update, momentum_out, basis_out)


def solution(mesh):
    placed = (
        P(("resp", "fsdp"), "head"),
        P(("resp", "fsdp"), "head"),
        P(("resp", "fsdp"), "head"),
        P(("resp", "fsdp"), "head"),
        P("resp", "fsdp", "head"),
        P("resp", "fsdp", "head"),
        P(),
        P(),
        P(),
        P(("resp", "fsdp")),
        P("fsdp", ("resp", "head")),
        P("fsdp", ("resp", "head")),
        P(("resp", "head"), None),
    )
    return jax.shard_map(
        on_device,
        mesh=mesh,
        in_specs=placed,
        out_specs=(
            P(("resp", "fsdp"), "head"),
            P(None, ("resp", "fsdp"), "head"),
            P(None, "resp", "fsdp", "head"),
            P("fsdp", ("resp", "head")),
            P("fsdp", ("resp", "head")),
            P(("resp", "head"), None),
        ),
        check_vma=False,
    )
```
